32 devices in a mesh: ctx: 8 (over y, x, core), head: 4 (over z).
Axes of the slice: x: 2, y: 2, z: 4, core: 2. Of those that a mesh axis runs over, the one named last changes fastest.
Arguments:
- queries: bfloat16 [512, 128, 192], P('ctx', 'head'), may hold values from -84 to 84
- latent_keys: bfloat16 [512, 576], P('ctx'), may hold values from -12 to 12
- out_grad: bfloat16 [512, 128, 128], P('ctx', 'head'), may hold values from -6 to 6
- up_weight: bfloat16 [512, 128, 256], P(None, 'head'), may hold values from -0.25 to 0.25
- segment_ids: int32 [512], replicated, may hold values from 0 to 15, never falling along the last dimension, each value on 1 to 64 neighbouring positions
Outputs:
- query_grad: float32 [512, 128, 192], P('ctx', 'head')
- key_grad: float32 [512, 576], P('ctx', 'head')
- weight_grad: float32 [512, 128, 256], P('ctx', 'head')
The draws below stay inside these ranges and needn't reach their ends.
Inputs may be any that keep to these rules, and one draw needn't show every extreme that they name: `segment_ids`: segment numbers never fall along the slab; each trace has 1 to 64 tokens and one has exactly 64.
All inputs are finite; a program needn't handle non-finite values.
Results may differ from the reference program's by a relative error of at most 0.0053.
Values may be sent and summed in bfloat16 or wider, within the bound.
No kernel may reach another device: no remote copies, remote signals or barrier semaphores. Data moves between devices by JAX's collectives and lax.ppermute only.
A program may use at most 128 MiB of HBM per device.

```python
import math
import jax
import jax.numpy as jnp
import numpy as np
from jax import lax

HEADS = 128
LAT = 512
ROPE = 64
PLAIN_WIDTH = 128
VDIM = 128
TOK_DEV = 64
REACH = 1
TOKENS = 512
MOST = 64
SEGS = 16
N_CTX = 8


def shared_rope(key):
    base = jax.random.normal(jax.random.fold_in(key, 11), (TOKENS, ROPE), jnp.float32)
    return jnp.clip(base, -4.0, 4.0)


def draw_latent_keys(key, part):
    latent = jnp.clip(jax.random.normal(jax.random.fold_in(key, 3), (TOKENS, LAT), jnp.float32), -4.0, 4.0)
    order = jax.random.permutation(jax.random.fold_in(key, 5), N_CTX)
    row_block = jnp.arange(TOKENS) // TOK_DEV
    col_block = jnp.arange(LAT) // (LAT // N_CTX)
    boost = jnp.where(order[row_block][:, None] == col_block[None, :], 3.0, 1.0)
    latent = latent * boost
    rope = shared_rope(key)
    return jnp.concatenate([latent, rope], 1).astype(jnp.bfloat16)


def draw_queries(key, part):
    base = jax.random.normal(jax.random.fold_in(key, 7), (TOKENS, HEADS, PLAIN_WIDTH + ROPE), jnp.float32)
    base = jnp.clip(base, -4.0, 4.0)
    return base.astype(jnp.bfloat16)


def block_scale(own_key, dims, pieces, low, high):
    def one(axis_at, shards_of):
        heights = jax.random.uniform(jax.random.fold_in(jax.random.fold_in(own_key, 6), axis_at), (shards_of,), jnp.float32, low / len(pieces), high / len(pieces))
        return jnp.repeat(jnp.exp(heights), dims[axis_at] // shards_of).reshape((-1,) + (1,) * (len(dims) - axis_at - 1))

    loudness = one(*pieces[0])
    for cut in pieces[1:]:
        loudness = loudness * one(*cut)
    return loudness


def profile(amount, total, most, skew):
    weights = [(1 << 20) // math.isqrt(rank ** skew) + 1 for rank in range(2, amount + 1)]
    spare, given = total - most - (amount - 1), [1] * (amount - 1)
    while spare > 0:
        movable = [i for i in range(amount - 1) if given[i] < most]
        pool, left = sum([weights[i] for i in movable]), spare
        for i in movable:
            addition = min(most - given[i], max(1, left * weights[i] // pool), spare)
            given[i] = given[i] + addition
            spare = spare - addition
    return np.array([most] + given)


def ragged_sizes(own_key, count, total, reach, lean):
    if count == 2:
        one = jax.random.randint(own_key, (), max(1, total - reach), min(reach, total - 1) + 1)
        return jnp.stack([one, total - one])
    sizes = jnp.asarray(profile(count, total, reach, lean), jnp.int32)
    couples = (count - 1) // 2
    source_of, taker = sizes[1:1 + 2 * couples:2], sizes[2:2 + 2 * couples:2]
    slack = jnp.minimum(source_of - 1, reach - taker)
    shifted = jax.random.randint(jax.random.fold_in(own_key, 1), (couples,), 0, 1 << 20) % (slack + 1)
    sizes = sizes.at[1:1 + 2 * couples:2].set(source_of - shifted).at[2:2 + 2 * couples:2].set(taker + shifted)
    return sizes[jax.random.permutation(jax.random.fold_in(own_key, 2), count)]


def noise(rng, shape, spread, bound, split=(), dtype=jnp.bfloat16):
    drawn = spread * jax.random.normal(rng, shape, jnp.float32)
    if split:
        drawn = drawn * block_scale(rng, shape, split, -0.22, 0.18)
    return jnp.clip(drawn, -bound, bound).astype(dtype)


def setup_inputs(seed: int = 0) -> dict:
    streams_of = jax.random.split(jax.random.key(seed), 6)
    return {
        "queries": draw_queries(jax.random.fold_in(streams_of[5], 71), 0),
        "latent_keys": draw_latent_keys(jax.random.fold_in(streams_of[5], 71), 0),
        "out_grad": noise(streams_of[2], (TOKENS, HEADS, VDIM), 1.0, 6.0, ((0, 8), (1, 4))),
        "up_weight": noise(streams_of[3], (LAT, HEADS, PLAIN_WIDTH + VDIM), LAT ** -0.5, 0.25, ((1, 4),)),
        "segment_ids": jnp.searchsorted(jnp.cumsum(ragged_sizes(streams_of[4], SEGS, TOKENS, MOST, 2)), jnp.arange(TOKENS), side="right").astype(jnp.int32),
    }


def fold_back(window_terms, nblk):
    shaped = window_terms.reshape((nblk, REACH + 1, TOK_DEV) + window_terms.shape[2:])
    total = jnp.zeros((nblk + REACH, TOK_DEV) + window_terms.shape[2:], jnp.float32)
    for j in range(REACH + 1):
        total = total.at[j:j + nblk].add(shaped[:, j])
    return total[REACH:].reshape((nblk * TOK_DEV,) + window_terms.shape[2:])

def reference(queries, latent_keys, out_grad, up_weight, segment_ids):
    scale = 1.0 / math.sqrt(PLAIN_WIDTH + ROPE)
    nblk = TOKENS // TOK_DEV
    width = (REACH + 1) * TOK_DEV
    group = 8
    ngroups = HEADS // group
    starts = (jnp.arange(nblk) * TOK_DEV).astype(jnp.int32)
    pad_keys = jnp.concatenate([jnp.zeros((REACH * TOK_DEV, LAT + ROPE), jnp.bfloat16), latent_keys], 0)
    pad_seg = jnp.concatenate([jnp.full((REACH * TOK_DEV,), -1, jnp.int32), segment_ids.astype(jnp.int32)], 0)
    windows = jax.vmap(lambda s: lax.dynamic_slice_in_dim(pad_keys, s, width, 0))(starts)
    seg_win = jax.vmap(lambda s: lax.dynamic_slice_in_dim(pad_seg, s, width, 0))(starts)
    seg_query = segment_ids.astype(jnp.int32).reshape(nblk, TOK_DEV)
    pos_key = jnp.arange(width)[None, :]
    pos_query = (jnp.arange(TOK_DEV) + REACH * TOK_DEV)[:, None]
    mask = (seg_query[:, :, None] == seg_win[:, None, :]) & (pos_key <= pos_query)[None]
    rotary_key_part = windows[..., LAT:].astype(jnp.float32)
    window_latent = windows[..., :LAT].astype(jnp.float32)
    q_groups = jnp.moveaxis(queries.reshape(TOKENS, ngroups, group, PLAIN_WIDTH + ROPE), 1, 0)
    g_groups = jnp.moveaxis(out_grad.reshape(TOKENS, ngroups, group, VDIM), 1, 0)
    w_groups = jnp.moveaxis(up_weight.reshape(LAT, ngroups, group, PLAIN_WIDTH + VDIM), 1, 0)

    def one_group(operands):
        q_g, g_g, w_g = operands
        flat_w = w_g.reshape(LAT, group * (PLAIN_WIDTH + VDIM))
        kv_tok = jnp.dot(latent_keys[:, :LAT], flat_w, preferred_element_type=jnp.float32).astype(jnp.bfloat16)
        pad_kv = jnp.concatenate([jnp.zeros((REACH * TOK_DEV, kv_tok.shape[1]), jnp.bfloat16), kv_tok], 0)
        kv_win = jax.vmap(lambda s: lax.dynamic_slice_in_dim(pad_kv, s, width, 0))(starts)
        kv_win = kv_win.reshape(nblk, width, group, PLAIN_WIDTH + VDIM).astype(jnp.float32)
        plain_key_part = kv_win[..., :PLAIN_WIDTH]
        values = kv_win[..., PLAIN_WIDTH:]
        query_up_matrix = q_g.reshape(nblk, TOK_DEV, group, PLAIN_WIDTH + ROPE).astype(jnp.float32)
        g_b = g_g.reshape(nblk, TOK_DEV, group, VDIM).astype(jnp.float32)
        attention_logits = jnp.einsum('zlmy,zcmy->zmlc', query_up_matrix[..., :PLAIN_WIDTH], plain_key_part) + jnp.einsum('pein,pmn->piem', query_up_matrix[..., PLAIN_WIDTH:], rotary_key_part)
        attention_logits = attention_logits * scale
        attention_logits = jnp.where(mask[:, None], attention_logits, -1e+30)
        top = lax.optimization_barrier(jnp.max(attention_logits, -1, keepdims=True))
        expo = jnp.where(mask[:, None], jnp.exp(attention_logits - top), 0.0)
        probs = expo / lax.optimization_barrier(jnp.sum(expo, -1, keepdims=True))
        dprobs = jnp.einsum('zlmy,zcmy->zmlc', g_b, values)
        delta = lax.optimization_barrier(jnp.sum(probs * dprobs, -1, keepdims=True))
        logit_gradient = lax.optimization_barrier((probs * (dprobs - delta) * scale).astype(jnp.bfloat16)).astype(jnp.float32)
        probs16 = lax.optimization_barrier(probs.astype(jnp.bfloat16)).astype(jnp.float32)
        query_gradient_rows = jnp.concatenate([jnp.einsum('zarp,zpay->zray', logit_gradient, plain_key_part), jnp.einsum('rnvc,rcj->rvnj', logit_gradient, rotary_key_part)], -1)
        dk = jnp.einsum('bhqk,bqhd->bkhd', logit_gradient, query_up_matrix[..., :PLAIN_WIDTH])
        dv = jnp.einsum('bhqk,bqhd->bkhd', probs16, g_b)
        rotary_key_gradient = jnp.einsum('vtau,vatc->vuc', logit_gradient, query_up_matrix[..., PLAIN_WIDTH:])
        dkv = lax.optimization_barrier(jnp.concatenate([dk, dv], -1).astype(jnp.bfloat16)).astype(jnp.float32)
        dkv_tok = fold_back(dkv, nblk).reshape(TOKENS, group * (PLAIN_WIDTH + VDIM))
        drope = fold_back(rotary_key_gradient, nblk)
        dlat = jnp.dot(dkv_tok, flat_w.astype(jnp.float32).T, precision=lax.Precision.HIGHEST)
        block_terms = jnp.einsum('bkl,bke->ble', window_latent, dkv.reshape(nblk, width, group * (PLAIN_WIDTH + VDIM)), precision=lax.Precision.HIGHEST)
        block_terms = lax.optimization_barrier(block_terms.astype(jnp.bfloat16)).astype(jnp.float32)
        dweight = lax.optimization_barrier(jnp.sum(block_terms, 0)).reshape(LAT, group, PLAIN_WIDTH + VDIM)
        return (query_gradient_rows.reshape(TOKENS, group, PLAIN_WIDTH + ROPE), jnp.concatenate([dlat, drope], -1), dweight)
    dq_all, dkeys_all, dw_all = lax.map(one_group, (q_groups, g_groups, w_groups))
    query_grad = jnp.moveaxis(dq_all, 0, 1).reshape(TOKENS, HEADS, PLAIN_WIDTH + ROPE)
    key_grad = lax.optimization_barrier(jnp.sum(dkeys_all, 0))
    weight_grad = jnp.moveaxis(dw_all, 0, 1).reshape(LAT, HEADS, PLAIN_WIDTH + VDIM)
    return (query_grad, key_grad, weight_grad)
```

```python
import math

import jax
import jax.numpy as jnp
from jax import lax
from jax.sharding import PartitionSpec as P

LAT = 512
ROPE = 64
PLAIN_WIDTH = 128
VDIM = 128
REACH = 1


def from_behind(value, axis, steps):
    count = lax.axis_size(axis)
    initial, last = (max(0, -steps), min(count, count - steps))
    return lax.ppermute(value, axis, [(source, source + steps) for source in range(initial, last)])


def shards(queries, latent_keys, out_grad, up_weight, segment_ids):
    tok = latent_keys.shape[0]
    heads = queries.shape[1]
    width = (REACH + 1) * tok
    here = lax.axis_index("ctx")
    scale = 1.0 / math.sqrt(PLAIN_WIDTH + ROPE)
    flat_weight = up_weight.reshape(LAT, heads * (PLAIN_WIDTH + VDIM))
    earlier = [from_behind(latent_keys, "ctx", REACH - 0)]
    window = jnp.concatenate(earlier + [latent_keys], 0)
    kv_win = jnp.dot(window[:, :LAT], flat_weight, preferred_element_type=jnp.float32).astype(
        jnp.bfloat16
    )
    pad_seg = jnp.concatenate([jnp.full((REACH * tok,), -1, jnp.int32), segment_ids], 0)
    seg_keys = lax.dynamic_slice_in_dim(pad_seg, here * tok, width, 0)
    seg_query = lax.dynamic_slice_in_dim(segment_ids, here * tok, tok, 0)
    pos_key = jnp.arange(width)[None, :]
    pos_query = (jnp.arange(tok) + REACH * tok)[:, None]
    visible = (seg_query[:, None] == seg_keys[None, :]) & (pos_key <= pos_query)
    kv_heads = kv_win.reshape(width, heads, PLAIN_WIDTH + VDIM)
    plain_key_part = kv_heads[..., :PLAIN_WIDTH]
    values = kv_heads[..., PLAIN_WIDTH:]
    k_rope = window[:, LAT:]
    q_nope = queries[..., :PLAIN_WIDTH]
    q_rope = queries[..., PLAIN_WIDTH:]
    attention_logits = jnp.einsum(
        "qhd,khd->hqk", q_nope, plain_key_part, preferred_element_type=jnp.float32
    )
    attention_logits = attention_logits + jnp.einsum(
        "qhd,kd->hqk", q_rope, k_rope, preferred_element_type=jnp.float32
    )
    attention_logits = jnp.where(visible[None], attention_logits * scale, -1e30)
    top = jnp.max(attention_logits, -1, keepdims=True)
    expo = jnp.where(visible[None], jnp.exp(attention_logits - top), 0.0)
    probs = expo / jnp.sum(expo, -1, keepdims=True)
    dprobs = jnp.einsum("qhd,khd->hqk", out_grad, values, preferred_element_type=jnp.float32)
    delta = jnp.sum(probs * dprobs, -1, keepdims=True)
    logit_gradient = (probs * (dprobs - delta) * scale).astype(jnp.bfloat16)
    probs16 = probs.astype(jnp.bfloat16)
    grad_nope = jnp.einsum(
        "hqk,khd->qhd", logit_gradient, plain_key_part, preferred_element_type=jnp.float32
    )
    grad_rope = jnp.einsum(
        "hqk,kd->qhd", logit_gradient, k_rope, preferred_element_type=jnp.float32
    )
    query_grad = jnp.concatenate([grad_nope, grad_rope], -1)
    dk_nope = jnp.einsum("hqk,qhd->khd", logit_gradient, q_nope, preferred_element_type=jnp.float32)
    dvalues = jnp.einsum("hqk,qhd->khd", probs16, out_grad, preferred_element_type=jnp.float32)
    dkey_rope = jnp.einsum(
        "hqk,qhd->kd", logit_gradient, q_rope, preferred_element_type=jnp.float32
    )
    dkv = (
        jnp.concatenate([dk_nope, dvalues], -1)
        .astype(jnp.bfloat16)
        .reshape(width, heads * (PLAIN_WIDTH + VDIM))
    )
    dlatent = jnp.einsum("ke,ie->ki", dkv, flat_weight, preferred_element_type=jnp.float32)
    key_terms = jnp.concatenate([dlatent, dkey_rope], -1)
    columns = lax.slice_in_dim(
        window, 0, LAT // lax.axis_size("ctx") * lax.axis_size("ctx"), axis=1
    )
    term = jnp.einsum("ki,ke->ie", columns, dkv, preferred_element_type=jnp.float32)
    weight_rows = lax.psum_scatter(
        term.astype(jnp.bfloat16),
        "ctx",
        scatter_dimension=0,
        tiled=True,
    )
    weight_grad = weight_rows.astype(jnp.float32).reshape(
        weight_rows.shape[0], heads, PLAIN_WIDTH + VDIM
    )
    pieces = key_terms.reshape(REACH + 1, tok, LAT + ROPE)
    shares = lax.psum_scatter(pieces, "head", scatter_dimension=2, tiled=True)
    key_grad = shares[REACH]
    key_grad = key_grad + from_behind(shares[0], "ctx", 0 - REACH)
    return (query_grad, key_grad, weight_grad)


def solution(mesh):
    return jax.shard_map(
        shards,
        mesh=mesh,
        in_specs=(
            P("ctx", "head", None),
            P("ctx", None),
            P("ctx", "head", None),
            P(None, "head", None),
            P(),
        ),
        out_specs=(P("ctx", "head", None), P("ctx", "head"), P("ctx", "head", None)),
        check_vma=False,
    )
```

```python
import functools
import math

import jax
import jax.numpy as jnp
from jax import lax
from jax.experimental import pallas as pl
from jax.experimental.pallas import tpu as pltpu
from jax.sharding import PartitionSpec as P

LAT = 512
ROPE = 64
PLAIN_WIDTH = 128
VDIM = 128
REACH = 1
LANES = 128
PAIR = PLAIN_WIDTH + VDIM
STEP_HEADS = 4
BF16 = jnp.bfloat16
F32 = jnp.float32
PARAMS = pltpu.CompilerParams(vmem_limit_bytes=32 * 1024 * 1024)


def from_behind(value, axis, steps):
    count = lax.axis_size(axis)
    initial, last = (max(0, -steps), min(count, count - steps))
    return lax.ppermute(value, axis, [(source, source + steps) for source in range(initial, last)])


def across(value, bit):
    count = lax.axis_size("ctx")
    return lax.ppermute(value, "ctx", [(source, source ^ bit) for source in range(count)])


def cost(flops, moved):
    return pl.CostEstimate(flops=int(flops), bytes_accessed=int(moved), transcendentals=0)


def dot(a, b, a_dim, b_dim):
    return lax.dot_general(a, b, (((a_dim,), (b_dim,)), ((), ())), preferred_element_type=F32)


def by_head_kernel(w_ref, q_ref, g_ref, wt_ref, qt_ref, gt_ref, rows_ref):
    depth, heads, _ = w_ref.shape
    tokens = q_ref.shape[0]

    def turn(block, out_ref, lanes, width):
        count = block.shape[0]
        rows_ref[: count * heads, :width] = block.astype(F32).reshape(count * heads, width)
        for h in range(heads):
            picked = rows_ref[pl.ds(h, count, stride=heads), :]
            if width < LANES:
                lane = lax.broadcasted_iota(jnp.int32, picked.shape, 1)
                picked = jnp.where(lane < width, picked, 0.0)
            out_ref[h, :, lanes : lanes + LANES] = picked.astype(BF16)

    turn(w_ref[:, :, :LANES], wt_ref, 0, LANES)
    turn(w_ref[:, :, LANES:], wt_ref, LANES, LANES)
    turn(q_ref[:, :, :PLAIN_WIDTH], qt_ref, 0, PLAIN_WIDTH)
    turn(q_ref[:, :, PLAIN_WIDTH:], qt_ref, PLAIN_WIDTH, ROPE)
    turn(g_ref[...], gt_ref, 0, VDIM)


def by_head(up_weight, queries, out_grad, chunk, heads):
    tok = queries.shape[0]
    steps = 4
    depth, rows = LAT // steps, tok // steps
    return pl.pallas_call(
        by_head_kernel,
        grid=(steps,),
        in_specs=[
            pl.BlockSpec((depth, heads, PAIR), lambda i: (i, chunk, 0)),
            pl.BlockSpec((rows, heads, PLAIN_WIDTH + ROPE), lambda i: (i, chunk, 0)),
            pl.BlockSpec((rows, heads, VDIM), lambda i: (i, chunk, 0)),
        ],
        out_specs=[
            pl.BlockSpec((heads, depth, PAIR), lambda i: (0, i, 0)),
            pl.BlockSpec((heads, rows, 2 * LANES), lambda i: (0, i, 0)),
            pl.BlockSpec((heads, rows, VDIM), lambda i: (0, i, 0)),
        ],
        out_shape=[
            jax.ShapeDtypeStruct((heads, LAT, PAIR), BF16),
            jax.ShapeDtypeStruct((heads, tok, 2 * LANES), BF16),
            jax.ShapeDtypeStruct((heads, tok, VDIM), BF16),
        ],
        scratch_shapes=[pltpu.VMEM((depth * heads, LANES), F32)],
        compiler_params=PARAMS,
        cost_estimate=cost(0, 4 * LAT * heads * PAIR),
        name="by_head",
    )(up_weight, queries, out_grad)


def attention_kernel(
    here_ref, prev_ref, own_ref, ids_ref, wt_ref, qt_ref, gt_ref, *refs, group, aliased
):
    refs = refs[1:] if aliased else refs
    dq_ref, dkv_ref, rope_ref, mine_ref, win_ref, krope_ref, vis_ref, dqn_ref, dqr_ref = refs
    i = pl.program_id(0)
    here = here_ref[0]
    tok = prev_ref.shape[0]
    width = 2 * tok
    heads = dq_ref.shape[1]
    scale = 1.0 / math.sqrt(PLAIN_WIDTH + ROPE)

    @pl.when(i == 0)
    def _():
        win_ref[:tok, :] = prev_ref[:, :LAT]
        win_ref[tok:, :] = own_ref[:, :LAT]
        krope_ref[...] = jnp.zeros_like(krope_ref)
        krope_ref[:tok, :ROPE] = prev_ref[:, LAT:]
        krope_ref[tok:, :ROPE] = own_ref[:, LAT:]
        behind = jnp.maximum(here - 1, 0)
        seg_prev = jnp.where(here > 0, ids_ref[pl.ds(behind, 1), :], -1)
        seg_own = ids_ref[pl.ds(here, 1), :]
        row = lax.broadcasted_iota(jnp.int32, (tok, tok), 0)
        col = lax.broadcasted_iota(jnp.int32, (tok, tok), 1)
        seg_query = jnp.sum(jnp.where(row == col, seg_own, 0), 1, keepdims=True)
        vis_ref[:, :tok] = (seg_query == seg_prev).astype(F32)
        vis_ref[:, tok:] = ((seg_query == seg_own) & (col <= row)).astype(F32)
        rope_ref[...] = jnp.zeros_like(rope_ref)
        if group is not None:
            source = lax.broadcasted_iota(jnp.int32, (LAT, LAT), 0)
            column = lax.broadcasted_iota(jnp.int32, (LAT, LAT), 1)
            place = column >> 6
            apart = ((place & 1) << 2) | (place & 2) | (place >> 2)
            wanted = ((here ^ apart) << 6) | (column & 63)
            ordered = dot(win_ref[...], (source == wanted).astype(BF16), 1, 0).astype(BF16)
            mine_ref[...] = ordered[:, : LAT // 2]
            dkv_ref[:, heads * PAIR :] = ordered[:, LAT // 2 :]

    visible = vis_ref[...] > 0.0
    window = win_ref[...]
    krope = krope_ref[...]
    count = wt_ref.shape[0]
    keys, values = [], []
    for h in range(count):
        kv = dot(window, wt_ref[h], 1, 0).astype(BF16)
        keys.append(jnp.concatenate([kv[:, :PLAIN_WIDTH], krope], 1))
        values.append(kv[:, PLAIN_WIDTH:])
    scores = [dot(qt_ref[h], keys[h], 1, 1) for h in range(count)]
    dprobs = [dot(gt_ref[h], values[h], 1, 1) for h in range(count)]
    dscores, probs16 = [], []
    for h in range(count):
        logits = jnp.where(visible, scores[h] * scale, -1e30)
        top = jnp.max(logits, -1, keepdims=True)
        expo = jnp.exp(logits - top)
        probs = expo / jnp.sum(expo, -1, keepdims=True)
        delta = jnp.sum(probs * dprobs[h], -1, keepdims=True)
        dscores.append((probs * (dprobs[h] - delta) * scale).astype(BF16))
        probs16.append(probs.astype(BF16))
    parts, rope = [], rope_ref[...]
    for h in range(count):
        dk = dot(dscores[h], qt_ref[h], 0, 0)
        dv = dot(probs16[h], gt_ref[h], 0, 0)
        parts.append(jnp.concatenate([dk[:, :PLAIN_WIDTH], dv], 1).astype(BF16))
        rope = rope + dk[:, PLAIN_WIDTH:]
    rope_ref[...] = rope
    dkv_ref[:, pl.ds(pl.multiple_of(i * (count * PAIR), count * PAIR), count * PAIR)] = (
        jnp.concatenate(parts, 1)
    )
    for h in range(count):
        dq = dot(dscores[h], keys[h], 1, 0)
        dqn_ref[pl.ds(i * count + h, tok, stride=heads), :] = dq[:, :PLAIN_WIDTH]
        dqr_ref[pl.ds(i * count + h, tok, stride=heads), :] = dq[:, PLAIN_WIDTH:]

    @pl.when(i == pl.num_programs(0) - 1)
    def _():
        dq_ref[:, :, :PLAIN_WIDTH] = dqn_ref[...].reshape(tok, heads, LANES)
        dq_ref[:, :, PLAIN_WIDTH:] = dqr_ref[...].reshape(tok, heads, LANES)[:, :, :ROPE]


def attention(here, prev, own, ids, turned, dq, chunk, all_heads, group):
    weight, queries, out_grad = turned
    heads, tok = queries.shape[:2]
    width = 2 * tok
    steps = heads // STEP_HEADS
    extra = LAT // 2 if group is not None else 0
    whole = lambda i, here: (0, 0)
    head_block = lambda i, here: (i, 0, 0)
    in_specs = [
        pl.BlockSpec((tok, LAT + ROPE), whole),
        pl.BlockSpec((tok, LAT + ROPE), whole),
        pl.BlockSpec(ids.shape, whole),
        pl.BlockSpec((STEP_HEADS, LAT, PAIR), head_block),
        pl.BlockSpec((STEP_HEADS, tok, 2 * LANES), head_block),
        pl.BlockSpec((STEP_HEADS, tok, VDIM), head_block),
    ]
    operands = [prev, own, ids, weight, queries, out_grad]
    if dq is not None:
        in_specs.append(pl.BlockSpec(memory_space=pl.ANY))
        operands.append(dq)
    return pl.pallas_call(
        functools.partial(attention_kernel, group=group, aliased=dq is not None),
        grid_spec=pltpu.PrefetchScalarGridSpec(
            num_scalar_prefetch=1,
            grid=(steps,),
            in_specs=in_specs,
            out_specs=[
                pl.BlockSpec((tok, heads, PLAIN_WIDTH + ROPE), lambda i, here: (0, chunk, 0)),
                pl.BlockSpec((width, heads * PAIR + extra), whole),
                pl.BlockSpec((width, LANES), whole),
                pl.BlockSpec((width, LAT // 2), whole),
            ],
            scratch_shapes=[
                pltpu.VMEM((width, LAT), BF16),
                pltpu.VMEM((width, LANES), BF16),
                pltpu.VMEM((tok, width), F32),
                pltpu.VMEM((tok * heads, LANES), F32),
                pltpu.VMEM((tok * heads, LANES), F32),
            ],
        ),
        out_shape=[
            jax.ShapeDtypeStruct((tok, all_heads, PLAIN_WIDTH + ROPE), F32),
            jax.ShapeDtypeStruct((width, heads * PAIR + extra), BF16),
            jax.ShapeDtypeStruct((width, LANES), F32),
            jax.ShapeDtypeStruct((width, LAT // 2), BF16),
        ],
        input_output_aliases={7: 0} if dq is not None else {},
        compiler_params=PARAMS,
        cost_estimate=cost(heads * width * 2 * (LAT * PAIR * 4), 4 * LAT * heads * PAIR),
        name="attention",
    )(here, *operands)


def terms_kernel(own_ref, other_ref, mine_ref, theirs_ref, keep_ref, send_ref, *, along_x):
    latents = jnp.concatenate([mine_ref[...], theirs_ref[...]], 0)
    grads = jnp.concatenate([own_ref[...], other_ref[...]], 0)
    term = dot(latents, grads, 0, 0)
    rows = term.shape[0] // 4
    first, second = (1, 2) if along_x else (2, 1)
    keep_ref[:rows] = term[:rows]
    keep_ref[rows:] = term[first * rows : (first + 1) * rows]
    send_ref[:rows] = term[second * rows : (second + 1) * rows].astype(BF16)
    send_ref[rows:] = term[3 * rows :].astype(BF16)


def terms(own, other, mine, along_x):
    width = own.shape[0]
    columns = own.shape[1] - LAT // 2
    block = 1024
    column_block = lambda i: (0, i)
    return pl.pallas_call(
        functools.partial(terms_kernel, along_x=along_x),
        grid=(columns // block,),
        in_specs=[
            pl.BlockSpec((width, block), column_block),
            pl.BlockSpec((width, block), column_block),
            pl.BlockSpec((width, LAT // 2), lambda i: (0, 0)),
            pl.BlockSpec((width, LAT // 2), lambda i: (0, columns // (LAT // 2))),
        ],
        out_specs=[pl.BlockSpec((LAT // 4, block), column_block)] * 2,
        out_shape=[
            jax.ShapeDtypeStruct((LAT // 4, columns), F32),
            jax.ShapeDtypeStruct((LAT // 4, columns), BF16),
        ],
        compiler_params=PARAMS,
        cost_estimate=cost(width * LAT * columns * 2, 4 * width * columns + 3 * LAT // 2 * columns),
        name="terms",
    )(own, other, mine, other)


def key_terms_kernel(*refs, chunks, steps, shares):
    head_ref = refs[0]
    dkv_refs, wt_refs, rope_refs = (
        refs[1 + k * chunks : 1 + (k + 1) * chunks] for k in range(3)
    )
    outs = refs[1 + 3 * chunks : -1]
    total_ref = refs[-1]
    i = pl.program_id(0)

    @pl.when(i == 0)
    def _():
        total_ref[...] = jnp.zeros_like(total_ref)

    for k in range(chunks):

        @pl.when(i // steps == k)
        def _(k=k):
            total = total_ref[...]
            for h in range(wt_refs[k].shape[0]):
                grads = dkv_refs[k][:, h * PAIR : (h + 1) * PAIR]
                total = total + dot(grads, wt_refs[k][h], 1, 1)
            total_ref[...] = total

    @pl.when(i == pl.num_programs(0) - 1)
    def _():
        rope = rope_refs[0][...]
        for k in range(1, chunks):
            rope = rope + rope_refs[k][...]
        both = jnp.concatenate([total_ref[...], rope], 1)
        if shares is None:
            outs[0][...] = both[:, : LAT + ROPE]
            return
        part = (LAT + ROPE) // shares
        for z in range(shares):
            piece = both[:, z * part : (z + 1) * part]
            for s in range(shares):

                @pl.when(lax.rem(head_ref[0] + s, shares) == z)
                def _(s=s, piece=piece):
                    outs[s][...] = piece


def key_terms(at_head, dkvs, weights, ropes, shares):
    chunks = len(dkvs)
    heads = weights[0].shape[0]
    width = dkvs[0].shape[0]
    steps = heads // STEP_HEADS
    near = lambda k: lambda i, at: jnp.clip(i - k * steps, 0, steps - 1)
    wide = (LAT + ROPE) // (shares or 1)
    return pl.pallas_call(
        functools.partial(key_terms_kernel, chunks=chunks, steps=steps, shares=shares),
        grid_spec=pltpu.PrefetchScalarGridSpec(
            num_scalar_prefetch=1,
            grid=(chunks * steps,),
            in_specs=[
                pl.BlockSpec((width, STEP_HEADS * PAIR), lambda i, at, k=k: (0, near(k)(i, at)))
                for k in range(chunks)
            ]
            + [
                pl.BlockSpec((STEP_HEADS, LAT, PAIR), lambda i, at, k=k: (near(k)(i, at), 0, 0))
                for k in range(chunks)
            ]
            + [pl.BlockSpec((width, LANES), lambda i, at: (0, 0))] * chunks,
            out_specs=[pl.BlockSpec((width, wide), lambda i, at: (0, 0))] * (shares or 1),
            scratch_shapes=[pltpu.VMEM((width, LAT), F32)],
        ),
        out_shape=[jax.ShapeDtypeStruct((width, wide), F32)] * (shares or 1),
        compiler_params=PARAMS,
        cost_estimate=cost(chunks * heads * width * LAT * PAIR * 2, 2 * chunks * heads * LAT * PAIR),
        name="key_terms",
    )(at_head, *dkvs, *weights, *ropes)


def weight_sum_kernel(*refs):
    outs = refs[-3:]
    out_ref, k_ref, v_ref = outs
    rows, heads, _ = out_ref.shape
    chunks = (len(refs) - 3) // 3
    each = heads // chunks
    for c in range(chunks):
        keep_ref, first_ref, second_ref = refs[3 * c : 3 * c + 3]
        for h in range(each):
            columns = slice(h * PAIR, (h + 1) * PAIR)
            total = keep_ref[:, columns] + first_ref[:, columns].astype(F32)
            total = total + second_ref[:, columns].astype(F32)
            k_ref[pl.ds(c * each + h, rows, stride=heads), :] = total[:, :LANES]
            v_ref[pl.ds(c * each + h, rows, stride=heads), :] = total[:, LANES:]
    out_ref[:, :, :LANES] = k_ref[...].reshape(rows, heads, LANES)
    out_ref[:, :, LANES:] = v_ref[...].reshape(rows, heads, LANES)


def weight_sum(parts, heads):
    rows = parts[0][2].shape[0]
    block = 16
    in_specs, operands = [], []
    for part in parts:
        for array in part:
            in_specs.append(pl.BlockSpec((block, array.shape[1]), lambda i: (i, 0)))
            operands.append(array)
    return pl.pallas_call(
        weight_sum_kernel,
        grid=(rows // block,),
        in_specs=in_specs,
        out_specs=pl.BlockSpec((block, heads, PAIR), lambda i: (i, 0, 0)),
        out_shape=jax.ShapeDtypeStruct((rows, heads, PAIR), F32),
        scratch_shapes=[pltpu.VMEM((block * heads, LANES), F32)] * 2,
        compiler_params=PARAMS,
        cost_estimate=cost(0, 12 * rows * heads * PAIR),
        name="weight_sum",
    )(*operands)


def shards(queries, latent_keys, out_grad, up_weight, segment_ids):
    tok = latent_keys.shape[0]
    heads = queries.shape[1]
    n_ctx, n_head = lax.axis_size("ctx"), lax.axis_size("head")
    paired = n_ctx == 8 and heads == 32 and n_head == 4
    here = lax.axis_index("ctx").astype(jnp.int32).reshape(1)
    at_head = lax.axis_index("head").astype(jnp.int32).reshape(1)
    ids = segment_ids.reshape(n_ctx, tok)
    prev = from_behind(latent_keys, "ctx", REACH)
    chunks = 2 if paired else 1
    each = heads // chunks
    group = 1 if paired else None
    dq, dkvs, weights, ropes, sums = None, [], [], [], []
    for c in range(chunks):
        turned = by_head(up_weight, queries, out_grad, c, each)
        dq, dkv, rope, mine = attention(
            here, prev, latent_keys, ids, turned, dq, c, heads, group
        )
        dkvs.append(dkv)
        weights.append(turned[0])
        ropes.append(rope)
        if paired:
            keep, send = terms(dkv, across(dkv, 1), mine, c == 0)
            got = across(send, 2 if c == 0 else 4)
            rest = keep[tok:] + got[tok:].astype(F32)
            last = across(rest.astype(BF16), 4 if c == 0 else 2)
            sums.append((keep, got, last))
    if paired:
        shares = key_terms(at_head, dkvs, weights, ropes, n_head)
        share = shares[0]
        for s in range(1, n_head):
            share = share + lax.ppermute(
                shares[s], "head", [(z, (z + s) % n_head) for z in range(n_head)]
            )
        share = share.reshape(REACH + 1, tok, -1)
        weight_grad = weight_sum(sums, heads)
    else:
        (both,) = key_terms(at_head, dkvs, weights, ropes, None)
        share = lax.psum_scatter(
            both.reshape(REACH + 1, tok, LAT + ROPE), "head", scatter_dimension=2, tiled=True
        )
        window = jnp.concatenate([prev, latent_keys], 0)
        term = jnp.einsum("ki,ke->ie", window[:, :LAT], dkvs[0], preferred_element_type=F32)
        rows = lax.psum_scatter(term.astype(BF16), "ctx", scatter_dimension=0, tiled=True)
        weight_grad = rows.astype(F32).reshape(rows.shape[0], heads, PAIR)
    key_grad = share[REACH] + from_behind(share[0], "ctx", 0 - REACH)
    return (dq, key_grad, weight_grad)


def solution(mesh):
    return jax.shard_map(
        shards,
        mesh=mesh,
        in_specs=(
            P("ctx", "head", None),
            P("ctx", None),
            P("ctx", "head", None),
            P(None, "head", None),
            P(),
        ),
        out_specs=(P("ctx", "head", None), P("ctx", "head"), P("ctx", "head", None)),
        check_vma=False,
    )
```

```python
import functools
import math

import jax
import jax.numpy as jnp
from jax import lax
from jax.experimental import pallas as pl
from jax.experimental.pallas import tpu as pltpu
from jax.sharding import PartitionSpec as P

LAT = 512
ROPE = 64
PLAIN_WIDTH = 128
VDIM = 128
REACH = 1
LANES = 128
PAIR = PLAIN_WIDTH + VDIM
STEP_HEADS = 4
BF16 = jnp.bfloat16
F32 = jnp.float32
WIDE = pltpu.CompilerParams(vmem_limit_bytes=56 * 1024 * 1024)
PARAMS = pltpu.CompilerParams(vmem_limit_bytes=32 * 1024 * 1024)


def from_behind(value, axis, steps):
    count = lax.axis_size(axis)
    initial, last = (max(0, -steps), min(count, count - steps))
    return lax.ppermute(value, axis, [(source, source + steps) for source in range(initial, last)])


def across(value, bit):
    count = lax.axis_size("ctx")
    return lax.ppermute(value, "ctx", [(source, source ^ bit) for source in range(count)])


def cost(share):
    return pl.CostEstimate(flops=int(share * 1e9), bytes_accessed=1024, transcendentals=0)


BY_HEAD, WINDOW, ATTENTION, TERMS, KEY_TERMS, WEIGHT_SUM = 3.0, 0.5, 3.0, 2.0, 0.1, 0.1


def dot(a, b, a_dim, b_dim):
    return lax.dot_general(a, b, (((a_dim,), (b_dim,)), ((), ())), preferred_element_type=F32)


def by_head_kernel(w_ref, q_ref, g_ref, wt_ref, qt_ref, gt_ref):
    heads = w_ref.shape[1]
    orders = {}

    def order(count):
        if count not in orders:
            size = count * heads
            row = lax.broadcasted_iota(jnp.int32, (size, size), 0)
            col = lax.broadcasted_iota(jnp.int32, (size, size), 1)
            wanted = (row % count) * heads + row // count
            orders[count] = (col == wanted).astype(BF16)
        return orders[count]

    def turn(ref, out_ref):
        rows, _, width = ref.shape
        count = min(rows, 256 // heads)
        for start in range(0, rows, count):
            block = ref[start : start + count].reshape(count * heads, width)
            turned = dot(order(count), block, 1, 0).astype(BF16)
            out_ref[:, start : start + count, :width] = turned.reshape(heads, count, width)

    turn(w_ref, wt_ref)
    qt_ref[...] = jnp.zeros_like(qt_ref)
    turn(q_ref, qt_ref)
    turn(g_ref, gt_ref)


def by_head(up_weight, queries, out_grad, chunk, heads):
    tok = queries.shape[0]
    steps = 4
    depth, rows = LAT // steps, tok // steps
    return pl.pallas_call(
        by_head_kernel,
        grid=(steps,),
        in_specs=[
            pl.BlockSpec((depth, heads, PAIR), lambda i: (i, chunk, 0)),
            pl.BlockSpec((rows, heads, PLAIN_WIDTH + ROPE), lambda i: (i, chunk, 0)),
            pl.BlockSpec((rows, heads, VDIM), lambda i: (i, chunk, 0)),
        ],
        out_specs=[
            pl.BlockSpec((heads, depth, PAIR), lambda i: (0, i, 0)),
            pl.BlockSpec((heads, rows, 2 * LANES), lambda i: (0, i, 0)),
            pl.BlockSpec((heads, rows, VDIM), lambda i: (0, i, 0)),
        ],
        out_shape=[
            jax.ShapeDtypeStruct((heads, LAT, PAIR), BF16),
            jax.ShapeDtypeStruct((heads, tok, 2 * LANES), BF16),
            jax.ShapeDtypeStruct((heads, tok, VDIM), BF16),
        ],
        compiler_params=WIDE,
        cost_estimate=cost(BY_HEAD),
        name="by_head",
    )(up_weight, queries, out_grad)


def window_kernel(here_ref, prev_ref, own_ref, ids_ref, *outs, paired):
    win_ref, krope_ref, vis_ref = outs[:3]
    here = here_ref[0]
    tok = prev_ref.shape[0]
    win_ref[:tok, :] = prev_ref[:, :LAT]
    win_ref[tok:, :] = own_ref[:, :LAT]
    krope_ref[...] = jnp.zeros_like(krope_ref)
    krope_ref[:tok, :ROPE] = prev_ref[:, LAT:]
    krope_ref[tok:, :ROPE] = own_ref[:, LAT:]
    behind = jnp.maximum(here - 1, 0)
    seg_prev = jnp.where(here > 0, ids_ref[pl.ds(behind, 1), :], -1)
    seg_own = ids_ref[pl.ds(here, 1), :]
    row = lax.broadcasted_iota(jnp.int32, (tok, tok), 0)
    col = lax.broadcasted_iota(jnp.int32, (tok, tok), 1)
    seg_query = jnp.sum(jnp.where(row == col, seg_own, 0), 1, keepdims=True)
    vis_ref[:, :tok] = (seg_query == seg_prev).astype(F32)
    vis_ref[:, tok:] = ((seg_query == seg_own) & (col <= row)).astype(F32)
    if paired:
        source = lax.broadcasted_iota(jnp.int32, (LAT, LAT), 0)
        column = lax.broadcasted_iota(jnp.int32, (LAT, LAT), 1)
        place = column >> 6
        apart = ((place & 1) << 2) | (place & 2) | (place >> 2)
        wanted = ((here ^ apart) << 6) | (column & 63)
        ordered = dot(win_ref[...], (source == wanted).astype(BF16), 1, 0).astype(BF16)
        outs[3][...] = ordered[:, : LAT // 2]
        outs[4][...] = ordered[:, LAT // 2 :]


def key_window(here, prev, own, ids, paired):
    tok = prev.shape[0]
    whole = lambda i, here: (0, 0)
    shapes = [((2 * tok, LAT), BF16), ((2 * tok, LANES), BF16), ((tok, 2 * tok), F32)]
    if paired:
        shapes = shapes + [((2 * tok, LAT // 2), BF16)] * 2
    return pl.pallas_call(
        functools.partial(window_kernel, paired=paired),
        grid_spec=pltpu.PrefetchScalarGridSpec(
            num_scalar_prefetch=1,
            grid=(1,),
            in_specs=[pl.BlockSpec(array.shape, whole) for array in (prev, own, ids)],
            out_specs=[pl.BlockSpec(shape, whole) for shape, _ in shapes],
        ),
        out_shape=[jax.ShapeDtypeStruct(*shape) for shape in shapes],
        compiler_params=PARAMS,
        cost_estimate=cost(WINDOW),
        name="key_window",
    )(here, prev, own, ids)


def attention_kernel(
    win_ref, krope_ref, vis_ref, wt_ref, qt_ref, gt_ref, *refs, aliased, extra
):
    latents_ref = refs[0] if extra else None
    refs = refs[1:] if extra else refs
    refs = refs[1:] if aliased else refs
    dq_ref, dkv_ref, rope_ref, dqn_ref, dqr_ref = refs
    i = pl.program_id(0)
    tok, heads = dq_ref.shape[:2]
    scale = 1.0 / math.sqrt(PLAIN_WIDTH + ROPE)

    @pl.when(i == 0)
    def _():
        rope_ref[...] = jnp.zeros_like(rope_ref)
        if extra:
            dkv_ref[:, heads * PAIR :] = latents_ref[...]

    visible = vis_ref[...] > 0.0
    window = win_ref[...]
    krope = krope_ref[...]
    count = wt_ref.shape[0]
    keys, values = [], []
    for h in range(count):
        kv = dot(window, wt_ref[h], 1, 0).astype(BF16)
        keys.append(jnp.concatenate([kv[:, :PLAIN_WIDTH], krope], 1))
        values.append(kv[:, PLAIN_WIDTH:])
    scores = [dot(qt_ref[h], keys[h], 1, 1) for h in range(count)]
    dprobs = [dot(gt_ref[h], values[h], 1, 1) for h in range(count)]
    dscores, probs16 = [], []
    for h in range(count):
        logits = jnp.where(visible, scores[h] * scale, -1e30)
        top = jnp.max(logits, -1, keepdims=True)
        expo = jnp.exp(logits - top)
        probs = expo / jnp.sum(expo, -1, keepdims=True)
        delta = jnp.sum(probs * dprobs[h], -1, keepdims=True)
        dscores.append((probs * (dprobs[h] - delta) * scale).astype(BF16))
        probs16.append(probs.astype(BF16))
    parts, rope = [], rope_ref[...]
    for h in range(count):
        dk = dot(dscores[h], qt_ref[h], 0, 0)
        dv = dot(probs16[h], gt_ref[h], 0, 0)
        parts.append(jnp.concatenate([dk[:, :PLAIN_WIDTH], dv], 1).astype(BF16))
        rope = rope + dk[:, PLAIN_WIDTH:]
    rope_ref[...] = rope
    dkv_ref[:, pl.ds(pl.multiple_of(i * (count * PAIR), count * PAIR), count * PAIR)] = (
        jnp.concatenate(parts, 1)
    )
    for h in range(count):
        dq = dot(dscores[h], keys[h], 1, 0)
        dqn_ref[pl.ds(i * count + h, tok, stride=heads), :] = dq[:, :PLAIN_WIDTH]
        dqr_ref[pl.ds(i * count + h, tok, stride=heads), :] = dq[:, PLAIN_WIDTH:]

    @pl.when(i == pl.num_programs(0) - 1)
    def _():
        dq_ref[:, :, :PLAIN_WIDTH] = dqn_ref[...].reshape(tok, heads, LANES)
        dq_ref[:, :, PLAIN_WIDTH:] = dqr_ref[...].reshape(tok, heads, LANES)[:, :, :ROPE]


def attention(window, turned, latents, dq, chunk, heads, first, all_heads):
    weight, queries, out_grad = turned
    tok = queries.shape[1]
    width = 2 * tok
    steps = heads // STEP_HEADS
    at = first // STEP_HEADS
    extra = LAT // 2 if latents is not None else 0
    whole = lambda i: (0, 0)
    head_block = lambda i: (at + i, 0, 0)
    operands = [*window, weight, queries, out_grad]
    in_specs = [pl.BlockSpec(array.shape, whole) for array in window] + [
        pl.BlockSpec((STEP_HEADS, LAT, PAIR), head_block),
        pl.BlockSpec((STEP_HEADS, tok, 2 * LANES), head_block),
        pl.BlockSpec((STEP_HEADS, tok, VDIM), head_block),
    ]
    if latents is not None:
        in_specs.append(pl.BlockSpec(latents.shape, whole))
        operands.append(latents)
    aliases = {}
    if dq is not None:
        aliases = {len(operands): 0}
        in_specs.append(pl.BlockSpec(memory_space=pl.ANY))
        operands.append(dq)
    return pl.pallas_call(
        functools.partial(attention_kernel, aliased=dq is not None, extra=latents is not None),
        grid=(steps,),
        in_specs=in_specs,
        out_specs=[
            pl.BlockSpec((tok, heads, PLAIN_WIDTH + ROPE), lambda i: (0, chunk, 0)),
            pl.BlockSpec((width, heads * PAIR + extra), whole),
            pl.BlockSpec((width, LANES), whole),
        ],
        scratch_shapes=[
            pltpu.VMEM((tok * heads, LANES), F32),
            pltpu.VMEM((tok * heads, LANES), F32),
        ],
        out_shape=[
            jax.ShapeDtypeStruct((tok, all_heads, PLAIN_WIDTH + ROPE), F32),
            jax.ShapeDtypeStruct((width, heads * PAIR + extra), BF16),
            jax.ShapeDtypeStruct((width, LANES), F32),
        ],
        input_output_aliases=aliases,
        compiler_params=WIDE,
        cost_estimate=cost(ATTENTION),
        name="attention",
    )(*operands)


def terms_kernel(
    own_ref, other_ref, mine_ref, theirs_ref, keep_ref, send_ref, latents_ref, *, along_x
):
    width = own_ref.shape[0]

    @pl.when(pl.program_id(0) == 0)
    def _():
        latents_ref[:, :width] = mine_ref[...].T
        latents_ref[:, width:] = theirs_ref[...].T

    grads = jnp.concatenate([own_ref[...], other_ref[...]], 0)
    term = dot(latents_ref[...], grads, 1, 0)
    rows = term.shape[0] // 4
    first, second = (1, 2) if along_x else (2, 1)
    keep_ref[:rows] = term[:rows]
    keep_ref[rows:] = term[first * rows : (first + 1) * rows]
    send_ref[:rows] = term[second * rows : (second + 1) * rows].astype(BF16)
    send_ref[rows:] = term[3 * rows :].astype(BF16)


def terms(own, other, mine, theirs, columns, along_x):
    width = own.shape[0]
    block = 1024
    at = theirs.shape[1] // (LAT // 2) - 1
    column_block = lambda i: (0, i)
    return pl.pallas_call(
        functools.partial(terms_kernel, along_x=along_x),
        grid=(columns // block,),
        in_specs=[
            pl.BlockSpec((width, block), column_block),
            pl.BlockSpec((width, block), column_block),
            pl.BlockSpec((width, LAT // 2), lambda i: (0, 0)),
            pl.BlockSpec((width, LAT // 2), lambda i: (0, at)),
        ],
        out_specs=[pl.BlockSpec((LAT // 4, block), column_block)] * 2,
        out_shape=[
            jax.ShapeDtypeStruct((LAT // 4, columns), F32),
            jax.ShapeDtypeStruct((LAT // 4, columns), BF16),
        ],
        scratch_shapes=[pltpu.VMEM((LAT // 2, 2 * width), BF16)],
        compiler_params=PARAMS,
        cost_estimate=cost(TERMS),
        name="terms",
    )(own, other, mine, theirs)


def key_terms_kernel(*refs, chunks, steps, turns, shares):
    head_ref = refs[0]
    dkv_refs = refs[1 : 1 + chunks]
    wt_refs = refs[1 + chunks : 1 + chunks + turns]
    rope_refs = refs[1 + chunks + turns : 1 + 2 * chunks + turns]
    outs = refs[1 + 2 * chunks + turns : -1]
    total_ref = refs[-1]
    i = pl.program_id(0)

    @pl.when(i == 0)
    def _():
        total_ref[...] = jnp.zeros_like(total_ref)

    for k in range(chunks):

        @pl.when(i // steps == k)
        def _(k=k):
            total = total_ref[...]
            weight_ref = wt_refs[k * turns // chunks]
            for h in range(weight_ref.shape[0]):
                grads = dkv_refs[k][:, h * PAIR : (h + 1) * PAIR]
                total = total + dot(grads, weight_ref[h], 1, 1)
            total_ref[...] = total

    @pl.when(i == pl.num_programs(0) - 1)
    def _():
        rope = rope_refs[0][...]
        for k in range(1, chunks):
            rope = rope + rope_refs[k][...]
        both = jnp.concatenate([total_ref[...], rope], 1)
        if shares is None:
            outs[0][...] = both[:, : LAT + ROPE]
            return
        part = (LAT + ROPE) // shares
        for z in range(shares):
            piece = both[:, z * part : (z + 1) * part]
            for s in range(shares):

                @pl.when(lax.rem(head_ref[0] + s, shares) == z)
                def _(s=s, piece=piece):
                    outs[s][...] = piece


def key_terms(at_head, dkvs, weights, ropes, shares):
    chunks, turns = len(dkvs), len(weights)
    heads = weights[0].shape[0] * turns // chunks
    width = dkvs[0].shape[0]
    steps = heads // STEP_HEADS
    span = steps * chunks // turns
    near = lambda k, many: lambda i, at: jnp.clip(i - k * many, 0, many - 1)
    wide = (LAT + ROPE) // (shares or 1)
    return pl.pallas_call(
        functools.partial(
            key_terms_kernel, chunks=chunks, steps=steps, turns=turns, shares=shares
        ),
        grid_spec=pltpu.PrefetchScalarGridSpec(
            num_scalar_prefetch=1,
            grid=(chunks * steps,),
            in_specs=[
                pl.BlockSpec((width, STEP_HEADS * PAIR), lambda i, at, k=k: (0, near(k, steps)(i, at)))
                for k in range(chunks)
            ]
            + [
                pl.BlockSpec(
                    (STEP_HEADS, LAT, PAIR), lambda i, at, k=k: (near(k, span)(i, at), 0, 0)
                )
                for k in range(turns)
            ]
            + [pl.BlockSpec((width, LANES), lambda i, at: (0, 0))] * chunks,
            out_specs=[pl.BlockSpec((width, wide), lambda i, at: (0, 0))] * (shares or 1),
            scratch_shapes=[pltpu.VMEM((width, LAT), F32)],
        ),
        out_shape=[jax.ShapeDtypeStruct((width, wide), F32)] * (shares or 1),
        compiler_params=WIDE,
        cost_estimate=cost(KEY_TERMS),
        name="key_terms",
    )(at_head, *dkvs, *weights, *ropes)


def weight_sum_kernel(keep_ref, first_ref, second_ref, *refs):
    out_ref, k_ref, v_ref = refs[-3:]
    rows, heads, _ = out_ref.shape
    for h in range(heads):
        columns = slice(h * PAIR, (h + 1) * PAIR)
        total = keep_ref[:, columns] + first_ref[:, columns].astype(F32)
        total = total + second_ref[:, columns].astype(F32)
        k_ref[pl.ds(h, rows, stride=heads), :] = total[:, :LANES]
        v_ref[pl.ds(h, rows, stride=heads), :] = total[:, LANES:]
    out_ref[:, :, :LANES] = k_ref[...].reshape(rows, heads, LANES)
    out_ref[:, :, LANES:] = v_ref[...].reshape(rows, heads, LANES)


def weight_sum(keep, first, second, total, chunk, all_heads):
    rows, columns = second.shape
    heads = columns // PAIR
    block = 32
    operands = [keep, first, second]
    in_specs = [pl.BlockSpec((block, columns), lambda i: (i, 0)) for _ in operands]
    aliases = {}
    if total is not None:
        aliases = {3: 0}
        in_specs.append(pl.BlockSpec(memory_space=pl.ANY))
        operands.append(total)
    return pl.pallas_call(
        weight_sum_kernel,
        grid=(rows // block,),
        in_specs=in_specs,
        out_specs=pl.BlockSpec((block, heads, PAIR), lambda i: (i, chunk, 0)),
        out_shape=jax.ShapeDtypeStruct((rows, all_heads, PAIR), F32),
        scratch_shapes=[pltpu.VMEM((block * heads, LANES), F32)] * 2,
        input_output_aliases=aliases,
        compiler_params=PARAMS,
        cost_estimate=cost(WEIGHT_SUM),
        name="weight_sum",
    )(*operands)


def after(values, earlier):
    return lax.optimization_barrier((values, earlier))[0]


def in_chunks(queries, latent_keys, out_grad, up_weight, here, at_head, ids):
    tok = latent_keys.shape[0]
    heads, each, turned_heads = 32, 8, 16
    n_head = lax.axis_size("head")
    prev = from_behind(latent_keys, "ctx", REACH)
    turned = [by_head(up_weight, queries, out_grad, 0, turned_heads), None]
    *window, mine, theirs = key_window(here, prev, latent_keys, ids, True)
    dq, dkvs, ropes, others, sent, keeps = None, [], [], [], [], []

    def attend(c):
        nonlocal dq
        dq, dkv, rope = attention(
            window,
            turned[c // 2],
            theirs if c == 0 else None,
            dq,
            c,
            each,
            c % 2 * each,
            heads,
        )
        dkvs.append(dkv)
        ropes.append(rope)
        others.append(across(dkv, 1))

    def send(c):
        keep, out = terms(dkvs[c], others[c], mine, others[0], each * PAIR, c % 2 == 0)
        keeps.append(keep)
        sent.append(across(out, 2 if c % 2 == 0 else 4))
        return out

    attend(0)
    attend(1)
    out = send(0)
    turned[1] = by_head(*after((up_weight, queries, out_grad), out), 1, turned_heads)
    out = send(1)
    turned[1] = after(turned[1], out)
    attend(2)
    attend(3)
    lasts = []

    def forward(c):
        rest = (keeps[c][tok:] + sent[c][tok:].astype(F32)).astype(BF16)
        lasts.append(across(rest, 4 if c % 2 == 0 else 2))
        return rest

    send(2)
    rest = [forward(0), forward(1)]
    others[3] = after(others[3], rest)
    out = send(3)
    dkvs = after(dkvs, out)
    shares = key_terms(at_head, dkvs, [t[0] for t in turned], ropes, n_head)
    got = [
        lax.ppermute(shares[s], "head", [(z, (z + s) % n_head) for z in range(n_head)])
        for s in range(1, n_head)
    ]
    rest = forward(2)
    share, got = after((shares[0], got), rest)
    for piece in got:
        share = share + piece
    share = share.reshape(REACH + 1, tok, -1)
    forward(3)
    weight_grad = None
    for c in range(4):
        weight_grad = weight_sum(keeps[c], sent[c], lasts[c], weight_grad, c, heads)
    return dq, share, weight_grad


def shards(queries, latent_keys, out_grad, up_weight, segment_ids):
    tok = latent_keys.shape[0]
    heads = queries.shape[1]
    n_ctx, n_head = lax.axis_size("ctx"), lax.axis_size("head")
    here = lax.axis_index("ctx").astype(jnp.int32).reshape(1)
    at_head = lax.axis_index("head").astype(jnp.int32).reshape(1)
    ids = segment_ids.reshape(n_ctx, tok)
    if n_ctx == 8 and heads == 32 and n_head == 4:
        dq, share, weight_grad = in_chunks(
            queries, latent_keys, out_grad, up_weight, here, at_head, ids
        )
    else:
        prev = from_behind(latent_keys, "ctx", REACH)
        turned = by_head(up_weight, queries, out_grad, 0, heads)
        window = key_window(here, prev, latent_keys, ids, False)
        dq, dkv, rope = attention(window, turned, None, None, 0, heads, 0, heads)
        (both,) = key_terms(at_head, [dkv], [turned[0]], [rope], None)
        share = lax.psum_scatter(
            both.reshape(REACH + 1, tok, LAT + ROPE), "head", scatter_dimension=2, tiled=True
        )
        term = jnp.einsum("ki,ke->ie", window[0], dkv, preferred_element_type=F32)
        rows = lax.psum_scatter(term.astype(BF16), "ctx", scatter_dimension=0, tiled=True)
        weight_grad = rows.astype(F32).reshape(rows.shape[0], heads, PAIR)
    key_grad = share[REACH] + from_behind(share[0], "ctx", 0 - REACH)
    return (dq, key_grad, weight_grad)


def solution(mesh):
    return jax.shard_map(
        shards,
        mesh=mesh,
        in_specs=(
            P("ctx", "head", None),
            P("ctx", None),
            P("ctx", "head", None),
            P(None, "head", None),
            P(),
        ),
        out_specs=(P("ctx", "head", None), P("ctx", "head"), P("ctx", "head", None)),
        check_vma=False,
    )
```

```python
import functools
import math

import jax
import jax.numpy as jnp
from jax import lax
from jax.experimental import pallas as pl
from jax.experimental.pallas import tpu as pltpu
from jax.sharding import PartitionSpec as P

LAT = 512
ROPE = 64
PLAIN_WIDTH = 128
VDIM = 128
REACH = 1
LANES = 128
PAIR = PLAIN_WIDTH + VDIM
STEP_HEADS = 4
BF16 = jnp.bfloat16
F32 = jnp.float32
WIDE = pltpu.CompilerParams(vmem_limit_bytes=56 * 1024 * 1024)
PARAMS = pltpu.CompilerParams(vmem_limit_bytes=32 * 1024 * 1024)


def from_behind(value, axis, steps):
    count = lax.axis_size(axis)
    initial, last = (max(0, -steps), min(count, count - steps))
    return lax.ppermute(value, axis, [(source, source + steps) for source in range(initial, last)])


def across(value, bit):
    count = lax.axis_size("ctx")
    return lax.ppermute(value, "ctx", [(source, source ^ bit) for source in range(count)])


def cost(share):
    return pl.CostEstimate(flops=int(share * 1e9), bytes_accessed=1024, transcendentals=0)


BY_HEAD, WINDOW, ATTENTION, TERMS, KEY_TERMS, WEIGHT_SUM = 3.0, 0.5, 2.0, 2.0, 2.0, 0.5


def dot(a, b, a_dim, b_dim):
    return lax.dot_general(a, b, (((a_dim,), (b_dim,)), ((), ())), preferred_element_type=F32)


def by_head_kernel(w_ref, q_ref, g_ref, wt_ref, qt_ref, gt_ref):
    heads = w_ref.shape[1]
    orders = {}

    def order(count):
        if count not in orders:
            size = count * heads
            row = lax.broadcasted_iota(jnp.int32, (size, size), 0)
            col = lax.broadcasted_iota(jnp.int32, (size, size), 1)
            wanted = (row % count) * heads + row // count
            orders[count] = (col == wanted).astype(BF16)
        return orders[count]

    def turn(ref, out_ref):
        rows, _, width = ref.shape
        count = min(rows, 256 // heads)
        for start in range(0, rows, count):
            block = ref[start : start + count].reshape(count * heads, width)
            turned = dot(order(count), block, 1, 0).astype(BF16)
            out_ref[:, start : start + count, :width] = turned.reshape(heads, count, width)

    turn(w_ref, wt_ref)
    qt_ref[...] = jnp.zeros_like(qt_ref)
    turn(q_ref, qt_ref)
    turn(g_ref, gt_ref)


def by_head(up_weight, queries, out_grad, chunk, heads):
    tok = queries.shape[0]
    steps = 4
    depth, rows = LAT // steps, tok // steps
    return pl.pallas_call(
        by_head_kernel,
        grid=(steps,),
        in_specs=[
            pl.BlockSpec((depth, heads, PAIR), lambda i: (i, chunk, 0)),
            pl.BlockSpec((rows, heads, PLAIN_WIDTH + ROPE), lambda i: (i, chunk, 0)),
            pl.BlockSpec((rows, heads, VDIM), lambda i: (i, chunk, 0)),
        ],
        out_specs=[
            pl.BlockSpec((heads, depth, PAIR), lambda i: (0, i, 0)),
            pl.BlockSpec((heads, rows, 2 * LANES), lambda i: (0, i, 0)),
            pl.BlockSpec((heads, rows, VDIM), lambda i: (0, i, 0)),
        ],
        out_shape=[
            jax.ShapeDtypeStruct((heads, LAT, PAIR), BF16),
            jax.ShapeDtypeStruct((heads, tok, 2 * LANES), BF16),
            jax.ShapeDtypeStruct((heads, tok, VDIM), BF16),
        ],
        compiler_params=WIDE,
        cost_estimate=cost(BY_HEAD),
        name="by_head",
    )(up_weight, queries, out_grad)


def window_kernel(here_ref, prev_ref, own_ref, ids_ref, *outs, paired):
    win_ref, krope_ref, vis_ref = outs[:3]
    here = here_ref[0]
    tok = prev_ref.shape[0]
    win_ref[:tok, :] = prev_ref[:, :LAT]
    win_ref[tok:, :] = own_ref[:, :LAT]
    krope_ref[...] = jnp.zeros_like(krope_ref)
    krope_ref[:tok, :ROPE] = prev_ref[:, LAT:]
    krope_ref[tok:, :ROPE] = own_ref[:, LAT:]
    behind = jnp.maximum(here - 1, 0)
    seg_prev = jnp.where(here > 0, ids_ref[pl.ds(behind, 1), :], -1)
    seg_own = ids_ref[pl.ds(here, 1), :]
    row = lax.broadcasted_iota(jnp.int32, (tok, tok), 0)
    col = lax.broadcasted_iota(jnp.int32, (tok, tok), 1)
    seg_query = jnp.sum(jnp.where(row == col, seg_own, 0), 1, keepdims=True)
    vis_ref[:, :tok] = (seg_query == seg_prev).astype(F32)
    vis_ref[:, tok:] = ((seg_query == seg_own) & (col <= row)).astype(F32)
    if paired:
        source = lax.broadcasted_iota(jnp.int32, (LAT, LAT), 0)
        column = lax.broadcasted_iota(jnp.int32, (LAT, LAT), 1)
        place = column >> 6
        apart = ((place & 1) << 2) | (place & 2) | (place >> 2)
        wanted = ((here ^ apart) << 6) | (column & 63)
        ordered = dot(win_ref[...], (source == wanted).astype(BF16), 1, 0).astype(BF16)
        outs[3][...] = ordered[:, : LAT // 2]
        outs[4][...] = ordered[:, LAT // 2 :]


def key_window(here, prev, own, ids, paired):
    tok = prev.shape[0]
    whole = lambda i, here: (0, 0)
    shapes = [((2 * tok, LAT), BF16), ((2 * tok, LANES), BF16), ((tok, 2 * tok), F32)]
    if paired:
        shapes = shapes + [((2 * tok, LAT // 2), BF16)] * 2
    return pl.pallas_call(
        functools.partial(window_kernel, paired=paired),
        grid_spec=pltpu.PrefetchScalarGridSpec(
            num_scalar_prefetch=1,
            grid=(1,),
            in_specs=[pl.BlockSpec(array.shape, whole) for array in (prev, own, ids)],
            out_specs=[pl.BlockSpec(shape, whole) for shape, _ in shapes],
        ),
        out_shape=[jax.ShapeDtypeStruct(*shape) for shape in shapes],
        compiler_params=PARAMS,
        cost_estimate=cost(WINDOW),
        name="key_window",
    )(here, prev, own, ids)


def attention_kernel(
    win_ref, krope_ref, vis_ref, wt_ref, qt_ref, gt_ref, *refs, aliased, extra
):
    latents_ref = refs[0] if extra else None
    refs = refs[1:] if extra else refs
    refs = refs[1:] if aliased else refs
    dq_ref, dkv_ref, rope_ref, dqn_ref, dqr_ref = refs
    i = pl.program_id(0)
    tok, heads = dq_ref.shape[:2]
    scale = 1.0 / math.sqrt(PLAIN_WIDTH + ROPE)

    @pl.when(i == 0)
    def _():
        rope_ref[...] = jnp.zeros_like(rope_ref)
        if extra:
            dkv_ref[:, heads * PAIR :] = latents_ref[...]

    visible = vis_ref[...] > 0.0
    window = win_ref[...]
    krope = krope_ref[...]
    count = wt_ref.shape[0]
    keys, values = [], []
    for h in range(count):
        kv = dot(window, wt_ref[h], 1, 0).astype(BF16)
        keys.append(jnp.concatenate([kv[:, :PLAIN_WIDTH], krope], 1))
        values.append(kv[:, PLAIN_WIDTH:])
    scores = [dot(qt_ref[h], keys[h], 1, 1) for h in range(count)]
    dprobs = [dot(gt_ref[h], values[h], 1, 1) for h in range(count)]
    dscores, probs16 = [], []
    for h in range(count):
        logits = jnp.where(visible, scores[h] * scale, -1e30)
        top = jnp.max(logits, -1, keepdims=True)
        expo = jnp.exp(logits - top)
        probs = expo / jnp.sum(expo, -1, keepdims=True)
        delta = jnp.sum(probs * dprobs[h], -1, keepdims=True)
        dscores.append((probs * (dprobs[h] - delta) * scale).astype(BF16))
        probs16.append(probs.astype(BF16))
    parts, rope = [], rope_ref[...]
    for h in range(count):
        dk = dot(dscores[h], qt_ref[h], 0, 0)
        dv = dot(probs16[h], gt_ref[h], 0, 0)
        parts.append(jnp.concatenate([dk[:, :PLAIN_WIDTH], dv], 1).astype(BF16))
        rope = rope + dk[:, PLAIN_WIDTH:]
    rope_ref[...] = rope
    dkv_ref[:, pl.ds(pl.multiple_of(i * (count * PAIR), count * PAIR), count * PAIR)] = (
        jnp.concatenate(parts, 1)
    )
    for h in range(count):
        dq = dot(dscores[h], keys[h], 1, 0)
        dqn_ref[pl.ds(i * count + h, tok, stride=heads), :] = dq[:, :PLAIN_WIDTH]
        dqr_ref[pl.ds(i * count + h, tok, stride=heads), :] = dq[:, PLAIN_WIDTH:]

    @pl.when(i == pl.num_programs(0) - 1)
    def _():
        dq_ref[:, :, :PLAIN_WIDTH] = dqn_ref[...].reshape(tok, heads, LANES)
        dq_ref[:, :, PLAIN_WIDTH:] = dqr_ref[...].reshape(tok, heads, LANES)[:, :, :ROPE]


def attention(window, turned, latents, dq, chunk, heads, first, all_heads):
    weight, queries, out_grad = turned
    tok = queries.shape[1]
    width = 2 * tok
    steps = heads // STEP_HEADS
    at = first // STEP_HEADS
    extra = LAT // 2 if latents is not None else 0
    whole = lambda i: (0, 0)
    head_block = lambda i: (at + i, 0, 0)
    operands = [*window, weight, queries, out_grad]
    in_specs = [pl.BlockSpec(array.shape, whole) for array in window] + [
        pl.BlockSpec((STEP_HEADS, LAT, PAIR), head_block),
        pl.BlockSpec((STEP_HEADS, tok, 2 * LANES), head_block),
        pl.BlockSpec((STEP_HEADS, tok, VDIM), head_block),
    ]
    if latents is not None:
        in_specs.append(pl.BlockSpec(latents.shape, whole))
        operands.append(latents)
    aliases = {}
    if dq is not None:
        aliases = {len(operands): 0}
        in_specs.append(pl.BlockSpec(memory_space=pl.ANY))
        operands.append(dq)
    return pl.pallas_call(
        functools.partial(attention_kernel, aliased=dq is not None, extra=latents is not None),
        grid=(steps,),
        in_specs=in_specs,
        out_specs=[
            pl.BlockSpec((tok, heads, PLAIN_WIDTH + ROPE), lambda i: (0, chunk, 0)),
            pl.BlockSpec((width, heads * PAIR + extra), whole),
            pl.BlockSpec((width, LANES), whole),
        ],
        scratch_shapes=[
            pltpu.VMEM((tok * heads, LANES), F32),
            pltpu.VMEM((tok * heads, LANES), F32),
        ],
        out_shape=[
            jax.ShapeDtypeStruct((tok, all_heads, PLAIN_WIDTH + ROPE), F32),
            jax.ShapeDtypeStruct((width, heads * PAIR + extra), BF16),
            jax.ShapeDtypeStruct((width, LANES), F32),
        ],
        input_output_aliases=aliases,
        compiler_params=WIDE,
        cost_estimate=cost(ATTENTION),
        name="attention",
    )(*operands)


def terms_kernel(
    own_ref, other_ref, mine_ref, theirs_ref, keep_ref, send_ref, latents_ref, *, along_x
):
    width = own_ref.shape[0]

    @pl.when(pl.program_id(0) == 0)
    def _():
        latents_ref[:, :width] = mine_ref[...].T
        latents_ref[:, width:] = theirs_ref[...].T

    grads = jnp.concatenate([own_ref[...], other_ref[...]], 0)
    term = dot(latents_ref[...], grads, 1, 0)
    rows = term.shape[0] // 4
    first, second = (1, 2) if along_x else (2, 1)
    keep_ref[:rows] = term[:rows]
    keep_ref[rows:] = term[first * rows : (first + 1) * rows]
    send_ref[:rows] = term[second * rows : (second + 1) * rows].astype(BF16)
    send_ref[rows:] = term[3 * rows :].astype(BF16)


def terms(own, other, mine, theirs, columns, along_x):
    width = own.shape[0]
    block = 1024
    at = theirs.shape[1] // (LAT // 2) - 1
    column_block = lambda i: (0, i)
    return pl.pallas_call(
        functools.partial(terms_kernel, along_x=along_x),
        grid=(columns // block,),
        in_specs=[
            pl.BlockSpec((width, block), column_block),
            pl.BlockSpec((width, block), column_block),
            pl.BlockSpec((width, LAT // 2), lambda i: (0, 0)),
            pl.BlockSpec((width, LAT // 2), lambda i: (0, at)),
        ],
        out_specs=[pl.BlockSpec((LAT // 4, block), column_block)] * 2,
        out_shape=[
            jax.ShapeDtypeStruct((LAT // 4, columns), F32),
            jax.ShapeDtypeStruct((LAT // 4, columns), BF16),
        ],
        scratch_shapes=[pltpu.VMEM((LAT // 2, 2 * width), BF16)],
        compiler_params=PARAMS,
        cost_estimate=cost(TERMS),
        name="terms",
    )(own, other, mine, theirs)


def key_terms_kernel(*refs, chunks, steps, turns, shares):
    head_ref = refs[0]
    dkv_refs = refs[1 : 1 + chunks]
    wt_refs = refs[1 + chunks : 1 + chunks + turns]
    rope_refs = refs[1 + chunks + turns : 1 + 2 * chunks + turns]
    outs = refs[1 + 2 * chunks + turns : -1]
    total_ref = refs[-1]
    i = pl.program_id(0)

    @pl.when(i == 0)
    def _():
        total_ref[...] = jnp.zeros_like(total_ref)

    for k in range(chunks):

        @pl.when(i // steps == k)
        def _(k=k):
            total = total_ref[...]
            weight_ref = wt_refs[k * turns // chunks]
            for h in range(weight_ref.shape[0]):
                grads = dkv_refs[k][:, h * PAIR : (h + 1) * PAIR]
                total = total + dot(grads, weight_ref[h], 1, 1)
            total_ref[...] = total

    @pl.when(i == pl.num_programs(0) - 1)
    def _():
        rope = rope_refs[0][...]
        for k in range(1, chunks):
            rope = rope + rope_refs[k][...]
        both = jnp.concatenate([total_ref[...], rope], 1)
        if shares is None:
            outs[0][...] = both[:, : LAT + ROPE]
            return
        part = (LAT + ROPE) // shares
        for z in range(shares):
            piece = both[:, z * part : (z + 1) * part]
            for s in range(shares):

                @pl.when(lax.rem(head_ref[0] + s, shares) == z)
                def _(s=s, piece=piece):
                    outs[s][...] = piece


def key_terms(at_head, dkvs, weights, ropes, shares):
    chunks, turns = len(dkvs), len(weights)
    heads = weights[0].shape[0] * turns // chunks
    width = dkvs[0].shape[0]
    steps = heads // STEP_HEADS
    span = steps * chunks // turns
    near = lambda k, many: lambda i, at: jnp.clip(i - k * many, 0, many - 1)
    wide = (LAT + ROPE) // (shares or 1)
    return pl.pallas_call(
        functools.partial(
            key_terms_kernel, chunks=chunks, steps=steps, turns=turns, shares=shares
        ),
        grid_spec=pltpu.PrefetchScalarGridSpec(
            num_scalar_prefetch=1,
            grid=(chunks * steps,),
            in_specs=[
                pl.BlockSpec((width, STEP_HEADS * PAIR), lambda i, at, k=k: (0, near(k, steps)(i, at)))
                for k in range(chunks)
            ]
            + [
                pl.BlockSpec(
                    (STEP_HEADS, LAT, PAIR), lambda i, at, k=k: (near(k, span)(i, at), 0, 0)
                )
                for k in range(turns)
            ]
            + [pl.BlockSpec((width, LANES), lambda i, at: (0, 0))] * chunks,
            out_specs=[pl.BlockSpec((width, wide), lambda i, at: (0, 0))] * (shares or 1),
            scratch_shapes=[pltpu.VMEM((width, LAT), F32)],
        ),
        out_shape=[jax.ShapeDtypeStruct((width, wide), F32)] * (shares or 1),
        compiler_params=WIDE,
        cost_estimate=cost(KEY_TERMS),
        name="key_terms",
    )(at_head, *dkvs, *weights, *ropes)


def weight_sum_kernel(keep_ref, first_ref, second_ref, *refs):
    out_ref, k_ref, v_ref = refs[-3:]
    rows, heads, _ = out_ref.shape
    for h in range(heads):
        columns = slice(h * PAIR, (h + 1) * PAIR)
        total = keep_ref[:, columns] + first_ref[:, columns].astype(F32)
        total = total + second_ref[:, columns].astype(F32)
        k_ref[pl.ds(h, rows, stride=heads), :] = total[:, :LANES]
        v_ref[pl.ds(h, rows, stride=heads), :] = total[:, LANES:]
    out_ref[:, :, :LANES] = k_ref[...].reshape(rows, heads, LANES)
    out_ref[:, :, LANES:] = v_ref[...].reshape(rows, heads, LANES)


def weight_sum(keep, first, second, total, chunk, all_heads):
    rows, columns = second.shape
    heads = columns // PAIR
    block = 32
    operands = [keep, first, second]
    in_specs = [pl.BlockSpec((block, columns), lambda i: (i, 0)) for _ in operands]
    aliases = {}
    if total is not None:
        aliases = {3: 0}
        in_specs.append(pl.BlockSpec(memory_space=pl.ANY))
        operands.append(total)
    return pl.pallas_call(
        weight_sum_kernel,
        grid=(rows // block,),
        in_specs=in_specs,
        out_specs=pl.BlockSpec((block, heads, PAIR), lambda i: (i, chunk, 0)),
        out_shape=jax.ShapeDtypeStruct((rows, all_heads, PAIR), F32),
        scratch_shapes=[pltpu.VMEM((block * heads, LANES), F32)] * 2,
        input_output_aliases=aliases,
        compiler_params=PARAMS,
        cost_estimate=cost(WEIGHT_SUM),
        name="weight_sum",
    )(*operands)


def after(values, earlier):
    return lax.optimization_barrier((values, earlier))[0]


def turn_rows(block):
    rows, heads, width = block.shape
    count = min(rows, 256 // heads)
    row = lax.broadcasted_iota(jnp.int32, (count * heads, count * heads), 0)
    col = lax.broadcasted_iota(jnp.int32, (count * heads, count * heads), 1)
    order = (col == (row % count) * heads + row // count).astype(BF16)
    for start in range(0, rows, count):
        part = block[start : start + count].reshape(count * heads, width)
        turned = dot(order, part, 1, 0).astype(BF16)
        yield slice(start, start + count), turned.reshape(heads, count, width)


def turn_weight_kernel(here_ref, w_ref, wt_ref):
    for rows, turned in turn_rows(w_ref[...]):
        wt_ref[:, rows, :] = turned


def turn_weight(here, up_weight, heads):
    steps = 4
    depth = LAT // steps
    return pl.pallas_call(
        turn_weight_kernel,
        grid_spec=pltpu.PrefetchScalarGridSpec(
            num_scalar_prefetch=1,
            grid=(steps,),
            in_specs=[
                pl.BlockSpec((depth, heads, PAIR), lambda i, here: (i, here[0] & 1, 0)),
            ],
            out_specs=pl.BlockSpec((heads, depth, PAIR), lambda i, here: (0, i, 0)),
        ),
        out_shape=jax.ShapeDtypeStruct((heads, LAT, PAIR), BF16),
        compiler_params=PARAMS,
        cost_estimate=cost(BY_HEAD),
        name="turn_weight",
    )(here, up_weight)


def turn_tokens_kernel(here_ref, q1_ref, g1_ref, q0_ref, g0_ref, give_ref, mine_ref):
    for q_ref, g_ref, out_ref in ((q1_ref, g1_ref, give_ref), (q0_ref, g0_ref, mine_ref)):
        out_ref[:, :, LANES : 2 * LANES] = jnp.zeros_like(out_ref[:, :, LANES : 2 * LANES])
        for rows, turned in turn_rows(q_ref[...]):
            out_ref[:, rows, : PLAIN_WIDTH + ROPE] = turned
        for rows, turned in turn_rows(g_ref[...]):
            out_ref[:, rows, 2 * LANES :] = turned


def turn_tokens(here, queries, out_grad, heads):
    tok = queries.shape[0]
    q_block, g_block = (tok, heads, PLAIN_WIDTH + ROPE), (tok, heads, VDIM)
    given = lambda i, here: (0, 1 - (here[0] & 1), 0)
    kept = lambda i, here: (0, here[0] & 1, 0)
    shape = (heads, tok, 3 * LANES)
    return pl.pallas_call(
        turn_tokens_kernel,
        grid_spec=pltpu.PrefetchScalarGridSpec(
            num_scalar_prefetch=1,
            grid=(1,),
            in_specs=[
                pl.BlockSpec(q_block, given),
                pl.BlockSpec(g_block, given),
                pl.BlockSpec(q_block, kept),
                pl.BlockSpec(g_block, kept),
            ],
            out_specs=[pl.BlockSpec(shape, lambda i, here: (0, 0, 0))] * 2,
        ),
        out_shape=[jax.ShapeDtypeStruct(shape, BF16)] * 2,
        compiler_params=PARAMS,
        cost_estimate=cost(WINDOW),
        name="turn_tokens",
    )(here, queries, out_grad, queries, out_grad)


def chip_window_kernel(
    here_ref, even_ref, odd_ref, own_ref, pal_ref, ids_ref, win_ref, krope_ref, vis_ref, lat_ref
):
    here = here_ref[0]
    tok = own_ref.shape[0]
    core, chip = here & 1, here >> 1
    first = core == 0
    prev = jnp.where(first, even_ref[...].astype(F32), odd_ref[...].astype(F32)).astype(BF16)
    own, pal = own_ref[...].astype(F32), pal_ref[...].astype(F32)
    low = jnp.where(first, own, pal).astype(BF16)
    high = jnp.where(first, pal, own).astype(BF16)
    krope_ref[...] = jnp.zeros_like(krope_ref)
    for at, block in enumerate((prev, low, high)):
        win_ref[at * tok : (at + 1) * tok, :] = block[:, :LAT]
        krope_ref[at * tok : (at + 1) * tok, :ROPE] = block[:, LAT:]
    behind = jnp.maximum(2 * chip - 1, 0)
    seg = [
        jnp.where(chip > 0, ids_ref[pl.ds(behind, 1), :], -1),
        ids_ref[pl.ds(2 * chip, 1), :],
        ids_ref[pl.ds(2 * chip + 1, 1), :],
    ]
    row = lax.broadcasted_iota(jnp.int32, (tok, tok), 0)
    col = lax.broadcasted_iota(jnp.int32, (tok, tok), 1)
    for b in range(2):
        seg_query = jnp.sum(jnp.where(row == col, seg[b + 1], 0), 1, keepdims=True)
        vis_ref[b, :, :tok] = (seg_query == seg[b]).astype(F32)
        vis_ref[b, :, tok:] = ((seg_query == seg[b + 1]) & (col <= row)).astype(F32)
    column = lax.broadcasted_iota(jnp.int32, (LAT, LAT), 0)
    source = lax.broadcasted_iota(jnp.int32, (LAT, LAT), 1)
    place = column >> 6
    apart = ((place & 2) << 1) | ((place & 4) >> 1) | (place & 1)
    wanted = ((here ^ apart) << 6) | (column & 63)
    order = (source == wanted).astype(BF16)
    lat_ref[...] = dot(order, win_ref[...], 1, 1).astype(BF16)


def chip_window(here, even, odd, own, pal, ids):
    tok = own.shape[0]
    whole = lambda i, here: (0, 0)
    return pl.pallas_call(
        chip_window_kernel,
        grid_spec=pltpu.PrefetchScalarGridSpec(
            num_scalar_prefetch=1,
            grid=(1,),
            in_specs=[pl.BlockSpec(array.shape, whole) for array in (even, odd, own, pal, ids)],
            out_specs=[
                pl.BlockSpec((3 * tok, LAT), whole),
                pl.BlockSpec((3 * tok, LANES), whole),
                pl.BlockSpec((2, tok, 2 * tok), lambda i, here: (0, 0, 0)),
                pl.BlockSpec((LAT, 3 * tok), whole),
            ],
        ),
        out_shape=[
            jax.ShapeDtypeStruct((3 * tok, LAT), BF16),
            jax.ShapeDtypeStruct((3 * tok, LANES), BF16),
            jax.ShapeDtypeStruct((2, tok, 2 * tok), F32),
            jax.ShapeDtypeStruct((LAT, 3 * tok), BF16),
        ],
        compiler_params=PARAMS,
        cost_estimate=cost(WINDOW),
        name="chip_window",
    )(here, even, odd, own, pal, ids)


def chunk_kernel(
    here_ref,
    win_ref,
    krope_ref,
    vis_ref,
    lat_ref,
    wt_ref,
    mine_ref,
    got_ref,
    *refs,
    chained,
    along_x,
):
    before_ref = refs[0] if chained else None
    refs = refs[3:] if chained else refs
    keep_ref, send_ref, key_ref, dq_ref, back_ref = refs
    tok = vis_ref.shape[1]
    heads = wt_ref.shape[0]
    first = (here_ref[0] & 1) == 0
    scale = 1.0 / math.sqrt(PLAIN_WIDTH + ROPE)
    window, krope = win_ref[...], krope_ref[...]
    visible = [vis_ref[b] > 0.0 for b in range(2)]
    keys, values, queries, grads = [], [], [], []
    for h in range(heads):
        kv = dot(window, wt_ref[h], 1, 0).astype(BF16)
        keys.append(jnp.concatenate([kv[:, :PLAIN_WIDTH], krope], 1))
        values.append(kv[:, PLAIN_WIDTH:])
        mine, got = mine_ref[h], got_ref[h]
        ordered = (jnp.where(first, mine, got), jnp.where(first, got, mine))
        queries.append([block[:, : 2 * LANES] for block in ordered])
        grads.append([block[:, 2 * LANES :] for block in ordered])
    reach = [slice(b * tok, (b + 2) * tok) for b in range(2)]
    units = [(h, b) for h in range(heads) for b in range(2)]
    scores = {(h, b): dot(queries[h][b], keys[h][reach[b]], 1, 1) for h, b in units}
    dprobs = {(h, b): dot(grads[h][b], values[h][reach[b]], 1, 1) for h, b in units}
    dscores, probs16 = {}, {}
    for unit in units:
        logits = jnp.where(visible[unit[1]], scores[unit] * scale, -1e30)
        top = jnp.max(logits, -1, keepdims=True)
        expo = jnp.exp(logits - top)
        probs = expo / jnp.sum(expo, -1, keepdims=True)
        delta = jnp.sum(probs * dprobs[unit], -1, keepdims=True)
        dscores[unit] = (probs * (dprobs[unit] - delta) * scale).astype(BF16)
        probs16[unit] = probs.astype(BF16)

    def fold(low, high):
        return jnp.concatenate([low[:tok], low[tok:] + high[:tok], high[tok:]], 0)

    parts, rope = [], None
    for h in range(heads):
        dk = fold(*[dot(dscores[h, b], queries[h][b], 0, 0) for b in range(2)])
        dv = fold(*[dot(probs16[h, b], grads[h][b], 0, 0) for b in range(2)])
        parts.append(jnp.concatenate([dk[:, :PLAIN_WIDTH], dv], 1).astype(BF16))
        rope = dk[:, PLAIN_WIDTH:] if rope is None else rope + dk[:, PLAIN_WIDTH:]
    dkv = jnp.concatenate(parts, 1)
    rows = lat_ref.shape[0] // 4
    kept = (0, 1) if along_x else (0, 2)
    sent = (2, 3) if along_x else (1, 3)
    for at, g in enumerate(sent):
        term = dot(lat_ref[g * rows : (g + 1) * rows, :], dkv, 1, 0)
        send_ref[at * rows : (at + 1) * rows, :] = term.astype(BF16)
    for at, g in enumerate(kept):
        keep_ref[at * rows : (at + 1) * rows, :] = dot(
            lat_ref[g * rows : (g + 1) * rows, :], dkv, 1, 0
        )
    total = before_ref[:, :LAT] if chained else None
    for h in range(heads):
        term = dot(parts[h], wt_ref[h], 1, 1)
        total = term if total is None else total + term
    key_ref[:, :LAT] = total
    key_ref[:, LAT:] = rope + before_ref[:, LAT:] if chained else rope
    for h in range(heads):
        low, high = (dot(dscores[h, b], keys[h][reach[b]], 1, 0) for b in range(2))
        dq_ref[h] = jnp.where(first, low, high)
        back_ref[h] = jnp.where(first, high, low)


def chunk(here, window, weight, mine, got, before, index, heads, along_x):
    tok = mine.shape[1]
    whole = lambda i, here: (0, 0)
    whole3 = lambda i, here: (0, 0, 0)
    at = lambda i, here: (index, 0, 0)
    columns = heads * PAIR
    operands = [*window, weight, mine, got]
    in_specs = [
        pl.BlockSpec(array.shape, whole3 if array.ndim == 3 else whole) for array in window
    ] + [
        pl.BlockSpec((heads, LAT, PAIR), at),
        pl.BlockSpec((heads, tok, 3 * LANES), at),
        pl.BlockSpec((heads, tok, 3 * LANES), at),
    ]
    aliases = {}
    if before is not None:
        key, dq, back = before
        aliases = {len(operands) + 2: 3, len(operands) + 3: 4}
        in_specs = in_specs + [
            pl.BlockSpec(key.shape, whole),
            pl.BlockSpec(memory_space=pl.ANY),
            pl.BlockSpec(memory_space=pl.ANY),
        ]
        operands = operands + [key, dq, back]
    turned = (weight.shape[0], tok, 2 * LANES)
    return pl.pallas_call(
        functools.partial(chunk_kernel, chained=before is not None, along_x=along_x),
        grid_spec=pltpu.PrefetchScalarGridSpec(
            num_scalar_prefetch=1,
            grid=(1,),
            in_specs=in_specs,
            out_specs=[
                pl.BlockSpec((LAT // 2, columns), whole),
                pl.BlockSpec((LAT // 2, columns), whole),
                pl.BlockSpec((3 * tok, LAT + LANES), whole),
                pl.BlockSpec((heads, tok, 2 * LANES), at),
                pl.BlockSpec((heads, tok, 2 * LANES), at),
            ],
        ),
        out_shape=[
            jax.ShapeDtypeStruct((LAT // 2, columns), F32),
            jax.ShapeDtypeStruct((LAT // 2, columns), BF16),
            jax.ShapeDtypeStruct((3 * tok, LAT + LANES), F32),
            jax.ShapeDtypeStruct(turned, F32),
            jax.ShapeDtypeStruct(turned, F32),
        ],
        input_output_aliases=aliases,
        compiler_params=PARAMS,
        cost_estimate=cost(ATTENTION),
        name="chunk",
    )(here, *operands)


def key_shares_kernel(at_ref, key_ref, *outs):
    shares = len(outs)
    part = (LAT + ROPE) // shares
    for z in range(shares):
        piece = key_ref[:, z * part : (z + 1) * part]
        for s in range(shares):

            @pl.when(lax.rem(at_ref[0] + s, shares) == z)
            def _(s=s, piece=piece):
                outs[s][...] = piece


def key_shares(at_head, key, shares):
    part = (LAT + ROPE) // shares
    whole = lambda i, at: (0, 0)
    return pl.pallas_call(
        key_shares_kernel,
        grid_spec=pltpu.PrefetchScalarGridSpec(
            num_scalar_prefetch=1,
            grid=(1,),
            in_specs=[pl.BlockSpec(key.shape, whole)],
            out_specs=[pl.BlockSpec((key.shape[0], part), whole)] * shares,
        ),
        out_shape=[jax.ShapeDtypeStruct((key.shape[0], part), F32)] * shares,
        compiler_params=PARAMS,
        cost_estimate=cost(KEY_TERMS),
        name="key_shares",
    )(at_head, key)


def query_grad_kernel(here_ref, mine_ref, got_ref, out_ref, n_ref, r_ref):
    tok, heads, _ = out_ref.shape

    def put(src_ref):
        for h in range(heads):
            n_ref[pl.ds(h, tok, stride=heads), :] = src_ref[h, :, :PLAIN_WIDTH]
            r_ref[pl.ds(h, tok, stride=heads), :] = src_ref[h, :, PLAIN_WIDTH:]

    pl.when(pl.program_id(0) == 0)(lambda: put(mine_ref))
    pl.when(pl.program_id(0) == 1)(lambda: put(got_ref))
    out_ref[:, :, :PLAIN_WIDTH] = n_ref[...].reshape(tok, heads, LANES)
    out_ref[:, :, PLAIN_WIDTH:] = r_ref[...].reshape(tok, heads, LANES)[:, :, :ROPE]


def query_grad(here, mine, got):
    heads, tok, _ = mine.shape
    whole = lambda i, here: (0, 0, 0)
    return pl.pallas_call(
        query_grad_kernel,
        grid_spec=pltpu.PrefetchScalarGridSpec(
            num_scalar_prefetch=1,
            grid=(2,),
            in_specs=[pl.BlockSpec(mine.shape, whole)] * 2,
            out_specs=pl.BlockSpec(
                (tok, heads, PLAIN_WIDTH + ROPE), lambda i, here: (0, (here[0] & 1) ^ i, 0)
            ),
            scratch_shapes=[pltpu.VMEM((tok * heads, LANES), F32)] * 2,
        ),
        out_shape=jax.ShapeDtypeStruct((tok, 2 * heads, PLAIN_WIDTH + ROPE), F32),
        compiler_params=PARAMS,
        cost_estimate=cost(WEIGHT_SUM),
        name="query_grad",
    )(here, mine, got)


def weight_grad_kernel(here_ref, *refs, count):
    sums, gots = refs[: 3 * count], refs[3 * count : 4 * count]
    out_ref, k_ref, v_ref = refs[-3:]
    rows, heads, _ = out_ref.shape
    each = heads // count

    def put(c, total):
        for h in range(each):
            at = pl.ds(c * each + h, rows, stride=heads)
            k_ref[at, :] = total[:, h * PAIR : h * PAIR + LANES]
            v_ref[at, :] = total[:, h * PAIR + LANES : (h + 1) * PAIR]

    @pl.when(pl.program_id(0) == 0)
    def _():
        for c in range(count):
            keep_ref, first_ref, second_ref = sums[3 * c : 3 * c + 3]
            put(c, keep_ref[...] + first_ref[...].astype(F32) + second_ref[...].astype(F32))

    @pl.when(pl.program_id(0) == 1)
    def _():
        for c in range(count):
            put(c, gots[c][...])

    out_ref[:, :, :LANES] = k_ref[...].reshape(rows, heads, LANES)
    out_ref[:, :, LANES:] = v_ref[...].reshape(rows, heads, LANES)


def weight_grad_pair(here, sums, gots, total, pair, pairs):
    count = len(sums)
    rows, columns = gots[0].shape
    heads = count * columns // PAIR
    whole = lambda i, here: (0, 0)
    operands = [array for part in sums for array in part] + list(gots)
    in_specs = [pl.BlockSpec((rows, columns), whole) for _ in operands]
    aliases = {}
    if total is not None:
        aliases = {1 + len(operands): 0}
        in_specs.append(pl.BlockSpec(memory_space=pl.ANY))
        operands.append(total)
    return pl.pallas_call(
        functools.partial(weight_grad_kernel, count=count),
        grid_spec=pltpu.PrefetchScalarGridSpec(
            num_scalar_prefetch=1,
            grid=(2,),
            in_specs=in_specs,
            out_specs=pl.BlockSpec(
                (rows, heads, PAIR), lambda i, here: (0, ((here[0] & 1) ^ i) * pairs + pair, 0)
            ),
            scratch_shapes=[pltpu.VMEM((rows * heads, LANES), F32)] * 2,
        ),
        out_shape=jax.ShapeDtypeStruct((rows, 2 * pairs * heads, PAIR), F32),
        input_output_aliases=aliases,
        compiler_params=PARAMS,
        cost_estimate=cost(WEIGHT_SUM),
        name="weight_grad",
    )(here, *operands)


def in_chunks(queries, latent_keys, out_grad, up_weight, here, at_head, ids):
    tok = latent_keys.shape[0]
    n_ctx, n_head = lax.axis_size("ctx"), lax.axis_size("head")
    chunks, each, heads = 4, 4, 16
    first = here[0] % 2 == 0
    give, mine = turn_tokens(here, queries, out_grad, heads)
    pal = across(latent_keys, 1)
    odd_devices = range(1, n_ctx - 1, 2)
    even = lax.ppermute(latent_keys, "ctx", [(source, source + 1) for source in odd_devices])
    odd = lax.ppermute(latent_keys, "ctx", [(source, source + 2) for source in odd_devices])
    got = across(give, 1)
    weight = turn_weight(here, up_weight, heads)
    window = chip_window(here, even, odd, latent_keys, pal, ids)
    before, keeps, sent = None, [], []
    for c in range(chunks):
        keep, out, *before = chunk(here, window, weight, mine, got, before, c, each, c % 2 == 0)
        keeps.append(keep)
        sent.append(across(out, 2 if c % 2 == 0 else 4))
    key, dq, back = before
    lasts, theirs = [], []

    def forward(c):
        rest = keeps[c][2 * tok :] + sent[c][2 * tok :].astype(F32)
        lasts.append(across(rest.astype(BF16), 4 if c % 2 == 0 else 2))
        return rest

    shares = key_shares(at_head, after(key, forward(0)), n_head)
    shares = after(shares, forward(1))
    share, pieces = shares[0], [
        lax.ppermute(shares[s], "head", [(z, (z + s) % n_head) for z in range(n_head)])
        for s in range(1, n_head)
    ]
    share, pieces = after((share, pieces), forward(2))
    for piece in pieces:
        share = share + piece
    behind, low, high = share[:tok], share[tok : 2 * tok], share[2 * tok :]
    swap = jnp.concatenate([jnp.where(first, high, low), behind], 0)
    swap = across(swap, 1)
    forward(3)
    key_grad = jnp.where(first, low, high) + swap[:tok]
    key_grad = key_grad + lax.ppermute(
        behind + swap[tok:], "ctx", [(source, source - 1) for source in range(2, n_ctx, 2)]
    )
    dq = query_grad(here, dq, across(back, 1))
    for c in range(chunks):
        part = slice(tok, 2 * tok)
        total = keeps[c][part] + sent[c][part].astype(F32) + lasts[c][part].astype(F32)
        theirs.append(across(total, 1))
    weight_grad = None
    for p in range(chunks // 2):
        pair = range(2 * p, 2 * p + 2)
        weight_grad = weight_grad_pair(
            here,
            [(keeps[c], sent[c], lasts[c]) for c in pair],
            [theirs[c] for c in pair],
            weight_grad,
            p,
            chunks // 2,
        )
    return dq, key_grad, weight_grad


def shards(queries, latent_keys, out_grad, up_weight, segment_ids):
    tok = latent_keys.shape[0]
    heads = queries.shape[1]
    n_ctx, n_head = lax.axis_size("ctx"), lax.axis_size("head")
    here = lax.axis_index("ctx").astype(jnp.int32).reshape(1)
    at_head = lax.axis_index("head").astype(jnp.int32).reshape(1)
    ids = segment_ids.reshape(n_ctx, tok)
    if n_ctx == 8 and heads == 32 and n_head == 4:
        return in_chunks(queries, latent_keys, out_grad, up_weight, here, at_head, ids)
    else:
        prev = from_behind(latent_keys, "ctx", REACH)
        turned = by_head(up_weight, queries, out_grad, 0, heads)
        window = key_window(here, prev, latent_keys, ids, False)
        dq, dkv, rope = attention(window, turned, None, None, 0, heads, 0, heads)
        (both,) = key_terms(at_head, [dkv], [turned[0]], [rope], None)
        share = lax.psum_scatter(
            both.reshape(REACH + 1, tok, LAT + ROPE), "head", scatter_dimension=2, tiled=True
        )
        term = jnp.einsum("ki,ke->ie", window[0], dkv, preferred_element_type=F32)
        rows = lax.psum_scatter(term.astype(BF16), "ctx", scatter_dimension=0, tiled=True)
        weight_grad = rows.astype(F32).reshape(rows.shape[0], heads, PAIR)
    key_grad = share[REACH] + from_behind(share[0], "ctx", 0 - REACH)
    return (dq, key_grad, weight_grad)


def solution(mesh):
    return jax.shard_map(
        shards,
        mesh=mesh,
        in_specs=(
            P("ctx", "head", None),
            P("ctx", None),
            P("ctx", "head", None),
            P(None, "head", None),
            P(),
        ),
        out_specs=(P("ctx", "head", None), P("ctx", "head"), P("ctx", "head", None)),
        check_vma=False,
    )
```

```python
import functools
import math

import jax
import jax.numpy as jnp
from jax import lax
from jax.experimental import pallas as pl
from jax.experimental.pallas import tpu as pltpu
from jax.sharding import PartitionSpec as P

LAT = 512
ROPE = 64
PLAIN_WIDTH = 128
VDIM = 128
REACH = 1
LANES = 128
PAIR = PLAIN_WIDTH + VDIM
STEP_HEADS = 4
BF16 = jnp.bfloat16
F32 = jnp.float32
WIDE = pltpu.CompilerParams(vmem_limit_bytes=56 * 1024 * 1024)
LARGE = pltpu.CompilerParams(vmem_limit_bytes=40 * 1024 * 1024)
PARAMS = pltpu.CompilerParams(vmem_limit_bytes=16 * 1024 * 1024)


def from_behind(value, axis, steps):
    count = lax.axis_size(axis)
    initial, last = (max(0, -steps), min(count, count - steps))
    return lax.ppermute(value, axis, [(source, source + steps) for source in range(initial, last)])


def across(value, bit):
    count = lax.axis_size("ctx")
    return lax.ppermute(value, "ctx", [(source, source ^ bit) for source in range(count)])


def cost(share):
    return pl.CostEstimate(flops=int(share * 1e9), bytes_accessed=1024, transcendentals=0)


TURN, WINDOW, CHUNK, SHARES, QUERY, SUM = 3.0, 0.5, 4.0, 0.5, 2.0, 1.0


def dot(a, b, a_dim, b_dim):
    return lax.dot_general(a, b, (((a_dim,), (b_dim,)), ((), ())), preferred_element_type=F32)


def by_head_kernel(w_ref, q_ref, g_ref, wt_ref, qt_ref, gt_ref):
    heads = w_ref.shape[1]
    orders = {}

    def order(count):
        if count not in orders:
            size = count * heads
            row = lax.broadcasted_iota(jnp.int32, (size, size), 0)
            col = lax.broadcasted_iota(jnp.int32, (size, size), 1)
            wanted = (row % count) * heads + row // count
            orders[count] = (col == wanted).astype(BF16)
        return orders[count]

    def turn(ref, out_ref):
        rows, _, width = ref.shape
        count = min(rows, 256 // heads)
        for start in range(0, rows, count):
            block = ref[start : start + count].reshape(count * heads, width)
            turned = dot(order(count), block, 1, 0).astype(BF16)
            out_ref[:, start : start + count, :width] = turned.reshape(heads, count, width)

    turn(w_ref, wt_ref)
    qt_ref[...] = jnp.zeros_like(qt_ref)
    turn(q_ref, qt_ref)
    turn(g_ref, gt_ref)


def by_head(up_weight, queries, out_grad, chunk, heads):
    tok = queries.shape[0]
    steps = 4
    depth, rows = LAT // steps, tok // steps
    return pl.pallas_call(
        by_head_kernel,
        grid=(steps,),
        in_specs=[
            pl.BlockSpec((depth, heads, PAIR), lambda i: (i, chunk, 0)),
            pl.BlockSpec((rows, heads, PLAIN_WIDTH + ROPE), lambda i: (i, chunk, 0)),
            pl.BlockSpec((rows, heads, VDIM), lambda i: (i, chunk, 0)),
        ],
        out_specs=[
            pl.BlockSpec((heads, depth, PAIR), lambda i: (0, i, 0)),
            pl.BlockSpec((heads, rows, 2 * LANES), lambda i: (0, i, 0)),
            pl.BlockSpec((heads, rows, VDIM), lambda i: (0, i, 0)),
        ],
        out_shape=[
            jax.ShapeDtypeStruct((heads, LAT, PAIR), BF16),
            jax.ShapeDtypeStruct((heads, tok, 2 * LANES), BF16),
            jax.ShapeDtypeStruct((heads, tok, VDIM), BF16),
        ],
        compiler_params=WIDE,
        cost_estimate=cost(TURN),
        name="by_head",
    )(up_weight, queries, out_grad)


def window_kernel(here_ref, prev_ref, own_ref, ids_ref, *outs, paired):
    win_ref, krope_ref, vis_ref = outs[:3]
    here = here_ref[0]
    tok = prev_ref.shape[0]
    win_ref[:tok, :] = prev_ref[:, :LAT]
    win_ref[tok:, :] = own_ref[:, :LAT]
    krope_ref[...] = jnp.zeros_like(krope_ref)
    krope_ref[:tok, :ROPE] = prev_ref[:, LAT:]
    krope_ref[tok:, :ROPE] = own_ref[:, LAT:]
    behind = jnp.maximum(here - 1, 0)
    seg_prev = jnp.where(here > 0, ids_ref[pl.ds(behind, 1), :], -1)
    seg_own = ids_ref[pl.ds(here, 1), :]
    row = lax.broadcasted_iota(jnp.int32, (tok, tok), 0)
    col = lax.broadcasted_iota(jnp.int32, (tok, tok), 1)
    seg_query = jnp.sum(jnp.where(row == col, seg_own, 0), 1, keepdims=True)
    vis_ref[:, :tok] = (seg_query == seg_prev).astype(F32)
    vis_ref[:, tok:] = ((seg_query == seg_own) & (col <= row)).astype(F32)
    if paired:
        source = lax.broadcasted_iota(jnp.int32, (LAT, LAT), 0)
        column = lax.broadcasted_iota(jnp.int32, (LAT, LAT), 1)
        place = column >> 6
        apart = ((place & 1) << 2) | (place & 2) | (place >> 2)
        wanted = ((here ^ apart) << 6) | (column & 63)
        ordered = dot(win_ref[...], (source == wanted).astype(BF16), 1, 0).astype(BF16)
        outs[3][...] = ordered[:, : LAT // 2]
        outs[4][...] = ordered[:, LAT // 2 :]


def key_window(here, prev, own, ids, paired):
    tok = prev.shape[0]
    whole = lambda i, here: (0, 0)
    shapes = [((2 * tok, LAT), BF16), ((2 * tok, LANES), BF16), ((tok, 2 * tok), F32)]
    if paired:
        shapes = shapes + [((2 * tok, LAT // 2), BF16)] * 2
    return pl.pallas_call(
        functools.partial(window_kernel, paired=paired),
        grid_spec=pltpu.PrefetchScalarGridSpec(
            num_scalar_prefetch=1,
            grid=(1,),
            in_specs=[pl.BlockSpec(array.shape, whole) for array in (prev, own, ids)],
            out_specs=[pl.BlockSpec(shape, whole) for shape, _ in shapes],
        ),
        out_shape=[jax.ShapeDtypeStruct(*shape) for shape in shapes],
        compiler_params=PARAMS,
        cost_estimate=cost(WINDOW),
        name="key_window",
    )(here, prev, own, ids)


def attention_kernel(
    win_ref, krope_ref, vis_ref, wt_ref, qt_ref, gt_ref, *refs, aliased, extra
):
    latents_ref = refs[0] if extra else None
    refs = refs[1:] if extra else refs
    refs = refs[1:] if aliased else refs
    dq_ref, dkv_ref, rope_ref, dqn_ref, dqr_ref = refs
    i = pl.program_id(0)
    tok, heads = dq_ref.shape[:2]
    scale = 1.0 / math.sqrt(PLAIN_WIDTH + ROPE)

    @pl.when(i == 0)
    def _():
        rope_ref[...] = jnp.zeros_like(rope_ref)
        if extra:
            dkv_ref[:, heads * PAIR :] = latents_ref[...]

    visible = vis_ref[...] > 0.0
    window = win_ref[...]
    krope = krope_ref[...]
    count = wt_ref.shape[0]
    keys, values = [], []
    for h in range(count):
        kv = dot(window, wt_ref[h], 1, 0).astype(BF16)
        keys.append(jnp.concatenate([kv[:, :PLAIN_WIDTH], krope], 1))
        values.append(kv[:, PLAIN_WIDTH:])
    scores = [dot(qt_ref[h], keys[h], 1, 1) for h in range(count)]
    dprobs = [dot(gt_ref[h], values[h], 1, 1) for h in range(count)]
    dscores, probs16 = [], []
    for h in range(count):
        logits = jnp.where(visible, scores[h] * scale, -1e30)
        top = jnp.max(logits, -1, keepdims=True)
        expo = jnp.exp(logits - top)
        probs = expo / jnp.sum(expo, -1, keepdims=True)
        delta = jnp.sum(probs * dprobs[h], -1, keepdims=True)
        dscores.append((probs * (dprobs[h] - delta) * scale).astype(BF16))
        probs16.append(probs.astype(BF16))
    parts, rope = [], rope_ref[...]
    for h in range(count):
        dk = dot(dscores[h], qt_ref[h], 0, 0)
        dv = dot(probs16[h], gt_ref[h], 0, 0)
        parts.append(jnp.concatenate([dk[:, :PLAIN_WIDTH], dv], 1).astype(BF16))
        rope = rope + dk[:, PLAIN_WIDTH:]
    rope_ref[...] = rope
    dkv_ref[:, pl.ds(pl.multiple_of(i * (count * PAIR), count * PAIR), count * PAIR)] = (
        jnp.concatenate(parts, 1)
    )
    for h in range(count):
        dq = dot(dscores[h], keys[h], 1, 0)
        dqn_ref[pl.ds(i * count + h, tok, stride=heads), :] = dq[:, :PLAIN_WIDTH]
        dqr_ref[pl.ds(i * count + h, tok, stride=heads), :] = dq[:, PLAIN_WIDTH:]

    @pl.when(i == pl.num_programs(0) - 1)
    def _():
        dq_ref[:, :, :PLAIN_WIDTH] = dqn_ref[...].reshape(tok, heads, LANES)
        dq_ref[:, :, PLAIN_WIDTH:] = dqr_ref[...].reshape(tok, heads, LANES)[:, :, :ROPE]


def attention(window, turned, latents, dq, chunk, heads, first, all_heads):
    weight, queries, out_grad = turned
    tok = queries.shape[1]
    width = 2 * tok
    steps = heads // STEP_HEADS
    at = first // STEP_HEADS
    extra = LAT // 2 if latents is not None else 0
    whole = lambda i: (0, 0)
    head_block = lambda i: (at + i, 0, 0)
    operands = [*window, weight, queries, out_grad]
    in_specs = [pl.BlockSpec(array.shape, whole) for array in window] + [
        pl.BlockSpec((STEP_HEADS, LAT, PAIR), head_block),
        pl.BlockSpec((STEP_HEADS, tok, 2 * LANES), head_block),
        pl.BlockSpec((STEP_HEADS, tok, VDIM), head_block),
    ]
    if latents is not None:
        in_specs.append(pl.BlockSpec(latents.shape, whole))
        operands.append(latents)
    aliases = {}
    if dq is not None:
        aliases = {len(operands): 0}
        in_specs.append(pl.BlockSpec(memory_space=pl.ANY))
        operands.append(dq)
    return pl.pallas_call(
        functools.partial(attention_kernel, aliased=dq is not None, extra=latents is not None),
        grid=(steps,),
        in_specs=in_specs,
        out_specs=[
            pl.BlockSpec((tok, heads, PLAIN_WIDTH + ROPE), lambda i: (0, chunk, 0)),
            pl.BlockSpec((width, heads * PAIR + extra), whole),
            pl.BlockSpec((width, LANES), whole),
        ],
        scratch_shapes=[
            pltpu.VMEM((tok * heads, LANES), F32),
            pltpu.VMEM((tok * heads, LANES), F32),
        ],
        out_shape=[
            jax.ShapeDtypeStruct((tok, all_heads, PLAIN_WIDTH + ROPE), F32),
            jax.ShapeDtypeStruct((width, heads * PAIR + extra), BF16),
            jax.ShapeDtypeStruct((width, LANES), F32),
        ],
        input_output_aliases=aliases,
        compiler_params=WIDE,
        cost_estimate=cost(CHUNK),
        name="attention",
    )(*operands)


def terms_kernel(
    own_ref, other_ref, mine_ref, theirs_ref, keep_ref, send_ref, latents_ref, *, along_x
):
    width = own_ref.shape[0]

    @pl.when(pl.program_id(0) == 0)
    def _():
        latents_ref[:, :width] = mine_ref[...].T
        latents_ref[:, width:] = theirs_ref[...].T

    grads = jnp.concatenate([own_ref[...], other_ref[...]], 0)
    term = dot(latents_ref[...], grads, 1, 0)
    rows = term.shape[0] // 4
    first, second = (1, 2) if along_x else (2, 1)
    keep_ref[:rows] = term[:rows]
    keep_ref[rows:] = term[first * rows : (first + 1) * rows]
    send_ref[:rows] = term[second * rows : (second + 1) * rows].astype(BF16)
    send_ref[rows:] = term[3 * rows :].astype(BF16)


def terms(own, other, mine, theirs, columns, along_x):
    width = own.shape[0]
    block = 1024
    at = theirs.shape[1] // (LAT // 2) - 1
    column_block = lambda i: (0, i)
    return pl.pallas_call(
        functools.partial(terms_kernel, along_x=along_x),
        grid=(columns // block,),
        in_specs=[
            pl.BlockSpec((width, block), column_block),
            pl.BlockSpec((width, block), column_block),
            pl.BlockSpec((width, LAT // 2), lambda i: (0, 0)),
            pl.BlockSpec((width, LAT // 2), lambda i: (0, at)),
        ],
        out_specs=[pl.BlockSpec((LAT // 4, block), column_block)] * 2,
        out_shape=[
            jax.ShapeDtypeStruct((LAT // 4, columns), F32),
            jax.ShapeDtypeStruct((LAT // 4, columns), BF16),
        ],
        scratch_shapes=[pltpu.VMEM((LAT // 2, 2 * width), BF16)],
        compiler_params=PARAMS,
        cost_estimate=cost(CHUNK),
        name="terms",
    )(own, other, mine, theirs)


def key_terms_kernel(*refs, chunks, steps, turns, shares):
    head_ref = refs[0]
    dkv_refs = refs[1 : 1 + chunks]
    wt_refs = refs[1 + chunks : 1 + chunks + turns]
    rope_refs = refs[1 + chunks + turns : 1 + 2 * chunks + turns]
    outs = refs[1 + 2 * chunks + turns : -1]
    total_ref = refs[-1]
    i = pl.program_id(0)

    @pl.when(i == 0)
    def _():
        total_ref[...] = jnp.zeros_like(total_ref)

    for k in range(chunks):

        @pl.when(i // steps == k)
        def _(k=k):
            total = total_ref[...]
            weight_ref = wt_refs[k * turns // chunks]
            for h in range(weight_ref.shape[0]):
                grads = dkv_refs[k][:, h * PAIR : (h + 1) * PAIR]
                total = total + dot(grads, weight_ref[h], 1, 1)
            total_ref[...] = total

    @pl.when(i == pl.num_programs(0) - 1)
    def _():
        rope = rope_refs[0][...]
        for k in range(1, chunks):
            rope = rope + rope_refs[k][...]
        both = jnp.concatenate([total_ref[...], rope], 1)
        if shares is None:
            outs[0][...] = both[:, : LAT + ROPE]
            return
        part = (LAT + ROPE) // shares
        for z in range(shares):
            piece = both[:, z * part : (z + 1) * part]
            for s in range(shares):

                @pl.when(lax.rem(head_ref[0] + s, shares) == z)
                def _(s=s, piece=piece):
                    outs[s][...] = piece


def key_terms(at_head, dkvs, weights, ropes, shares):
    chunks, turns = len(dkvs), len(weights)
    heads = weights[0].shape[0] * turns // chunks
    width = dkvs[0].shape[0]
    steps = heads // STEP_HEADS
    span = steps * chunks // turns
    near = lambda k, many: lambda i, at: jnp.clip(i - k * many, 0, many - 1)
    wide = (LAT + ROPE) // (shares or 1)
    return pl.pallas_call(
        functools.partial(
            key_terms_kernel, chunks=chunks, steps=steps, turns=turns, shares=shares
        ),
        grid_spec=pltpu.PrefetchScalarGridSpec(
            num_scalar_prefetch=1,
            grid=(chunks * steps,),
            in_specs=[
                pl.BlockSpec((width, STEP_HEADS * PAIR), lambda i, at, k=k: (0, near(k, steps)(i, at)))
                for k in range(chunks)
            ]
            + [
                pl.BlockSpec(
                    (STEP_HEADS, LAT, PAIR), lambda i, at, k=k: (near(k, span)(i, at), 0, 0)
                )
                for k in range(turns)
            ]
            + [pl.BlockSpec((width, LANES), lambda i, at: (0, 0))] * chunks,
            out_specs=[pl.BlockSpec((width, wide), lambda i, at: (0, 0))] * (shares or 1),
            scratch_shapes=[pltpu.VMEM((width, LAT), F32)],
        ),
        out_shape=[jax.ShapeDtypeStruct((width, wide), F32)] * (shares or 1),
        compiler_params=WIDE,
        cost_estimate=cost(CHUNK),
        name="key_terms",
    )(at_head, *dkvs, *weights, *ropes)


def weight_sum_kernel(keep_ref, first_ref, second_ref, *refs):
    out_ref, k_ref, v_ref = refs[-3:]
    rows, heads, _ = out_ref.shape
    for h in range(heads):
        columns = slice(h * PAIR, (h + 1) * PAIR)
        total = keep_ref[:, columns] + first_ref[:, columns].astype(F32)
        total = total + second_ref[:, columns].astype(F32)
        k_ref[pl.ds(h, rows, stride=heads), :] = total[:, :LANES]
        v_ref[pl.ds(h, rows, stride=heads), :] = total[:, LANES:]
    out_ref[:, :, :LANES] = k_ref[...].reshape(rows, heads, LANES)
    out_ref[:, :, LANES:] = v_ref[...].reshape(rows, heads, LANES)


def weight_sum(keep, first, second, total, chunk, all_heads):
    rows, columns = second.shape
    heads = columns // PAIR
    block = 32
    operands = [keep, first, second]
    in_specs = [pl.BlockSpec((block, columns), lambda i: (i, 0)) for _ in operands]
    aliases = {}
    if total is not None:
        aliases = {3: 0}
        in_specs.append(pl.BlockSpec(memory_space=pl.ANY))
        operands.append(total)
    return pl.pallas_call(
        weight_sum_kernel,
        grid=(rows // block,),
        in_specs=in_specs,
        out_specs=pl.BlockSpec((block, heads, PAIR), lambda i: (i, chunk, 0)),
        out_shape=jax.ShapeDtypeStruct((rows, all_heads, PAIR), F32),
        scratch_shapes=[pltpu.VMEM((block * heads, LANES), F32)] * 2,
        input_output_aliases=aliases,
        compiler_params=PARAMS,
        cost_estimate=cost(SUM),
        name="weight_sum",
    )(*operands)


def after(values, earlier):
    return lax.optimization_barrier((values, earlier))[0]


def turn_rows(block):
    rows, heads, width = block.shape
    count = min(rows, 256 // heads)
    row = lax.broadcasted_iota(jnp.int32, (count * heads, count * heads), 0)
    col = lax.broadcasted_iota(jnp.int32, (count * heads, count * heads), 1)
    order = (col == (row % count) * heads + row // count).astype(BF16)
    for start in range(0, rows, count):
        part = block[start : start + count].reshape(count * heads, width)
        turned = dot(order, part, 1, 0).astype(BF16)
        yield slice(start, start + count), turned.reshape(heads, count, width)


def in_hbm(array):
    return pltpu.with_memory_space_constraint(array, pltpu.HBM)


def turn_weight_kernel(here_ref, *refs):
    *parts, wt_ref = refs
    depth = parts[0].shape[0]
    for at, w_ref in enumerate(parts):
        for rows, turned in turn_rows(w_ref[...]):
            wt_ref[:, at * depth + rows.start : at * depth + rows.stop, :] = turned


def turn_weight(here, up_weight, heads):
    steps, parts = 4, 4
    depth = LAT // steps // parts
    part = lambda p: lambda i, here: (i * parts + p, here[0] & 1, 0)
    return pl.pallas_call(
        turn_weight_kernel,
        grid_spec=pltpu.PrefetchScalarGridSpec(
            num_scalar_prefetch=1,
            grid=(steps,),
            in_specs=[pl.BlockSpec((depth, heads, PAIR), part(p)) for p in range(parts)],
            out_specs=pl.BlockSpec((heads, depth * parts, PAIR), lambda i, here: (0, i, 0)),
        ),
        out_shape=jax.ShapeDtypeStruct((heads, LAT, PAIR), BF16),
        compiler_params=PARAMS,
        cost_estimate=cost(TURN),
        name="turn_weight",
    )(here, *[in_hbm(up_weight)] * parts)


def turn_tokens_kernel(here_ref, q1_ref, g1_ref, q0_ref, g0_ref, own_ref, give_ref, mine_ref):
    heads = mine_ref.shape[0]
    for q_ref, g_ref, out_ref in ((q1_ref, g1_ref, give_ref), (q0_ref, g0_ref, mine_ref)):
        out_ref[:, :, LANES : 2 * LANES] = jnp.zeros_like(out_ref[:, :, LANES : 2 * LANES])
        for rows, turned in turn_rows(q_ref[...]):
            out_ref[:heads, rows, : PLAIN_WIDTH + ROPE] = turned
        for rows, turned in turn_rows(g_ref[...]):
            out_ref[:heads, rows, 2 * LANES :] = turned
    rest = LAT + ROPE - 3 * LANES
    give_ref[heads] = own_ref[:, : 3 * LANES]
    give_ref[heads + 1] = jnp.zeros_like(give_ref[heads + 1])
    give_ref[heads + 1, :, :rest] = own_ref[:, 3 * LANES :]


def turn_tokens(here, queries, out_grad, latent_keys, heads):
    tok = queries.shape[0]
    q_block, g_block = (tok, heads, PLAIN_WIDTH + ROPE), (tok, heads, VDIM)
    given = lambda i, here: (0, 1 - (here[0] & 1), 0)
    kept = lambda i, here: (0, here[0] & 1, 0)
    whole = lambda i, here: (0, 0, 0)
    give, mine = (heads + 2, tok, 3 * LANES), (heads, tok, 3 * LANES)
    queries, out_grad, latent_keys = (in_hbm(x) for x in (queries, out_grad, latent_keys))
    return pl.pallas_call(
        turn_tokens_kernel,
        grid_spec=pltpu.PrefetchScalarGridSpec(
            num_scalar_prefetch=1,
            grid=(1,),
            in_specs=[
                pl.BlockSpec(q_block, given),
                pl.BlockSpec(g_block, given),
                pl.BlockSpec(q_block, kept),
                pl.BlockSpec(g_block, kept),
                pl.BlockSpec(latent_keys.shape, lambda i, here: (0, 0)),
            ],
            out_specs=[pl.BlockSpec(give, whole), pl.BlockSpec(mine, whole)],
        ),
        out_shape=[jax.ShapeDtypeStruct(give, BF16), jax.ShapeDtypeStruct(mine, BF16)],
        compiler_params=PARAMS,
        cost_estimate=cost(WINDOW),
        name="turn_tokens",
    )(here, queries, out_grad, queries, out_grad, latent_keys)


def chip_window_kernel(
    here_ref, even_ref, odd_ref, own_ref, pal_ref, ids_ref, win_ref, krope_ref, vis_ref, lat_ref
):
    here = here_ref[0]
    tok = own_ref.shape[0]
    core, chip = here & 1, here >> 1
    first = core == 0
    prev = jnp.where(first, even_ref[...].astype(F32), odd_ref[...].astype(F32)).astype(BF16)
    pal = jnp.concatenate([pal_ref[0], pal_ref[1, :, : LAT + ROPE - 3 * LANES]], 1).astype(F32)
    own = own_ref[...].astype(F32)
    low = jnp.where(first, own, pal).astype(BF16)
    high = jnp.where(first, pal, own).astype(BF16)
    krope_ref[...] = jnp.zeros_like(krope_ref)
    for at, block in enumerate((prev, low, high)):
        win_ref[at * tok : (at + 1) * tok, :] = block[:, :LAT]
        krope_ref[at * tok : (at + 1) * tok, :ROPE] = block[:, LAT:]
    behind = jnp.maximum(2 * chip - 1, 0)
    seg = [
        jnp.where(chip > 0, ids_ref[pl.ds(behind, 1), :], -1),
        ids_ref[pl.ds(2 * chip, 1), :],
        ids_ref[pl.ds(2 * chip + 1, 1), :],
    ]
    row = lax.broadcasted_iota(jnp.int32, (tok, tok), 0)
    col = lax.broadcasted_iota(jnp.int32, (tok, tok), 1)
    for b in range(2):
        seg_query = jnp.sum(jnp.where(row == col, seg[b + 1], 0), 1, keepdims=True)
        vis_ref[b, :, :tok] = (seg_query == seg[b]).astype(F32)
        vis_ref[b, :, tok:] = ((seg_query == seg[b + 1]) & (col <= row)).astype(F32)
    column = lax.broadcasted_iota(jnp.int32, (LAT, LAT), 0)
    source = lax.broadcasted_iota(jnp.int32, (LAT, LAT), 1)
    place = column >> 6
    apart = ((place & 2) << 1) | ((place & 4) >> 1) | (place & 1)
    wanted = ((here ^ apart) << 6) | (column & 63)
    order = (source == wanted).astype(BF16)
    lat_ref[...] = dot(order, win_ref[...], 1, 1).astype(BF16)


def chip_window(here, even, odd, own, got, ids):
    tok = own.shape[0]
    whole = lambda i, here: (0, 0)
    return pl.pallas_call(
        chip_window_kernel,
        grid_spec=pltpu.PrefetchScalarGridSpec(
            num_scalar_prefetch=1,
            grid=(1,),
            in_specs=[pl.BlockSpec(array.shape, whole) for array in (even, odd, own)]
            + [
                pl.BlockSpec((2,) + got.shape[1:], lambda i, here: (got.shape[0] // 2 - 1, 0, 0)),
                pl.BlockSpec(ids.shape, whole),
            ],
            out_specs=[
                pl.BlockSpec((3 * tok, LAT), whole),
                pl.BlockSpec((3 * tok, LANES), whole),
                pl.BlockSpec((2, tok, 2 * tok), lambda i, here: (0, 0, 0)),
                pl.BlockSpec((LAT, 3 * tok), whole),
            ],
        ),
        out_shape=[
            jax.ShapeDtypeStruct((3 * tok, LAT), BF16),
            jax.ShapeDtypeStruct((3 * tok, LANES), BF16),
            jax.ShapeDtypeStruct((2, tok, 2 * tok), F32),
            jax.ShapeDtypeStruct((LAT, 3 * tok), BF16),
        ],
        compiler_params=PARAMS,
        cost_estimate=cost(WINDOW),
        name="chip_window",
    )(here, even, odd, own, got, ids)


def chunk_kernel(
    here_ref,
    win_ref,
    krope_ref,
    vis_ref,
    lat_ref,
    wt_ref,
    mine_ref,
    got_ref,
    *refs,
    chained,
    along_x,
):
    before_ref = refs[0] if chained else None
    refs = refs[3:] if chained else refs
    keep_ref, send_ref, key_ref, dq_ref, back_ref = refs
    tok = vis_ref.shape[1]
    heads = wt_ref.shape[0]
    first = (here_ref[0] & 1) == 0
    scale = 1.0 / math.sqrt(PLAIN_WIDTH + ROPE)
    window, krope = win_ref[...], krope_ref[...]
    visible = [vis_ref[b] > 0.0 for b in range(2)]
    keys, values, queries, grads = [], [], [], []
    for h in range(heads):
        kv = dot(window, wt_ref[h], 1, 0).astype(BF16)
        keys.append(jnp.concatenate([kv[:, :PLAIN_WIDTH], krope], 1))
        values.append(kv[:, PLAIN_WIDTH:])
        mine, got = mine_ref[h], got_ref[h]
        ordered = (jnp.where(first, mine, got), jnp.where(first, got, mine))
        queries.append([block[:, : 2 * LANES] for block in ordered])
        grads.append([block[:, 2 * LANES :] for block in ordered])
    reach = [slice(b * tok, (b + 2) * tok) for b in range(2)]
    units = [(h, b) for h in range(heads) for b in range(2)]
    scores = {(h, b): dot(queries[h][b], keys[h][reach[b]], 1, 1) for h, b in units}
    dprobs = {(h, b): dot(grads[h][b], values[h][reach[b]], 1, 1) for h, b in units}
    dscores, probs16 = {}, {}
    for unit in units:
        logits = jnp.where(visible[unit[1]], scores[unit] * scale, -1e30)
        top = jnp.max(logits, -1, keepdims=True)
        expo = jnp.exp(logits - top)
        probs = expo / jnp.sum(expo, -1, keepdims=True)
        delta = jnp.sum(probs * dprobs[unit], -1, keepdims=True)
        dscores[unit] = (probs * (dprobs[unit] - delta) * scale).astype(BF16)
        probs16[unit] = probs.astype(BF16)

    def fold(low, high):
        return jnp.concatenate([low[:tok], low[tok:] + high[:tok], high[tok:]], 0)

    parts, rope = [], None
    for h in range(heads):
        dk = fold(*[dot(dscores[h, b], queries[h][b], 0, 0) for b in range(2)])
        dv = fold(*[dot(probs16[h, b], grads[h][b], 0, 0) for b in range(2)])
        parts.append(jnp.concatenate([dk[:, :PLAIN_WIDTH], dv], 1).astype(BF16))
        rope = dk[:, PLAIN_WIDTH:] if rope is None else rope + dk[:, PLAIN_WIDTH:]
    dkv = jnp.concatenate(parts, 1)
    rows = lat_ref.shape[0] // 4
    kept = (0, 1) if along_x else (0, 2)
    sent = (2, 3) if along_x else (1, 3)
    for at, g in enumerate(sent):
        term = dot(lat_ref[g * rows : (g + 1) * rows, :], dkv, 1, 0)
        send_ref[at * rows : (at + 1) * rows, :] = term.astype(BF16)
    for at, g in enumerate(kept):
        keep_ref[at * rows : (at + 1) * rows, :] = dot(
            lat_ref[g * rows : (g + 1) * rows, :], dkv, 1, 0
        )
    total = before_ref[:, :LAT] if chained else None
    for h in range(heads):
        term = dot(parts[h], wt_ref[h], 1, 1)
        total = term if total is None else total + term
    key_ref[:, :LAT] = total
    key_ref[:, LAT:] = rope + before_ref[:, LAT:] if chained else rope
    for h in range(heads):
        low, high = (dot(dscores[h, b], keys[h][reach[b]], 1, 0) for b in range(2))
        dq_ref[h] = jnp.where(first, low, high)
        back_ref[h] = jnp.where(first, high, low)


def chunk(here, window, weight, mine, got, before, index, heads, along_x):
    tok = mine.shape[1]
    whole = lambda i, here: (0, 0)
    whole3 = lambda i, here: (0, 0, 0)
    at = lambda i, here: (index, 0, 0)
    columns = heads * PAIR
    operands = [*window, weight, mine, got]
    in_specs = [
        pl.BlockSpec(array.shape, whole3 if array.ndim == 3 else whole) for array in window
    ] + [
        pl.BlockSpec((heads, LAT, PAIR), at),
        pl.BlockSpec((heads, tok, 3 * LANES), at),
        pl.BlockSpec((heads, tok, 3 * LANES), at),
    ]
    aliases = {}
    if before is not None:
        key, dq, back = before
        aliases = {len(operands) + 2: 3, len(operands) + 3: 4}
        in_specs = in_specs + [
            pl.BlockSpec(key.shape, whole),
            pl.BlockSpec(memory_space=pl.ANY),
            pl.BlockSpec(memory_space=pl.ANY),
        ]
        operands = operands + [key, dq, back]
    turned = (weight.shape[0], tok, 2 * LANES)
    return pl.pallas_call(
        functools.partial(chunk_kernel, chained=before is not None, along_x=along_x),
        grid_spec=pltpu.PrefetchScalarGridSpec(
            num_scalar_prefetch=1,
            grid=(1,),
            in_specs=in_specs,
            out_specs=[
                pl.BlockSpec((LAT // 2, columns), whole),
                pl.BlockSpec((LAT // 2, columns), whole),
                pl.BlockSpec((3 * tok, LAT + LANES), whole),
                pl.BlockSpec((heads, tok, 2 * LANES), at),
                pl.BlockSpec((heads, tok, 2 * LANES), at),
            ],
        ),
        out_shape=[
            jax.ShapeDtypeStruct((LAT // 2, columns), F32),
            jax.ShapeDtypeStruct((LAT // 2, columns), BF16),
            jax.ShapeDtypeStruct((3 * tok, LAT + LANES), F32),
            jax.ShapeDtypeStruct(turned, F32),
            jax.ShapeDtypeStruct(turned, F32),
        ],
        input_output_aliases=aliases,
        compiler_params=LARGE,
        cost_estimate=cost(CHUNK),
        name="chunk",
    )(here, *operands)


def key_shares_kernel(at_ref, key_ref, *outs):
    shares = len(outs)
    part = (LAT + ROPE) // shares
    for z in range(shares):
        piece = key_ref[:, z * part : (z + 1) * part]
        for s in range(shares):

            @pl.when(lax.rem(at_ref[0] + s, shares) == z)
            def _(s=s, piece=piece):
                outs[s][...] = piece


def key_shares(at_head, key, shares):
    part = (LAT + ROPE) // shares
    whole = lambda i, at: (0, 0)
    return pl.pallas_call(
        key_shares_kernel,
        grid_spec=pltpu.PrefetchScalarGridSpec(
            num_scalar_prefetch=1,
            grid=(1,),
            in_specs=[pl.BlockSpec(key.shape, whole)],
            out_specs=[pl.BlockSpec((key.shape[0], part), whole)] * shares,
        ),
        out_shape=[jax.ShapeDtypeStruct((key.shape[0], part), F32)] * shares,
        compiler_params=PARAMS,
        cost_estimate=cost(SHARES),
        name="key_shares",
    )(at_head, key)


def query_grad_kernel(here_ref, mine_ref, got_ref, out_ref, n_ref, r_ref):
    tok, heads, _ = out_ref.shape

    def put(src_ref):
        for h in range(heads):
            n_ref[pl.ds(h, tok, stride=heads), :] = src_ref[h, :, :PLAIN_WIDTH]
            r_ref[pl.ds(h, tok, stride=heads), :] = src_ref[h, :, PLAIN_WIDTH:]

    pl.when(pl.program_id(0) == 0)(lambda: put(mine_ref))
    pl.when(pl.program_id(0) == 1)(lambda: put(got_ref))
    out_ref[:, :, :PLAIN_WIDTH] = n_ref[...].reshape(tok, heads, LANES)
    out_ref[:, :, PLAIN_WIDTH:] = r_ref[...].reshape(tok, heads, LANES)[:, :, :ROPE]


def query_grad(here, mine, got):
    heads, tok, _ = mine.shape
    whole = lambda i, here: (0, 0, 0)
    return pl.pallas_call(
        query_grad_kernel,
        grid_spec=pltpu.PrefetchScalarGridSpec(
            num_scalar_prefetch=1,
            grid=(2,),
            in_specs=[pl.BlockSpec(mine.shape, whole)] * 2,
            out_specs=pl.BlockSpec(
                (tok, heads, PLAIN_WIDTH + ROPE), lambda i, here: (0, (here[0] & 1) ^ i, 0)
            ),
            scratch_shapes=[pltpu.VMEM((tok * heads, LANES), F32)] * 2,
        ),
        out_shape=jax.ShapeDtypeStruct((tok, 2 * heads, PLAIN_WIDTH + ROPE), F32),
        compiler_params=PARAMS,
        cost_estimate=cost(QUERY),
        name="query_grad",
    )(here, mine, got)


def weight_grad_kernel(here_ref, keep_ref, first_ref, second_ref, got_ref, *refs):
    out_ref, k_ref, v_ref = refs[-3:]
    rows, heads, _ = out_ref.shape

    def put(total):
        for h in range(heads):
            at = pl.ds(h, rows, stride=heads)
            k_ref[at, :] = total[:, h * PAIR : h * PAIR + LANES]
            v_ref[at, :] = total[:, h * PAIR + LANES : (h + 1) * PAIR]

    @pl.when(pl.program_id(0) == 0)
    def _():
        put(keep_ref[...] + first_ref[...].astype(F32) + second_ref[...].astype(F32))

    @pl.when(pl.program_id(0) == 1)
    def _():
        put(got_ref[...])

    out_ref[:, :, :LANES] = k_ref[...].reshape(rows, heads, LANES)
    out_ref[:, :, LANES:] = v_ref[...].reshape(rows, heads, LANES)


def weight_grad_part(here, parts, got, total, chunk, chunks):
    rows, columns = got.shape
    heads = columns // PAIR
    operands = [*parts, got]
    in_specs = [pl.BlockSpec((rows, columns), lambda i, here: (0, 0)) for _ in operands]
    aliases = {}
    if total is not None:
        aliases = {1 + len(operands): 0}
        in_specs.append(pl.BlockSpec(memory_space=pl.ANY))
        operands.append(total)
    return pl.pallas_call(
        weight_grad_kernel,
        grid_spec=pltpu.PrefetchScalarGridSpec(
            num_scalar_prefetch=1,
            grid=(2,),
            in_specs=in_specs,
            out_specs=pl.BlockSpec(
                (rows, heads, PAIR), lambda i, here: (0, ((here[0] & 1) ^ i) * chunks + chunk, 0)
            ),
            scratch_shapes=[pltpu.VMEM((rows * heads, LANES), F32)] * 2,
        ),
        out_shape=jax.ShapeDtypeStruct((rows, 2 * chunks * heads, PAIR), F32),
        input_output_aliases=aliases,
        compiler_params=PARAMS,
        cost_estimate=cost(SUM),
        name="weight_grad",
    )(here, *operands)


def in_chunks(queries, latent_keys, out_grad, up_weight, here, at_head, ids):
    tok = latent_keys.shape[0]
    n_ctx, n_head = lax.axis_size("ctx"), lax.axis_size("head")
    chunks, each, heads = 2, 8, 16
    first = here[0] % 2 == 0
    give, mine = turn_tokens(here, queries, out_grad, latent_keys, heads)
    odd_devices = range(1, n_ctx - 1, 2)
    even = lax.ppermute(latent_keys, "ctx", [(source, source + 1) for source in odd_devices])
    odd = lax.ppermute(latent_keys, "ctx", [(source, source + 2) for source in odd_devices])
    got = across(give, 1)
    weight = turn_weight(here, up_weight, heads)
    window = chip_window(here, even, odd, latent_keys, got, ids)
    before, keeps, sent = None, [], []
    for c in range(chunks):
        keep, out, *before = chunk(here, window, weight, mine, got, before, c, each, c % 2 == 0)
        keeps.append(keep)
        sent.append(across(out, 2 if c % 2 == 0 else 4))
    key, dq, back = before
    lasts, theirs = [], []

    def forward(c):
        rest = keeps[c][2 * tok :] + sent[c][2 * tok :].astype(F32)
        lasts.append(across(rest.astype(BF16), 4 if c % 2 == 0 else 2))
        return rest

    shares = key_shares(at_head, key, n_head)
    share, pieces = shares[0], [
        lax.ppermute(shares[s], "head", [(z, (z + s) % n_head) for z in range(n_head)])
        for s in range(1, n_head)
    ]
    back = across(back, 1)
    for piece in pieces:
        share = share + piece
    dq = query_grad(here, dq, back)
    keeps[0] = after(keeps[0], dq)
    share = after(share, [forward(0), forward(1)])
    behind, low, high = share[:tok], share[tok : 2 * tok], share[2 * tok :]
    swap = jnp.concatenate([jnp.where(first, high, low), behind], 0)
    swap = across(swap, 1)
    key_grad = jnp.where(first, low, high) + swap[:tok]
    key_grad = key_grad + lax.ppermute(
        behind + swap[tok:], "ctx", [(source, source - 1) for source in range(2, n_ctx, 2)]
    )
    for c in range(chunks):
        part = slice(tok, 2 * tok)
        total = keeps[c][part] + sent[c][part].astype(F32) + lasts[c][part].astype(F32)
        theirs.append(across(total, 1))
    weight_grad = None
    for c in range(chunks):
        weight_grad = weight_grad_part(
            here, (keeps[c], sent[c], lasts[c]), theirs[c], weight_grad, c, chunks
        )
    return dq, key_grad, weight_grad


def shards(queries, latent_keys, out_grad, up_weight, segment_ids):
    tok = latent_keys.shape[0]
    heads = queries.shape[1]
    n_ctx, n_head = lax.axis_size("ctx"), lax.axis_size("head")
    here = lax.axis_index("ctx").astype(jnp.int32).reshape(1)
    at_head = lax.axis_index("head").astype(jnp.int32).reshape(1)
    ids = segment_ids.reshape(n_ctx, tok)
    if n_ctx == 8 and heads == 32 and n_head == 4:
        return in_chunks(queries, latent_keys, out_grad, up_weight, here, at_head, ids)
    else:
        prev = from_behind(latent_keys, "ctx", REACH)
        turned = by_head(up_weight, queries, out_grad, 0, heads)
        window = key_window(here, prev, latent_keys, ids, False)
        dq, dkv, rope = attention(window, turned, None, None, 0, heads, 0, heads)
        (both,) = key_terms(at_head, [dkv], [turned[0]], [rope], None)
        share = lax.psum_scatter(
            both.reshape(REACH + 1, tok, LAT + ROPE), "head", scatter_dimension=2, tiled=True
        )
        term = jnp.einsum("ki,ke->ie", window[0], dkv, preferred_element_type=F32)
        rows = lax.psum_scatter(term.astype(BF16), "ctx", scatter_dimension=0, tiled=True)
        weight_grad = rows.astype(F32).reshape(rows.shape[0], heads, PAIR)
    key_grad = share[REACH] + from_behind(share[0], "ctx", 0 - REACH)
    return (dq, key_grad, weight_grad)


def solution(mesh):
    return jax.shard_map(
        shards,
        mesh=mesh,
        in_specs=(
            P("ctx", "head", None),
            P("ctx", None),
            P("ctx", "head", None),
            P(None, "head", None),
            P(),
        ),
        out_specs=(P("ctx", "head", None), P("ctx", "head"), P("ctx", "head", None)),
        check_vma=False,
    )
```

```python
import functools
import math

import jax
import jax.numpy as jnp
from jax import lax
from jax.experimental import pallas as pl
from jax.experimental.pallas import tpu as pltpu
from jax.sharding import PartitionSpec as P

LAT = 512
ROPE = 64
PLAIN_WIDTH = 128
VDIM = 128
REACH = 1
LANES = 128
PAIR = PLAIN_WIDTH + VDIM
STEP_HEADS = 4
BF16 = jnp.bfloat16
F32 = jnp.float32
WIDE = pltpu.CompilerParams(vmem_limit_bytes=56 * 1024 * 1024)
PARAMS = pltpu.CompilerParams(vmem_limit_bytes=32 * 1024 * 1024)


def from_behind(value, axis, steps):
    count = lax.axis_size(axis)
    initial, last = (max(0, -steps), min(count, count - steps))
    return lax.ppermute(value, axis, [(source, source + steps) for source in range(initial, last)])


def across(value, bit):
    count = lax.axis_size("ctx")
    return lax.ppermute(value, "ctx", [(source, source ^ bit) for source in range(count)])


def cost(share):
    return pl.CostEstimate(flops=int(share * 1e9), bytes_accessed=1024, transcendentals=0)


TURN, WINDOW, CHUNK, SHARES, QUERY, SUM = 3.0, 0.5, 4.0, 0.5, 2.0, 1.0


def dot(a, b, a_dim, b_dim):
    return lax.dot_general(a, b, (((a_dim,), (b_dim,)), ((), ())), preferred_element_type=F32)


def by_head_kernel(w_ref, q_ref, g_ref, wt_ref, qt_ref, gt_ref):
    heads = w_ref.shape[1]
    orders = {}

    def order(count):
        if count not in orders:
            size = count * heads
            row = lax.broadcasted_iota(jnp.int32, (size, size), 0)
            col = lax.broadcasted_iota(jnp.int32, (size, size), 1)
            wanted = (row % count) * heads + row // count
            orders[count] = (col == wanted).astype(BF16)
        return orders[count]

    def turn(ref, out_ref):
        rows, _, width = ref.shape
        count = min(rows, 256 // heads)
        for start in range(0, rows, count):
            block = ref[start : start + count].reshape(count * heads, width)
            turned = dot(order(count), block, 1, 0).astype(BF16)
            out_ref[:, start : start + count, :width] = turned.reshape(heads, count, width)

    turn(w_ref, wt_ref)
    qt_ref[...] = jnp.zeros_like(qt_ref)
    turn(q_ref, qt_ref)
    turn(g_ref, gt_ref)


def by_head(up_weight, queries, out_grad, chunk, heads):
    tok = queries.shape[0]
    steps = 4
    depth, rows = LAT // steps, tok // steps
    return pl.pallas_call(
        by_head_kernel,
        grid=(steps,),
        in_specs=[
            pl.BlockSpec((depth, heads, PAIR), lambda i: (i, chunk, 0)),
            pl.BlockSpec((rows, heads, PLAIN_WIDTH + ROPE), lambda i: (i, chunk, 0)),
            pl.BlockSpec((rows, heads, VDIM), lambda i: (i, chunk, 0)),
        ],
        out_specs=[
            pl.BlockSpec((heads, depth, PAIR), lambda i: (0, i, 0)),
            pl.BlockSpec((heads, rows, 2 * LANES), lambda i: (0, i, 0)),
            pl.BlockSpec((heads, rows, VDIM), lambda i: (0, i, 0)),
        ],
        out_shape=[
            jax.ShapeDtypeStruct((heads, LAT, PAIR), BF16),
            jax.ShapeDtypeStruct((heads, tok, 2 * LANES), BF16),
            jax.ShapeDtypeStruct((heads, tok, VDIM), BF16),
        ],
        compiler_params=WIDE,
        cost_estimate=cost(TURN),
        name="by_head",
    )(up_weight, queries, out_grad)


def window_kernel(here_ref, prev_ref, own_ref, ids_ref, *outs, paired):
    win_ref, krope_ref, vis_ref = outs[:3]
    here = here_ref[0]
    tok = prev_ref.shape[0]
    win_ref[:tok, :] = prev_ref[:, :LAT]
    win_ref[tok:, :] = own_ref[:, :LAT]
    krope_ref[...] = jnp.zeros_like(krope_ref)
    krope_ref[:tok, :ROPE] = prev_ref[:, LAT:]
    krope_ref[tok:, :ROPE] = own_ref[:, LAT:]
    behind = jnp.maximum(here - 1, 0)
    seg_prev = jnp.where(here > 0, ids_ref[pl.ds(behind, 1), :], -1)
    seg_own = ids_ref[pl.ds(here, 1), :]
    row = lax.broadcasted_iota(jnp.int32, (tok, tok), 0)
    col = lax.broadcasted_iota(jnp.int32, (tok, tok), 1)
    seg_query = jnp.sum(jnp.where(row == col, seg_own, 0), 1, keepdims=True)
    vis_ref[:, :tok] = (seg_query == seg_prev).astype(F32)
    vis_ref[:, tok:] = ((seg_query == seg_own) & (col <= row)).astype(F32)
    if paired:
        source = lax.broadcasted_iota(jnp.int32, (LAT, LAT), 0)
        column = lax.broadcasted_iota(jnp.int32, (LAT, LAT), 1)
        place = column >> 6
        apart = ((place & 1) << 2) | (place & 2) | (place >> 2)
        wanted = ((here ^ apart) << 6) | (column & 63)
        ordered = dot(win_ref[...], (source == wanted).astype(BF16), 1, 0).astype(BF16)
        outs[3][...] = ordered[:, : LAT // 2]
        outs[4][...] = ordered[:, LAT // 2 :]


def key_window(here, prev, own, ids, paired):
    tok = prev.shape[0]
    whole = lambda i, here: (0, 0)
    shapes = [((2 * tok, LAT), BF16), ((2 * tok, LANES), BF16), ((tok, 2 * tok), F32)]
    if paired:
        shapes = shapes + [((2 * tok, LAT // 2), BF16)] * 2
    return pl.pallas_call(
        functools.partial(window_kernel, paired=paired),
        grid_spec=pltpu.PrefetchScalarGridSpec(
            num_scalar_prefetch=1,
            grid=(1,),
            in_specs=[pl.BlockSpec(array.shape, whole) for array in (prev, own, ids)],
            out_specs=[pl.BlockSpec(shape, whole) for shape, _ in shapes],
        ),
        out_shape=[jax.ShapeDtypeStruct(*shape) for shape in shapes],
        compiler_params=PARAMS,
        cost_estimate=cost(WINDOW),
        name="key_window",
    )(here, prev, own, ids)


def attention_kernel(
    win_ref, krope_ref, vis_ref, wt_ref, qt_ref, gt_ref, *refs, aliased, extra
):
    latents_ref = refs[0] if extra else None
    refs = refs[1:] if extra else refs
    refs = refs[1:] if aliased else refs
    dq_ref, dkv_ref, rope_ref, dqn_ref, dqr_ref = refs
    i = pl.program_id(0)
    tok, heads = dq_ref.shape[:2]
    scale = 1.0 / math.sqrt(PLAIN_WIDTH + ROPE)

    @pl.when(i == 0)
    def _():
        rope_ref[...] = jnp.zeros_like(rope_ref)
        if extra:
            dkv_ref[:, heads * PAIR :] = latents_ref[...]

    visible = vis_ref[...] > 0.0
    window = win_ref[...]
    krope = krope_ref[...]
    count = wt_ref.shape[0]
    keys, values = [], []
    for h in range(count):
        kv = dot(window, wt_ref[h], 1, 0).astype(BF16)
        keys.append(jnp.concatenate([kv[:, :PLAIN_WIDTH], krope], 1))
        values.append(kv[:, PLAIN_WIDTH:])
    scores = [dot(qt_ref[h], keys[h], 1, 1) for h in range(count)]
    dprobs = [dot(gt_ref[h], values[h], 1, 1) for h in range(count)]
    dscores, probs16 = [], []
    for h in range(count):
        logits = jnp.where(visible, scores[h] * scale, -1e30)
        top = jnp.max(logits, -1, keepdims=True)
        expo = jnp.exp(logits - top)
        probs = expo / jnp.sum(expo, -1, keepdims=True)
        delta = jnp.sum(probs * dprobs[h], -1, keepdims=True)
        dscores.append((probs * (dprobs[h] - delta) * scale).astype(BF16))
        probs16.append(probs.astype(BF16))
    parts, rope = [], rope_ref[...]
    for h in range(count):
        dk = dot(dscores[h], qt_ref[h], 0, 0)
        dv = dot(probs16[h], gt_ref[h], 0, 0)
        parts.append(jnp.concatenate([dk[:, :PLAIN_WIDTH], dv], 1).astype(BF16))
        rope = rope + dk[:, PLAIN_WIDTH:]
    rope_ref[...] = rope
    dkv_ref[:, pl.ds(pl.multiple_of(i * (count * PAIR), count * PAIR), count * PAIR)] = (
        jnp.concatenate(parts, 1)
    )
    for h in range(count):
        dq = dot(dscores[h], keys[h], 1, 0)
        dqn_ref[pl.ds(i * count + h, tok, stride=heads), :] = dq[:, :PLAIN_WIDTH]
        dqr_ref[pl.ds(i * count + h, tok, stride=heads), :] = dq[:, PLAIN_WIDTH:]

    @pl.when(i == pl.num_programs(0) - 1)
    def _():
        dq_ref[:, :, :PLAIN_WIDTH] = dqn_ref[...].reshape(tok, heads, LANES)
        dq_ref[:, :, PLAIN_WIDTH:] = dqr_ref[...].reshape(tok, heads, LANES)[:, :, :ROPE]


def attention(window, turned, latents, dq, chunk, heads, first, all_heads):
    weight, queries, out_grad = turned
    tok = queries.shape[1]
    width = 2 * tok
    steps = heads // STEP_HEADS
    at = first // STEP_HEADS
    extra = LAT // 2 if latents is not None else 0
    whole = lambda i: (0, 0)
    head_block = lambda i: (at + i, 0, 0)
    operands = [*window, weight, queries, out_grad]
    in_specs = [pl.BlockSpec(array.shape, whole) for array in window] + [
        pl.BlockSpec((STEP_HEADS, LAT, PAIR), head_block),
        pl.BlockSpec((STEP_HEADS, tok, 2 * LANES), head_block),
        pl.BlockSpec((STEP_HEADS, tok, VDIM), head_block),
    ]
    if latents is not None:
        in_specs.append(pl.BlockSpec(latents.shape, whole))
        operands.append(latents)
    aliases = {}
    if dq is not None:
        aliases = {len(operands): 0}
        in_specs.append(pl.BlockSpec(memory_space=pl.ANY))
        operands.append(dq)
    return pl.pallas_call(
        functools.partial(attention_kernel, aliased=dq is not None, extra=latents is not None),
        grid=(steps,),
        in_specs=in_specs,
        out_specs=[
            pl.BlockSpec((tok, heads, PLAIN_WIDTH + ROPE), lambda i: (0, chunk, 0)),
            pl.BlockSpec((width, heads * PAIR + extra), whole),
            pl.BlockSpec((width, LANES), whole),
        ],
        scratch_shapes=[
            pltpu.VMEM((tok * heads, LANES), F32),
            pltpu.VMEM((tok * heads, LANES), F32),
        ],
        out_shape=[
            jax.ShapeDtypeStruct((tok, all_heads, PLAIN_WIDTH + ROPE), F32),
            jax.ShapeDtypeStruct((width, heads * PAIR + extra), BF16),
            jax.ShapeDtypeStruct((width, LANES), F32),
        ],
        input_output_aliases=aliases,
        compiler_params=WIDE,
        cost_estimate=cost(CHUNK),
        name="attention",
    )(*operands)


def terms_kernel(
    own_ref, other_ref, mine_ref, theirs_ref, keep_ref, send_ref, latents_ref, *, along_x
):
    width = own_ref.shape[0]

    @pl.when(pl.program_id(0) == 0)
    def _():
        latents_ref[:, :width] = mine_ref[...].T
        latents_ref[:, width:] = theirs_ref[...].T

    grads = jnp.concatenate([own_ref[...], other_ref[...]], 0)
    term = dot(latents_ref[...], grads, 1, 0)
    rows = term.shape[0] // 4
    first, second = (1, 2) if along_x else (2, 1)
    keep_ref[:rows] = term[:rows]
    keep_ref[rows:] = term[first * rows : (first + 1) * rows]
    send_ref[:rows] = term[second * rows : (second + 1) * rows].astype(BF16)
    send_ref[rows:] = term[3 * rows :].astype(BF16)


def terms(own, other, mine, theirs, columns, along_x):
    width = own.shape[0]
    block = 1024
    at = theirs.shape[1] // (LAT // 2) - 1
    column_block = lambda i: (0, i)
    return pl.pallas_call(
        functools.partial(terms_kernel, along_x=along_x),
        grid=(columns // block,),
        in_specs=[
            pl.BlockSpec((width, block), column_block),
            pl.BlockSpec((width, block), column_block),
            pl.BlockSpec((width, LAT // 2), lambda i: (0, 0)),
            pl.BlockSpec((width, LAT // 2), lambda i: (0, at)),
        ],
        out_specs=[pl.BlockSpec((LAT // 4, block), column_block)] * 2,
        out_shape=[
            jax.ShapeDtypeStruct((LAT // 4, columns), F32),
            jax.ShapeDtypeStruct((LAT // 4, columns), BF16),
        ],
        scratch_shapes=[pltpu.VMEM((LAT // 2, 2 * width), BF16)],
        compiler_params=PARAMS,
        cost_estimate=cost(CHUNK),
        name="terms",
    )(own, other, mine, theirs)


def key_terms_kernel(*refs, chunks, steps, turns, shares):
    head_ref = refs[0]
    dkv_refs = refs[1 : 1 + chunks]
    wt_refs = refs[1 + chunks : 1 + chunks + turns]
    rope_refs = refs[1 + chunks + turns : 1 + 2 * chunks + turns]
    outs = refs[1 + 2 * chunks + turns : -1]
    total_ref = refs[-1]
    i = pl.program_id(0)

    @pl.when(i == 0)
    def _():
        total_ref[...] = jnp.zeros_like(total_ref)

    for k in range(chunks):

        @pl.when(i // steps == k)
        def _(k=k):
            total = total_ref[...]
            weight_ref = wt_refs[k * turns // chunks]
            for h in range(weight_ref.shape[0]):
                grads = dkv_refs[k][:, h * PAIR : (h + 1) * PAIR]
                total = total + dot(grads, weight_ref[h], 1, 1)
            total_ref[...] = total

    @pl.when(i == pl.num_programs(0) - 1)
    def _():
        rope = rope_refs[0][...]
        for k in range(1, chunks):
            rope = rope + rope_refs[k][...]
        both = jnp.concatenate([total_ref[...], rope], 1)
        if shares is None:
            outs[0][...] = both[:, : LAT + ROPE]
            return
        part = (LAT + ROPE) // shares
        for z in range(shares):
            piece = both[:, z * part : (z + 1) * part]
            for s in range(shares):

                @pl.when(lax.rem(head_ref[0] + s, shares) == z)
                def _(s=s, piece=piece):
                    outs[s][...] = piece


def key_terms(at_head, dkvs, weights, ropes, shares):
    chunks, turns = len(dkvs), len(weights)
    heads = weights[0].shape[0] * turns // chunks
    width = dkvs[0].shape[0]
    steps = heads // STEP_HEADS
    span = steps * chunks // turns
    near = lambda k, many: lambda i, at: jnp.clip(i - k * many, 0, many - 1)
    wide = (LAT + ROPE) // (shares or 1)
    return pl.pallas_call(
        functools.partial(
            key_terms_kernel, chunks=chunks, steps=steps, turns=turns, shares=shares
        ),
        grid_spec=pltpu.PrefetchScalarGridSpec(
            num_scalar_prefetch=1,
            grid=(chunks * steps,),
            in_specs=[
                pl.BlockSpec((width, STEP_HEADS * PAIR), lambda i, at, k=k: (0, near(k, steps)(i, at)))
                for k in range(chunks)
            ]
            + [
                pl.BlockSpec(
                    (STEP_HEADS, LAT, PAIR), lambda i, at, k=k: (near(k, span)(i, at), 0, 0)
                )
                for k in range(turns)
            ]
            + [pl.BlockSpec((width, LANES), lambda i, at: (0, 0))] * chunks,
            out_specs=[pl.BlockSpec((width, wide), lambda i, at: (0, 0))] * (shares or 1),
            scratch_shapes=[pltpu.VMEM((width, LAT), F32)],
        ),
        out_shape=[jax.ShapeDtypeStruct((width, wide), F32)] * (shares or 1),
        compiler_params=WIDE,
        cost_estimate=cost(CHUNK),
        name="key_terms",
    )(at_head, *dkvs, *weights, *ropes)


def weight_sum_kernel(keep_ref, first_ref, second_ref, *refs):
    out_ref, k_ref, v_ref = refs[-3:]
    rows, heads, _ = out_ref.shape
    for h in range(heads):
        columns = slice(h * PAIR, (h + 1) * PAIR)
        total = keep_ref[:, columns] + first_ref[:, columns].astype(F32)
        total = total + second_ref[:, columns].astype(F32)
        k_ref[pl.ds(h, rows, stride=heads), :] = total[:, :LANES]
        v_ref[pl.ds(h, rows, stride=heads), :] = total[:, LANES:]
    out_ref[:, :, :LANES] = k_ref[...].reshape(rows, heads, LANES)
    out_ref[:, :, LANES:] = v_ref[...].reshape(rows, heads, LANES)


def weight_sum(keep, first, second, total, chunk, all_heads):
    rows, columns = second.shape
    heads = columns // PAIR
    block = 32
    operands = [keep, first, second]
    in_specs = [pl.BlockSpec((block, columns), lambda i: (i, 0)) for _ in operands]
    aliases = {}
    if total is not None:
        aliases = {3: 0}
        in_specs.append(pl.BlockSpec(memory_space=pl.ANY))
        operands.append(total)
    return pl.pallas_call(
        weight_sum_kernel,
        grid=(rows // block,),
        in_specs=in_specs,
        out_specs=pl.BlockSpec((block, heads, PAIR), lambda i: (i, chunk, 0)),
        out_shape=jax.ShapeDtypeStruct((rows, all_heads, PAIR), F32),
        scratch_shapes=[pltpu.VMEM((block * heads, LANES), F32)] * 2,
        input_output_aliases=aliases,
        compiler_params=PARAMS,
        cost_estimate=cost(SUM),
        name="weight_sum",
    )(*operands)


def after(values, earlier):
    return lax.optimization_barrier((values, earlier))[0]


def turn_rows(block):
    rows, heads, width = block.shape
    count = min(rows, 256 // heads)
    row = lax.broadcasted_iota(jnp.int32, (count * heads, count * heads), 0)
    col = lax.broadcasted_iota(jnp.int32, (count * heads, count * heads), 1)
    order = (col == (row % count) * heads + row // count).astype(BF16)
    for start in range(0, rows, count):
        part = block[start : start + count].reshape(count * heads, width)
        turned = dot(order, part, 1, 0).astype(BF16)
        yield slice(start, start + count), turned.reshape(heads, count, width)


def in_hbm(array):
    return pltpu.with_memory_space_constraint(array, pltpu.HBM)


def turn_weight_kernel(here_ref, *refs):
    *parts, wt_ref = refs
    depth = parts[0].shape[0]
    for at, w_ref in enumerate(parts):
        for rows, turned in turn_rows(w_ref[...]):
            wt_ref[:, at * depth + rows.start : at * depth + rows.stop, :] = turned


def turn_weight(here, up_weight, heads):
    steps, parts = 4, 4
    depth = LAT // steps // parts
    part = lambda p: lambda i, here: (i * parts + p, here[0] & 1, 0)
    return pl.pallas_call(
        turn_weight_kernel,
        grid_spec=pltpu.PrefetchScalarGridSpec(
            num_scalar_prefetch=1,
            grid=(steps,),
            in_specs=[pl.BlockSpec((depth, heads, PAIR), part(p)) for p in range(parts)],
            out_specs=pl.BlockSpec((heads, depth * parts, PAIR), lambda i, here: (0, i, 0)),
        ),
        out_shape=jax.ShapeDtypeStruct((heads, LAT, PAIR), BF16),
        compiler_params=PARAMS,
        cost_estimate=cost(TURN),
        name="turn_weight",
    )(here, *[in_hbm(up_weight)] * parts)


def turn_tokens_kernel(here_ref, q1_ref, g1_ref, q0_ref, g0_ref, own_ref, give_ref, mine_ref):
    heads = mine_ref.shape[0]
    for q_ref, g_ref, out_ref in ((q1_ref, g1_ref, give_ref), (q0_ref, g0_ref, mine_ref)):
        out_ref[:, :, LANES : 2 * LANES] = jnp.zeros_like(out_ref[:, :, LANES : 2 * LANES])
        for rows, turned in turn_rows(q_ref[...]):
            out_ref[:heads, rows, : PLAIN_WIDTH + ROPE] = turned
        for rows, turned in turn_rows(g_ref[...]):
            out_ref[:heads, rows, 2 * LANES :] = turned
    rest = LAT + ROPE - 3 * LANES
    give_ref[heads] = own_ref[:, : 3 * LANES]
    give_ref[heads + 1] = jnp.zeros_like(give_ref[heads + 1])
    give_ref[heads + 1, :, :rest] = own_ref[:, 3 * LANES :]


def turn_tokens(here, queries, out_grad, latent_keys, heads):
    tok = queries.shape[0]
    q_block, g_block = (tok, heads, PLAIN_WIDTH + ROPE), (tok, heads, VDIM)
    given = lambda i, here: (0, 1 - (here[0] & 1), 0)
    kept = lambda i, here: (0, here[0] & 1, 0)
    whole = lambda i, here: (0, 0, 0)
    give, mine = (heads + 2, tok, 3 * LANES), (heads, tok, 3 * LANES)
    queries, out_grad, latent_keys = (in_hbm(x) for x in (queries, out_grad, latent_keys))
    return pl.pallas_call(
        turn_tokens_kernel,
        grid_spec=pltpu.PrefetchScalarGridSpec(
            num_scalar_prefetch=1,
            grid=(1,),
            in_specs=[
                pl.BlockSpec(q_block, given),
                pl.BlockSpec(g_block, given),
                pl.BlockSpec(q_block, kept),
                pl.BlockSpec(g_block, kept),
                pl.BlockSpec(latent_keys.shape, lambda i, here: (0, 0)),
            ],
            out_specs=[pl.BlockSpec(give, whole), pl.BlockSpec(mine, whole)],
        ),
        out_shape=[jax.ShapeDtypeStruct(give, BF16), jax.ShapeDtypeStruct(mine, BF16)],
        compiler_params=PARAMS,
        cost_estimate=cost(WINDOW),
        name="turn_tokens",
    )(here, queries, out_grad, queries, out_grad, latent_keys)


def chip_window_kernel(
    here_ref, even_ref, odd_ref, own_ref, pal_ref, ids_ref, win_ref, krope_ref, vis_ref, lat_ref
):
    here = here_ref[0]
    tok = own_ref.shape[0]
    core, chip = here & 1, here >> 1
    first = core == 0
    prev = jnp.where(first, even_ref[...].astype(F32), odd_ref[...].astype(F32)).astype(BF16)
    pal = jnp.concatenate([pal_ref[0], pal_ref[1, :, : LAT + ROPE - 3 * LANES]], 1).astype(F32)
    own = own_ref[...].astype(F32)
    low = jnp.where(first, own, pal).astype(BF16)
    high = jnp.where(first, pal, own).astype(BF16)
    krope_ref[...] = jnp.zeros_like(krope_ref)
    for at, block in enumerate((prev, low, high)):
        win_ref[at * tok : (at + 1) * tok, :] = block[:, :LAT]
        krope_ref[at * tok : (at + 1) * tok, :ROPE] = block[:, LAT:]
    behind = jnp.maximum(2 * chip - 1, 0)
    seg = [
        jnp.where(chip > 0, ids_ref[pl.ds(behind, 1), :], -1),
        ids_ref[pl.ds(2 * chip, 1), :],
        ids_ref[pl.ds(2 * chip + 1, 1), :],
    ]
    row = lax.broadcasted_iota(jnp.int32, (tok, tok), 0)
    col = lax.broadcasted_iota(jnp.int32, (tok, tok), 1)
    for b in range(2):
        seg_query = jnp.sum(jnp.where(row == col, seg[b + 1], 0), 1, keepdims=True)
        vis_ref[b, :, :tok] = (seg_query == seg[b]).astype(F32)
        vis_ref[b, :, tok:] = ((seg_query == seg[b + 1]) & (col <= row)).astype(F32)
    column = lax.broadcasted_iota(jnp.int32, (LAT, LAT), 0)
    source = lax.broadcasted_iota(jnp.int32, (LAT, LAT), 1)
    place = column >> 6
    apart = ((place & 2) << 1) | ((place & 4) >> 1) | (place & 1)
    wanted = ((here ^ apart) << 6) | (column & 63)
    order = (source == wanted).astype(BF16)
    lat_ref[...] = dot(order, win_ref[...], 1, 1).astype(BF16)


def chip_window(here, even, odd, own, got, ids):
    tok = own.shape[0]
    whole = lambda i, here: (0, 0)
    return pl.pallas_call(
        chip_window_kernel,
        grid_spec=pltpu.PrefetchScalarGridSpec(
            num_scalar_prefetch=1,
            grid=(1,),
            in_specs=[pl.BlockSpec(array.shape, whole) for array in (even, odd, own)]
            + [
                pl.BlockSpec((2,) + got.shape[1:], lambda i, here: (got.shape[0] // 2 - 1, 0, 0)),
                pl.BlockSpec(ids.shape, whole),
            ],
            out_specs=[
                pl.BlockSpec((3 * tok, LAT), whole),
                pl.BlockSpec((3 * tok, LANES), whole),
                pl.BlockSpec((2, tok, 2 * tok), lambda i, here: (0, 0, 0)),
                pl.BlockSpec((LAT, 3 * tok), whole),
            ],
        ),
        out_shape=[
            jax.ShapeDtypeStruct((3 * tok, LAT), BF16),
            jax.ShapeDtypeStruct((3 * tok, LANES), BF16),
            jax.ShapeDtypeStruct((2, tok, 2 * tok), F32),
            jax.ShapeDtypeStruct((LAT, 3 * tok), BF16),
        ],
        compiler_params=PARAMS,
        cost_estimate=cost(WINDOW),
        name="chip_window",
    )(here, even, odd, own, got, ids)


def chunk_kernel(
    here_ref,
    win_ref,
    krope_ref,
    vis_ref,
    lat_ref,
    wt_ref,
    mine_ref,
    got_ref,
    *refs,
    chained,
    along_x,
):
    before_ref = refs[0] if chained else None
    refs = refs[3:] if chained else refs
    keep_ref, send_ref, key_ref, dq_ref, back_ref = refs

    @pl.when(pl.program_id(0) == 0)
    def _():
        key_ref[...] = before_ref[...] if chained else jnp.zeros_like(key_ref)

    tok = vis_ref.shape[1]
    heads = wt_ref.shape[0]
    first = (here_ref[0] & 1) == 0
    scale = 1.0 / math.sqrt(PLAIN_WIDTH + ROPE)
    window, krope = win_ref[...], krope_ref[...]
    visible = [vis_ref[b] > 0.0 for b in range(2)]
    keys, values, queries, grads = [], [], [], []
    for h in range(heads):
        kv = dot(window, wt_ref[h], 1, 0).astype(BF16)
        keys.append(jnp.concatenate([kv[:, :PLAIN_WIDTH], krope], 1))
        values.append(kv[:, PLAIN_WIDTH:])
        mine, got = mine_ref[h], got_ref[h]
        ordered = (jnp.where(first, mine, got), jnp.where(first, got, mine))
        queries.append([block[:, : 2 * LANES] for block in ordered])
        grads.append([block[:, 2 * LANES :] for block in ordered])
    reach = [slice(b * tok, (b + 2) * tok) for b in range(2)]
    units = [(h, b) for h in range(heads) for b in range(2)]
    scores = {(h, b): dot(queries[h][b], keys[h][reach[b]], 1, 1) for h, b in units}
    dprobs = {(h, b): dot(grads[h][b], values[h][reach[b]], 1, 1) for h, b in units}
    dscores, probs16 = {}, {}
    for unit in units:
        logits = jnp.where(visible[unit[1]], scores[unit] * scale, -1e30)
        top = jnp.max(logits, -1, keepdims=True)
        expo = jnp.exp(logits - top)
        probs = expo / jnp.sum(expo, -1, keepdims=True)
        delta = jnp.sum(probs * dprobs[unit], -1, keepdims=True)
        dscores[unit] = (probs * (dprobs[unit] - delta) * scale).astype(BF16)
        probs16[unit] = probs.astype(BF16)

    def fold(low, high):
        return jnp.concatenate([low[:tok], low[tok:] + high[:tok], high[tok:]], 0)

    parts, rope = [], None
    for h in range(heads):
        dk = fold(*[dot(dscores[h, b], queries[h][b], 0, 0) for b in range(2)])
        dv = fold(*[dot(probs16[h, b], grads[h][b], 0, 0) for b in range(2)])
        parts.append(jnp.concatenate([dk[:, :PLAIN_WIDTH], dv], 1).astype(BF16))
        rope = dk[:, PLAIN_WIDTH:] if rope is None else rope + dk[:, PLAIN_WIDTH:]
    dkv = jnp.concatenate(parts, 1)
    rows = lat_ref.shape[0] // 4
    kept = (0, 1) if along_x else (0, 2)
    sent = (2, 3) if along_x else (1, 3)
    for at, g in enumerate(sent):
        term = dot(lat_ref[g * rows : (g + 1) * rows, :], dkv, 1, 0)
        send_ref[at * rows : (at + 1) * rows, :] = term.astype(BF16)
    for at, g in enumerate(kept):
        keep_ref[at * rows : (at + 1) * rows, :] = dot(
            lat_ref[g * rows : (g + 1) * rows, :], dkv, 1, 0
        )
    total = key_ref[:, :LAT]
    for h in range(heads):
        total = total + dot(parts[h], wt_ref[h], 1, 1)
    key_ref[:, :LAT] = total
    key_ref[:, LAT:] = key_ref[:, LAT:] + rope
    for h in range(heads):
        low, high = (dot(dscores[h, b], keys[h][reach[b]], 1, 0) for b in range(2))
        dq_ref[h] = jnp.where(first, low, high)
        back_ref[h] = jnp.where(first, high, low)


def chunk(here, window, weight, mine, got, before, index, heads, along_x):
    tok = mine.shape[1]
    whole = lambda i, here: (0, 0)
    whole3 = lambda i, here: (0, 0, 0)
    step = min(heads, STEP_HEADS)
    steps = heads // step
    at = lambda i, here: (index * steps + i, 0, 0)
    across_columns = lambda i, here: (0, i)
    columns = heads * PAIR
    operands = [*window, weight, mine, got]
    in_specs = [
        pl.BlockSpec(array.shape, whole3 if array.ndim == 3 else whole) for array in window
    ] + [
        pl.BlockSpec((step, LAT, PAIR), at),
        pl.BlockSpec((step, tok, 3 * LANES), at),
        pl.BlockSpec((step, tok, 3 * LANES), at),
    ]
    aliases = {}
    if before is not None:
        key, dq, back = before
        aliases = {len(operands) + 2: 3, len(operands) + 3: 4}
        in_specs = in_specs + [
            pl.BlockSpec(key.shape, whole),
            pl.BlockSpec(memory_space=pl.ANY),
            pl.BlockSpec(memory_space=pl.ANY),
        ]
        operands = operands + [key, dq, back]
    turned = (weight.shape[0], tok, 2 * LANES)
    return pl.pallas_call(
        functools.partial(chunk_kernel, chained=before is not None, along_x=along_x),
        grid_spec=pltpu.PrefetchScalarGridSpec(
            num_scalar_prefetch=1,
            grid=(steps,),
            in_specs=in_specs,
            out_specs=[
                pl.BlockSpec((LAT // 2, step * PAIR), across_columns),
                pl.BlockSpec((LAT // 2, step * PAIR), across_columns),
                pl.BlockSpec((3 * tok, LAT + LANES), whole),
                pl.BlockSpec((step, tok, 2 * LANES), at),
                pl.BlockSpec((step, tok, 2 * LANES), at),
            ],
        ),
        out_shape=[
            jax.ShapeDtypeStruct((LAT // 2, columns), F32),
            jax.ShapeDtypeStruct((LAT // 2, columns), BF16),
            jax.ShapeDtypeStruct((3 * tok, LAT + LANES), F32),
            jax.ShapeDtypeStruct(turned, F32),
            jax.ShapeDtypeStruct(turned, F32),
        ],
        input_output_aliases=aliases,
        compiler_params=PARAMS,
        cost_estimate=cost(CHUNK),
        name="chunk",
    )(here, *operands)


def add_rows_kernel(*refs):
    total = refs[0][...].astype(F32)
    for ref in refs[1:-1]:
        total = total + ref[...].astype(F32)
    refs[-1][...] = total.astype(refs[-1].dtype)


def add_rows(arrays, rows, index, dtype):
    columns = arrays[0].shape[1]
    return pl.pallas_call(
        add_rows_kernel,
        grid=(1,),
        in_specs=[pl.BlockSpec((rows, columns), lambda i: (index, 0)) for _ in arrays],
        out_specs=pl.BlockSpec((rows, columns), lambda i: (0, 0)),
        out_shape=jax.ShapeDtypeStruct((rows, columns), dtype),
        compiler_params=PARAMS,
        cost_estimate=cost(SHARES),
        name="add_rows",
    )(*arrays)


def key_split_kernel(here_ref, key_ref, keep_ref, give_ref):
    tok = keep_ref.shape[0] // 2
    first = (here_ref[0] & 1) == 0
    behind, low, high = (key_ref[b * tok : (b + 1) * tok, :] for b in range(3))
    keep_ref[:tok] = jnp.where(first, low, high)
    keep_ref[tok:] = behind
    give_ref[:tok] = jnp.where(first, high, low)
    give_ref[tok:] = behind


def key_split(here, key):
    rows = key.shape[0] // 3 * 2
    whole = lambda i, here: (0, 0)
    return pl.pallas_call(
        key_split_kernel,
        grid_spec=pltpu.PrefetchScalarGridSpec(
            num_scalar_prefetch=1,
            grid=(1,),
            in_specs=[pl.BlockSpec(key.shape, whole)],
            out_specs=[pl.BlockSpec((rows, key.shape[1]), whole)] * 2,
        ),
        out_shape=[jax.ShapeDtypeStruct((rows, key.shape[1]), F32)] * 2,
        compiler_params=PARAMS,
        cost_estimate=cost(SHARES),
        name="key_split",
    )(here, key)


def key_shares_kernel(at_ref, keep_ref, got_ref, *outs):
    shares = len(outs)
    part = (LAT + ROPE) // shares
    total = keep_ref[...] + got_ref[...]
    for z in range(shares):
        piece = total[:, z * part : (z + 1) * part]
        for s in range(shares):

            @pl.when(lax.rem(at_ref[0] + s, shares) == z)
            def _(s=s, piece=piece):
                outs[s][...] = piece.astype(outs[s].dtype)


def key_shares(at_head, keep, got, shares):
    part = (LAT + ROPE) // shares
    rows = keep.shape[0]
    whole = lambda i, at: (0, 0)
    types = [F32] + [BF16] * (shares - 1)
    return pl.pallas_call(
        key_shares_kernel,
        grid_spec=pltpu.PrefetchScalarGridSpec(
            num_scalar_prefetch=1,
            grid=(1,),
            in_specs=[pl.BlockSpec(keep.shape, whole)] * 2,
            out_specs=[pl.BlockSpec((rows, part), whole)] * shares,
        ),
        out_shape=[jax.ShapeDtypeStruct((rows, part), kind) for kind in types],
        compiler_params=PARAMS,
        cost_estimate=cost(SHARES),
        name="key_shares",
    )(at_head, keep, got)


def query_grad_kernel(here_ref, mine_ref, got_ref, out_ref, n_ref, r_ref):
    tok, heads, _ = out_ref.shape

    def put(src_ref):
        for h in range(heads):
            n_ref[pl.ds(h, tok, stride=heads), :] = src_ref[h, :, :PLAIN_WIDTH]
            r_ref[pl.ds(h, tok, stride=heads), :] = src_ref[h, :, PLAIN_WIDTH:]

    pl.when(pl.program_id(0) == 0)(lambda: put(mine_ref))
    pl.when(pl.program_id(0) == 1)(lambda: put(got_ref))
    out_ref[:, :, :PLAIN_WIDTH] = n_ref[...].reshape(tok, heads, LANES)
    out_ref[:, :, PLAIN_WIDTH:] = r_ref[...].reshape(tok, heads, LANES)[:, :, :ROPE]


def query_grad(here, mine, got):
    heads, tok, _ = mine.shape
    whole = lambda i, here: (0, 0, 0)
    return pl.pallas_call(
        query_grad_kernel,
        grid_spec=pltpu.PrefetchScalarGridSpec(
            num_scalar_prefetch=1,
            grid=(2,),
            in_specs=[pl.BlockSpec(mine.shape, whole)] * 2,
            out_specs=pl.BlockSpec(
                (tok, heads, PLAIN_WIDTH + ROPE), lambda i, here: (0, (here[0] & 1) ^ i, 0)
            ),
            scratch_shapes=[pltpu.VMEM((tok * heads, LANES), F32)] * 2,
        ),
        out_shape=jax.ShapeDtypeStruct((tok, 2 * heads, PLAIN_WIDTH + ROPE), F32),
        compiler_params=PARAMS,
        cost_estimate=cost(QUERY),
        name="query_grad",
    )(here, mine, got)


def weight_grad_kernel(here_ref, *refs, count):
    sums, gots = refs[: 3 * count], refs[3 * count : 4 * count]
    out_ref, k_ref, v_ref = refs[-3:]
    rows, heads, _ = out_ref.shape
    each = heads // count

    def put(c, total):
        for h in range(each):
            at = pl.ds(c * each + h, rows, stride=heads)
            k_ref[at, :] = total[:, h * PAIR : h * PAIR + LANES]
            v_ref[at, :] = total[:, h * PAIR + LANES : (h + 1) * PAIR]

    @pl.when(pl.program_id(0) == 0)
    def _():
        for c in range(count):
            keep_ref, first_ref, second_ref = sums[3 * c : 3 * c + 3]
            put(c, keep_ref[...] + first_ref[...].astype(F32) + second_ref[...].astype(F32))

    @pl.when(pl.program_id(0) == 1)
    def _():
        for c in range(count):
            put(c, gots[c][...])

    out_ref[:, :, :LANES] = k_ref[...].reshape(rows, heads, LANES)
    out_ref[:, :, LANES:] = v_ref[...].reshape(rows, heads, LANES)


def weight_grad_part(here, sums, gots, total, part, parts):
    count = len(sums)
    rows, columns = gots[0].shape
    heads = count * columns // PAIR
    operands = [array for group in sums for array in group] + list(gots)
    in_specs = [pl.BlockSpec((rows, columns), lambda i, here: (0, 0)) for _ in operands]
    aliases = {}
    if total is not None:
        aliases = {1 + len(operands): 0}
        in_specs.append(pl.BlockSpec(memory_space=pl.ANY))
        operands.append(total)
    return pl.pallas_call(
        functools.partial(weight_grad_kernel, count=count),
        grid_spec=pltpu.PrefetchScalarGridSpec(
            num_scalar_prefetch=1,
            grid=(2,),
            in_specs=in_specs,
            out_specs=pl.BlockSpec(
                (rows, heads, PAIR), lambda i, here: (0, ((here[0] & 1) ^ i) * parts + part, 0)
            ),
            scratch_shapes=[pltpu.VMEM((rows * heads, LANES), F32)] * 2,
        ),
        out_shape=jax.ShapeDtypeStruct((rows, 2 * parts * heads, PAIR), F32),
        input_output_aliases=aliases,
        compiler_params=PARAMS,
        cost_estimate=cost(SUM),
        name="weight_grad",
    )(here, *operands)


def in_chunks(queries, latent_keys, out_grad, up_weight, here, at_head, ids):
    tok = latent_keys.shape[0]
    n_ctx, n_head = lax.axis_size("ctx"), lax.axis_size("head")
    chunks, each, heads = 2, 8, 16
    queries = after(queries, ids)
    give, mine = turn_tokens(here, queries, out_grad, latent_keys, heads)
    odd_devices = range(1, n_ctx - 1, 2)
    even = lax.ppermute(latent_keys, "ctx", [(source, source + 1) for source in odd_devices])
    odd = lax.ppermute(latent_keys, "ctx", [(source, source + 2) for source in odd_devices])
    got = across(give, 1)
    weight = turn_weight(here, up_weight, heads)
    window = chip_window(here, even, odd, latent_keys, got, ids)
    before, keeps, sent, lasts = None, [], [], []
    for c in range(chunks):
        keep, out, *before = chunk(here, window, weight, mine, got, before, c, each, c % 2 == 0)
        keeps.append(keep)
        sent.append(across(out, 2 if c % 2 == 0 else 4))
    key, dq, back = before

    def forward(c):
        rest = add_rows((keeps[c], sent[c]), 2 * tok, 1, BF16)
        lasts.append(across(rest, 4 if c % 2 == 0 else 2))
        return rest

    key_keep, key_give = key_split(here, key)
    shares = key_shares(at_head, key_keep, across(key_give, 1), n_head)
    pieces = [
        lax.ppermute(shares[s], "head", [(z, (z + s) % n_head) for z in range(n_head)])
        for s in range(1, n_head)
    ]
    dq = query_grad(here, dq, across(back, 1))
    share = add_rows((shares[0], *pieces), 2 * tok, 0, F32)
    keeps[0] = after(keeps[0], share)
    rests = [forward(c) for c in range(chunks)]
    share = after(share, rests)
    behind = lax.ppermute(
        share[tok:], "ctx", [(source, source - 1) for source in range(2, n_ctx, 2)]
    )
    keeps[0] = after(keeps[0], dq)
    theirs = [
        across(add_rows((keeps[c], sent[c], lasts[c]), tok, 1, F32), 1) for c in range(chunks)
    ]
    weight_grad, parts, count = None, heads // 8, 8 // each
    for p in range(parts):
        group = range(p * count, (p + 1) * count)
        weight_grad = weight_grad_part(
            here,
            [(keeps[c], sent[c], lasts[c]) for c in group],
            [theirs[c] for c in group],
            weight_grad,
            p,
            parts,
        )
    return dq, share[:tok] + behind, weight_grad


def shards(queries, latent_keys, out_grad, up_weight, segment_ids):
    tok = latent_keys.shape[0]
    heads = queries.shape[1]
    n_ctx, n_head = lax.axis_size("ctx"), lax.axis_size("head")
    here = lax.axis_index("ctx").astype(jnp.int32).reshape(1)
    at_head = lax.axis_index("head").astype(jnp.int32).reshape(1)
    ids = segment_ids.reshape(n_ctx, tok)
    if n_ctx == 8 and heads == 32 and n_head == 4:
        return in_chunks(queries, latent_keys, out_grad, up_weight, here, at_head, ids)
    else:
        prev = from_behind(latent_keys, "ctx", REACH)
        turned = by_head(up_weight, queries, out_grad, 0, heads)
        window = key_window(here, prev, latent_keys, ids, False)
        dq, dkv, rope = attention(window, turned, None, None, 0, heads, 0, heads)
        (both,) = key_terms(at_head, [dkv], [turned[0]], [rope], None)
        share = lax.psum_scatter(
            both.reshape(REACH + 1, tok, LAT + ROPE), "head", scatter_dimension=2, tiled=True
        )
        term = jnp.einsum("ki,ke->ie", window[0], dkv, preferred_element_type=F32)
        rows = lax.psum_scatter(term.astype(BF16), "ctx", scatter_dimension=0, tiled=True)
        weight_grad = rows.astype(F32).reshape(rows.shape[0], heads, PAIR)
    key_grad = share[REACH] + from_behind(share[0], "ctx", 0 - REACH)
    return (dq, key_grad, weight_grad)


def solution(mesh):
    return jax.shard_map(
        shards,
        mesh=mesh,
        in_specs=(
            P("ctx", "head", None),
            P("ctx", None),
            P("ctx", "head", None),
            P(None, "head", None),
            P(),
        ),
        out_specs=(P("ctx", "head", None), P("ctx", "head"), P("ctx", "head", None)),
        check_vma=False,
    )
```

```python
import functools
import math

import jax
import jax.numpy as jnp
from jax import lax
from jax.experimental import pallas as pl
from jax.experimental.pallas import tpu as pltpu
from jax.sharding import PartitionSpec as P

LAT = 512
ROPE = 64
PLAIN_WIDTH = 128
VDIM = 128
REACH = 1
LANES = 128
PAIR = PLAIN_WIDTH + VDIM
STEP_HEADS = 4
BF16 = jnp.bfloat16
F32 = jnp.float32
WIDE = pltpu.CompilerParams(vmem_limit_bytes=56 * 1024 * 1024)
PARAMS = pltpu.CompilerParams(vmem_limit_bytes=20 * 1024 * 1024)


def from_behind(value, axis, steps):
    count = lax.axis_size(axis)
    initial, last = (max(0, -steps), min(count, count - steps))
    return lax.ppermute(value, axis, [(source, source + steps) for source in range(initial, last)])


def across(value, bit):
    count = lax.axis_size("ctx")
    return lax.ppermute(value, "ctx", [(source, source ^ bit) for source in range(count)])


def cost(share):
    return pl.CostEstimate(flops=int(share * 1e9), bytes_accessed=1024, transcendentals=0)


TURN, WINDOW, CHUNK, SHARES, QUERY, SUM = 3.0, 0.5, 1.5, 0.1, 0.1, 0.1


def dot(a, b, a_dim, b_dim):
    return lax.dot_general(a, b, (((a_dim,), (b_dim,)), ((), ())), preferred_element_type=F32)


def by_head_kernel(w_ref, q_ref, g_ref, wt_ref, qt_ref, gt_ref):
    heads = w_ref.shape[1]
    orders = {}

    def order(count):
        if count not in orders:
            size = count * heads
            row = lax.broadcasted_iota(jnp.int32, (size, size), 0)
            col = lax.broadcasted_iota(jnp.int32, (size, size), 1)
            wanted = (row % count) * heads + row // count
            orders[count] = (col == wanted).astype(BF16)
        return orders[count]

    def turn(ref, out_ref):
        rows, _, width = ref.shape
        count = min(rows, 256 // heads)
        for start in range(0, rows, count):
            block = ref[start : start + count].reshape(count * heads, width)
            turned = dot(order(count), block, 1, 0).astype(BF16)
            out_ref[:, start : start + count, :width] = turned.reshape(heads, count, width)

    turn(w_ref, wt_ref)
    qt_ref[...] = jnp.zeros_like(qt_ref)
    turn(q_ref, qt_ref)
    turn(g_ref, gt_ref)


def by_head(up_weight, queries, out_grad, chunk, heads):
    tok = queries.shape[0]
    steps = 4
    depth, rows = LAT // steps, tok // steps
    return pl.pallas_call(
        by_head_kernel,
        grid=(steps,),
        in_specs=[
            pl.BlockSpec((depth, heads, PAIR), lambda i: (i, chunk, 0)),
            pl.BlockSpec((rows, heads, PLAIN_WIDTH + ROPE), lambda i: (i, chunk, 0)),
            pl.BlockSpec((rows, heads, VDIM), lambda i: (i, chunk, 0)),
        ],
        out_specs=[
            pl.BlockSpec((heads, depth, PAIR), lambda i: (0, i, 0)),
            pl.BlockSpec((heads, rows, 2 * LANES), lambda i: (0, i, 0)),
            pl.BlockSpec((heads, rows, VDIM), lambda i: (0, i, 0)),
        ],
        out_shape=[
            jax.ShapeDtypeStruct((heads, LAT, PAIR), BF16),
            jax.ShapeDtypeStruct((heads, tok, 2 * LANES), BF16),
            jax.ShapeDtypeStruct((heads, tok, VDIM), BF16),
        ],
        compiler_params=WIDE,
        cost_estimate=cost(TURN),
        name="by_head",
    )(up_weight, queries, out_grad)


def window_kernel(here_ref, prev_ref, own_ref, ids_ref, *outs, paired):
    win_ref, krope_ref, vis_ref = outs[:3]
    here = here_ref[0]
    tok = prev_ref.shape[0]
    win_ref[:tok, :] = prev_ref[:, :LAT]
    win_ref[tok:, :] = own_ref[:, :LAT]
    krope_ref[...] = jnp.zeros_like(krope_ref)
    krope_ref[:tok, :ROPE] = prev_ref[:, LAT:]
    krope_ref[tok:, :ROPE] = own_ref[:, LAT:]
    behind = jnp.maximum(here - 1, 0)
    seg_prev = jnp.where(here > 0, ids_ref[pl.ds(behind, 1), :], -1)
    seg_own = ids_ref[pl.ds(here, 1), :]
    row = lax.broadcasted_iota(jnp.int32, (tok, tok), 0)
    col = lax.broadcasted_iota(jnp.int32, (tok, tok), 1)
    seg_query = jnp.sum(jnp.where(row == col, seg_own, 0), 1, keepdims=True)
    vis_ref[:, :tok] = (seg_query == seg_prev).astype(F32)
    vis_ref[:, tok:] = ((seg_query == seg_own) & (col <= row)).astype(F32)
    if paired:
        source = lax.broadcasted_iota(jnp.int32, (LAT, LAT), 0)
        column = lax.broadcasted_iota(jnp.int32, (LAT, LAT), 1)
        place = column >> 6
        apart = ((place & 1) << 2) | (place & 2) | (place >> 2)
        wanted = ((here ^ apart) << 6) | (column & 63)
        ordered = dot(win_ref[...], (source == wanted).astype(BF16), 1, 0).astype(BF16)
        outs[3][...] = ordered[:, : LAT // 2]
        outs[4][...] = ordered[:, LAT // 2 :]


def key_window(here, prev, own, ids, paired):
    tok = prev.shape[0]
    whole = lambda i, here: (0, 0)
    shapes = [((2 * tok, LAT), BF16), ((2 * tok, LANES), BF16), ((tok, 2 * tok), F32)]
    if paired:
        shapes = shapes + [((2 * tok, LAT // 2), BF16)] * 2
    return pl.pallas_call(
        functools.partial(window_kernel, paired=paired),
        grid_spec=pltpu.PrefetchScalarGridSpec(
            num_scalar_prefetch=1,
            grid=(1,),
            in_specs=[pl.BlockSpec(array.shape, whole) for array in (prev, own, ids)],
            out_specs=[pl.BlockSpec(shape, whole) for shape, _ in shapes],
        ),
        out_shape=[jax.ShapeDtypeStruct(*shape) for shape in shapes],
        compiler_params=PARAMS,
        cost_estimate=cost(WINDOW),
        name="key_window",
    )(here, prev, own, ids)


def attention_kernel(
    win_ref, krope_ref, vis_ref, wt_ref, qt_ref, gt_ref, *refs, aliased, extra
):
    latents_ref = refs[0] if extra else None
    refs = refs[1:] if extra else refs
    refs = refs[1:] if aliased else refs
    dq_ref, dkv_ref, rope_ref, dqn_ref, dqr_ref = refs
    i = pl.program_id(0)
    tok, heads = dq_ref.shape[:2]
    scale = 1.0 / math.sqrt(PLAIN_WIDTH + ROPE)

    @pl.when(i == 0)
    def _():
        rope_ref[...] = jnp.zeros_like(rope_ref)
        if extra:
            dkv_ref[:, heads * PAIR :] = latents_ref[...]

    visible = vis_ref[...] > 0.0
    window = win_ref[...]
    krope = krope_ref[...]
    count = wt_ref.shape[0]
    keys, values = [], []
    for h in range(count):
        kv = dot(window, wt_ref[h], 1, 0).astype(BF16)
        keys.append(jnp.concatenate([kv[:, :PLAIN_WIDTH], krope], 1))
        values.append(kv[:, PLAIN_WIDTH:])
    scores = [dot(qt_ref[h], keys[h], 1, 1) for h in range(count)]
    dprobs = [dot(gt_ref[h], values[h], 1, 1) for h in range(count)]
    dscores, probs16 = [], []
    for h in range(count):
        logits = jnp.where(visible, scores[h] * scale, -1e30)
        top = jnp.max(logits, -1, keepdims=True)
        expo = jnp.exp(logits - top)
        probs = expo / jnp.sum(expo, -1, keepdims=True)
        delta = jnp.sum(probs * dprobs[h], -1, keepdims=True)
        dscores.append((probs * (dprobs[h] - delta) * scale).astype(BF16))
        probs16.append(probs.astype(BF16))
    parts, rope = [], rope_ref[...]
    for h in range(count):
        dk = dot(dscores[h], qt_ref[h], 0, 0)
        dv = dot(probs16[h], gt_ref[h], 0, 0)
        parts.append(jnp.concatenate([dk[:, :PLAIN_WIDTH], dv], 1).astype(BF16))
        rope = rope + dk[:, PLAIN_WIDTH:]
    rope_ref[...] = rope
    dkv_ref[:, pl.ds(pl.multiple_of(i * (count * PAIR), count * PAIR), count * PAIR)] = (
        jnp.concatenate(parts, 1)
    )
    for h in range(count):
        dq = dot(dscores[h], keys[h], 1, 0)
        dqn_ref[pl.ds(i * count + h, tok, stride=heads), :] = dq[:, :PLAIN_WIDTH]
        dqr_ref[pl.ds(i * count + h, tok, stride=heads), :] = dq[:, PLAIN_WIDTH:]

    @pl.when(i == pl.num_programs(0) - 1)
    def _():
        dq_ref[:, :, :PLAIN_WIDTH] = dqn_ref[...].reshape(tok, heads, LANES)
        dq_ref[:, :, PLAIN_WIDTH:] = dqr_ref[...].reshape(tok, heads, LANES)[:, :, :ROPE]


def attention(window, turned, latents, dq, chunk, heads, first, all_heads):
    weight, queries, out_grad = turned
    tok = queries.shape[1]
    width = 2 * tok
    steps = heads // STEP_HEADS
    at = first // STEP_HEADS
    extra = LAT // 2 if latents is not None else 0
    whole = lambda i: (0, 0)
    head_block = lambda i: (at + i, 0, 0)
    operands = [*window, weight, queries, out_grad]
    in_specs = [pl.BlockSpec(array.shape, whole) for array in window] + [
        pl.BlockSpec((STEP_HEADS, LAT, PAIR), head_block),
        pl.BlockSpec((STEP_HEADS, tok, 2 * LANES), head_block),
        pl.BlockSpec((STEP_HEADS, tok, VDIM), head_block),
    ]
    if latents is not None:
        in_specs.append(pl.BlockSpec(latents.shape, whole))
        operands.append(latents)
    aliases = {}
    if dq is not None:
        aliases = {len(operands): 0}
        in_specs.append(pl.BlockSpec(memory_space=pl.ANY))
        operands.append(dq)
    return pl.pallas_call(
        functools.partial(attention_kernel, aliased=dq is not None, extra=latents is not None),
        grid=(steps,),
        in_specs=in_specs,
        out_specs=[
            pl.BlockSpec((tok, heads, PLAIN_WIDTH + ROPE), lambda i: (0, chunk, 0)),
            pl.BlockSpec((width, heads * PAIR + extra), whole),
            pl.BlockSpec((width, LANES), whole),
        ],
        scratch_shapes=[
            pltpu.VMEM((tok * heads, LANES), F32),
            pltpu.VMEM((tok * heads, LANES), F32),
        ],
        out_shape=[
            jax.ShapeDtypeStruct((tok, all_heads, PLAIN_WIDTH + ROPE), F32),
            jax.ShapeDtypeStruct((width, heads * PAIR + extra), BF16),
            jax.ShapeDtypeStruct((width, LANES), F32),
        ],
        input_output_aliases=aliases,
        compiler_params=WIDE,
        cost_estimate=cost(CHUNK),
        name="attention",
    )(*operands)


def terms_kernel(
    own_ref, other_ref, mine_ref, theirs_ref, keep_ref, send_ref, latents_ref, *, along_x
):
    width = own_ref.shape[0]

    @pl.when(pl.program_id(0) == 0)
    def _():
        latents_ref[:, :width] = mine_ref[...].T
        latents_ref[:, width:] = theirs_ref[...].T

    grads = jnp.concatenate([own_ref[...], other_ref[...]], 0)
    term = dot(latents_ref[...], grads, 1, 0)
    rows = term.shape[0] // 4
    first, second = (1, 2) if along_x else (2, 1)
    keep_ref[:rows] = term[:rows]
    keep_ref[rows:] = term[first * rows : (first + 1) * rows]
    send_ref[:rows] = term[second * rows : (second + 1) * rows].astype(BF16)
    send_ref[rows:] = term[3 * rows :].astype(BF16)


def terms(own, other, mine, theirs, columns, along_x):
    width = own.shape[0]
    block = 1024
    at = theirs.shape[1] // (LAT // 2) - 1
    column_block = lambda i: (0, i)
    return pl.pallas_call(
        functools.partial(terms_kernel, along_x=along_x),
        grid=(columns // block,),
        in_specs=[
            pl.BlockSpec((width, block), column_block),
            pl.BlockSpec((width, block), column_block),
            pl.BlockSpec((width, LAT // 2), lambda i: (0, 0)),
            pl.BlockSpec((width, LAT // 2), lambda i: (0, at)),
        ],
        out_specs=[pl.BlockSpec((LAT // 4, block), column_block)] * 2,
        out_shape=[
            jax.ShapeDtypeStruct((LAT // 4, columns), F32),
            jax.ShapeDtypeStruct((LAT // 4, columns), BF16),
        ],
        scratch_shapes=[pltpu.VMEM((LAT // 2, 2 * width), BF16)],
        compiler_params=PARAMS,
        cost_estimate=cost(CHUNK),
        name="terms",
    )(own, other, mine, theirs)


def key_terms_kernel(*refs, chunks, steps, turns, shares):
    head_ref = refs[0]
    dkv_refs = refs[1 : 1 + chunks]
    wt_refs = refs[1 + chunks : 1 + chunks + turns]
    rope_refs = refs[1 + chunks + turns : 1 + 2 * chunks + turns]
    outs = refs[1 + 2 * chunks + turns : -1]
    total_ref = refs[-1]
    i = pl.program_id(0)

    @pl.when(i == 0)
    def _():
        total_ref[...] = jnp.zeros_like(total_ref)

    for k in range(chunks):

        @pl.when(i // steps == k)
        def _(k=k):
            total = total_ref[...]
            weight_ref = wt_refs[k * turns // chunks]
            for h in range(weight_ref.shape[0]):
                grads = dkv_refs[k][:, h * PAIR : (h + 1) * PAIR]
                total = total + dot(grads, weight_ref[h], 1, 1)
            total_ref[...] = total

    @pl.when(i == pl.num_programs(0) - 1)
    def _():
        rope = rope_refs[0][...]
        for k in range(1, chunks):
            rope = rope + rope_refs[k][...]
        both = jnp.concatenate([total_ref[...], rope], 1)
        if shares is None:
            outs[0][...] = both[:, : LAT + ROPE]
            return
        part = (LAT + ROPE) // shares
        for z in range(shares):
            piece = both[:, z * part : (z + 1) * part]
            for s in range(shares):

                @pl.when(lax.rem(head_ref[0] + s, shares) == z)
                def _(s=s, piece=piece):
                    outs[s][...] = piece


def key_terms(at_head, dkvs, weights, ropes, shares):
    chunks, turns = len(dkvs), len(weights)
    heads = weights[0].shape[0] * turns // chunks
    width = dkvs[0].shape[0]
    steps = heads // STEP_HEADS
    span = steps * chunks // turns
    near = lambda k, many: lambda i, at: jnp.clip(i - k * many, 0, many - 1)
    wide = (LAT + ROPE) // (shares or 1)
    return pl.pallas_call(
        functools.partial(
            key_terms_kernel, chunks=chunks, steps=steps, turns=turns, shares=shares
        ),
        grid_spec=pltpu.PrefetchScalarGridSpec(
            num_scalar_prefetch=1,
            grid=(chunks * steps,),
            in_specs=[
                pl.BlockSpec((width, STEP_HEADS * PAIR), lambda i, at, k=k: (0, near(k, steps)(i, at)))
                for k in range(chunks)
            ]
            + [
                pl.BlockSpec(
                    (STEP_HEADS, LAT, PAIR), lambda i, at, k=k: (near(k, span)(i, at), 0, 0)
                )
                for k in range(turns)
            ]
            + [pl.BlockSpec((width, LANES), lambda i, at: (0, 0))] * chunks,
            out_specs=[pl.BlockSpec((width, wide), lambda i, at: (0, 0))] * (shares or 1),
            scratch_shapes=[pltpu.VMEM((width, LAT), F32)],
        ),
        out_shape=[jax.ShapeDtypeStruct((width, wide), F32)] * (shares or 1),
        compiler_params=WIDE,
        cost_estimate=cost(CHUNK),
        name="key_terms",
    )(at_head, *dkvs, *weights, *ropes)


def weight_sum_kernel(keep_ref, first_ref, second_ref, *refs):
    out_ref, k_ref, v_ref = refs[-3:]
    rows, heads, _ = out_ref.shape
    for h in range(heads):
        columns = slice(h * PAIR, (h + 1) * PAIR)
        total = keep_ref[:, columns] + first_ref[:, columns].astype(F32)
        total = total + second_ref[:, columns].astype(F32)
        k_ref[pl.ds(h, rows, stride=heads), :] = total[:, :LANES]
        v_ref[pl.ds(h, rows, stride=heads), :] = total[:, LANES:]
    out_ref[:, :, :LANES] = k_ref[...].reshape(rows, heads, LANES)
    out_ref[:, :, LANES:] = v_ref[...].reshape(rows, heads, LANES)


def weight_sum(keep, first, second, total, chunk, all_heads):
    rows, columns = second.shape
    heads = columns // PAIR
    block = 32
    operands = [keep, first, second]
    in_specs = [pl.BlockSpec((block, columns), lambda i: (i, 0)) for _ in operands]
    aliases = {}
    if total is not None:
        aliases = {3: 0}
        in_specs.append(pl.BlockSpec(memory_space=pl.ANY))
        operands.append(total)
    return pl.pallas_call(
        weight_sum_kernel,
        grid=(rows // block,),
        in_specs=in_specs,
        out_specs=pl.BlockSpec((block, heads, PAIR), lambda i: (i, chunk, 0)),
        out_shape=jax.ShapeDtypeStruct((rows, all_heads, PAIR), F32),
        scratch_shapes=[pltpu.VMEM((block * heads, LANES), F32)] * 2,
        input_output_aliases=aliases,
        compiler_params=PARAMS,
        cost_estimate=cost(SUM),
        name="weight_sum",
    )(*operands)


def after(values, earlier):
    return lax.optimization_barrier((values, earlier))[0]


def turn_rows(block):
    rows, heads, width = block.shape
    count = min(rows, 256 // heads)
    row = lax.broadcasted_iota(jnp.int32, (count * heads, count * heads), 0)
    col = lax.broadcasted_iota(jnp.int32, (count * heads, count * heads), 1)
    order = (col == (row % count) * heads + row // count).astype(BF16)
    for start in range(0, rows, count):
        part = block[start : start + count].reshape(count * heads, width)
        turned = dot(order, part, 1, 0).astype(BF16)
        yield slice(start, start + count), turned.reshape(heads, count, width)


def in_hbm(array):
    return pltpu.with_memory_space_constraint(array, pltpu.HBM)


def turn_weight_kernel(here_ref, *refs):
    *parts, wt_ref = refs
    depth = parts[0].shape[0]
    for at, w_ref in enumerate(parts):
        for rows, turned in turn_rows(w_ref[...]):
            wt_ref[:, at * depth + rows.start : at * depth + rows.stop, :] = turned


def turn_weight(here, up_weight, heads):
    steps, parts = 4, 4
    depth = LAT // steps // parts
    part = lambda p: lambda i, here: (i * parts + p, here[0] & 1, 0)
    return pl.pallas_call(
        turn_weight_kernel,
        grid_spec=pltpu.PrefetchScalarGridSpec(
            num_scalar_prefetch=1,
            grid=(steps,),
            in_specs=[pl.BlockSpec((depth, heads, PAIR), part(p)) for p in range(parts)],
            out_specs=pl.BlockSpec((heads, depth * parts, PAIR), lambda i, here: (0, i, 0)),
        ),
        out_shape=jax.ShapeDtypeStruct((heads, LAT, PAIR), BF16),
        compiler_params=PARAMS,
        cost_estimate=cost(TURN),
        name="turn_weight",
    )(here, *[in_hbm(up_weight)] * parts)


def turn_tokens_kernel(here_ref, q1_ref, g1_ref, q0_ref, g0_ref, own_ref, give_ref, mine_ref):
    heads = mine_ref.shape[0]
    for q_ref, g_ref, out_ref in ((q1_ref, g1_ref, give_ref), (q0_ref, g0_ref, mine_ref)):
        out_ref[:, :, LANES : 2 * LANES] = jnp.zeros_like(out_ref[:, :, LANES : 2 * LANES])
        for rows, turned in turn_rows(q_ref[...]):
            out_ref[:heads, rows, : PLAIN_WIDTH + ROPE] = turned
        for rows, turned in turn_rows(g_ref[...]):
            out_ref[:heads, rows, 2 * LANES :] = turned
    rest = LAT + ROPE - 3 * LANES
    give_ref[heads] = own_ref[:, : 3 * LANES]
    give_ref[heads + 1] = jnp.zeros_like(give_ref[heads + 1])
    give_ref[heads + 1, :, :rest] = own_ref[:, 3 * LANES :]


def turn_tokens(here, queries, out_grad, latent_keys, heads):
    tok = queries.shape[0]
    q_block, g_block = (tok, heads, PLAIN_WIDTH + ROPE), (tok, heads, VDIM)
    given = lambda i, here: (0, 1 - (here[0] & 1), 0)
    kept = lambda i, here: (0, here[0] & 1, 0)
    whole = lambda i, here: (0, 0, 0)
    give, mine = (heads + 2, tok, 3 * LANES), (heads, tok, 3 * LANES)
    queries, out_grad, latent_keys = (in_hbm(x) for x in (queries, out_grad, latent_keys))
    return pl.pallas_call(
        turn_tokens_kernel,
        grid_spec=pltpu.PrefetchScalarGridSpec(
            num_scalar_prefetch=1,
            grid=(1,),
            in_specs=[
                pl.BlockSpec(q_block, given),
                pl.BlockSpec(g_block, given),
                pl.BlockSpec(q_block, kept),
                pl.BlockSpec(g_block, kept),
                pl.BlockSpec(latent_keys.shape, lambda i, here: (0, 0)),
            ],
            out_specs=[pl.BlockSpec(give, whole), pl.BlockSpec(mine, whole)],
        ),
        out_shape=[jax.ShapeDtypeStruct(give, BF16), jax.ShapeDtypeStruct(mine, BF16)],
        compiler_params=PARAMS,
        cost_estimate=cost(WINDOW),
        name="turn_tokens",
    )(here, queries, out_grad, queries, out_grad, latent_keys)


def chip_window_kernel(
    here_ref, even_ref, odd_ref, own_ref, pal_ref, ids_ref, win_ref, krope_ref, vis_ref, lat_ref
):
    here = here_ref[0]
    tok = own_ref.shape[0]
    core, chip = here & 1, here >> 1
    first = core == 0
    prev = jnp.where(first, even_ref[...].astype(F32), odd_ref[...].astype(F32)).astype(BF16)
    pal = jnp.concatenate([pal_ref[0], pal_ref[1, :, : LAT + ROPE - 3 * LANES]], 1).astype(F32)
    own = own_ref[...].astype(F32)
    low = jnp.where(first, own, pal).astype(BF16)
    high = jnp.where(first, pal, own).astype(BF16)
    krope_ref[...] = jnp.zeros_like(krope_ref)
    for at, block in enumerate((prev, low, high)):
        win_ref[at * tok : (at + 1) * tok, :] = block[:, :LAT]
        krope_ref[at * tok : (at + 1) * tok, :ROPE] = block[:, LAT:]
    behind = jnp.maximum(2 * chip - 1, 0)
    seg = [
        jnp.where(chip > 0, ids_ref[pl.ds(behind, 1), :], -1),
        ids_ref[pl.ds(2 * chip, 1), :],
        ids_ref[pl.ds(2 * chip + 1, 1), :],
    ]
    row = lax.broadcasted_iota(jnp.int32, (tok, tok), 0)
    col = lax.broadcasted_iota(jnp.int32, (tok, tok), 1)
    for b in range(2):
        seg_query = jnp.sum(jnp.where(row == col, seg[b + 1], 0), 1, keepdims=True)
        vis_ref[b, :, :tok] = (seg_query == seg[b]).astype(F32)
        vis_ref[b, :, tok:] = ((seg_query == seg[b + 1]) & (col <= row)).astype(F32)
    column = lax.broadcasted_iota(jnp.int32, (LAT, LAT), 0)
    source = lax.broadcasted_iota(jnp.int32, (LAT, LAT), 1)
    place = column >> 6
    apart = ((place & 2) << 1) | ((place & 4) >> 1) | (place & 1)
    wanted = ((here ^ apart) << 6) | (column & 63)
    order = (source == wanted).astype(BF16)
    lat_ref[...] = dot(order, win_ref[...], 1, 1).astype(BF16)


def chip_window(here, even, odd, own, got, ids):
    tok = own.shape[0]
    whole = lambda i, here: (0, 0)
    return pl.pallas_call(
        chip_window_kernel,
        grid_spec=pltpu.PrefetchScalarGridSpec(
            num_scalar_prefetch=1,
            grid=(1,),
            in_specs=[pl.BlockSpec(array.shape, whole) for array in (even, odd, own)]
            + [
                pl.BlockSpec((2,) + got.shape[1:], lambda i, here: (got.shape[0] // 2 - 1, 0, 0)),
                pl.BlockSpec(ids.shape, whole),
            ],
            out_specs=[
                pl.BlockSpec((3 * tok, LAT), whole),
                pl.BlockSpec((3 * tok, LANES), whole),
                pl.BlockSpec((2, tok, 2 * tok), lambda i, here: (0, 0, 0)),
                pl.BlockSpec((LAT, 3 * tok), whole),
            ],
        ),
        out_shape=[
            jax.ShapeDtypeStruct((3 * tok, LAT), BF16),
            jax.ShapeDtypeStruct((3 * tok, LANES), BF16),
            jax.ShapeDtypeStruct((2, tok, 2 * tok), F32),
            jax.ShapeDtypeStruct((LAT, 3 * tok), BF16),
        ],
        compiler_params=PARAMS,
        cost_estimate=cost(WINDOW),
        name="chip_window",
    )(here, even, odd, own, got, ids)


def chunk_kernel(
    here_ref,
    win_ref,
    krope_ref,
    vis_ref,
    lat_ref,
    wt_ref,
    mine_ref,
    got_ref,
    *refs,
    chained,
    along_x,
):
    before_ref = refs[0] if chained else None
    refs = refs[3:] if chained else refs
    keep_ref, send_ref, key_ref, dq_ref, back_ref = refs

    @pl.when(pl.program_id(0) == 0)
    def _():
        key_ref[...] = before_ref[...] if chained else jnp.zeros_like(key_ref)

    tok = vis_ref.shape[1]
    heads = wt_ref.shape[0]
    first = (here_ref[0] & 1) == 0
    scale = 1.0 / math.sqrt(PLAIN_WIDTH + ROPE)
    window, krope = win_ref[...], krope_ref[...]
    visible = [vis_ref[b] > 0.0 for b in range(2)]
    keys, values, queries, grads = [], [], [], []
    for h in range(heads):
        kv = dot(window, wt_ref[h], 1, 0).astype(BF16)
        keys.append(jnp.concatenate([kv[:, :PLAIN_WIDTH], krope], 1))
        values.append(kv[:, PLAIN_WIDTH:])
        mine, got = mine_ref[h], got_ref[h]
        ordered = (jnp.where(first, mine, got), jnp.where(first, got, mine))
        queries.append([block[:, : 2 * LANES] for block in ordered])
        grads.append([block[:, 2 * LANES :] for block in ordered])
    reach = [slice(b * tok, (b + 2) * tok) for b in range(2)]
    units = [(h, b) for h in range(heads) for b in range(2)]
    scores = {(h, b): dot(queries[h][b], keys[h][reach[b]], 1, 1) for h, b in units}
    dprobs = {(h, b): dot(grads[h][b], values[h][reach[b]], 1, 1) for h, b in units}
    dscores, probs16 = {}, {}
    for unit in units:
        logits = jnp.where(visible[unit[1]], scores[unit] * scale, -1e30)
        top = jnp.max(logits, -1, keepdims=True)
        expo = jnp.exp(logits - top)
        probs = expo / jnp.sum(expo, -1, keepdims=True)
        delta = jnp.sum(probs * dprobs[unit], -1, keepdims=True)
        dscores[unit] = (probs * (dprobs[unit] - delta) * scale).astype(BF16)
        probs16[unit] = probs.astype(BF16)

    def fold(low, high):
        return jnp.concatenate([low[:tok], low[tok:] + high[:tok], high[tok:]], 0)

    parts, rope = [], None
    for h in range(heads):
        dk = fold(*[dot(dscores[h, b], queries[h][b], 0, 0) for b in range(2)])
        dv = fold(*[dot(probs16[h, b], grads[h][b], 0, 0) for b in range(2)])
        parts.append(jnp.concatenate([dk[:, :PLAIN_WIDTH], dv], 1).astype(BF16))
        rope = dk[:, PLAIN_WIDTH:] if rope is None else rope + dk[:, PLAIN_WIDTH:]
    dkv = jnp.concatenate(parts, 1)
    rows = lat_ref.shape[0] // 4
    kept = (0, 1) if along_x else (0, 2)
    sent = (2, 3) if along_x else (1, 3)
    for at, g in enumerate(sent):
        term = dot(lat_ref[g * rows : (g + 1) * rows, :], dkv, 1, 0)
        send_ref[at * rows : (at + 1) * rows, :] = term.astype(BF16)
    for at, g in enumerate(kept):
        keep_ref[at * rows : (at + 1) * rows, :] = dot(
            lat_ref[g * rows : (g + 1) * rows, :], dkv, 1, 0
        )
    total = key_ref[:, :LAT]
    for h in range(heads):
        total = total + dot(parts[h], wt_ref[h], 1, 1)
    key_ref[:, :LAT] = total
    key_ref[:, LAT:] = key_ref[:, LAT:] + rope
    for h in range(heads):
        low, high = (dot(dscores[h, b], keys[h][reach[b]], 1, 0) for b in range(2))
        dq_ref[h] = jnp.where(first, low, high)
        back_ref[h] = jnp.where(first, high, low)


def chunk(here, window, weight, mine, got, before, index, heads, along_x):
    tok = mine.shape[1]
    whole = lambda i, here: (0, 0)
    whole3 = lambda i, here: (0, 0, 0)
    step = min(heads, STEP_HEADS)
    steps = heads // step
    at = lambda i, here: (index * steps + i, 0, 0)
    across_columns = lambda i, here: (0, i)
    columns = heads * PAIR
    operands = [*window, weight, mine, got]
    in_specs = [
        pl.BlockSpec(array.shape, whole3 if array.ndim == 3 else whole) for array in window
    ] + [
        pl.BlockSpec((step, LAT, PAIR), at),
        pl.BlockSpec((step, tok, 3 * LANES), at),
        pl.BlockSpec((step, tok, 3 * LANES), at),
    ]
    aliases = {}
    if before is not None:
        key, dq, back = before
        aliases = {len(operands) + 2: 3, len(operands) + 3: 4}
        in_specs = in_specs + [
            pl.BlockSpec(key.shape, whole),
            pl.BlockSpec(memory_space=pl.ANY),
            pl.BlockSpec(memory_space=pl.ANY),
        ]
        operands = operands + [key, dq, back]
    turned = (weight.shape[0], tok, 2 * LANES)
    return pl.pallas_call(
        functools.partial(chunk_kernel, chained=before is not None, along_x=along_x),
        grid_spec=pltpu.PrefetchScalarGridSpec(
            num_scalar_prefetch=1,
            grid=(steps,),
            in_specs=in_specs,
            out_specs=[
                pl.BlockSpec((LAT // 2, step * PAIR), across_columns),
                pl.BlockSpec((LAT // 2, step * PAIR), across_columns),
                pl.BlockSpec((3 * tok, LAT + LANES), whole),
                pl.BlockSpec((step, tok, 2 * LANES), at),
                pl.BlockSpec((step, tok, 2 * LANES), at),
            ],
        ),
        out_shape=[
            jax.ShapeDtypeStruct((LAT // 2, columns), F32),
            jax.ShapeDtypeStruct((LAT // 2, columns), BF16),
            jax.ShapeDtypeStruct((3 * tok, LAT + LANES), F32),
            jax.ShapeDtypeStruct(turned, F32),
            jax.ShapeDtypeStruct(turned, F32),
        ],
        input_output_aliases=aliases,
        compiler_params=PARAMS,
        cost_estimate=cost(CHUNK),
        name="chunk",
    )(here, *operands)


def add_rows_kernel(*refs, count, wide):
    total = refs[0][...].astype(F32)
    for ref in refs[1 : count + wide]:
        total = total + ref[...].astype(F32)
    refs[-1][...] = total.astype(refs[-1].dtype)


def add_rows(arrays, rows, index, dtype, wide=(), place=0, places=1, before=None):
    columns = arrays[0].shape[1]
    operands = [*arrays, *wide]
    in_specs = [pl.BlockSpec((rows, columns), lambda i: (index, 0)) for _ in arrays]
    in_specs = in_specs + [pl.BlockSpec((rows, columns), lambda i: (index, place)) for _ in wide]
    aliases = {}
    if before is not None:
        aliases = {len(operands): 0}
        in_specs.append(pl.BlockSpec(memory_space=pl.ANY))
        operands.append(before)
    return pl.pallas_call(
        functools.partial(add_rows_kernel, count=len(arrays), wide=len(wide)),
        grid=(1,),
        in_specs=in_specs,
        out_specs=pl.BlockSpec((rows, columns), lambda i: (0, place)),
        out_shape=jax.ShapeDtypeStruct((rows, places * columns), dtype),
        input_output_aliases=aliases,
        compiler_params=PARAMS,
        cost_estimate=cost(SHARES),
        name="add_rows",
    )(*operands)


def key_split_kernel(here_ref, key_ref, keep_ref, give_ref):
    tok = keep_ref.shape[0] // 2
    first = (here_ref[0] & 1) == 0
    behind, low, high = (key_ref[b * tok : (b + 1) * tok, :] for b in range(3))
    keep_ref[:tok] = jnp.where(first, low, high)
    keep_ref[tok:] = behind
    give_ref[:tok] = jnp.where(first, high, low)
    give_ref[tok:] = behind


def key_split(here, key):
    rows = key.shape[0] // 3 * 2
    whole = lambda i, here: (0, 0)
    return pl.pallas_call(
        key_split_kernel,
        grid_spec=pltpu.PrefetchScalarGridSpec(
            num_scalar_prefetch=1,
            grid=(1,),
            in_specs=[pl.BlockSpec(key.shape, whole)],
            out_specs=[pl.BlockSpec((rows, key.shape[1]), whole)] * 2,
        ),
        out_shape=[jax.ShapeDtypeStruct((rows, key.shape[1]), F32)] * 2,
        compiler_params=PARAMS,
        cost_estimate=cost(SHARES),
        name="key_split",
    )(here, key)


def key_shares_kernel(at_ref, keep_ref, got_ref, *outs):
    shares = len(outs)
    part = (LAT + ROPE) // shares
    total = keep_ref[...] + got_ref[...]
    for z in range(shares):
        piece = total[:, z * part : (z + 1) * part]
        for s in range(shares):

            @pl.when(lax.rem(at_ref[0] + s, shares) == z)
            def _(s=s, piece=piece):
                outs[s][...] = piece.astype(outs[s].dtype)


def key_shares(at_head, keep, got, shares):
    part = (LAT + ROPE) // shares
    rows = keep.shape[0]
    whole = lambda i, at: (0, 0)
    types = [F32] + [BF16] * (shares - 1)
    return pl.pallas_call(
        key_shares_kernel,
        grid_spec=pltpu.PrefetchScalarGridSpec(
            num_scalar_prefetch=1,
            grid=(1,),
            in_specs=[pl.BlockSpec(keep.shape, whole)] * 2,
            out_specs=[pl.BlockSpec((rows, part), whole)] * shares,
        ),
        out_shape=[jax.ShapeDtypeStruct((rows, part), kind) for kind in types],
        compiler_params=PARAMS,
        cost_estimate=cost(SHARES),
        name="key_shares",
    )(at_head, keep, got)


def query_grad_kernel(here_ref, mine_ref, got_ref, out_ref, n_ref, r_ref):
    tok, heads, _ = out_ref.shape

    def put(src_ref):
        for h in range(heads):
            n_ref[pl.ds(h, tok, stride=heads), :] = src_ref[h, :, :PLAIN_WIDTH]
            r_ref[pl.ds(h, tok, stride=heads), :] = src_ref[h, :, PLAIN_WIDTH:]

    pl.when(pl.program_id(0) == 0)(lambda: put(mine_ref))
    pl.when(pl.program_id(0) == 1)(lambda: put(got_ref))
    out_ref[:, :, :PLAIN_WIDTH] = n_ref[...].reshape(tok, heads, LANES)
    out_ref[:, :, PLAIN_WIDTH:] = r_ref[...].reshape(tok, heads, LANES)[:, :, :ROPE]


def query_grad(here, mine, got):
    heads, tok, _ = mine.shape
    whole = lambda i, here: (0, 0, 0)
    return pl.pallas_call(
        query_grad_kernel,
        grid_spec=pltpu.PrefetchScalarGridSpec(
            num_scalar_prefetch=1,
            grid=(2,),
            in_specs=[pl.BlockSpec(mine.shape, whole)] * 2,
            out_specs=pl.BlockSpec(
                (tok, heads, PLAIN_WIDTH + ROPE), lambda i, here: (0, (here[0] & 1) ^ i, 0)
            ),
            scratch_shapes=[pltpu.VMEM((tok * heads, LANES), F32)] * 2,
        ),
        out_shape=jax.ShapeDtypeStruct((tok, 2 * heads, PLAIN_WIDTH + ROPE), F32),
        compiler_params=PARAMS,
        cost_estimate=cost(QUERY),
        name="query_grad",
    )(here, mine, got)


def weight_grad_kernel(here_ref, *refs, count):
    narrow, last_ref, got_ref = refs[: 2 * count], refs[2 * count], refs[2 * count + 1]
    out_ref, k_ref, v_ref = refs[-3:]
    rows, heads, _ = out_ref.shape
    each = heads // count

    def put(c, total):
        for h in range(each):
            at = pl.ds(c * each + h, rows, stride=heads)
            k_ref[at, :] = total[:, h * PAIR : h * PAIR + LANES]
            v_ref[at, :] = total[:, h * PAIR + LANES : (h + 1) * PAIR]

    for c in range(count):
        columns = slice(c * each * PAIR, (c + 1) * each * PAIR)

        @pl.when(pl.program_id(0) == 0)
        def _(c=c, columns=columns):
            keep_ref, first_ref = narrow[2 * c : 2 * c + 2]
            total = keep_ref[...] + first_ref[...].astype(F32)
            put(c, total + last_ref[:, columns].astype(F32))

        @pl.when(pl.program_id(0) == 1)
        def _(c=c, columns=columns):
            put(c, got_ref[:, columns])

    out_ref[:, :, :LANES] = k_ref[...].reshape(rows, heads, LANES)
    out_ref[:, :, LANES:] = v_ref[...].reshape(rows, heads, LANES)


def weight_grad_part(here, groups, last, got, total, part, parts):
    count = len(groups)
    rows, columns = got.shape
    heads = columns // PAIR
    operands = [array for group in groups for array in group] + [last, got]
    whole = lambda i, here: (0, 0)
    in_specs = [pl.BlockSpec((rows, columns // count), whole)] * (2 * count)
    in_specs = in_specs + [pl.BlockSpec((rows, columns), whole)] * 2
    aliases = {}
    if total is not None:
        aliases = {1 + len(operands): 0}
        in_specs.append(pl.BlockSpec(memory_space=pl.ANY))
        operands.append(total)
    return pl.pallas_call(
        functools.partial(weight_grad_kernel, count=count),
        grid_spec=pltpu.PrefetchScalarGridSpec(
            num_scalar_prefetch=1,
            grid=(2,),
            in_specs=in_specs,
            out_specs=pl.BlockSpec(
                (rows, heads, PAIR), lambda i, here: (0, ((here[0] & 1) ^ i) * parts + part, 0)
            ),
            scratch_shapes=[pltpu.VMEM((rows * heads, LANES), F32)] * 2,
        ),
        out_shape=jax.ShapeDtypeStruct((rows, 2 * parts * heads, PAIR), F32),
        input_output_aliases=aliases,
        compiler_params=PARAMS,
        cost_estimate=cost(SUM),
        name="weight_grad",
    )(here, *operands)


def in_chunks(queries, latent_keys, out_grad, up_weight, here, at_head, ids):
    tok = latent_keys.shape[0]
    n_ctx, n_head = lax.axis_size("ctx"), lax.axis_size("head")
    heads, each = 16, 4
    queries = after(queries, ids)
    give, mine = turn_tokens(here, queries, out_grad, latent_keys, heads)
    odd_devices = range(1, n_ctx - 1, 2)
    even = lax.ppermute(latent_keys, "ctx", [(source, source + 1) for source in odd_devices])
    odd = lax.ppermute(latent_keys, "ctx", [(source, source + 2) for source in odd_devices])
    got = across(give, 1)
    weight = turn_weight(here, up_weight, heads)
    window = chip_window(here, even, odd, latent_keys, got, ids)
    ways, blocks = ((2, 4), (4, 2)), (0, 2, 1, 3)
    before, keeps, sent = None, [], []
    for c, block in enumerate(blocks):
        keep, out, *before = chunk(
            here, window, weight, mine, got, before, block, each, c % 2 == 0
        )
        keeps.append(keep)
        sent.append(across(out, ways[c % 2][0]))
    key, dq, back = before

    def rest(c, earlier):
        return add_rows(
            (keeps[c], sent[c]), 2 * tok, 1, BF16, place=c // 2, places=2, before=earlier
        )

    key_keep, key_give = key_split(here, key)
    key_got = across(key_give, 1)
    rests = [rest(0, None), rest(1, None)]
    key_got = after(key_got, rests)
    shares = key_shares(at_head, key_keep, key_got, n_head)
    pieces = [
        lax.ppermute(shares[s], "head", [(z, (z + s) % n_head) for z in range(n_head)])
        for s in range(1, n_head)
    ]
    dq = query_grad(here, dq, across(back, 1))
    share = add_rows((shares[0], *pieces), 2 * tok, 0, F32)
    keeps[2] = after(keeps[2], share)
    rests = [rest(2, rests[0]), rest(3, rests[1])]
    lasts = [across(rests[p], ways[p][1]) for p in range(2)]
    behind = lax.ppermute(
        share[tok:], "ctx", [(source, source - 1) for source in range(2, n_ctx, 2)]
    )
    key_grad = share[:tok] + behind
    keeps[0] = after(keeps[0], (dq, key_grad))
    theirs = []
    for p in range(2):
        total = None
        for place, c in enumerate((p, p + 2)):
            total = add_rows(
                (keeps[c], sent[c]),
                tok,
                1,
                F32,
                wide=(lasts[p],),
                place=place,
                places=2,
                before=total,
            )
        theirs.append(across(total, 1))
    weight_grad = None
    for p in range(2):
        groups = [(keeps[c], sent[c]) for c in (p, p + 2)]
        weight_grad = weight_grad_part(here, groups, lasts[p], theirs[p], weight_grad, p, 2)
    return dq, key_grad, weight_grad


def shards(queries, latent_keys, out_grad, up_weight, segment_ids):
    tok = latent_keys.shape[0]
    heads = queries.shape[1]
    n_ctx, n_head = lax.axis_size("ctx"), lax.axis_size("head")
    here = lax.axis_index("ctx").astype(jnp.int32).reshape(1)
    at_head = lax.axis_index("head").astype(jnp.int32).reshape(1)
    ids = segment_ids.reshape(n_ctx, tok)
    if n_ctx == 8 and heads == 32 and n_head == 4:
        return in_chunks(queries, latent_keys, out_grad, up_weight, here, at_head, ids)
    else:
        prev = from_behind(latent_keys, "ctx", REACH)
        turned = by_head(up_weight, queries, out_grad, 0, heads)
        window = key_window(here, prev, latent_keys, ids, False)
        dq, dkv, rope = attention(window, turned, None, None, 0, heads, 0, heads)
        (both,) = key_terms(at_head, [dkv], [turned[0]], [rope], None)
        share = lax.psum_scatter(
            both.reshape(REACH + 1, tok, LAT + ROPE), "head", scatter_dimension=2, tiled=True
        )
        term = jnp.einsum("ki,ke->ie", window[0], dkv, preferred_element_type=F32)
        rows = lax.psum_scatter(term.astype(BF16), "ctx", scatter_dimension=0, tiled=True)
        weight_grad = rows.astype(F32).reshape(rows.shape[0], heads, PAIR)
    key_grad = share[REACH] + from_behind(share[0], "ctx", 0 - REACH)
    return (dq, key_grad, weight_grad)


def solution(mesh):
    return jax.shard_map(
        shards,
        mesh=mesh,
        in_specs=(
            P("ctx", "head", None),
            P("ctx", None),
            P("ctx", "head", None),
            P(None, "head", None),
            P(),
        ),
        out_specs=(P("ctx", "head", None), P("ctx", "head"), P("ctx", "head", None)),
        check_vma=False,
    )
```

```python
import functools
import math

import jax
import jax.numpy as jnp
from jax import lax
from jax.experimental import pallas as pl
from jax.experimental.pallas import tpu as pltpu
from jax.sharding import PartitionSpec as P

LAT = 512
ROPE = 64
PLAIN_WIDTH = 128
VDIM = 128
REACH = 1
LANES = 128
PAIR = PLAIN_WIDTH + VDIM
STEP_HEADS = 4
BF16 = jnp.bfloat16
F32 = jnp.float32
WIDE = pltpu.CompilerParams(vmem_limit_bytes=56 * 1024 * 1024)
PARAMS = pltpu.CompilerParams(vmem_limit_bytes=20 * 1024 * 1024)


def from_behind(value, axis, steps):
    count = lax.axis_size(axis)
    initial, last = (max(0, -steps), min(count, count - steps))
    return lax.ppermute(value, axis, [(source, source + steps) for source in range(initial, last)])


def across(value, bit):
    count = lax.axis_size("ctx")
    return lax.ppermute(value, "ctx", [(source, source ^ bit) for source in range(count)])


def cost(share):
    return pl.CostEstimate(flops=int(share * 1e9), bytes_accessed=1024, transcendentals=0)


TURN, WINDOW, CHUNK, SHARES, QUERY, SUM = 3.0, 0.5, 1.5, 0.1, 0.1, 0.1


def dot(a, b, a_dim, b_dim):
    return lax.dot_general(a, b, (((a_dim,), (b_dim,)), ((), ())), preferred_element_type=F32)


def by_head_kernel(w_ref, q_ref, g_ref, wt_ref, qt_ref, gt_ref):
    heads = w_ref.shape[1]
    orders = {}

    def order(count):
        if count not in orders:
            size = count * heads
            row = lax.broadcasted_iota(jnp.int32, (size, size), 0)
            col = lax.broadcasted_iota(jnp.int32, (size, size), 1)
            wanted = (row % count) * heads + row // count
            orders[count] = (col == wanted).astype(BF16)
        return orders[count]

    def turn(ref, out_ref):
        rows, _, width = ref.shape
        count = min(rows, 256 // heads)
        for start in range(0, rows, count):
            block = ref[start : start + count].reshape(count * heads, width)
            turned = dot(order(count), block, 1, 0).astype(BF16)
            out_ref[:, start : start + count, :width] = turned.reshape(heads, count, width)

    turn(w_ref, wt_ref)
    qt_ref[...] = jnp.zeros_like(qt_ref)
    turn(q_ref, qt_ref)
    turn(g_ref, gt_ref)


def by_head(up_weight, queries, out_grad, chunk, heads):
    tok = queries.shape[0]
    steps = 4
    depth, rows = LAT // steps, tok // steps
    return pl.pallas_call(
        by_head_kernel,
        grid=(steps,),
        in_specs=[
            pl.BlockSpec((depth, heads, PAIR), lambda i: (i, chunk, 0)),
            pl.BlockSpec((rows, heads, PLAIN_WIDTH + ROPE), lambda i: (i, chunk, 0)),
            pl.BlockSpec((rows, heads, VDIM), lambda i: (i, chunk, 0)),
        ],
        out_specs=[
            pl.BlockSpec((heads, depth, PAIR), lambda i: (0, i, 0)),
            pl.BlockSpec((heads, rows, 2 * LANES), lambda i: (0, i, 0)),
            pl.BlockSpec((heads, rows, VDIM), lambda i: (0, i, 0)),
        ],
        out_shape=[
            jax.ShapeDtypeStruct((heads, LAT, PAIR), BF16),
            jax.ShapeDtypeStruct((heads, tok, 2 * LANES), BF16),
            jax.ShapeDtypeStruct((heads, tok, VDIM), BF16),
        ],
        compiler_params=WIDE,
        cost_estimate=cost(TURN),
        name="by_head",
    )(up_weight, queries, out_grad)


def window_kernel(here_ref, prev_ref, own_ref, ids_ref, *outs, paired):
    win_ref, krope_ref, vis_ref = outs[:3]
    here = here_ref[0]
    tok = prev_ref.shape[0]
    win_ref[:tok, :] = prev_ref[:, :LAT]
    win_ref[tok:, :] = own_ref[:, :LAT]
    krope_ref[...] = jnp.zeros_like(krope_ref)
    krope_ref[:tok, :ROPE] = prev_ref[:, LAT:]
    krope_ref[tok:, :ROPE] = own_ref[:, LAT:]
    behind = jnp.maximum(here - 1, 0)
    seg_prev = jnp.where(here > 0, ids_ref[pl.ds(behind, 1), :], -1)
    seg_own = ids_ref[pl.ds(here, 1), :]
    row = lax.broadcasted_iota(jnp.int32, (tok, tok), 0)
    col = lax.broadcasted_iota(jnp.int32, (tok, tok), 1)
    seg_query = jnp.sum(jnp.where(row == col, seg_own, 0), 1, keepdims=True)
    vis_ref[:, :tok] = (seg_query == seg_prev).astype(F32)
    vis_ref[:, tok:] = ((seg_query == seg_own) & (col <= row)).astype(F32)
    if paired:
        source = lax.broadcasted_iota(jnp.int32, (LAT, LAT), 0)
        column = lax.broadcasted_iota(jnp.int32, (LAT, LAT), 1)
        place = column >> 6
        apart = ((place & 1) << 2) | (place & 2) | (place >> 2)
        wanted = ((here ^ apart) << 6) | (column & 63)
        ordered = dot(win_ref[...], (source == wanted).astype(BF16), 1, 0).astype(BF16)
        outs[3][...] = ordered[:, : LAT // 2]
        outs[4][...] = ordered[:, LAT // 2 :]


def key_window(here, prev, own, ids, paired):
    tok = prev.shape[0]
    whole = lambda i, here: (0, 0)
    shapes = [((2 * tok, LAT), BF16), ((2 * tok, LANES), BF16), ((tok, 2 * tok), F32)]
    if paired:
        shapes = shapes + [((2 * tok, LAT // 2), BF16)] * 2
    return pl.pallas_call(
        functools.partial(window_kernel, paired=paired),
        grid_spec=pltpu.PrefetchScalarGridSpec(
            num_scalar_prefetch=1,
            grid=(1,),
            in_specs=[pl.BlockSpec(array.shape, whole) for array in (prev, own, ids)],
            out_specs=[pl.BlockSpec(shape, whole) for shape, _ in shapes],
        ),
        out_shape=[jax.ShapeDtypeStruct(*shape) for shape in shapes],
        compiler_params=PARAMS,
        cost_estimate=cost(WINDOW),
        name="key_window",
    )(here, prev, own, ids)


def attention_kernel(
    win_ref, krope_ref, vis_ref, wt_ref, qt_ref, gt_ref, *refs, aliased, extra
):
    latents_ref = refs[0] if extra else None
    refs = refs[1:] if extra else refs
    refs = refs[1:] if aliased else refs
    dq_ref, dkv_ref, rope_ref, dqn_ref, dqr_ref = refs
    i = pl.program_id(0)
    tok, heads = dq_ref.shape[:2]
    scale = 1.0 / math.sqrt(PLAIN_WIDTH + ROPE)

    @pl.when(i == 0)
    def _():
        rope_ref[...] = jnp.zeros_like(rope_ref)
        if extra:
            dkv_ref[:, heads * PAIR :] = latents_ref[...]

    visible = vis_ref[...] > 0.0
    window = win_ref[...]
    krope = krope_ref[...]
    count = wt_ref.shape[0]
    keys, values = [], []
    for h in range(count):
        kv = dot(window, wt_ref[h], 1, 0).astype(BF16)
        keys.append(jnp.concatenate([kv[:, :PLAIN_WIDTH], krope], 1))
        values.append(kv[:, PLAIN_WIDTH:])
    scores = [dot(qt_ref[h], keys[h], 1, 1) for h in range(count)]
    dprobs = [dot(gt_ref[h], values[h], 1, 1) for h in range(count)]
    dscores, probs16 = [], []
    for h in range(count):
        logits = jnp.where(visible, scores[h] * scale, -1e30)
        top = jnp.max(logits, -1, keepdims=True)
        expo = jnp.exp(logits - top)
        probs = expo / jnp.sum(expo, -1, keepdims=True)
        delta = jnp.sum(probs * dprobs[h], -1, keepdims=True)
        dscores.append((probs * (dprobs[h] - delta) * scale).astype(BF16))
        probs16.append(probs.astype(BF16))
    parts, rope = [], rope_ref[...]
    for h in range(count):
        dk = dot(dscores[h], qt_ref[h], 0, 0)
        dv = dot(probs16[h], gt_ref[h], 0, 0)
        parts.append(jnp.concatenate([dk[:, :PLAIN_WIDTH], dv], 1).astype(BF16))
        rope = rope + dk[:, PLAIN_WIDTH:]
    rope_ref[...] = rope
    dkv_ref[:, pl.ds(pl.multiple_of(i * (count * PAIR), count * PAIR), count * PAIR)] = (
        jnp.concatenate(parts, 1)
    )
    for h in range(count):
        dq = dot(dscores[h], keys[h], 1, 0)
        dqn_ref[pl.ds(i * count + h, tok, stride=heads), :] = dq[:, :PLAIN_WIDTH]
        dqr_ref[pl.ds(i * count + h, tok, stride=heads), :] = dq[:, PLAIN_WIDTH:]

    @pl.when(i == pl.num_programs(0) - 1)
    def _():
        dq_ref[:, :, :PLAIN_WIDTH] = dqn_ref[...].reshape(tok, heads, LANES)
        dq_ref[:, :, PLAIN_WIDTH:] = dqr_ref[...].reshape(tok, heads, LANES)[:, :, :ROPE]


def attention(window, turned, latents, dq, chunk, heads, first, all_heads):
    weight, queries, out_grad = turned
    tok = queries.shape[1]
    width = 2 * tok
    steps = heads // STEP_HEADS
    at = first // STEP_HEADS
    extra = LAT // 2 if latents is not None else 0
    whole = lambda i: (0, 0)
    head_block = lambda i: (at + i, 0, 0)
    operands = [*window, weight, queries, out_grad]
    in_specs = [pl.BlockSpec(array.shape, whole) for array in window] + [
        pl.BlockSpec((STEP_HEADS, LAT, PAIR), head_block),
        pl.BlockSpec((STEP_HEADS, tok, 2 * LANES), head_block),
        pl.BlockSpec((STEP_HEADS, tok, VDIM), head_block),
    ]
    if latents is not None:
        in_specs.append(pl.BlockSpec(latents.shape, whole))
        operands.append(latents)
    aliases = {}
    if dq is not None:
        aliases = {len(operands): 0}
        in_specs.append(pl.BlockSpec(memory_space=pl.ANY))
        operands.append(dq)
    return pl.pallas_call(
        functools.partial(attention_kernel, aliased=dq is not None, extra=latents is not None),
        grid=(steps,),
        in_specs=in_specs,
        out_specs=[
            pl.BlockSpec((tok, heads, PLAIN_WIDTH + ROPE), lambda i: (0, chunk, 0)),
            pl.BlockSpec((width, heads * PAIR + extra), whole),
            pl.BlockSpec((width, LANES), whole),
        ],
        scratch_shapes=[
            pltpu.VMEM((tok * heads, LANES), F32),
            pltpu.VMEM((tok * heads, LANES), F32),
        ],
        out_shape=[
            jax.ShapeDtypeStruct((tok, all_heads, PLAIN_WIDTH + ROPE), F32),
            jax.ShapeDtypeStruct((width, heads * PAIR + extra), BF16),
            jax.ShapeDtypeStruct((width, LANES), F32),
        ],
        input_output_aliases=aliases,
        compiler_params=WIDE,
        cost_estimate=cost(CHUNK),
        name="attention",
    )(*operands)


def terms_kernel(
    own_ref, other_ref, mine_ref, theirs_ref, keep_ref, send_ref, latents_ref, *, along_x
):
    width = own_ref.shape[0]

    @pl.when(pl.program_id(0) == 0)
    def _():
        latents_ref[:, :width] = mine_ref[...].T
        latents_ref[:, width:] = theirs_ref[...].T

    grads = jnp.concatenate([own_ref[...], other_ref[...]], 0)
    term = dot(latents_ref[...], grads, 1, 0)
    rows = term.shape[0] // 4
    first, second = (1, 2) if along_x else (2, 1)
    keep_ref[:rows] = term[:rows]
    keep_ref[rows:] = term[first * rows : (first + 1) * rows]
    send_ref[:rows] = term[second * rows : (second + 1) * rows].astype(BF16)
    send_ref[rows:] = term[3 * rows :].astype(BF16)


def terms(own, other, mine, theirs, columns, along_x):
    width = own.shape[0]
    block = 1024
    at = theirs.shape[1] // (LAT // 2) - 1
    column_block = lambda i: (0, i)
    return pl.pallas_call(
        functools.partial(terms_kernel, along_x=along_x),
        grid=(columns // block,),
        in_specs=[
            pl.BlockSpec((width, block), column_block),
            pl.BlockSpec((width, block), column_block),
            pl.BlockSpec((width, LAT // 2), lambda i: (0, 0)),
            pl.BlockSpec((width, LAT // 2), lambda i: (0, at)),
        ],
        out_specs=[pl.BlockSpec((LAT // 4, block), column_block)] * 2,
        out_shape=[
            jax.ShapeDtypeStruct((LAT // 4, columns), F32),
            jax.ShapeDtypeStruct((LAT // 4, columns), BF16),
        ],
        scratch_shapes=[pltpu.VMEM((LAT // 2, 2 * width), BF16)],
        compiler_params=PARAMS,
        cost_estimate=cost(CHUNK),
        name="terms",
    )(own, other, mine, theirs)


def key_terms_kernel(*refs, chunks, steps, turns, shares):
    head_ref = refs[0]
    dkv_refs = refs[1 : 1 + chunks]
    wt_refs = refs[1 + chunks : 1 + chunks + turns]
    rope_refs = refs[1 + chunks + turns : 1 + 2 * chunks + turns]
    outs = refs[1 + 2 * chunks + turns : -1]
    total_ref = refs[-1]
    i = pl.program_id(0)

    @pl.when(i == 0)
    def _():
        total_ref[...] = jnp.zeros_like(total_ref)

    for k in range(chunks):

        @pl.when(i // steps == k)
        def _(k=k):
            total = total_ref[...]
            weight_ref = wt_refs[k * turns // chunks]
            for h in range(weight_ref.shape[0]):
                grads = dkv_refs[k][:, h * PAIR : (h + 1) * PAIR]
                total = total + dot(grads, weight_ref[h], 1, 1)
            total_ref[...] = total

    @pl.when(i == pl.num_programs(0) - 1)
    def _():
        rope = rope_refs[0][...]
        for k in range(1, chunks):
            rope = rope + rope_refs[k][...]
        both = jnp.concatenate([total_ref[...], rope], 1)
        if shares is None:
            outs[0][...] = both[:, : LAT + ROPE]
            return
        part = (LAT + ROPE) // shares
        for z in range(shares):
            piece = both[:, z * part : (z + 1) * part]
            for s in range(shares):

                @pl.when(lax.rem(head_ref[0] + s, shares) == z)
                def _(s=s, piece=piece):
                    outs[s][...] = piece


def key_terms(at_head, dkvs, weights, ropes, shares):
    chunks, turns = len(dkvs), len(weights)
    heads = weights[0].shape[0] * turns // chunks
    width = dkvs[0].shape[0]
    steps = heads // STEP_HEADS
    span = steps * chunks // turns
    near = lambda k, many: lambda i, at: jnp.clip(i - k * many, 0, many - 1)
    wide = (LAT + ROPE) // (shares or 1)
    return pl.pallas_call(
        functools.partial(
            key_terms_kernel, chunks=chunks, steps=steps, turns=turns, shares=shares
        ),
        grid_spec=pltpu.PrefetchScalarGridSpec(
            num_scalar_prefetch=1,
            grid=(chunks * steps,),
            in_specs=[
                pl.BlockSpec((width, STEP_HEADS * PAIR), lambda i, at, k=k: (0, near(k, steps)(i, at)))
                for k in range(chunks)
            ]
            + [
                pl.BlockSpec(
                    (STEP_HEADS, LAT, PAIR), lambda i, at, k=k: (near(k, span)(i, at), 0, 0)
                )
                for k in range(turns)
            ]
            + [pl.BlockSpec((width, LANES), lambda i, at: (0, 0))] * chunks,
            out_specs=[pl.BlockSpec((width, wide), lambda i, at: (0, 0))] * (shares or 1),
            scratch_shapes=[pltpu.VMEM((width, LAT), F32)],
        ),
        out_shape=[jax.ShapeDtypeStruct((width, wide), F32)] * (shares or 1),
        compiler_params=WIDE,
        cost_estimate=cost(CHUNK),
        name="key_terms",
    )(at_head, *dkvs, *weights, *ropes)


def weight_sum_kernel(keep_ref, first_ref, second_ref, *refs):
    out_ref, k_ref, v_ref = refs[-3:]
    rows, heads, _ = out_ref.shape
    for h in range(heads):
        columns = slice(h * PAIR, (h + 1) * PAIR)
        total = keep_ref[:, columns] + first_ref[:, columns].astype(F32)
        total = total + second_ref[:, columns].astype(F32)
        k_ref[pl.ds(h, rows, stride=heads), :] = total[:, :LANES]
        v_ref[pl.ds(h, rows, stride=heads), :] = total[:, LANES:]
    out_ref[:, :, :LANES] = k_ref[...].reshape(rows, heads, LANES)
    out_ref[:, :, LANES:] = v_ref[...].reshape(rows, heads, LANES)


def weight_sum(keep, first, second, total, chunk, all_heads):
    rows, columns = second.shape
    heads = columns // PAIR
    block = 32
    operands = [keep, first, second]
    in_specs = [pl.BlockSpec((block, columns), lambda i: (i, 0)) for _ in operands]
    aliases = {}
    if total is not None:
        aliases = {3: 0}
        in_specs.append(pl.BlockSpec(memory_space=pl.ANY))
        operands.append(total)
    return pl.pallas_call(
        weight_sum_kernel,
        grid=(rows // block,),
        in_specs=in_specs,
        out_specs=pl.BlockSpec((block, heads, PAIR), lambda i: (i, chunk, 0)),
        out_shape=jax.ShapeDtypeStruct((rows, all_heads, PAIR), F32),
        scratch_shapes=[pltpu.VMEM((block * heads, LANES), F32)] * 2,
        input_output_aliases=aliases,
        compiler_params=PARAMS,
        cost_estimate=cost(SUM),
        name="weight_sum",
    )(*operands)


def after(values, earlier):
    return lax.optimization_barrier((values, earlier))[0]


def turn_rows(block):
    rows, heads, width = block.shape
    count = min(rows, 256 // heads)
    row = lax.broadcasted_iota(jnp.int32, (count * heads, count * heads), 0)
    col = lax.broadcasted_iota(jnp.int32, (count * heads, count * heads), 1)
    order = (col == (row % count) * heads + row // count).astype(BF16)
    for start in range(0, rows, count):
        part = block[start : start + count].reshape(count * heads, width)
        turned = dot(order, part, 1, 0).astype(BF16)
        yield slice(start, start + count), turned.reshape(heads, count, width)


def in_hbm(array):
    return pltpu.with_memory_space_constraint(array, pltpu.HBM)


def turn_weight_kernel(here_ref, *refs):
    *parts, wt_ref = refs
    depth = parts[0].shape[0]
    for at, w_ref in enumerate(parts):
        for rows, turned in turn_rows(w_ref[...]):
            wt_ref[:, at * depth + rows.start : at * depth + rows.stop, :] = turned


def turn_weight(here, up_weight, heads):
    steps, parts = 4, 8
    depth = LAT // steps // parts
    part = lambda p: lambda i, here: (i * parts + p, here[0] & 1, 0)
    return pl.pallas_call(
        turn_weight_kernel,
        grid_spec=pltpu.PrefetchScalarGridSpec(
            num_scalar_prefetch=1,
            grid=(steps,),
            in_specs=[pl.BlockSpec((depth, heads, PAIR), part(p)) for p in range(parts)],
            out_specs=pl.BlockSpec((heads, depth * parts, PAIR), lambda i, here: (0, i, 0)),
        ),
        out_shape=jax.ShapeDtypeStruct((heads, LAT, PAIR), BF16),
        compiler_params=PARAMS,
        cost_estimate=cost(TURN),
        name="turn_weight",
    )(here, *[in_hbm(up_weight)] * parts)


def turn_tokens_kernel(here_ref, q1_ref, g1_ref, q0_ref, g0_ref, own_ref, give_ref, mine_ref):
    heads = mine_ref.shape[0]
    for q_ref, g_ref, out_ref in ((q1_ref, g1_ref, give_ref), (q0_ref, g0_ref, mine_ref)):
        out_ref[:, :, LANES : 2 * LANES] = jnp.zeros_like(out_ref[:, :, LANES : 2 * LANES])
        for rows, turned in turn_rows(q_ref[...]):
            out_ref[:heads, rows, : PLAIN_WIDTH + ROPE] = turned
        for rows, turned in turn_rows(g_ref[...]):
            out_ref[:heads, rows, 2 * LANES :] = turned
    rest = LAT + ROPE - 3 * LANES
    give_ref[heads] = own_ref[:, : 3 * LANES]
    give_ref[heads + 1] = jnp.zeros_like(give_ref[heads + 1])
    give_ref[heads + 1, :, :rest] = own_ref[:, 3 * LANES :]


def turn_tokens(here, queries, out_grad, latent_keys, heads):
    tok = queries.shape[0]
    q_block, g_block = (tok, heads, PLAIN_WIDTH + ROPE), (tok, heads, VDIM)
    given = lambda i, here: (0, 1 - (here[0] & 1), 0)
    kept = lambda i, here: (0, here[0] & 1, 0)
    whole = lambda i, here: (0, 0, 0)
    give, mine = (heads + 2, tok, 3 * LANES), (heads, tok, 3 * LANES)
    queries, out_grad, latent_keys = (in_hbm(x) for x in (queries, out_grad, latent_keys))
    return pl.pallas_call(
        turn_tokens_kernel,
        grid_spec=pltpu.PrefetchScalarGridSpec(
            num_scalar_prefetch=1,
            grid=(1,),
            in_specs=[
                pl.BlockSpec(q_block, given),
                pl.BlockSpec(g_block, given),
                pl.BlockSpec(q_block, kept),
                pl.BlockSpec(g_block, kept),
                pl.BlockSpec(latent_keys.shape, lambda i, here: (0, 0)),
            ],
            out_specs=[pl.BlockSpec(give, whole), pl.BlockSpec(mine, whole)],
        ),
        out_shape=[jax.ShapeDtypeStruct(give, BF16), jax.ShapeDtypeStruct(mine, BF16)],
        compiler_params=PARAMS,
        cost_estimate=cost(WINDOW),
        name="turn_tokens",
    )(here, queries, out_grad, queries, out_grad, latent_keys)


def chip_window_kernel(
    here_ref, even_ref, odd_ref, own_ref, pal_ref, ids_ref, win_ref, krope_ref, vis_ref, lat_ref
):
    here = here_ref[0]
    tok = own_ref.shape[0]
    core, chip = here & 1, here >> 1
    first = core == 0
    prev = jnp.where(first, even_ref[...].astype(F32), odd_ref[...].astype(F32)).astype(BF16)
    pal = jnp.concatenate([pal_ref[0], pal_ref[1, :, : LAT + ROPE - 3 * LANES]], 1).astype(F32)
    own = own_ref[...].astype(F32)
    low = jnp.where(first, own, pal).astype(BF16)
    high = jnp.where(first, pal, own).astype(BF16)
    krope_ref[...] = jnp.zeros_like(krope_ref)
    for at, block in enumerate((prev, low, high)):
        win_ref[at * tok : (at + 1) * tok, :] = block[:, :LAT]
        krope_ref[at * tok : (at + 1) * tok, :ROPE] = block[:, LAT:]
    behind = ids_ref[pl.ds(jnp.maximum(chip - 1, 0), 1), :]
    both = ids_ref[pl.ds(chip, 1), :]
    seg = [jnp.where(chip > 0, behind[:, tok:], -1), both[:, :tok], both[:, tok:]]
    row = lax.broadcasted_iota(jnp.int32, (tok, tok), 0)
    col = lax.broadcasted_iota(jnp.int32, (tok, tok), 1)
    for b in range(2):
        seg_query = jnp.sum(jnp.where(row == col, seg[b + 1], 0), 1, keepdims=True)
        vis_ref[b, :, :tok] = (seg_query == seg[b]).astype(F32)
        vis_ref[b, :, tok:] = ((seg_query == seg[b + 1]) & (col <= row)).astype(F32)
    column = lax.broadcasted_iota(jnp.int32, (LAT, LAT), 0)
    source = lax.broadcasted_iota(jnp.int32, (LAT, LAT), 1)
    place = column >> 6
    apart = ((place & 2) << 1) | ((place & 4) >> 1) | (place & 1)
    wanted = ((here ^ apart) << 6) | (column & 63)
    order = (source == wanted).astype(BF16)
    lat_ref[...] = dot(order, win_ref[...], 1, 1).astype(BF16)


def chip_window(here, even, odd, own, got, ids):
    tok = own.shape[0]
    whole = lambda i, here: (0, 0)
    return pl.pallas_call(
        chip_window_kernel,
        grid_spec=pltpu.PrefetchScalarGridSpec(
            num_scalar_prefetch=1,
            grid=(1,),
            in_specs=[pl.BlockSpec(array.shape, whole) for array in (even, odd, own)]
            + [
                pl.BlockSpec((2,) + got.shape[1:], lambda i, here: (got.shape[0] // 2 - 1, 0, 0)),
                pl.BlockSpec(ids.shape, whole),
            ],
            out_specs=[
                pl.BlockSpec((3 * tok, LAT), whole),
                pl.BlockSpec((3 * tok, LANES), whole),
                pl.BlockSpec((2, tok, 2 * tok), lambda i, here: (0, 0, 0)),
                pl.BlockSpec((LAT, 3 * tok), whole),
            ],
        ),
        out_shape=[
            jax.ShapeDtypeStruct((3 * tok, LAT), BF16),
            jax.ShapeDtypeStruct((3 * tok, LANES), BF16),
            jax.ShapeDtypeStruct((2, tok, 2 * tok), F32),
            jax.ShapeDtypeStruct((LAT, 3 * tok), BF16),
        ],
        compiler_params=PARAMS,
        cost_estimate=cost(WINDOW),
        name="chip_window",
    )(here, even, odd, own, got, ids)


def chunk_kernel(
    here_ref,
    win_ref,
    krope_ref,
    vis_ref,
    lat_ref,
    wt_ref,
    mine_ref,
    got_ref,
    *refs,
    chained,
    along_x,
):
    before_ref = refs[0] if chained else None
    refs = refs[3:] if chained else refs
    keep_ref, send_ref, key_ref, dq_ref, back_ref = refs

    @pl.when(pl.program_id(0) == 0)
    def _():
        key_ref[...] = before_ref[...] if chained else jnp.zeros_like(key_ref)

    tok = vis_ref.shape[1]
    heads = wt_ref.shape[0]
    first = (here_ref[0] & 1) == 0
    scale = 1.0 / math.sqrt(PLAIN_WIDTH + ROPE)
    window, krope = win_ref[...], krope_ref[...]
    visible = [vis_ref[b] > 0.0 for b in range(2)]
    keys, values, queries, grads = [], [], [], []
    for h in range(heads):
        kv = dot(window, wt_ref[h], 1, 0).astype(BF16)
        keys.append(jnp.concatenate([kv[:, :PLAIN_WIDTH], krope], 1))
        values.append(kv[:, PLAIN_WIDTH:])
        mine, got = mine_ref[h], got_ref[h]
        ordered = (jnp.where(first, mine, got), jnp.where(first, got, mine))
        queries.append([block[:, : 2 * LANES] for block in ordered])
        grads.append([block[:, 2 * LANES :] for block in ordered])
    reach = [slice(b * tok, (b + 2) * tok) for b in range(2)]
    units = [(h, b) for h in range(heads) for b in range(2)]
    scores = {(h, b): dot(queries[h][b], keys[h][reach[b]], 1, 1) for h, b in units}
    dprobs = {(h, b): dot(grads[h][b], values[h][reach[b]], 1, 1) for h, b in units}
    dscores, probs16 = {}, {}
    for unit in units:
        logits = jnp.where(visible[unit[1]], scores[unit] * scale, -1e30)
        top = jnp.max(logits, -1, keepdims=True)
        expo = jnp.exp(logits - top)
        probs = expo / jnp.sum(expo, -1, keepdims=True)
        delta = jnp.sum(probs * dprobs[unit], -1, keepdims=True)
        dscores[unit] = (probs * (dprobs[unit] - delta) * scale).astype(BF16)
        probs16[unit] = probs.astype(BF16)

    def fold(low, high):
        return jnp.concatenate([low[:tok], low[tok:] + high[:tok], high[tok:]], 0)

    parts, rope = [], None
    for h in range(heads):
        dk = fold(*[dot(dscores[h, b], queries[h][b], 0, 0) for b in range(2)])
        dv = fold(*[dot(probs16[h, b], grads[h][b], 0, 0) for b in range(2)])
        parts.append(jnp.concatenate([dk[:, :PLAIN_WIDTH], dv], 1).astype(BF16))
        rope = dk[:, PLAIN_WIDTH:] if rope is None else rope + dk[:, PLAIN_WIDTH:]
    dkv = jnp.concatenate(parts, 1)
    rows = lat_ref.shape[0] // 4
    kept = (0, 1) if along_x else (0, 2)
    sent = (2, 3) if along_x else (1, 3)
    for at, g in enumerate(sent):
        term = dot(lat_ref[g * rows : (g + 1) * rows, :], dkv, 1, 0)
        send_ref[at * rows : (at + 1) * rows, :] = term.astype(BF16)
    for at, g in enumerate(kept):
        keep_ref[at * rows : (at + 1) * rows, :] = dot(
            lat_ref[g * rows : (g + 1) * rows, :], dkv, 1, 0
        )
    total = key_ref[:, :LAT]
    for h in range(heads):
        total = total + dot(parts[h], wt_ref[h], 1, 1)
    key_ref[:, :LAT] = total
    key_ref[:, LAT:] = key_ref[:, LAT:] + rope
    for h in range(heads):
        low, high = (dot(dscores[h, b], keys[h][reach[b]], 1, 0) for b in range(2))
        dq_ref[h] = jnp.where(first, low, high)
        back_ref[h] = jnp.where(first, high, low)


def chunk(here, window, weight, mine, got, before, index, heads, along_x):
    tok = mine.shape[1]
    whole = lambda i, here: (0, 0)
    whole3 = lambda i, here: (0, 0, 0)
    step = min(heads, STEP_HEADS)
    steps = heads // step
    at = lambda i, here: (index * steps + i, 0, 0)
    across_columns = lambda i, here: (0, i)
    columns = heads * PAIR
    operands = [*window, weight, mine, got]
    in_specs = [
        pl.BlockSpec(array.shape, whole3 if array.ndim == 3 else whole) for array in window
    ] + [
        pl.BlockSpec((step, LAT, PAIR), at),
        pl.BlockSpec((step, tok, 3 * LANES), at),
        pl.BlockSpec((step, tok, 3 * LANES), at),
    ]
    aliases = {}
    if before is not None:
        key, dq, back = before
        aliases = {len(operands) + 2: 3, len(operands) + 3: 4}
        in_specs = in_specs + [
            pl.BlockSpec(key.shape, whole),
            pl.BlockSpec(memory_space=pl.ANY),
            pl.BlockSpec(memory_space=pl.ANY),
        ]
        operands = operands + [key, dq, back]
    turned = (weight.shape[0], tok, 2 * LANES)
    return pl.pallas_call(
        functools.partial(chunk_kernel, chained=before is not None, along_x=along_x),
        grid_spec=pltpu.PrefetchScalarGridSpec(
            num_scalar_prefetch=1,
            grid=(steps,),
            in_specs=in_specs,
            out_specs=[
                pl.BlockSpec((LAT // 2, step * PAIR), across_columns),
                pl.BlockSpec((LAT // 2, step * PAIR), across_columns),
                pl.BlockSpec((3 * tok, LAT + LANES), whole),
                pl.BlockSpec((step, tok, 2 * LANES), at),
                pl.BlockSpec((step, tok, 2 * LANES), at),
            ],
        ),
        out_shape=[
            jax.ShapeDtypeStruct((LAT // 2, columns), F32),
            jax.ShapeDtypeStruct((LAT // 2, columns), BF16),
            jax.ShapeDtypeStruct((3 * tok, LAT + LANES), F32),
            jax.ShapeDtypeStruct(turned, F32),
            jax.ShapeDtypeStruct(turned, F32),
        ],
        input_output_aliases=aliases,
        compiler_params=PARAMS,
        cost_estimate=cost(CHUNK),
        name="chunk",
    )(here, *operands)


def add_rows_kernel(*refs, count, wide):
    total = refs[0][...].astype(F32)
    for ref in refs[1 : count + wide]:
        total = total + ref[...].astype(F32)
    refs[-1][...] = total.astype(refs[-1].dtype)


def add_rows(arrays, rows, index, dtype, wide=(), place=0, places=1, before=None):
    columns = arrays[0].shape[1]
    operands = [*arrays, *wide]
    in_specs = [pl.BlockSpec((rows, columns), lambda i: (index, 0)) for _ in arrays]
    in_specs = in_specs + [pl.BlockSpec((rows, columns), lambda i: (index, place)) for _ in wide]
    aliases = {}
    if before is not None:
        aliases = {len(operands): 0}
        in_specs.append(pl.BlockSpec(memory_space=pl.ANY))
        operands.append(before)
    return pl.pallas_call(
        functools.partial(add_rows_kernel, count=len(arrays), wide=len(wide)),
        grid=(1,),
        in_specs=in_specs,
        out_specs=pl.BlockSpec((rows, columns), lambda i: (0, place)),
        out_shape=jax.ShapeDtypeStruct((rows, places * columns), dtype),
        input_output_aliases=aliases,
        compiler_params=PARAMS,
        cost_estimate=cost(SHARES),
        name="add_rows",
    )(*operands)


def key_split_kernel(here_ref, key_ref, keep_ref, give_ref):
    tok = keep_ref.shape[0] // 2
    first = (here_ref[0] & 1) == 0
    behind, low, high = (key_ref[b * tok : (b + 1) * tok, :] for b in range(3))
    keep_ref[:tok] = jnp.where(first, low, high)
    keep_ref[tok:] = behind
    give_ref[:tok] = jnp.where(first, high, low)
    give_ref[tok:] = behind


def key_split(here, key):
    rows = key.shape[0] // 3 * 2
    whole = lambda i, here: (0, 0)
    return pl.pallas_call(
        key_split_kernel,
        grid_spec=pltpu.PrefetchScalarGridSpec(
            num_scalar_prefetch=1,
            grid=(1,),
            in_specs=[pl.BlockSpec(key.shape, whole)],
            out_specs=[pl.BlockSpec((rows, key.shape[1]), whole)] * 2,
        ),
        out_shape=[jax.ShapeDtypeStruct((rows, key.shape[1]), F32)] * 2,
        compiler_params=PARAMS,
        cost_estimate=cost(SHARES),
        name="key_split",
    )(here, key)


def key_shares_kernel(at_ref, keep_ref, got_ref, *outs):
    shares = len(outs)
    part = (LAT + ROPE) // shares
    total = keep_ref[...] + got_ref[...]
    for z in range(shares):
        piece = total[:, z * part : (z + 1) * part]
        for s in range(shares):

            @pl.when(lax.rem(at_ref[0] + s, shares) == z)
            def _(s=s, piece=piece):
                outs[s][...] = piece.astype(outs[s].dtype)


def key_shares(at_head, keep, got, shares):
    part = (LAT + ROPE) // shares
    rows = keep.shape[0]
    whole = lambda i, at: (0, 0)
    types = [F32] + [BF16] * (shares - 1)
    return pl.pallas_call(
        key_shares_kernel,
        grid_spec=pltpu.PrefetchScalarGridSpec(
            num_scalar_prefetch=1,
            grid=(1,),
            in_specs=[pl.BlockSpec(keep.shape, whole)] * 2,
            out_specs=[pl.BlockSpec((rows, part), whole)] * shares,
        ),
        out_shape=[jax.ShapeDtypeStruct((rows, part), kind) for kind in types],
        compiler_params=PARAMS,
        cost_estimate=cost(SHARES),
        name="key_shares",
    )(at_head, keep, got)


def query_grad_kernel(here_ref, mine_ref, got_ref, out_ref, n_ref, r_ref):
    tok, heads, _ = out_ref.shape

    def put(src_ref):
        for h in range(heads):
            n_ref[pl.ds(h, tok, stride=heads), :] = src_ref[h, :, :PLAIN_WIDTH]
            r_ref[pl.ds(h, tok, stride=heads), :] = src_ref[h, :, PLAIN_WIDTH:]

    pl.when(pl.program_id(0) == 0)(lambda: put(mine_ref))
    pl.when(pl.program_id(0) == 1)(lambda: put(got_ref))
    out_ref[:, :, :PLAIN_WIDTH] = n_ref[...].reshape(tok, heads, LANES)
    out_ref[:, :, PLAIN_WIDTH:] = r_ref[...].reshape(tok, heads, LANES)[:, :, :ROPE]


def query_grad(here, mine, got):
    heads, tok, _ = mine.shape
    whole = lambda i, here: (0, 0, 0)
    return pl.pallas_call(
        query_grad_kernel,
        grid_spec=pltpu.PrefetchScalarGridSpec(
            num_scalar_prefetch=1,
            grid=(2,),
            in_specs=[pl.BlockSpec(mine.shape, whole)] * 2,
            out_specs=pl.BlockSpec(
                (tok, heads, PLAIN_WIDTH + ROPE), lambda i, here: (0, (here[0] & 1) ^ i, 0)
            ),
            scratch_shapes=[pltpu.VMEM((tok * heads, LANES), F32)] * 2,
        ),
        out_shape=jax.ShapeDtypeStruct((tok, 2 * heads, PLAIN_WIDTH + ROPE), F32),
        compiler_params=PARAMS,
        cost_estimate=cost(QUERY),
        name="query_grad",
    )(here, mine, got)


def weight_grad_kernel(here_ref, *refs, count):
    narrow, last_ref, got_ref = refs[: 2 * count], refs[2 * count], refs[2 * count + 1]
    out_ref, k_ref, v_ref = refs[-3:]
    rows, heads, _ = out_ref.shape
    each = heads // count

    def put(c, total):
        for h in range(each):
            at = pl.ds(c * each + h, rows, stride=heads)
            k_ref[at, :] = total[:, h * PAIR : h * PAIR + LANES]
            v_ref[at, :] = total[:, h * PAIR + LANES : (h + 1) * PAIR]

    for c in range(count):
        columns = slice(c * each * PAIR, (c + 1) * each * PAIR)

        @pl.when(pl.program_id(0) == 0)
        def _(c=c, columns=columns):
            keep_ref, first_ref = narrow[2 * c : 2 * c + 2]
            total = keep_ref[...] + first_ref[...].astype(F32)
            put(c, total + last_ref[:, columns].astype(F32))

        @pl.when(pl.program_id(0) == 1)
        def _(c=c, columns=columns):
            put(c, got_ref[:, columns])

    out_ref[:, :, :LANES] = k_ref[...].reshape(rows, heads, LANES)
    out_ref[:, :, LANES:] = v_ref[...].reshape(rows, heads, LANES)


def weight_grad_part(here, groups, last, got, total, part, parts):
    count = len(groups)
    rows, columns = got.shape
    heads = columns // PAIR
    operands = [array for group in groups for array in group] + [last, got]
    whole = lambda i, here: (0, 0)
    in_specs = [pl.BlockSpec((rows, columns // count), whole)] * (2 * count)
    in_specs = in_specs + [pl.BlockSpec((rows, columns), whole)] * 2
    aliases = {}
    if total is not None:
        aliases = {1 + len(operands): 0}
        in_specs.append(pl.BlockSpec(memory_space=pl.ANY))
        operands.append(total)
    return pl.pallas_call(
        functools.partial(weight_grad_kernel, count=count),
        grid_spec=pltpu.PrefetchScalarGridSpec(
            num_scalar_prefetch=1,
            grid=(2,),
            in_specs=in_specs,
            out_specs=pl.BlockSpec(
                (rows, heads, PAIR), lambda i, here: (0, ((here[0] & 1) ^ i) * parts + part, 0)
            ),
            scratch_shapes=[pltpu.VMEM((rows * heads, LANES), F32)] * 2,
        ),
        out_shape=jax.ShapeDtypeStruct((rows, 2 * parts * heads, PAIR), F32),
        input_output_aliases=aliases,
        compiler_params=PARAMS,
        cost_estimate=cost(SUM),
        name="weight_grad",
    )(here, *operands)


def in_chunks(queries, latent_keys, out_grad, up_weight, here, at_head, ids):
    tok = latent_keys.shape[0]
    n_ctx, n_head = lax.axis_size("ctx"), lax.axis_size("head")
    heads, each = 16, 4
    queries = after(queries, ids)
    give, mine = turn_tokens(here, queries, out_grad, latent_keys, heads)
    odd_devices = range(1, n_ctx - 1, 2)
    even = lax.ppermute(latent_keys, "ctx", [(source, source + 1) for source in odd_devices])
    odd = lax.ppermute(latent_keys, "ctx", [(source, source + 2) for source in odd_devices])
    got = across(give, 1)
    weight = turn_weight(here, up_weight, heads)
    window = chip_window(here, even, odd, latent_keys, got, ids)
    ways, blocks = ((2, 4), (4, 2)), (0, 2, 1, 3)
    before, keeps, sent = None, [], []
    for c, block in enumerate(blocks):
        keep, out, *before = chunk(
            here, window, weight, mine, got, before, block, each, c % 2 == 0
        )
        keeps.append(keep)
        sent.append(across(out, ways[c % 2][0]))
    key, dq, back = before

    def rest(c, earlier):
        return add_rows(
            (keeps[c], sent[c]), 2 * tok, 1, BF16, place=c // 2, places=2, before=earlier
        )

    key_keep, key_give = key_split(here, key)
    key_got = across(key_give, 1)
    rests = [rest(0, None), rest(1, None)]
    key_got = after(key_got, rests)
    shares = key_shares(at_head, key_keep, key_got, n_head)
    pieces = [
        lax.ppermute(shares[s], "head", [(z, (z + s) % n_head) for z in range(n_head)])
        for s in range(1, n_head)
    ]
    dq = query_grad(here, dq, across(after(back, key_keep), 1))
    share = add_rows((shares[0], *pieces), 2 * tok, 0, F32)
    keeps[2] = after(keeps[2], share)
    behind = lax.ppermute(
        share[tok:], "ctx", [(source, source - 1) for source in range(2, n_ctx, 2)]
    )
    key_grad = add_rows((share, behind), tok, 0, F32)
    keeps[3] = after(keeps[3], key_grad)
    rests = [rest(2, rests[0]), rest(3, rests[1])]
    lasts = [across(rests[p], ways[p][1]) for p in range(2)]
    keeps[0] = after(keeps[0], dq)
    theirs = []
    for p in range(2):
        total = None
        for place, c in enumerate((p, p + 2)):
            total = add_rows(
                (keeps[c], sent[c]),
                tok,
                1,
                F32,
                wide=(lasts[p],),
                place=place,
                places=2,
                before=total,
            )
        theirs.append(across(total, 1))
    weight_grad = None
    for p in range(2):
        groups = [(keeps[c], sent[c]) for c in (p, p + 2)]
        weight_grad = weight_grad_part(here, groups, lasts[p], theirs[p], weight_grad, p, 2)
    return dq, key_grad, weight_grad


def shards(queries, latent_keys, out_grad, up_weight, segment_ids):
    tok = latent_keys.shape[0]
    heads = queries.shape[1]
    n_ctx, n_head = lax.axis_size("ctx"), lax.axis_size("head")
    here = lax.axis_index("ctx").astype(jnp.int32).reshape(1)
    at_head = lax.axis_index("head").astype(jnp.int32).reshape(1)
    if n_ctx == 8 and heads == 32 and n_head == 4:
        ids = segment_ids.reshape(n_ctx // 2, 2 * tok)
        return in_chunks(queries, latent_keys, out_grad, up_weight, here, at_head, ids)
    else:
        ids = segment_ids.reshape(n_ctx, tok)
        prev = from_behind(latent_keys, "ctx", REACH)
        turned = by_head(up_weight, queries, out_grad, 0, heads)
        window = key_window(here, prev, latent_keys, ids, False)
        dq, dkv, rope = attention(window, turned, None, None, 0, heads, 0, heads)
        (both,) = key_terms(at_head, [dkv], [turned[0]], [rope], None)
        share = lax.psum_scatter(
            both.reshape(REACH + 1, tok, LAT + ROPE), "head", scatter_dimension=2, tiled=True
        )
        term = jnp.einsum("ki,ke->ie", window[0], dkv, preferred_element_type=F32)
        rows = lax.psum_scatter(term.astype(BF16), "ctx", scatter_dimension=0, tiled=True)
        weight_grad = rows.astype(F32).reshape(rows.shape[0], heads, PAIR)
    key_grad = share[REACH] + from_behind(share[0], "ctx", 0 - REACH)
    return (dq, key_grad, weight_grad)


def solution(mesh):
    return jax.shard_map(
        shards,
        mesh=mesh,
        in_specs=(
            P("ctx", "head", None),
            P("ctx", None),
            P("ctx", "head", None),
            P(None, "head", None),
            P(),
        ),
        out_specs=(P("ctx", "head", None), P("ctx", "head"), P("ctx", "head", None)),
        check_vma=False,
    )
```

```python
import functools
import math

import jax
import jax.numpy as jnp
from jax import lax
from jax.experimental import pallas as pl
from jax.experimental.pallas import tpu as pltpu
from jax.sharding import PartitionSpec as P

LAT = 512
ROPE = 64
PLAIN_WIDTH = 128
VDIM = 128
REACH = 1
LANES = 128
PAIR = PLAIN_WIDTH + VDIM
STEP_HEADS = 4
BF16 = jnp.bfloat16
F32 = jnp.float32
WIDE = pltpu.CompilerParams(vmem_limit_bytes=56 * 1024 * 1024)
PARAMS = pltpu.CompilerParams(vmem_limit_bytes=20 * 1024 * 1024)


def from_behind(value, axis, steps):
    count = lax.axis_size(axis)
    initial, last = (max(0, -steps), min(count, count - steps))
    return lax.ppermute(value, axis, [(source, source + steps) for source in range(initial, last)])


def across(value, bit):
    count = lax.axis_size("ctx")
    return lax.ppermute(value, "ctx", [(source, source ^ bit) for source in range(count)])


def cost(share):
    return pl.CostEstimate(flops=int(share * 1e9), bytes_accessed=1024, transcendentals=0)


TURN, WINDOW, CHUNK, SHARES, QUERY, SUM = 3.0, 0.5, 1.5, 0.1, 0.1, 0.1


def dot(a, b, a_dim, b_dim):
    return lax.dot_general(a, b, (((a_dim,), (b_dim,)), ((), ())), preferred_element_type=F32)


def by_head_kernel(w_ref, q_ref, g_ref, wt_ref, qt_ref, gt_ref):
    heads = w_ref.shape[1]
    orders = {}

    def order(count):
        if count not in orders:
            size = count * heads
            row = lax.broadcasted_iota(jnp.int32, (size, size), 0)
            col = lax.broadcasted_iota(jnp.int32, (size, size), 1)
            wanted = (row % count) * heads + row // count
            orders[count] = (col == wanted).astype(BF16)
        return orders[count]

    def turn(ref, out_ref):
        rows, _, width = ref.shape
        count = min(rows, 256 // heads)
        for start in range(0, rows, count):
            block = ref[start : start + count].reshape(count * heads, width)
            turned = dot(order(count), block, 1, 0).astype(BF16)
            out_ref[:, start : start + count, :width] = turned.reshape(heads, count, width)

    turn(w_ref, wt_ref)
    qt_ref[...] = jnp.zeros_like(qt_ref)
    turn(q_ref, qt_ref)
    turn(g_ref, gt_ref)


def by_head(up_weight, queries, out_grad, chunk, heads):
    tok = queries.shape[0]
    steps = 4
    depth, rows = LAT // steps, tok // steps
    return pl.pallas_call(
        by_head_kernel,
        grid=(steps,),
        in_specs=[
            pl.BlockSpec((depth, heads, PAIR), lambda i: (i, chunk, 0)),
            pl.BlockSpec((rows, heads, PLAIN_WIDTH + ROPE), lambda i: (i, chunk, 0)),
            pl.BlockSpec((rows, heads, VDIM), lambda i: (i, chunk, 0)),
        ],
        out_specs=[
            pl.BlockSpec((heads, depth, PAIR), lambda i: (0, i, 0)),
            pl.BlockSpec((heads, rows, 2 * LANES), lambda i: (0, i, 0)),
            pl.BlockSpec((heads, rows, VDIM), lambda i: (0, i, 0)),
        ],
        out_shape=[
            jax.ShapeDtypeStruct((heads, LAT, PAIR), BF16),
            jax.ShapeDtypeStruct((heads, tok, 2 * LANES), BF16),
            jax.ShapeDtypeStruct((heads, tok, VDIM), BF16),
        ],
        compiler_params=WIDE,
        cost_estimate=cost(TURN),
        name="by_head",
    )(up_weight, queries, out_grad)


def window_kernel(here_ref, prev_ref, own_ref, ids_ref, *outs, paired):
    win_ref, krope_ref, vis_ref = outs[:3]
    here = here_ref[0]
    tok = prev_ref.shape[0]
    win_ref[:tok, :] = prev_ref[:, :LAT]
    win_ref[tok:, :] = own_ref[:, :LAT]
    krope_ref[...] = jnp.zeros_like(krope_ref)
    krope_ref[:tok, :ROPE] = prev_ref[:, LAT:]
    krope_ref[tok:, :ROPE] = own_ref[:, LAT:]
    behind = jnp.maximum(here - 1, 0)
    seg_prev = jnp.where(here > 0, ids_ref[pl.ds(behind, 1), :], -1)
    seg_own = ids_ref[pl.ds(here, 1), :]
    row = lax.broadcasted_iota(jnp.int32, (tok, tok), 0)
    col = lax.broadcasted_iota(jnp.int32, (tok, tok), 1)
    seg_query = jnp.sum(jnp.where(row == col, seg_own, 0), 1, keepdims=True)
    vis_ref[:, :tok] = (seg_query == seg_prev).astype(F32)
    vis_ref[:, tok:] = ((seg_query == seg_own) & (col <= row)).astype(F32)
    if paired:
        source = lax.broadcasted_iota(jnp.int32, (LAT, LAT), 0)
        column = lax.broadcasted_iota(jnp.int32, (LAT, LAT), 1)
        place = column >> 6
        apart = ((place & 1) << 2) | (place & 2) | (place >> 2)
        wanted = ((here ^ apart) << 6) | (column & 63)
        ordered = dot(win_ref[...], (source == wanted).astype(BF16), 1, 0).astype(BF16)
        outs[3][...] = ordered[:, : LAT // 2]
        outs[4][...] = ordered[:, LAT // 2 :]


def key_window(here, prev, own, ids, paired):
    tok = prev.shape[0]
    whole = lambda i, here: (0, 0)
    shapes = [((2 * tok, LAT), BF16), ((2 * tok, LANES), BF16), ((tok, 2 * tok), F32)]
    if paired:
        shapes = shapes + [((2 * tok, LAT // 2), BF16)] * 2
    return pl.pallas_call(
        functools.partial(window_kernel, paired=paired),
        grid_spec=pltpu.PrefetchScalarGridSpec(
            num_scalar_prefetch=1,
            grid=(1,),
            in_specs=[pl.BlockSpec(array.shape, whole) for array in (prev, own, ids)],
            out_specs=[pl.BlockSpec(shape, whole) for shape, _ in shapes],
        ),
        out_shape=[jax.ShapeDtypeStruct(*shape) for shape in shapes],
        compiler_params=PARAMS,
        cost_estimate=cost(WINDOW),
        name="key_window",
    )(here, prev, own, ids)


def attention_kernel(
    win_ref, krope_ref, vis_ref, wt_ref, qt_ref, gt_ref, *refs, aliased, extra
):
    latents_ref = refs[0] if extra else None
    refs = refs[1:] if extra else refs
    refs = refs[1:] if aliased else refs
    dq_ref, dkv_ref, rope_ref, dqn_ref, dqr_ref = refs
    i = pl.program_id(0)
    tok, heads = dq_ref.shape[:2]
    scale = 1.0 / math.sqrt(PLAIN_WIDTH + ROPE)

    @pl.when(i == 0)
    def _():
        rope_ref[...] = jnp.zeros_like(rope_ref)
        if extra:
            dkv_ref[:, heads * PAIR :] = latents_ref[...]

    visible = vis_ref[...] > 0.0
    window = win_ref[...]
    krope = krope_ref[...]
    count = wt_ref.shape[0]
    keys, values = [], []
    for h in range(count):
        kv = dot(window, wt_ref[h], 1, 0).astype(BF16)
        keys.append(jnp.concatenate([kv[:, :PLAIN_WIDTH], krope], 1))
        values.append(kv[:, PLAIN_WIDTH:])
    scores = [dot(qt_ref[h], keys[h], 1, 1) for h in range(count)]
    dprobs = [dot(gt_ref[h], values[h], 1, 1) for h in range(count)]
    dscores, probs16 = [], []
    for h in range(count):
        logits = jnp.where(visible, scores[h] * scale, -1e30)
        top = jnp.max(logits, -1, keepdims=True)
        expo = jnp.exp(logits - top)
        probs = expo / jnp.sum(expo, -1, keepdims=True)
        delta = jnp.sum(probs * dprobs[h], -1, keepdims=True)
        dscores.append((probs * (dprobs[h] - delta) * scale).astype(BF16))
        probs16.append(probs.astype(BF16))
    parts, rope = [], rope_ref[...]
    for h in range(count):
        dk = dot(dscores[h], qt_ref[h], 0, 0)
        dv = dot(probs16[h], gt_ref[h], 0, 0)
        parts.append(jnp.concatenate([dk[:, :PLAIN_WIDTH], dv], 1).astype(BF16))
        rope = rope + dk[:, PLAIN_WIDTH:]
    rope_ref[...] = rope
    dkv_ref[:, pl.ds(pl.multiple_of(i * (count * PAIR), count * PAIR), count * PAIR)] = (
        jnp.concatenate(parts, 1)
    )
    for h in range(count):
        dq = dot(dscores[h], keys[h], 1, 0)
        dqn_ref[pl.ds(i * count + h, tok, stride=heads), :] = dq[:, :PLAIN_WIDTH]
        dqr_ref[pl.ds(i * count + h, tok, stride=heads), :] = dq[:, PLAIN_WIDTH:]

    @pl.when(i == pl.num_programs(0) - 1)
    def _():
        dq_ref[:, :, :PLAIN_WIDTH] = dqn_ref[...].reshape(tok, heads, LANES)
        dq_ref[:, :, PLAIN_WIDTH:] = dqr_ref[...].reshape(tok, heads, LANES)[:, :, :ROPE]


def attention(window, turned, latents, dq, chunk, heads, first, all_heads):
    weight, queries, out_grad = turned
    tok = queries.shape[1]
    width = 2 * tok
    steps = heads // STEP_HEADS
    at = first // STEP_HEADS
    extra = LAT // 2 if latents is not None else 0
    whole = lambda i: (0, 0)
    head_block = lambda i: (at + i, 0, 0)
    operands = [*window, weight, queries, out_grad]
    in_specs = [pl.BlockSpec(array.shape, whole) for array in window] + [
        pl.BlockSpec((STEP_HEADS, LAT, PAIR), head_block),
        pl.BlockSpec((STEP_HEADS, tok, 2 * LANES), head_block),
        pl.BlockSpec((STEP_HEADS, tok, VDIM), head_block),
    ]
    if latents is not None:
        in_specs.append(pl.BlockSpec(latents.shape, whole))
        operands.append(latents)
    aliases = {}
    if dq is not None:
        aliases = {len(operands): 0}
        in_specs.append(pl.BlockSpec(memory_space=pl.ANY))
        operands.append(dq)
    return pl.pallas_call(
        functools.partial(attention_kernel, aliased=dq is not None, extra=latents is not None),
        grid=(steps,),
        in_specs=in_specs,
        out_specs=[
            pl.BlockSpec((tok, heads, PLAIN_WIDTH + ROPE), lambda i: (0, chunk, 0)),
            pl.BlockSpec((width, heads * PAIR + extra), whole),
            pl.BlockSpec((width, LANES), whole),
        ],
        scratch_shapes=[
            pltpu.VMEM((tok * heads, LANES), F32),
            pltpu.VMEM((tok * heads, LANES), F32),
        ],
        out_shape=[
            jax.ShapeDtypeStruct((tok, all_heads, PLAIN_WIDTH + ROPE), F32),
            jax.ShapeDtypeStruct((width, heads * PAIR + extra), BF16),
            jax.ShapeDtypeStruct((width, LANES), F32),
        ],
        input_output_aliases=aliases,
        compiler_params=WIDE,
        cost_estimate=cost(CHUNK),
        name="attention",
    )(*operands)


def terms_kernel(
    own_ref, other_ref, mine_ref, theirs_ref, keep_ref, send_ref, latents_ref, *, along_x
):
    width = own_ref.shape[0]

    @pl.when(pl.program_id(0) == 0)
    def _():
        latents_ref[:, :width] = mine_ref[...].T
        latents_ref[:, width:] = theirs_ref[...].T

    grads = jnp.concatenate([own_ref[...], other_ref[...]], 0)
    term = dot(latents_ref[...], grads, 1, 0)
    rows = term.shape[0] // 4
    first, second = (1, 2) if along_x else (2, 1)
    keep_ref[:rows] = term[:rows]
    keep_ref[rows:] = term[first * rows : (first + 1) * rows]
    send_ref[:rows] = term[second * rows : (second + 1) * rows].astype(BF16)
    send_ref[rows:] = term[3 * rows :].astype(BF16)


def terms(own, other, mine, theirs, columns, along_x):
    width = own.shape[0]
    block = 1024
    at = theirs.shape[1] // (LAT // 2) - 1
    column_block = lambda i: (0, i)
    return pl.pallas_call(
        functools.partial(terms_kernel, along_x=along_x),
        grid=(columns // block,),
        in_specs=[
            pl.BlockSpec((width, block), column_block),
            pl.BlockSpec((width, block), column_block),
            pl.BlockSpec((width, LAT // 2), lambda i: (0, 0)),
            pl.BlockSpec((width, LAT // 2), lambda i: (0, at)),
        ],
        out_specs=[pl.BlockSpec((LAT // 4, block), column_block)] * 2,
        out_shape=[
            jax.ShapeDtypeStruct((LAT // 4, columns), F32),
            jax.ShapeDtypeStruct((LAT // 4, columns), BF16),
        ],
        scratch_shapes=[pltpu.VMEM((LAT // 2, 2 * width), BF16)],
        compiler_params=PARAMS,
        cost_estimate=cost(CHUNK),
        name="terms",
    )(own, other, mine, theirs)


def key_terms_kernel(*refs, chunks, steps, turns, shares):
    head_ref = refs[0]
    dkv_refs = refs[1 : 1 + chunks]
    wt_refs = refs[1 + chunks : 1 + chunks + turns]
    rope_refs = refs[1 + chunks + turns : 1 + 2 * chunks + turns]
    outs = refs[1 + 2 * chunks + turns : -1]
    total_ref = refs[-1]
    i = pl.program_id(0)

    @pl.when(i == 0)
    def _():
        total_ref[...] = jnp.zeros_like(total_ref)

    for k in range(chunks):

        @pl.when(i // steps == k)
        def _(k=k):
            total = total_ref[...]
            weight_ref = wt_refs[k * turns // chunks]
            for h in range(weight_ref.shape[0]):
                grads = dkv_refs[k][:, h * PAIR : (h + 1) * PAIR]
                total = total + dot(grads, weight_ref[h], 1, 1)
            total_ref[...] = total

    @pl.when(i == pl.num_programs(0) - 1)
    def _():
        rope = rope_refs[0][...]
        for k in range(1, chunks):
            rope = rope + rope_refs[k][...]
        both = jnp.concatenate([total_ref[...], rope], 1)
        if shares is None:
            outs[0][...] = both[:, : LAT + ROPE]
            return
        part = (LAT + ROPE) // shares
        for z in range(shares):
            piece = both[:, z * part : (z + 1) * part]
            for s in range(shares):

                @pl.when(lax.rem(head_ref[0] + s, shares) == z)
                def _(s=s, piece=piece):
                    outs[s][...] = piece


def key_terms(at_head, dkvs, weights, ropes, shares):
    chunks, turns = len(dkvs), len(weights)
    heads = weights[0].shape[0] * turns // chunks
    width = dkvs[0].shape[0]
    steps = heads // STEP_HEADS
    span = steps * chunks // turns
    near = lambda k, many: lambda i, at: jnp.clip(i - k * many, 0, many - 1)
    wide = (LAT + ROPE) // (shares or 1)
    return pl.pallas_call(
        functools.partial(
            key_terms_kernel, chunks=chunks, steps=steps, turns=turns, shares=shares
        ),
        grid_spec=pltpu.PrefetchScalarGridSpec(
            num_scalar_prefetch=1,
            grid=(chunks * steps,),
            in_specs=[
                pl.BlockSpec((width, STEP_HEADS * PAIR), lambda i, at, k=k: (0, near(k, steps)(i, at)))
                for k in range(chunks)
            ]
            + [
                pl.BlockSpec(
                    (STEP_HEADS, LAT, PAIR), lambda i, at, k=k: (near(k, span)(i, at), 0, 0)
                )
                for k in range(turns)
            ]
            + [pl.BlockSpec((width, LANES), lambda i, at: (0, 0))] * chunks,
            out_specs=[pl.BlockSpec((width, wide), lambda i, at: (0, 0))] * (shares or 1),
            scratch_shapes=[pltpu.VMEM((width, LAT), F32)],
        ),
        out_shape=[jax.ShapeDtypeStruct((width, wide), F32)] * (shares or 1),
        compiler_params=WIDE,
        cost_estimate=cost(CHUNK),
        name="key_terms",
    )(at_head, *dkvs, *weights, *ropes)


def weight_sum_kernel(keep_ref, first_ref, second_ref, *refs):
    out_ref, k_ref, v_ref = refs[-3:]
    rows, heads, _ = out_ref.shape
    for h in range(heads):
        columns = slice(h * PAIR, (h + 1) * PAIR)
        total = keep_ref[:, columns] + first_ref[:, columns].astype(F32)
        total = total + second_ref[:, columns].astype(F32)
        k_ref[pl.ds(h, rows, stride=heads), :] = total[:, :LANES]
        v_ref[pl.ds(h, rows, stride=heads), :] = total[:, LANES:]
    out_ref[:, :, :LANES] = k_ref[...].reshape(rows, heads, LANES)
    out_ref[:, :, LANES:] = v_ref[...].reshape(rows, heads, LANES)


def weight_sum(keep, first, second, total, chunk, all_heads):
    rows, columns = second.shape
    heads = columns // PAIR
    block = 32
    operands = [keep, first, second]
    in_specs = [pl.BlockSpec((block, columns), lambda i: (i, 0)) for _ in operands]
    aliases = {}
    if total is not None:
        aliases = {3: 0}
        in_specs.append(pl.BlockSpec(memory_space=pl.ANY))
        operands.append(total)
    return pl.pallas_call(
        weight_sum_kernel,
        grid=(rows // block,),
        in_specs=in_specs,
        out_specs=pl.BlockSpec((block, heads, PAIR), lambda i: (i, chunk, 0)),
        out_shape=jax.ShapeDtypeStruct((rows, all_heads, PAIR), F32),
        scratch_shapes=[pltpu.VMEM((block * heads, LANES), F32)] * 2,
        input_output_aliases=aliases,
        compiler_params=PARAMS,
        cost_estimate=cost(SUM),
        name="weight_sum",
    )(*operands)


def after(values, earlier):
    return lax.optimization_barrier((values, earlier))[0]


def turn_rows(block):
    rows, heads, width = block.shape
    count = min(rows, 256 // heads)
    row = lax.broadcasted_iota(jnp.int32, (count * heads, count * heads), 0)
    col = lax.broadcasted_iota(jnp.int32, (count * heads, count * heads), 1)
    order = (col == (row % count) * heads + row // count).astype(BF16)
    for start in range(0, rows, count):
        part = block[start : start + count].reshape(count * heads, width)
        turned = dot(order, part, 1, 0).astype(BF16)
        yield slice(start, start + count), turned.reshape(heads, count, width)


def in_hbm(array):
    return pltpu.with_memory_space_constraint(array, pltpu.HBM)


def turn_weight_kernel(here_ref, *refs):
    *parts, wt_ref = refs
    depth = parts[0].shape[0]
    for at, w_ref in enumerate(parts):
        for rows, turned in turn_rows(w_ref[...]):
            wt_ref[:, at * depth + rows.start : at * depth + rows.stop, :] = turned


def turn_weight(here, up_weight, heads):
    steps, parts = 4, 4
    depth = LAT // steps // parts
    part = lambda p: lambda i, here: (i * parts + p, here[0] & 1, 0)
    return pl.pallas_call(
        turn_weight_kernel,
        grid_spec=pltpu.PrefetchScalarGridSpec(
            num_scalar_prefetch=1,
            grid=(steps,),
            in_specs=[pl.BlockSpec((depth, heads, PAIR), part(p)) for p in range(parts)],
            out_specs=pl.BlockSpec((heads, depth * parts, PAIR), lambda i, here: (0, i, 0)),
        ),
        out_shape=jax.ShapeDtypeStruct((heads, LAT, PAIR), BF16),
        compiler_params=PARAMS,
        cost_estimate=cost(TURN),
        name="turn_weight",
    )(here, *[in_hbm(up_weight)] * parts)


def turn_tokens_kernel(here_ref, q1_ref, g1_ref, q0_ref, g0_ref, own_ref, give_ref, mine_ref):
    heads = mine_ref.shape[0]
    for q_ref, g_ref, out_ref in ((q1_ref, g1_ref, give_ref), (q0_ref, g0_ref, mine_ref)):
        out_ref[:, :, LANES : 2 * LANES] = jnp.zeros_like(out_ref[:, :, LANES : 2 * LANES])
        for rows, turned in turn_rows(q_ref[...]):
            out_ref[:heads, rows, : PLAIN_WIDTH + ROPE] = turned
        for rows, turned in turn_rows(g_ref[...]):
            out_ref[:heads, rows, 2 * LANES :] = turned
    rest = LAT + ROPE - 3 * LANES
    give_ref[heads] = own_ref[:, : 3 * LANES]
    give_ref[heads + 1] = jnp.zeros_like(give_ref[heads + 1])
    give_ref[heads + 1, :, :rest] = own_ref[:, 3 * LANES :]


def turn_tokens(here, queries, out_grad, latent_keys, heads):
    tok = queries.shape[0]
    q_block, g_block = (tok, heads, PLAIN_WIDTH + ROPE), (tok, heads, VDIM)
    given = lambda i, here: (0, 1 - (here[0] & 1), 0)
    kept = lambda i, here: (0, here[0] & 1, 0)
    whole = lambda i, here: (0, 0, 0)
    give, mine = (heads + 2, tok, 3 * LANES), (heads, tok, 3 * LANES)
    queries, out_grad, latent_keys = (in_hbm(x) for x in (queries, out_grad, latent_keys))
    return pl.pallas_call(
        turn_tokens_kernel,
        grid_spec=pltpu.PrefetchScalarGridSpec(
            num_scalar_prefetch=1,
            grid=(1,),
            in_specs=[
                pl.BlockSpec(q_block, given),
                pl.BlockSpec(g_block, given),
                pl.BlockSpec(q_block, kept),
                pl.BlockSpec(g_block, kept),
                pl.BlockSpec(latent_keys.shape, lambda i, here: (0, 0)),
            ],
            out_specs=[pl.BlockSpec(give, whole), pl.BlockSpec(mine, whole)],
        ),
        out_shape=[jax.ShapeDtypeStruct(give, BF16), jax.ShapeDtypeStruct(mine, BF16)],
        compiler_params=PARAMS,
        cost_estimate=cost(WINDOW),
        name="turn_tokens",
    )(here, queries, out_grad, queries, out_grad, latent_keys)


def chip_window_kernel(
    here_ref, even_ref, odd_ref, own_ref, pal_ref, ids_ref, win_ref, krope_ref, vis_ref, lat_ref
):
    here = here_ref[0]
    tok = own_ref.shape[0]
    core, chip = here & 1, here >> 1
    first = core == 0
    prev = jnp.where(first, even_ref[...].astype(F32), odd_ref[...].astype(F32)).astype(BF16)
    pal = jnp.concatenate([pal_ref[0], pal_ref[1, :, : LAT + ROPE - 3 * LANES]], 1).astype(F32)
    own = own_ref[...].astype(F32)
    low = jnp.where(first, own, pal).astype(BF16)
    high = jnp.where(first, pal, own).astype(BF16)
    krope_ref[...] = jnp.zeros_like(krope_ref)
    for at, block in enumerate((prev, low, high)):
        win_ref[at * tok : (at + 1) * tok, :] = block[:, :LAT]
        krope_ref[at * tok : (at + 1) * tok, :ROPE] = block[:, LAT:]
    behind = ids_ref[pl.ds(jnp.maximum(chip - 1, 0), 1), :]
    both = ids_ref[pl.ds(chip, 1), :]
    seg = [jnp.where(chip > 0, behind[:, tok:], -1), both[:, :tok], both[:, tok:]]
    row = lax.broadcasted_iota(jnp.int32, (tok, tok), 0)
    col = lax.broadcasted_iota(jnp.int32, (tok, tok), 1)
    for b in range(2):
        seg_query = jnp.sum(jnp.where(row == col, seg[b + 1], 0), 1, keepdims=True)
        vis_ref[b, :, :tok] = (seg_query == seg[b]).astype(F32)
        vis_ref[b, :, tok:] = ((seg_query == seg[b + 1]) & (col <= row)).astype(F32)
    column = lax.broadcasted_iota(jnp.int32, (LAT, LAT), 0)
    source = lax.broadcasted_iota(jnp.int32, (LAT, LAT), 1)
    place = column >> 6
    apart = ((place & 2) << 1) | ((place & 4) >> 1) | (place & 1)
    wanted = ((here ^ apart) << 6) | (column & 63)
    order = (source == wanted).astype(BF16)
    lat_ref[...] = dot(order, win_ref[...], 1, 1).astype(BF16)


def chip_window(here, even, odd, own, got, ids):
    tok = own.shape[0]
    whole = lambda i, here: (0, 0)
    return pl.pallas_call(
        chip_window_kernel,
        grid_spec=pltpu.PrefetchScalarGridSpec(
            num_scalar_prefetch=1,
            grid=(1,),
            in_specs=[pl.BlockSpec(array.shape, whole) for array in (even, odd, own)]
            + [
                pl.BlockSpec((2,) + got.shape[1:], lambda i, here: (got.shape[0] // 2 - 1, 0, 0)),
                pl.BlockSpec(ids.shape, whole),
            ],
            out_specs=[
                pl.BlockSpec((3 * tok, LAT), whole),
                pl.BlockSpec((3 * tok, LANES), whole),
                pl.BlockSpec((2, tok, 2 * tok), lambda i, here: (0, 0, 0)),
                pl.BlockSpec((LAT, 3 * tok), whole),
            ],
        ),
        out_shape=[
            jax.ShapeDtypeStruct((3 * tok, LAT), BF16),
            jax.ShapeDtypeStruct((3 * tok, LANES), BF16),
            jax.ShapeDtypeStruct((2, tok, 2 * tok), F32),
            jax.ShapeDtypeStruct((LAT, 3 * tok), BF16),
        ],
        compiler_params=PARAMS,
        cost_estimate=cost(WINDOW),
        name="chip_window",
    )(here, even, odd, own, got, ids)


def chunk_kernel(
    here_ref,
    win_ref,
    krope_ref,
    vis_ref,
    lat_ref,
    wt_ref,
    mine_ref,
    got_ref,
    *refs,
    chained,
    along_x,
):
    before_ref = refs[0] if chained else None
    refs = refs[3:] if chained else refs
    keep_ref, send_ref, key_ref, dq_ref, back_ref = refs

    @pl.when(pl.program_id(0) == 0)
    def _():
        key_ref[...] = before_ref[...] if chained else jnp.zeros_like(key_ref)

    tok = vis_ref.shape[1]
    heads = wt_ref.shape[0]
    first = (here_ref[0] & 1) == 0
    scale = 1.0 / math.sqrt(PLAIN_WIDTH + ROPE)
    window, krope = win_ref[...], krope_ref[...]
    visible = [vis_ref[b] > 0.0 for b in range(2)]
    keys, values, queries, grads = [], [], [], []
    for h in range(heads):
        kv = dot(window, wt_ref[h], 1, 0).astype(BF16)
        keys.append(jnp.concatenate([kv[:, :PLAIN_WIDTH], krope], 1))
        values.append(kv[:, PLAIN_WIDTH:])
        mine, got = mine_ref[h], got_ref[h]
        ordered = (jnp.where(first, mine, got), jnp.where(first, got, mine))
        queries.append([block[:, : 2 * LANES] for block in ordered])
        grads.append([block[:, 2 * LANES :] for block in ordered])
    reach = [slice(b * tok, (b + 2) * tok) for b in range(2)]
    units = [(h, b) for h in range(heads) for b in range(2)]
    scores = {(h, b): dot(queries[h][b], keys[h][reach[b]], 1, 1) for h, b in units}
    dprobs = {(h, b): dot(grads[h][b], values[h][reach[b]], 1, 1) for h, b in units}
    dscores, probs16 = {}, {}
    for unit in units:
        logits = jnp.where(visible[unit[1]], scores[unit] * scale, -1e30)
        top = jnp.max(logits, -1, keepdims=True)
        expo = jnp.exp(logits - top)
        probs = expo / jnp.sum(expo, -1, keepdims=True)
        delta = jnp.sum(probs * dprobs[unit], -1, keepdims=True)
        dscores[unit] = (probs * (dprobs[unit] - delta) * scale).astype(BF16)
        probs16[unit] = probs.astype(BF16)

    def fold(low, high):
        return jnp.concatenate([low[:tok], low[tok:] + high[:tok], high[tok:]], 0)

    parts, rope = [], None
    for h in range(heads):
        dk = fold(*[dot(dscores[h, b], queries[h][b], 0, 0) for b in range(2)])
        dv = fold(*[dot(probs16[h, b], grads[h][b], 0, 0) for b in range(2)])
        parts.append(jnp.concatenate([dk[:, :PLAIN_WIDTH], dv], 1).astype(BF16))
        rope = dk[:, PLAIN_WIDTH:] if rope is None else rope + dk[:, PLAIN_WIDTH:]
    dkv = jnp.concatenate(parts, 1)
    rows = lat_ref.shape[0] // 4
    kept = (0, 1) if along_x else (0, 2)
    sent = (2, 3) if along_x else (1, 3)
    for at, g in enumerate(sent):
        term = dot(lat_ref[g * rows : (g + 1) * rows, :], dkv, 1, 0)
        send_ref[at * rows : (at + 1) * rows, :] = term.astype(BF16)
    for at, g in enumerate(kept):
        keep_ref[at * rows : (at + 1) * rows, :] = dot(
            lat_ref[g * rows : (g + 1) * rows, :], dkv, 1, 0
        )
    total = key_ref[:, :LAT]
    for h in range(heads):
        total = total + dot(parts[h], wt_ref[h], 1, 1)
    key_ref[:, :LAT] = total
    key_ref[:, LAT:] = key_ref[:, LAT:] + rope
    for h in range(heads):
        low, high = (dot(dscores[h, b], keys[h][reach[b]], 1, 0) for b in range(2))
        dq_ref[h] = jnp.where(first, low, high)
        back_ref[h] = jnp.where(first, high, low)


def chunk(here, window, weight, mine, got, before, index, heads, along_x):
    tok = mine.shape[1]
    whole = lambda i, here: (0, 0)
    whole3 = lambda i, here: (0, 0, 0)
    step = min(heads, STEP_HEADS)
    steps = heads // step
    at = lambda i, here: (index * steps + i, 0, 0)
    across_columns = lambda i, here: (0, i)
    columns = heads * PAIR
    operands = [*window, weight, mine, got]
    in_specs = [
        pl.BlockSpec(array.shape, whole3 if array.ndim == 3 else whole) for array in window
    ] + [
        pl.BlockSpec((step, LAT, PAIR), at),
        pl.BlockSpec((step, tok, 3 * LANES), at),
        pl.BlockSpec((step, tok, 3 * LANES), at),
    ]
    aliases = {}
    if before is not None:
        key, dq, back = before
        aliases = {len(operands) + 2: 3, len(operands) + 3: 4}
        in_specs = in_specs + [
            pl.BlockSpec(key.shape, whole),
            pl.BlockSpec(memory_space=pl.ANY),
            pl.BlockSpec(memory_space=pl.ANY),
        ]
        operands = operands + [key, dq, back]
    turned = (weight.shape[0], tok, 2 * LANES)
    return pl.pallas_call(
        functools.partial(chunk_kernel, chained=before is not None, along_x=along_x),
        grid_spec=pltpu.PrefetchScalarGridSpec(
            num_scalar_prefetch=1,
            grid=(steps,),
            in_specs=in_specs,
            out_specs=[
                pl.BlockSpec((LAT // 2, step * PAIR), across_columns),
                pl.BlockSpec((LAT // 2, step * PAIR), across_columns),
                pl.BlockSpec((3 * tok, LAT + LANES), whole),
                pl.BlockSpec((step, tok, 2 * LANES), at),
                pl.BlockSpec((step, tok, 2 * LANES), at),
            ],
        ),
        out_shape=[
            jax.ShapeDtypeStruct((LAT // 2, columns), F32),
            jax.ShapeDtypeStruct((LAT // 2, columns), BF16),
            jax.ShapeDtypeStruct((3 * tok, LAT + LANES), F32),
            jax.ShapeDtypeStruct(turned, F32),
            jax.ShapeDtypeStruct(turned, F32),
        ],
        input_output_aliases=aliases,
        compiler_params=PARAMS,
        cost_estimate=cost(CHUNK),
        name="chunk",
    )(here, *operands)


def add_rows_kernel(*refs, count, wide):
    total = refs[0][...].astype(F32)
    for ref in refs[1 : count + wide]:
        total = total + ref[...].astype(F32)
    refs[-1][...] = total.astype(refs[-1].dtype)


def add_rows(arrays, rows, index, dtype, wide=(), place=0, places=1, before=None):
    columns = arrays[0].shape[1]
    operands = [*arrays, *wide]
    in_specs = [pl.BlockSpec((rows, columns), lambda i: (index, 0)) for _ in arrays]
    in_specs = in_specs + [pl.BlockSpec((rows, columns), lambda i: (index, place)) for _ in wide]
    aliases = {}
    if before is not None:
        aliases = {len(operands): 0}
        in_specs.append(pl.BlockSpec(memory_space=pl.ANY))
        operands.append(before)
    return pl.pallas_call(
        functools.partial(add_rows_kernel, count=len(arrays), wide=len(wide)),
        grid=(1,),
        in_specs=in_specs,
        out_specs=pl.BlockSpec((rows, columns), lambda i: (0, place)),
        out_shape=jax.ShapeDtypeStruct((rows, places * columns), dtype),
        input_output_aliases=aliases,
        compiler_params=PARAMS,
        cost_estimate=cost(SHARES),
        name="add_rows",
    )(*operands)


def key_split_kernel(here_ref, key_ref, keep_ref, give_ref):
    tok = keep_ref.shape[0] // 2
    first = (here_ref[0] & 1) == 0
    behind, low, high = (key_ref[b * tok : (b + 1) * tok, :] for b in range(3))
    keep_ref[:tok] = jnp.where(first, low, high)
    keep_ref[tok:] = behind
    give_ref[:tok] = jnp.where(first, high, low)
    give_ref[tok:] = behind


def key_split(here, key):
    rows = key.shape[0] // 3 * 2
    whole = lambda i, here: (0, 0)
    return pl.pallas_call(
        key_split_kernel,
        grid_spec=pltpu.PrefetchScalarGridSpec(
            num_scalar_prefetch=1,
            grid=(1,),
            in_specs=[pl.BlockSpec(key.shape, whole)],
            out_specs=[pl.BlockSpec((rows, key.shape[1]), whole)] * 2,
        ),
        out_shape=[jax.ShapeDtypeStruct((rows, key.shape[1]), F32)] * 2,
        compiler_params=PARAMS,
        cost_estimate=cost(SHARES),
        name="key_split",
    )(here, key)


def key_shares_kernel(at_ref, keep_ref, got_ref, *outs):
    shares = len(outs)
    part = (LAT + ROPE) // shares
    total = keep_ref[...] + got_ref[...]
    for z in range(shares):
        piece = total[:, z * part : (z + 1) * part]
        for s in range(shares):

            @pl.when(lax.rem(at_ref[0] + s, shares) == z)
            def _(s=s, piece=piece):
                outs[s][...] = piece.astype(outs[s].dtype)


def key_shares(at_head, keep, got, shares):
    part = (LAT + ROPE) // shares
    rows = keep.shape[0]
    whole = lambda i, at: (0, 0)
    types = [F32] + [BF16] * (shares - 1)
    return pl.pallas_call(
        key_shares_kernel,
        grid_spec=pltpu.PrefetchScalarGridSpec(
            num_scalar_prefetch=1,
            grid=(1,),
            in_specs=[pl.BlockSpec(keep.shape, whole)] * 2,
            out_specs=[pl.BlockSpec((rows, part), whole)] * shares,
        ),
        out_shape=[jax.ShapeDtypeStruct((rows, part), kind) for kind in types],
        compiler_params=PARAMS,
        cost_estimate=cost(SHARES),
        name="key_shares",
    )(at_head, keep, got)


def query_grad_kernel(here_ref, mine_ref, got_ref, out_ref, n_ref, r_ref):
    tok, heads, _ = out_ref.shape

    def put(src_ref):
        for h in range(heads):
            n_ref[pl.ds(h, tok, stride=heads), :] = src_ref[h, :, :PLAIN_WIDTH]
            r_ref[pl.ds(h, tok, stride=heads), :] = src_ref[h, :, PLAIN_WIDTH:]

    pl.when(pl.program_id(0) == 0)(lambda: put(mine_ref))
    pl.when(pl.program_id(0) == 1)(lambda: put(got_ref))
    out_ref[:, :, :PLAIN_WIDTH] = n_ref[...].reshape(tok, heads, LANES)
    out_ref[:, :, PLAIN_WIDTH:] = r_ref[...].reshape(tok, heads, LANES)[:, :, :ROPE]


def query_grad(here, mine, got):
    heads, tok, _ = mine.shape
    whole = lambda i, here: (0, 0, 0)
    return pl.pallas_call(
        query_grad_kernel,
        grid_spec=pltpu.PrefetchScalarGridSpec(
            num_scalar_prefetch=1,
            grid=(2,),
            in_specs=[pl.BlockSpec(mine.shape, whole)] * 2,
            out_specs=pl.BlockSpec(
                (tok, heads, PLAIN_WIDTH + ROPE), lambda i, here: (0, (here[0] & 1) ^ i, 0)
            ),
            scratch_shapes=[pltpu.VMEM((tok * heads, LANES), F32)] * 2,
        ),
        out_shape=jax.ShapeDtypeStruct((tok, 2 * heads, PLAIN_WIDTH + ROPE), F32),
        compiler_params=PARAMS,
        cost_estimate=cost(QUERY),
        name="query_grad",
    )(here, mine, got)


def weight_grad_kernel(here_ref, *refs, count):
    narrow, last_ref, got_ref = refs[: 2 * count], refs[2 * count], refs[2 * count + 1]
    out_ref, k_ref, v_ref = refs[-3:]
    rows, heads, _ = out_ref.shape
    each = heads // count

    def put(c, total):
        for h in range(each):
            at = pl.ds(c * each + h, rows, stride=heads)
            k_ref[at, :] = total[:, h * PAIR : h * PAIR + LANES]
            v_ref[at, :] = total[:, h * PAIR + LANES : (h + 1) * PAIR]

    for c in range(count):
        columns = slice(c * each * PAIR, (c + 1) * each * PAIR)

        @pl.when(pl.program_id(0) == 0)
        def _(c=c, columns=columns):
            keep_ref, first_ref = narrow[2 * c : 2 * c + 2]
            total = keep_ref[...] + first_ref[...].astype(F32)
            put(c, total + last_ref[:, columns].astype(F32))

        @pl.when(pl.program_id(0) == 1)
        def _(c=c, columns=columns):
            put(c, got_ref[:, columns])

    out_ref[:, :, :LANES] = k_ref[...].reshape(rows, heads, LANES)
    out_ref[:, :, LANES:] = v_ref[...].reshape(rows, heads, LANES)


def weight_grad_part(here, groups, last, got, total, part, parts):
    count = len(groups)
    rows, columns = got.shape
    heads = columns // PAIR
    operands = [array for group in groups for array in group] + [last, got]
    whole = lambda i, here: (0, 0)
    in_specs = [pl.BlockSpec((rows, columns // count), whole)] * (2 * count)
    in_specs = in_specs + [pl.BlockSpec((rows, columns), whole)] * 2
    aliases = {}
    if total is not None:
        aliases = {1 + len(operands): 0}
        in_specs.append(pl.BlockSpec(memory_space=pl.ANY))
        operands.append(total)
    return pl.pallas_call(
        functools.partial(weight_grad_kernel, count=count),
        grid_spec=pltpu.PrefetchScalarGridSpec(
            num_scalar_prefetch=1,
            grid=(2,),
            in_specs=in_specs,
            out_specs=pl.BlockSpec(
                (rows, heads, PAIR), lambda i, here: (0, ((here[0] & 1) ^ i) * parts + part, 0)
            ),
            scratch_shapes=[pltpu.VMEM((rows * heads, LANES), F32)] * 2,
        ),
        out_shape=jax.ShapeDtypeStruct((rows, 2 * parts * heads, PAIR), F32),
        input_output_aliases=aliases,
        compiler_params=PARAMS,
        cost_estimate=cost(SUM),
        name="weight_grad",
    )(here, *operands)


def in_chunks(queries, latent_keys, out_grad, up_weight, here, at_head, ids):
    tok = latent_keys.shape[0]
    n_ctx, n_head = lax.axis_size("ctx"), lax.axis_size("head")
    heads, each = 16, 4
    queries = after(queries, (ids, here, at_head))
    give, mine = turn_tokens(here, queries, out_grad, latent_keys, heads)
    odd_devices = range(1, n_ctx - 1, 2)
    even = lax.ppermute(latent_keys, "ctx", [(source, source + 1) for source in odd_devices])
    odd = lax.ppermute(latent_keys, "ctx", [(source, source + 2) for source in odd_devices])
    got = across(give, 1)
    weight = turn_weight(here, up_weight, heads)
    window = chip_window(here, even, odd, latent_keys, got, ids)
    ways, blocks = ((2, 4), (4, 2)), (0, 2, 1, 3)
    before, keeps, sent = None, [], []
    for c, block in enumerate(blocks):
        keep, out, *before = chunk(
            here, window, weight, mine, got, before, block, each, c % 2 == 0
        )
        keeps.append(keep)
        sent.append(across(out, ways[c % 2][0]))
    key, dq, back = before

    def rest(c, earlier):
        return add_rows(
            (keeps[c], sent[c]), 2 * tok, 1, BF16, place=c // 2, places=2, before=earlier
        )

    key_keep, key_give = key_split(here, key)
    key_got = across(key_give, 1)
    rests = [rest(0, None), rest(1, None)]
    key_got = after(key_got, rests)
    shares = key_shares(at_head, key_keep, key_got, n_head)
    pieces = [
        lax.ppermute(shares[s], "head", [(z, (z + s) % n_head) for z in range(n_head)])
        for s in range(1, n_head)
    ]
    dq = query_grad(here, dq, across(after(back, key_keep), 1))
    share, behind = (add_rows((shares[0], *pieces), tok, b, F32) for b in range(2))
    keeps[2] = after(keeps[2], (share, behind))
    behind = lax.ppermute(behind, "ctx", [(source, source - 1) for source in range(2, n_ctx, 2)])
    key_grad = add_rows((share, behind), tok, 0, F32)
    keeps[3] = after(keeps[3], key_grad)
    rests = [rest(2, rests[0]), rest(3, rests[1])]
    lasts = [across(rests[p], ways[p][1]) for p in range(2)]
    keeps[0] = after(keeps[0], dq)
    theirs = []
    for p in range(2):
        total = None
        for place, c in enumerate((p, p + 2)):
            total = add_rows(
                (keeps[c], sent[c]),
                tok,
                1,
                F32,
                wide=(lasts[p],),
                place=place,
                places=2,
                before=total,
            )
        theirs.append(across(total, 1))
    weight_grad = None
    for p in range(2):
        groups = [(keeps[c], sent[c]) for c in (p, p + 2)]
        weight_grad = weight_grad_part(here, groups, lasts[p], theirs[p], weight_grad, p, 2)
    return dq, key_grad, weight_grad


def shards(queries, latent_keys, out_grad, up_weight, segment_ids):
    tok = latent_keys.shape[0]
    heads = queries.shape[1]
    n_ctx, n_head = lax.axis_size("ctx"), lax.axis_size("head")
    here = lax.axis_index("ctx").astype(jnp.int32).reshape(1)
    at_head = lax.axis_index("head").astype(jnp.int32).reshape(1)
    if n_ctx == 8 and heads == 32 and n_head == 4:
        ids = segment_ids.reshape(n_ctx // 2, 2 * tok)
        return in_chunks(queries, latent_keys, out_grad, up_weight, here, at_head, ids)
    else:
        ids = segment_ids.reshape(n_ctx, tok)
        prev = from_behind(latent_keys, "ctx", REACH)
        turned = by_head(up_weight, queries, out_grad, 0, heads)
        window = key_window(here, prev, latent_keys, ids, False)
        dq, dkv, rope = attention(window, turned, None, None, 0, heads, 0, heads)
        (both,) = key_terms(at_head, [dkv], [turned[0]], [rope], None)
        share = lax.psum_scatter(
            both.reshape(REACH + 1, tok, LAT + ROPE), "head", scatter_dimension=2, tiled=True
        )
        term = jnp.einsum("ki,ke->ie", window[0], dkv, preferred_element_type=F32)
        rows = lax.psum_scatter(term.astype(BF16), "ctx", scatter_dimension=0, tiled=True)
        weight_grad = rows.astype(F32).reshape(rows.shape[0], heads, PAIR)
    key_grad = share[REACH] + from_behind(share[0], "ctx", 0 - REACH)
    return (dq, key_grad, weight_grad)


def solution(mesh):
    return jax.shard_map(
        shards,
        mesh=mesh,
        in_specs=(
            P("ctx", "head", None),
            P("ctx", None),
            P("ctx", "head", None),
            P(None, "head", None),
            P(),
        ),
        out_specs=(P("ctx", "head", None), P("ctx", "head"), P("ctx", "head", None)),
        check_vma=False,
    )
```

```python
import functools
import math

import jax
import jax.numpy as jnp
from jax import lax
from jax.experimental import pallas as pl
from jax.experimental.pallas import tpu as pltpu
from jax.sharding import PartitionSpec as P

LAT = 512
ROPE = 64
PLAIN_WIDTH = 128
VDIM = 128
REACH = 1
LANES = 128
PAIR = PLAIN_WIDTH + VDIM
STEP_HEADS = 4
BF16 = jnp.bfloat16
F32 = jnp.float32
WIDE = pltpu.CompilerParams(vmem_limit_bytes=56 * 1024 * 1024)
PARAMS = pltpu.CompilerParams(vmem_limit_bytes=20 * 1024 * 1024)


def from_behind(value, axis, steps):
    count = lax.axis_size(axis)
    initial, last = (max(0, -steps), min(count, count - steps))
    return lax.ppermute(value, axis, [(source, source + steps) for source in range(initial, last)])


def across(value, bit):
    count = lax.axis_size("ctx")
    return lax.ppermute(value, "ctx", [(source, source ^ bit) for source in range(count)])


def cost(share):
    return pl.CostEstimate(flops=int(share * 1e9), bytes_accessed=1024, transcendentals=0)


TURN, WINDOW, CHUNK, SHARES, QUERY, SUM = 3.0, 0.5, 1.5, 0.1, 0.1, 0.1


def dot(a, b, a_dim, b_dim):
    return lax.dot_general(a, b, (((a_dim,), (b_dim,)), ((), ())), preferred_element_type=F32)


def by_head_kernel(w_ref, q_ref, g_ref, wt_ref, qt_ref, gt_ref):
    heads = w_ref.shape[1]
    orders = {}

    def order(count):
        if count not in orders:
            size = count * heads
            row = lax.broadcasted_iota(jnp.int32, (size, size), 0)
            col = lax.broadcasted_iota(jnp.int32, (size, size), 1)
            wanted = (row % count) * heads + row // count
            orders[count] = (col == wanted).astype(BF16)
        return orders[count]

    def turn(ref, out_ref):
        rows, _, width = ref.shape
        count = min(rows, 256 // heads)
        for start in range(0, rows, count):
            block = ref[start : start + count].reshape(count * heads, width)
            turned = dot(order(count), block, 1, 0).astype(BF16)
            out_ref[:, start : start + count, :width] = turned.reshape(heads, count, width)

    turn(w_ref, wt_ref)
    qt_ref[...] = jnp.zeros_like(qt_ref)
    turn(q_ref, qt_ref)
    turn(g_ref, gt_ref)


def by_head(up_weight, queries, out_grad, chunk, heads):
    tok = queries.shape[0]
    steps = 4
    depth, rows = LAT // steps, tok // steps
    return pl.pallas_call(
        by_head_kernel,
        grid=(steps,),
        in_specs=[
            pl.BlockSpec((depth, heads, PAIR), lambda i: (i, chunk, 0)),
            pl.BlockSpec((rows, heads, PLAIN_WIDTH + ROPE), lambda i: (i, chunk, 0)),
            pl.BlockSpec((rows, heads, VDIM), lambda i: (i, chunk, 0)),
        ],
        out_specs=[
            pl.BlockSpec((heads, depth, PAIR), lambda i: (0, i, 0)),
            pl.BlockSpec((heads, rows, 2 * LANES), lambda i: (0, i, 0)),
            pl.BlockSpec((heads, rows, VDIM), lambda i: (0, i, 0)),
        ],
        out_shape=[
            jax.ShapeDtypeStruct((heads, LAT, PAIR), BF16),
            jax.ShapeDtypeStruct((heads, tok, 2 * LANES), BF16),
            jax.ShapeDtypeStruct((heads, tok, VDIM), BF16),
        ],
        compiler_params=WIDE,
        cost_estimate=cost(TURN),
        name="by_head",
    )(up_weight, queries, out_grad)


def window_kernel(here_ref, prev_ref, own_ref, ids_ref, *outs, paired):
    win_ref, krope_ref, vis_ref = outs[:3]
    here = here_ref[0]
    tok = prev_ref.shape[0]
    win_ref[:tok, :] = prev_ref[:, :LAT]
    win_ref[tok:, :] = own_ref[:, :LAT]
    krope_ref[...] = jnp.zeros_like(krope_ref)
    krope_ref[:tok, :ROPE] = prev_ref[:, LAT:]
    krope_ref[tok:, :ROPE] = own_ref[:, LAT:]
    behind = jnp.maximum(here - 1, 0)
    seg_prev = jnp.where(here > 0, ids_ref[pl.ds(behind, 1), :], -1)
    seg_own = ids_ref[pl.ds(here, 1), :]
    row = lax.broadcasted_iota(jnp.int32, (tok, tok), 0)
    col = lax.broadcasted_iota(jnp.int32, (tok, tok), 1)
    seg_query = jnp.sum(jnp.where(row == col, seg_own, 0), 1, keepdims=True)
    vis_ref[:, :tok] = (seg_query == seg_prev).astype(F32)
    vis_ref[:, tok:] = ((seg_query == seg_own) & (col <= row)).astype(F32)
    if paired:
        source = lax.broadcasted_iota(jnp.int32, (LAT, LAT), 0)
        column = lax.broadcasted_iota(jnp.int32, (LAT, LAT), 1)
        place = column >> 6
        apart = ((place & 1) << 2) | (place & 2) | (place >> 2)
        wanted = ((here ^ apart) << 6) | (column & 63)
        ordered = dot(win_ref[...], (source == wanted).astype(BF16), 1, 0).astype(BF16)
        outs[3][...] = ordered[:, : LAT // 2]
        outs[4][...] = ordered[:, LAT // 2 :]


def key_window(here, prev, own, ids, paired):
    tok = prev.shape[0]
    whole = lambda i, here: (0, 0)
    shapes = [((2 * tok, LAT), BF16), ((2 * tok, LANES), BF16), ((tok, 2 * tok), F32)]
    if paired:
        shapes = shapes + [((2 * tok, LAT // 2), BF16)] * 2
    return pl.pallas_call(
        functools.partial(window_kernel, paired=paired),
        grid_spec=pltpu.PrefetchScalarGridSpec(
            num_scalar_prefetch=1,
            grid=(1,),
            in_specs=[pl.BlockSpec(array.shape, whole) for array in (prev, own, ids)],
            out_specs=[pl.BlockSpec(shape, whole) for shape, _ in shapes],
        ),
        out_shape=[jax.ShapeDtypeStruct(*shape) for shape in shapes],
        compiler_params=PARAMS,
        cost_estimate=cost(WINDOW),
        name="key_window",
    )(here, prev, own, ids)


def attention_kernel(
    win_ref, krope_ref, vis_ref, wt_ref, qt_ref, gt_ref, *refs, aliased, extra
):
    latents_ref = refs[0] if extra else None
    refs = refs[1:] if extra else refs
    refs = refs[1:] if aliased else refs
    dq_ref, dkv_ref, rope_ref, dqn_ref, dqr_ref = refs
    i = pl.program_id(0)
    tok, heads = dq_ref.shape[:2]
    scale = 1.0 / math.sqrt(PLAIN_WIDTH + ROPE)

    @pl.when(i == 0)
    def _():
        rope_ref[...] = jnp.zeros_like(rope_ref)
        if extra:
            dkv_ref[:, heads * PAIR :] = latents_ref[...]

    visible = vis_ref[...] > 0.0
    window = win_ref[...]
    krope = krope_ref[...]
    count = wt_ref.shape[0]
    keys, values = [], []
    for h in range(count):
        kv = dot(window, wt_ref[h], 1, 0).astype(BF16)
        keys.append(jnp.concatenate([kv[:, :PLAIN_WIDTH], krope], 1))
        values.append(kv[:, PLAIN_WIDTH:])
    scores = [dot(qt_ref[h], keys[h], 1, 1) for h in range(count)]
    dprobs = [dot(gt_ref[h], values[h], 1, 1) for h in range(count)]
    dscores, probs16 = [], []
    for h in range(count):
        logits = jnp.where(visible, scores[h] * scale, -1e30)
        top = jnp.max(logits, -1, keepdims=True)
        expo = jnp.exp(logits - top)
        probs = expo / jnp.sum(expo, -1, keepdims=True)
        delta = jnp.sum(probs * dprobs[h], -1, keepdims=True)
        dscores.append((probs * (dprobs[h] - delta) * scale).astype(BF16))
        probs16.append(probs.astype(BF16))
    parts, rope = [], rope_ref[...]
    for h in range(count):
        dk = dot(dscores[h], qt_ref[h], 0, 0)
        dv = dot(probs16[h], gt_ref[h], 0, 0)
        parts.append(jnp.concatenate([dk[:, :PLAIN_WIDTH], dv], 1).astype(BF16))
        rope = rope + dk[:, PLAIN_WIDTH:]
    rope_ref[...] = rope
    dkv_ref[:, pl.ds(pl.multiple_of(i * (count * PAIR), count * PAIR), count * PAIR)] = (
        jnp.concatenate(parts, 1)
    )
    for h in range(count):
        dq = dot(dscores[h], keys[h], 1, 0)
        dqn_ref[pl.ds(i * count + h, tok, stride=heads), :] = dq[:, :PLAIN_WIDTH]
        dqr_ref[pl.ds(i * count + h, tok, stride=heads), :] = dq[:, PLAIN_WIDTH:]

    @pl.when(i == pl.num_programs(0) - 1)
    def _():
        dq_ref[:, :, :PLAIN_WIDTH] = dqn_ref[...].reshape(tok, heads, LANES)
        dq_ref[:, :, PLAIN_WIDTH:] = dqr_ref[...].reshape(tok, heads, LANES)[:, :, :ROPE]


def attention(window, turned, latents, dq, chunk, heads, first, all_heads):
    weight, queries, out_grad = turned
    tok = queries.shape[1]
    width = 2 * tok
    steps = heads // STEP_HEADS
    at = first // STEP_HEADS
    extra = LAT // 2 if latents is not None else 0
    whole = lambda i: (0, 0)
    head_block = lambda i: (at + i, 0, 0)
    operands = [*window, weight, queries, out_grad]
    in_specs = [pl.BlockSpec(array.shape, whole) for array in window] + [
        pl.BlockSpec((STEP_HEADS, LAT, PAIR), head_block),
        pl.BlockSpec((STEP_HEADS, tok, 2 * LANES), head_block),
        pl.BlockSpec((STEP_HEADS, tok, VDIM), head_block),
    ]
    if latents is not None:
        in_specs.append(pl.BlockSpec(latents.shape, whole))
        operands.append(latents)
    aliases = {}
    if dq is not None:
        aliases = {len(operands): 0}
        in_specs.append(pl.BlockSpec(memory_space=pl.ANY))
        operands.append(dq)
    return pl.pallas_call(
        functools.partial(attention_kernel, aliased=dq is not None, extra=latents is not None),
        grid=(steps,),
        in_specs=in_specs,
        out_specs=[
            pl.BlockSpec((tok, heads, PLAIN_WIDTH + ROPE), lambda i: (0, chunk, 0)),
            pl.BlockSpec((width, heads * PAIR + extra), whole),
            pl.BlockSpec((width, LANES), whole),
        ],
        scratch_shapes=[
            pltpu.VMEM((tok * heads, LANES), F32),
            pltpu.VMEM((tok * heads, LANES), F32),
        ],
        out_shape=[
            jax.ShapeDtypeStruct((tok, all_heads, PLAIN_WIDTH + ROPE), F32),
            jax.ShapeDtypeStruct((width, heads * PAIR + extra), BF16),
            jax.ShapeDtypeStruct((width, LANES), F32),
        ],
        input_output_aliases=aliases,
        compiler_params=WIDE,
        cost_estimate=cost(CHUNK),
        name="attention",
    )(*operands)


def terms_kernel(
    own_ref, other_ref, mine_ref, theirs_ref, keep_ref, send_ref, latents_ref, *, along_x
):
    width = own_ref.shape[0]

    @pl.when(pl.program_id(0) == 0)
    def _():
        latents_ref[:, :width] = mine_ref[...].T
        latents_ref[:, width:] = theirs_ref[...].T

    grads = jnp.concatenate([own_ref[...], other_ref[...]], 0)
    term = dot(latents_ref[...], grads, 1, 0)
    rows = term.shape[0] // 4
    first, second = (1, 2) if along_x else (2, 1)
    keep_ref[:rows] = term[:rows]
    keep_ref[rows:] = term[first * rows : (first + 1) * rows]
    send_ref[:rows] = term[second * rows : (second + 1) * rows].astype(BF16)
    send_ref[rows:] = term[3 * rows :].astype(BF16)


def terms(own, other, mine, theirs, columns, along_x):
    width = own.shape[0]
    block = 1024
    at = theirs.shape[1] // (LAT // 2) - 1
    column_block = lambda i: (0, i)
    return pl.pallas_call(
        functools.partial(terms_kernel, along_x=along_x),
        grid=(columns // block,),
        in_specs=[
            pl.BlockSpec((width, block), column_block),
            pl.BlockSpec((width, block), column_block),
            pl.BlockSpec((width, LAT // 2), lambda i: (0, 0)),
            pl.BlockSpec((width, LAT // 2), lambda i: (0, at)),
        ],
        out_specs=[pl.BlockSpec((LAT // 4, block), column_block)] * 2,
        out_shape=[
            jax.ShapeDtypeStruct((LAT // 4, columns), F32),
            jax.ShapeDtypeStruct((LAT // 4, columns), BF16),
        ],
        scratch_shapes=[pltpu.VMEM((LAT // 2, 2 * width), BF16)],
        compiler_params=PARAMS,
        cost_estimate=cost(CHUNK),
        name="terms",
    )(own, other, mine, theirs)


def key_terms_kernel(*refs, chunks, steps, turns, shares):
    head_ref = refs[0]
    dkv_refs = refs[1 : 1 + chunks]
    wt_refs = refs[1 + chunks : 1 + chunks + turns]
    rope_refs = refs[1 + chunks + turns : 1 + 2 * chunks + turns]
    outs = refs[1 + 2 * chunks + turns : -1]
    total_ref = refs[-1]
    i = pl.program_id(0)

    @pl.when(i == 0)
    def _():
        total_ref[...] = jnp.zeros_like(total_ref)

    for k in range(chunks):

        @pl.when(i // steps == k)
        def _(k=k):
            total = total_ref[...]
            weight_ref = wt_refs[k * turns // chunks]
            for h in range(weight_ref.shape[0]):
                grads = dkv_refs[k][:, h * PAIR : (h + 1) * PAIR]
                total = total + dot(grads, weight_ref[h], 1, 1)
            total_ref[...] = total

    @pl.when(i == pl.num_programs(0) - 1)
    def _():
        rope = rope_refs[0][...]
        for k in range(1, chunks):
            rope = rope + rope_refs[k][...]
        both = jnp.concatenate([total_ref[...], rope], 1)
        if shares is None:
            outs[0][...] = both[:, : LAT + ROPE]
            return
        part = (LAT + ROPE) // shares
        for z in range(shares):
            piece = both[:, z * part : (z + 1) * part]
            for s in range(shares):

                @pl.when(lax.rem(head_ref[0] + s, shares) == z)
                def _(s=s, piece=piece):
                    outs[s][...] = piece


def key_terms(at_head, dkvs, weights, ropes, shares):
    chunks, turns = len(dkvs), len(weights)
    heads = weights[0].shape[0] * turns // chunks
    width = dkvs[0].shape[0]
    steps = heads // STEP_HEADS
    span = steps * chunks // turns
    near = lambda k, many: lambda i, at: jnp.clip(i - k * many, 0, many - 1)
    wide = (LAT + ROPE) // (shares or 1)
    return pl.pallas_call(
        functools.partial(
            key_terms_kernel, chunks=chunks, steps=steps, turns=turns, shares=shares
        ),
        grid_spec=pltpu.PrefetchScalarGridSpec(
            num_scalar_prefetch=1,
            grid=(chunks * steps,),
            in_specs=[
                pl.BlockSpec((width, STEP_HEADS * PAIR), lambda i, at, k=k: (0, near(k, steps)(i, at)))
                for k in range(chunks)
            ]
            + [
                pl.BlockSpec(
                    (STEP_HEADS, LAT, PAIR), lambda i, at, k=k: (near(k, span)(i, at), 0, 0)
                )
                for k in range(turns)
            ]
            + [pl.BlockSpec((width, LANES), lambda i, at: (0, 0))] * chunks,
            out_specs=[pl.BlockSpec((width, wide), lambda i, at: (0, 0))] * (shares or 1),
            scratch_shapes=[pltpu.VMEM((width, LAT), F32)],
        ),
        out_shape=[jax.ShapeDtypeStruct((width, wide), F32)] * (shares or 1),
        compiler_params=WIDE,
        cost_estimate=cost(CHUNK),
        name="key_terms",
    )(at_head, *dkvs, *weights, *ropes)


def weight_sum_kernel(keep_ref, first_ref, second_ref, *refs):
    out_ref, k_ref, v_ref = refs[-3:]
    rows, heads, _ = out_ref.shape
    for h in range(heads):
        columns = slice(h * PAIR, (h + 1) * PAIR)
        total = keep_ref[:, columns] + first_ref[:, columns].astype(F32)
        total = total + second_ref[:, columns].astype(F32)
        k_ref[pl.ds(h, rows, stride=heads), :] = total[:, :LANES]
        v_ref[pl.ds(h, rows, stride=heads), :] = total[:, LANES:]
    out_ref[:, :, :LANES] = k_ref[...].reshape(rows, heads, LANES)
    out_ref[:, :, LANES:] = v_ref[...].reshape(rows, heads, LANES)


def weight_sum(keep, first, second, total, chunk, all_heads):
    rows, columns = second.shape
    heads = columns // PAIR
    block = 32
    operands = [keep, first, second]
    in_specs = [pl.BlockSpec((block, columns), lambda i: (i, 0)) for _ in operands]
    aliases = {}
    if total is not None:
        aliases = {3: 0}
        in_specs.append(pl.BlockSpec(memory_space=pl.ANY))
        operands.append(total)
    return pl.pallas_call(
        weight_sum_kernel,
        grid=(rows // block,),
        in_specs=in_specs,
        out_specs=pl.BlockSpec((block, heads, PAIR), lambda i: (i, chunk, 0)),
        out_shape=jax.ShapeDtypeStruct((rows, all_heads, PAIR), F32),
        scratch_shapes=[pltpu.VMEM((block * heads, LANES), F32)] * 2,
        input_output_aliases=aliases,
        compiler_params=PARAMS,
        cost_estimate=cost(SUM),
        name="weight_sum",
    )(*operands)


def after(values, earlier):
    return lax.optimization_barrier((values, earlier))[0]


def turn_rows(block):
    rows, heads, width = block.shape
    count = min(rows, 256 // heads)
    row = lax.broadcasted_iota(jnp.int32, (count * heads, count * heads), 0)
    col = lax.broadcasted_iota(jnp.int32, (count * heads, count * heads), 1)
    order = (col == (row % count) * heads + row // count).astype(BF16)
    for start in range(0, rows, count):
        part = block[start : start + count].reshape(count * heads, width)
        turned = dot(order, part, 1, 0).astype(BF16)
        yield slice(start, start + count), turned.reshape(heads, count, width)


def in_hbm(array):
    return pltpu.with_memory_space_constraint(array, pltpu.HBM)


def turn_weight_kernel(here_ref, *refs):
    *parts, wt_ref = refs
    depth = parts[0].shape[0]
    for at, w_ref in enumerate(parts):
        for rows, turned in turn_rows(w_ref[...]):
            wt_ref[:, at * depth + rows.start : at * depth + rows.stop, :] = turned


def turn_weight(here, up_weight, heads):
    steps, parts = 4, 4
    depth = LAT // steps // parts
    part = lambda p: lambda i, here: (i * parts + p, here[0] & 1, 0)
    return pl.pallas_call(
        turn_weight_kernel,
        grid_spec=pltpu.PrefetchScalarGridSpec(
            num_scalar_prefetch=1,
            grid=(steps,),
            in_specs=[pl.BlockSpec((depth, heads, PAIR), part(p)) for p in range(parts)],
            out_specs=pl.BlockSpec((heads, depth * parts, PAIR), lambda i, here: (0, i, 0)),
        ),
        out_shape=jax.ShapeDtypeStruct((heads, LAT, PAIR), BF16),
        compiler_params=PARAMS,
        cost_estimate=cost(TURN),
        name="turn_weight",
    )(here, *[in_hbm(up_weight)] * parts)


def turn_tokens_kernel(here_ref, q1_ref, g1_ref, q0_ref, g0_ref, own_ref, give_ref, mine_ref):
    heads = mine_ref.shape[0]
    for q_ref, g_ref, out_ref in ((q1_ref, g1_ref, give_ref), (q0_ref, g0_ref, mine_ref)):
        out_ref[:, :, LANES : 2 * LANES] = jnp.zeros_like(out_ref[:, :, LANES : 2 * LANES])
        for rows, turned in turn_rows(q_ref[...]):
            out_ref[:heads, rows, : PLAIN_WIDTH + ROPE] = turned
        for rows, turned in turn_rows(g_ref[...]):
            out_ref[:heads, rows, 2 * LANES :] = turned
    rest = LAT + ROPE - 3 * LANES
    give_ref[heads] = own_ref[:, : 3 * LANES]
    give_ref[heads + 1] = jnp.zeros_like(give_ref[heads + 1])
    give_ref[heads + 1, :, :rest] = own_ref[:, 3 * LANES :]


def turn_tokens(here, queries, out_grad, latent_keys, heads):
    tok = queries.shape[0]
    q_block, g_block = (tok, heads, PLAIN_WIDTH + ROPE), (tok, heads, VDIM)
    given = lambda i, here: (0, 1 - (here[0] & 1), 0)
    kept = lambda i, here: (0, here[0] & 1, 0)
    whole = lambda i, here: (0, 0, 0)
    give, mine = (heads + 2, tok, 3 * LANES), (heads, tok, 3 * LANES)
    queries, out_grad, latent_keys = (in_hbm(x) for x in (queries, out_grad, latent_keys))
    return pl.pallas_call(
        turn_tokens_kernel,
        grid_spec=pltpu.PrefetchScalarGridSpec(
            num_scalar_prefetch=1,
            grid=(1,),
            in_specs=[
                pl.BlockSpec(q_block, given),
                pl.BlockSpec(g_block, given),
                pl.BlockSpec(q_block, kept),
                pl.BlockSpec(g_block, kept),
                pl.BlockSpec(latent_keys.shape, lambda i, here: (0, 0)),
            ],
            out_specs=[pl.BlockSpec(give, whole), pl.BlockSpec(mine, whole)],
        ),
        out_shape=[jax.ShapeDtypeStruct(give, BF16), jax.ShapeDtypeStruct(mine, BF16)],
        compiler_params=PARAMS,
        cost_estimate=cost(WINDOW),
        name="turn_tokens",
    )(here, queries, out_grad, queries, out_grad, latent_keys)


def chip_window_kernel(
    here_ref, even_ref, odd_ref, own_ref, pal_ref, ids_ref, win_ref, krope_ref, vis_ref, lat_ref
):
    here = here_ref[0]
    tok = own_ref.shape[0]
    core, chip = here & 1, here >> 1
    first = core == 0
    prev = jnp.where(first, even_ref[...].astype(F32), odd_ref[...].astype(F32)).astype(BF16)
    pal = jnp.concatenate([pal_ref[0], pal_ref[1, :, : LAT + ROPE - 3 * LANES]], 1).astype(F32)
    own = own_ref[...].astype(F32)
    low = jnp.where(first, own, pal).astype(BF16)
    high = jnp.where(first, pal, own).astype(BF16)
    krope_ref[...] = jnp.zeros_like(krope_ref)
    for at, block in enumerate((prev, low, high)):
        win_ref[at * tok : (at + 1) * tok, :] = block[:, :LAT]
        krope_ref[at * tok : (at + 1) * tok, :ROPE] = block[:, LAT:]
    behind = ids_ref[pl.ds(jnp.maximum(chip - 1, 0), 1), :]
    both = ids_ref[pl.ds(chip, 1), :]
    seg = [jnp.where(chip > 0, behind[:, tok:], -1), both[:, :tok], both[:, tok:]]
    row = lax.broadcasted_iota(jnp.int32, (tok, tok), 0)
    col = lax.broadcasted_iota(jnp.int32, (tok, tok), 1)
    for b in range(2):
        seg_query = jnp.sum(jnp.where(row == col, seg[b + 1], 0), 1, keepdims=True)
        vis_ref[b, :, :tok] = (seg_query == seg[b]).astype(F32)
        vis_ref[b, :, tok:] = ((seg_query == seg[b + 1]) & (col <= row)).astype(F32)
    column = lax.broadcasted_iota(jnp.int32, (LAT, LAT), 0)
    source = lax.broadcasted_iota(jnp.int32, (LAT, LAT), 1)
    place = column >> 6
    apart = ((place & 2) << 1) | ((place & 4) >> 1) | (place & 1)
    wanted = ((here ^ apart) << 6) | (column & 63)
    order = (source == wanted).astype(BF16)
    lat_ref[...] = dot(order, win_ref[...], 1, 1).astype(BF16)


def chip_window(here, even, odd, own, got, ids):
    tok = own.shape[0]
    whole = lambda i, here: (0, 0)
    return pl.pallas_call(
        chip_window_kernel,
        grid_spec=pltpu.PrefetchScalarGridSpec(
            num_scalar_prefetch=1,
            grid=(1,),
            in_specs=[pl.BlockSpec(array.shape, whole) for array in (even, odd, own)]
            + [
                pl.BlockSpec((2,) + got.shape[1:], lambda i, here: (got.shape[0] // 2 - 1, 0, 0)),
                pl.BlockSpec(ids.shape, whole),
            ],
            out_specs=[
                pl.BlockSpec((3 * tok, LAT), whole),
                pl.BlockSpec((3 * tok, LANES), whole),
                pl.BlockSpec((2, tok, 2 * tok), lambda i, here: (0, 0, 0)),
                pl.BlockSpec((LAT, 3 * tok), whole),
            ],
        ),
        out_shape=[
            jax.ShapeDtypeStruct((3 * tok, LAT), BF16),
            jax.ShapeDtypeStruct((3 * tok, LANES), BF16),
            jax.ShapeDtypeStruct((2, tok, 2 * tok), F32),
            jax.ShapeDtypeStruct((LAT, 3 * tok), BF16),
        ],
        compiler_params=PARAMS,
        cost_estimate=cost(WINDOW),
        name="chip_window",
    )(here, even, odd, own, got, ids)


def chunk_kernel(
    here_ref,
    win_ref,
    krope_ref,
    vis_ref,
    lat_ref,
    wt_ref,
    mine_ref,
    got_ref,
    *refs,
    chained,
    along_x,
):
    before_ref = refs[0] if chained else None
    refs = refs[3:] if chained else refs
    keep_ref, send_ref, key_ref, dq_ref, back_ref = refs

    @pl.when(pl.program_id(0) == 0)
    def _():
        key_ref[...] = before_ref[...] if chained else jnp.zeros_like(key_ref)

    tok = vis_ref.shape[1]
    heads = wt_ref.shape[0]
    first = (here_ref[0] & 1) == 0
    scale = 1.0 / math.sqrt(PLAIN_WIDTH + ROPE)
    window, krope = win_ref[...], krope_ref[...]
    visible = [vis_ref[b] > 0.0 for b in range(2)]
    keys, values, queries, grads = [], [], [], []
    for h in range(heads):
        kv = dot(window, wt_ref[h], 1, 0).astype(BF16)
        keys.append(jnp.concatenate([kv[:, :PLAIN_WIDTH], krope], 1))
        values.append(kv[:, PLAIN_WIDTH:])
        mine, got = mine_ref[h], got_ref[h]
        ordered = (jnp.where(first, mine, got), jnp.where(first, got, mine))
        queries.append([block[:, : 2 * LANES] for block in ordered])
        grads.append([block[:, 2 * LANES :] for block in ordered])
    reach = [slice(b * tok, (b + 2) * tok) for b in range(2)]
    units = [(h, b) for h in range(heads) for b in range(2)]
    scores = {(h, b): dot(queries[h][b], keys[h][reach[b]], 1, 1) for h, b in units}
    dprobs = {(h, b): dot(grads[h][b], values[h][reach[b]], 1, 1) for h, b in units}
    dscores, probs16 = {}, {}
    for unit in units:
        logits = jnp.where(visible[unit[1]], scores[unit] * scale, -1e30)
        top = jnp.max(logits, -1, keepdims=True)
        expo = jnp.exp(logits - top)
        probs = expo / jnp.sum(expo, -1, keepdims=True)
        delta = jnp.sum(probs * dprobs[unit], -1, keepdims=True)
        dscores[unit] = (probs * (dprobs[unit] - delta) * scale).astype(BF16)
        probs16[unit] = probs.astype(BF16)

    def fold(low, high):
        return jnp.concatenate([low[:tok], low[tok:] + high[:tok], high[tok:]], 0)

    parts, rope = [], None
    for h in range(heads):
        dk = fold(*[dot(dscores[h, b], queries[h][b], 0, 0) for b in range(2)])
        dv = fold(*[dot(probs16[h, b], grads[h][b], 0, 0) for b in range(2)])
        parts.append(jnp.concatenate([dk[:, :PLAIN_WIDTH], dv], 1).astype(BF16))
        rope = dk[:, PLAIN_WIDTH:] if rope is None else rope + dk[:, PLAIN_WIDTH:]
    dkv = jnp.concatenate(parts, 1)
    rows = lat_ref.shape[0] // 4
    kept = (0, 1) if along_x else (0, 2)
    sent = (2, 3) if along_x else (1, 3)
    for at, g in enumerate(sent):
        term = dot(lat_ref[g * rows : (g + 1) * rows, :], dkv, 1, 0)
        send_ref[at * rows : (at + 1) * rows, :] = term.astype(BF16)
    for at, g in enumerate(kept):
        keep_ref[at * rows : (at + 1) * rows, :] = dot(
            lat_ref[g * rows : (g + 1) * rows, :], dkv, 1, 0
        )
    total = key_ref[:, :LAT]
    for h in range(heads):
        total = total + dot(parts[h], wt_ref[h], 1, 1)
    key_ref[:, :LAT] = total
    key_ref[:, LAT:] = key_ref[:, LAT:] + rope
    for h in range(heads):
        low, high = (dot(dscores[h, b], keys[h][reach[b]], 1, 0) for b in range(2))
        dq_ref[h] = jnp.where(first, low, high)
        back_ref[h] = jnp.where(first, high, low)


def chunk(here, window, weight, mine, got, before, index, heads, along_x):
    tok = mine.shape[1]
    whole = lambda i, here: (0, 0)
    whole3 = lambda i, here: (0, 0, 0)
    step = min(heads, STEP_HEADS)
    steps = heads // step
    at = lambda i, here: (index * steps + i, 0, 0)
    across_columns = lambda i, here: (0, i)
    columns = heads * PAIR
    operands = [*window, weight, mine, got]
    in_specs = [
        pl.BlockSpec(array.shape, whole3 if array.ndim == 3 else whole) for array in window
    ] + [
        pl.BlockSpec((step, LAT, PAIR), at),
        pl.BlockSpec((step, tok, 3 * LANES), at),
        pl.BlockSpec((step, tok, 3 * LANES), at),
    ]
    aliases = {}
    if before is not None:
        key, dq, back = before
        aliases = {len(operands) + 2: 3, len(operands) + 3: 4}
        in_specs = in_specs + [
            pl.BlockSpec(key.shape, whole),
            pl.BlockSpec(memory_space=pl.ANY),
            pl.BlockSpec(memory_space=pl.ANY),
        ]
        operands = operands + [key, dq, back]
    turned = (weight.shape[0], tok, 2 * LANES)
    return pl.pallas_call(
        functools.partial(chunk_kernel, chained=before is not None, along_x=along_x),
        grid_spec=pltpu.PrefetchScalarGridSpec(
            num_scalar_prefetch=1,
            grid=(steps,),
            in_specs=in_specs,
            out_specs=[
                pl.BlockSpec((LAT // 2, step * PAIR), across_columns),
                pl.BlockSpec((LAT // 2, step * PAIR), across_columns),
                pl.BlockSpec((3 * tok, LAT + LANES), whole),
                pl.BlockSpec((step, tok, 2 * LANES), at),
                pl.BlockSpec((step, tok, 2 * LANES), at),
            ],
        ),
        out_shape=[
            jax.ShapeDtypeStruct((LAT // 2, columns), F32),
            jax.ShapeDtypeStruct((LAT // 2, columns), BF16),
            jax.ShapeDtypeStruct((3 * tok, LAT + LANES), F32),
            jax.ShapeDtypeStruct(turned, F32),
            jax.ShapeDtypeStruct(turned, F32),
        ],
        input_output_aliases=aliases,
        compiler_params=PARAMS,
        cost_estimate=cost(CHUNK),
        name="chunk",
    )(here, *operands)


def add_rows_kernel(*refs, count, wide):
    total = refs[0][...].astype(F32)
    for ref in refs[1 : count + wide]:
        total = total + ref[...].astype(F32)
    refs[-1][...] = total.astype(refs[-1].dtype)


def add_rows(arrays, rows, index, dtype, wide=(), place=0, places=1, before=None):
    columns = arrays[0].shape[1]
    operands = [*arrays, *wide]
    in_specs = [pl.BlockSpec((rows, columns), lambda i: (index, 0)) for _ in arrays]
    in_specs = in_specs + [pl.BlockSpec((rows, columns), lambda i: (index, place)) for _ in wide]
    aliases = {}
    if before is not None:
        aliases = {len(operands): 0}
        in_specs.append(pl.BlockSpec(memory_space=pl.ANY))
        operands.append(before)
    return pl.pallas_call(
        functools.partial(add_rows_kernel, count=len(arrays), wide=len(wide)),
        grid=(1,),
        in_specs=in_specs,
        out_specs=pl.BlockSpec((rows, columns), lambda i: (0, place)),
        out_shape=jax.ShapeDtypeStruct((rows, places * columns), dtype),
        input_output_aliases=aliases,
        compiler_params=PARAMS,
        cost_estimate=cost(SHARES),
        name="add_rows",
    )(*operands)


def key_split_kernel(here_ref, key_ref, keep_ref, give_ref):
    tok = keep_ref.shape[0] // 2
    first = (here_ref[0] & 1) == 0
    behind, low, high = (key_ref[b * tok : (b + 1) * tok, :] for b in range(3))
    keep_ref[:tok] = jnp.where(first, low, high)
    keep_ref[tok:] = behind
    give_ref[:tok] = jnp.where(first, high, low)
    give_ref[tok:] = behind


def key_split(here, key):
    rows = key.shape[0] // 3 * 2
    whole = lambda i, here: (0, 0)
    return pl.pallas_call(
        key_split_kernel,
        grid_spec=pltpu.PrefetchScalarGridSpec(
            num_scalar_prefetch=1,
            grid=(1,),
            in_specs=[pl.BlockSpec(key.shape, whole)],
            out_specs=[pl.BlockSpec((rows, key.shape[1]), whole)] * 2,
        ),
        out_shape=[jax.ShapeDtypeStruct((rows, key.shape[1]), F32)] * 2,
        compiler_params=PARAMS,
        cost_estimate=cost(SHARES),
        name="key_split",
    )(here, key)


def key_shares_kernel(at_ref, keep_ref, got_ref, *outs):
    shares = len(outs)
    part = (LAT + ROPE) // shares
    total = keep_ref[...] + got_ref[...]
    for z in range(shares):
        piece = total[:, z * part : (z + 1) * part]
        for s in range(shares):

            @pl.when(lax.rem(at_ref[0] + s, shares) == z)
            def _(s=s, piece=piece):
                outs[s][...] = piece.astype(outs[s].dtype)


def key_shares(at_head, keep, got, shares):
    part = (LAT + ROPE) // shares
    rows = keep.shape[0]
    whole = lambda i, at: (0, 0)
    types = [F32] + [BF16] * (shares - 1)
    return pl.pallas_call(
        key_shares_kernel,
        grid_spec=pltpu.PrefetchScalarGridSpec(
            num_scalar_prefetch=1,
            grid=(1,),
            in_specs=[pl.BlockSpec(keep.shape, whole)] * 2,
            out_specs=[pl.BlockSpec((rows, part), whole)] * shares,
        ),
        out_shape=[jax.ShapeDtypeStruct((rows, part), kind) for kind in types],
        compiler_params=PARAMS,
        cost_estimate=cost(SHARES),
        name="key_shares",
    )(at_head, keep, got)


def query_grad_kernel(here_ref, mine_ref, got_ref, out_ref, n_ref, r_ref):
    tok, heads, _ = out_ref.shape

    def put(src_ref):
        for h in range(heads):
            n_ref[pl.ds(h, tok, stride=heads), :] = src_ref[h, :, :PLAIN_WIDTH]
            r_ref[pl.ds(h, tok, stride=heads), :] = src_ref[h, :, PLAIN_WIDTH:]

    pl.when(pl.program_id(0) == 0)(lambda: put(mine_ref))
    pl.when(pl.program_id(0) == 1)(lambda: put(got_ref))
    out_ref[:, :, :PLAIN_WIDTH] = n_ref[...].reshape(tok, heads, LANES)
    out_ref[:, :, PLAIN_WIDTH:] = r_ref[...].reshape(tok, heads, LANES)[:, :, :ROPE]


def query_grad(here, mine, got):
    heads, tok, _ = mine.shape
    whole = lambda i, here: (0, 0, 0)
    return pl.pallas_call(
        query_grad_kernel,
        grid_spec=pltpu.PrefetchScalarGridSpec(
            num_scalar_prefetch=1,
            grid=(2,),
            in_specs=[pl.BlockSpec(mine.shape, whole)] * 2,
            out_specs=pl.BlockSpec(
                (tok, heads, PLAIN_WIDTH + ROPE), lambda i, here: (0, (here[0] & 1) ^ i, 0)
            ),
            scratch_shapes=[pltpu.VMEM((tok * heads, LANES), F32)] * 2,
        ),
        out_shape=jax.ShapeDtypeStruct((tok, 2 * heads, PLAIN_WIDTH + ROPE), F32),
        compiler_params=PARAMS,
        cost_estimate=cost(QUERY),
        name="query_grad",
    )(here, mine, got)


def weight_grad_kernel(here_ref, *refs, count):
    narrow, last_ref, got_ref = refs[: 2 * count], refs[2 * count], refs[2 * count + 1]
    out_ref, k_ref, v_ref = refs[-3:]
    rows, heads, _ = out_ref.shape
    each = heads // count

    def put(c, total):
        for h in range(each):
            at = pl.ds(c * each + h, rows, stride=heads)
            k_ref[at, :] = total[:, h * PAIR : h * PAIR + LANES]
            v_ref[at, :] = total[:, h * PAIR + LANES : (h + 1) * PAIR]

    for c in range(count):
        columns = slice(c * each * PAIR, (c + 1) * each * PAIR)

        @pl.when(pl.program_id(0) == 0)
        def _(c=c, columns=columns):
            keep_ref, first_ref = narrow[2 * c : 2 * c + 2]
            total = keep_ref[...] + first_ref[...].astype(F32)
            put(c, total + last_ref[:, columns].astype(F32))

        @pl.when(pl.program_id(0) == 1)
        def _(c=c, columns=columns):
            put(c, got_ref[:, columns])

    out_ref[:, :, :LANES] = k_ref[...].reshape(rows, heads, LANES)
    out_ref[:, :, LANES:] = v_ref[...].reshape(rows, heads, LANES)


def weight_grad_part(here, groups, last, got, total, part, parts):
    count = len(groups)
    rows, columns = got.shape
    heads = columns // PAIR
    operands = [array for group in groups for array in group] + [last, got]
    whole = lambda i, here: (0, 0)
    in_specs = [pl.BlockSpec((rows, columns // count), whole)] * (2 * count)
    in_specs = in_specs + [pl.BlockSpec((rows, columns), whole)] * 2
    aliases = {}
    if total is not None:
        aliases = {1 + len(operands): 0}
        in_specs.append(pl.BlockSpec(memory_space=pl.ANY))
        operands.append(total)
    return pl.pallas_call(
        functools.partial(weight_grad_kernel, count=count),
        grid_spec=pltpu.PrefetchScalarGridSpec(
            num_scalar_prefetch=1,
            grid=(2,),
            in_specs=in_specs,
            out_specs=pl.BlockSpec(
                (rows, heads, PAIR), lambda i, here: (0, ((here[0] & 1) ^ i) * parts + part, 0)
            ),
            scratch_shapes=[pltpu.VMEM((rows * heads, LANES), F32)] * 2,
        ),
        out_shape=jax.ShapeDtypeStruct((rows, 2 * parts * heads, PAIR), F32),
        input_output_aliases=aliases,
        compiler_params=PARAMS,
        cost_estimate=cost(SUM),
        name="weight_grad",
    )(here, *operands)


def in_chunks(queries, latent_keys, out_grad, up_weight, here, at_head, ids):
    tok = latent_keys.shape[0]
    n_ctx, n_head = lax.axis_size("ctx"), lax.axis_size("head")
    heads, each = 16, 4
    queries = after(queries, (ids, here, at_head))
    give, mine = turn_tokens(here, queries, out_grad, latent_keys, heads)
    odd_devices = range(1, n_ctx - 1, 2)
    even = lax.ppermute(latent_keys, "ctx", [(source, source + 1) for source in odd_devices])
    odd = lax.ppermute(latent_keys, "ctx", [(source, source + 2) for source in odd_devices])
    got = across(give, 1)
    weight = turn_weight(here, up_weight, heads)
    window = chip_window(here, even, odd, latent_keys, got, ids)
    ways, blocks = ((2, 4), (4, 2)), (0, 2, 1, 3)
    before, keeps, sent = None, [], []
    for c, block in enumerate(blocks):
        keep, out, *before = chunk(
            here, window, weight, mine, got, before, block, each, c % 2 == 0
        )
        keeps.append(keep)
        sent.append(across(out, ways[c % 2][0]))
    key, dq, back = before

    def rest(c, earlier):
        return add_rows(
            (keeps[c], sent[c]), 2 * tok, 1, BF16, place=c // 2, places=2, before=earlier
        )

    key_keep, key_give = key_split(here, key)
    key_got = across(key_give, 1)
    rests = [rest(0, None)]
    keeps[1] = after(keeps[1], rests[0])
    rests.append(rest(1, None))
    key_got = after(key_got, rests)
    shares = key_shares(at_head, key_keep, key_got, n_head)
    pieces = [
        lax.ppermute(shares[s], "head", [(z, (z + s) % n_head) for z in range(n_head)])
        for s in range(1, n_head)
    ]
    back = across(after(back, key_keep), 1)
    share, behind = (add_rows((shares[0], *pieces), tok, b, F32) for b in range(2))
    keeps[2] = after(keeps[2], (share, behind))
    behind = lax.ppermute(behind, "ctx", [(source, source - 1) for source in range(2, n_ctx, 2)])
    rests = [rest(2, rests[0]), rest(3, rests[1])]
    lasts = [across(rests[p], ways[p][1]) for p in range(2)]
    dq = query_grad(here, after(dq, rests), back)
    key_grad = add_rows((after(share, dq), behind), tok, 0, F32)
    keeps[0] = after(keeps[0], key_grad)
    theirs = []
    for p in range(2):
        total = None
        for place, c in enumerate((p, p + 2)):
            total = add_rows(
                (keeps[c], sent[c]),
                tok,
                1,
                F32,
                wide=(lasts[p],),
                place=place,
                places=2,
                before=total,
            )
        theirs.append(across(total, 1))
    weight_grad = None
    for p in range(2):
        groups = [(keeps[c], sent[c]) for c in (p, p + 2)]
        weight_grad = weight_grad_part(here, groups, lasts[p], theirs[p], weight_grad, p, 2)
    return dq, key_grad, weight_grad


def shards(queries, latent_keys, out_grad, up_weight, segment_ids):
    tok = latent_keys.shape[0]
    heads = queries.shape[1]
    n_ctx, n_head = lax.axis_size("ctx"), lax.axis_size("head")
    here = lax.axis_index("ctx").astype(jnp.int32).reshape(1)
    at_head = lax.axis_index("head").astype(jnp.int32).reshape(1)
    if n_ctx == 8 and heads == 32 and n_head == 4:
        ids = segment_ids.reshape(n_ctx // 2, 2 * tok)
        return in_chunks(queries, latent_keys, out_grad, up_weight, here, at_head, ids)
    else:
        ids = segment_ids.reshape(n_ctx, tok)
        prev = from_behind(latent_keys, "ctx", REACH)
        turned = by_head(up_weight, queries, out_grad, 0, heads)
        window = key_window(here, prev, latent_keys, ids, False)
        dq, dkv, rope = attention(window, turned, None, None, 0, heads, 0, heads)
        (both,) = key_terms(at_head, [dkv], [turned[0]], [rope], None)
        share = lax.psum_scatter(
            both.reshape(REACH + 1, tok, LAT + ROPE), "head", scatter_dimension=2, tiled=True
        )
        term = jnp.einsum("ki,ke->ie", window[0], dkv, preferred_element_type=F32)
        rows = lax.psum_scatter(term.astype(BF16), "ctx", scatter_dimension=0, tiled=True)
        weight_grad = rows.astype(F32).reshape(rows.shape[0], heads, PAIR)
    key_grad = share[REACH] + from_behind(share[0], "ctx", 0 - REACH)
    return (dq, key_grad, weight_grad)


def solution(mesh):
    return jax.shard_map(
        shards,
        mesh=mesh,
        in_specs=(
            P("ctx", "head", None),
            P("ctx", None),
            P("ctx", "head", None),
            P(None, "head", None),
            P(),
        ),
        out_specs=(P("ctx", "head", None), P("ctx", "head"), P("ctx", "head", None)),
        check_vma=False,
    )
```

```python
import functools
import math

import jax
import jax.numpy as jnp
from jax import lax
from jax.experimental import pallas as pl
from jax.experimental.pallas import tpu as pltpu
from jax.sharding import PartitionSpec as P

LAT = 512
ROPE = 64
PLAIN_WIDTH = 128
VDIM = 128
REACH = 1
LANES = 128
PAIR = PLAIN_WIDTH + VDIM
STEP_HEADS = 4
BF16 = jnp.bfloat16
F32 = jnp.float32
WIDE = pltpu.CompilerParams(vmem_limit_bytes=56 * 1024 * 1024)
PARAMS = pltpu.CompilerParams(vmem_limit_bytes=20 * 1024 * 1024)


def from_behind(value, axis, steps):
    count = lax.axis_size(axis)
    initial, last = (max(0, -steps), min(count, count - steps))
    return lax.ppermute(value, axis, [(source, source + steps) for source in range(initial, last)])


def across(value, bit):
    count = lax.axis_size("ctx")
    return lax.ppermute(value, "ctx", [(source, source ^ bit) for source in range(count)])


def cost(share):
    return pl.CostEstimate(flops=int(share * 1e9), bytes_accessed=1024, transcendentals=0)


TURN, WINDOW, CHUNK, SHARES, QUERY, SUM = 3.0, 0.5, 1.5, 0.1, 0.1, 0.1


def dot(a, b, a_dim, b_dim):
    return lax.dot_general(a, b, (((a_dim,), (b_dim,)), ((), ())), preferred_element_type=F32)


def by_head_kernel(w_ref, q_ref, g_ref, wt_ref, qt_ref, gt_ref):
    heads = w_ref.shape[1]
    orders = {}

    def order(count):
        if count not in orders:
            size = count * heads
            row = lax.broadcasted_iota(jnp.int32, (size, size), 0)
            col = lax.broadcasted_iota(jnp.int32, (size, size), 1)
            wanted = (row % count) * heads + row // count
            orders[count] = (col == wanted).astype(BF16)
        return orders[count]

    def turn(ref, out_ref):
        rows, _, width = ref.shape
        count = min(rows, 256 // heads)
        for start in range(0, rows, count):
            block = ref[start : start + count].reshape(count * heads, width)
            turned = dot(order(count), block, 1, 0).astype(BF16)
            out_ref[:, start : start + count, :width] = turned.reshape(heads, count, width)

    turn(w_ref, wt_ref)
    qt_ref[...] = jnp.zeros_like(qt_ref)
    turn(q_ref, qt_ref)
    turn(g_ref, gt_ref)


def by_head(up_weight, queries, out_grad, chunk, heads):
    tok = queries.shape[0]
    steps = 4
    depth, rows = LAT // steps, tok // steps
    return pl.pallas_call(
        by_head_kernel,
        grid=(steps,),
        in_specs=[
            pl.BlockSpec((depth, heads, PAIR), lambda i: (i, chunk, 0)),
            pl.BlockSpec((rows, heads, PLAIN_WIDTH + ROPE), lambda i: (i, chunk, 0)),
            pl.BlockSpec((rows, heads, VDIM), lambda i: (i, chunk, 0)),
        ],
        out_specs=[
            pl.BlockSpec((heads, depth, PAIR), lambda i: (0, i, 0)),
            pl.BlockSpec((heads, rows, 2 * LANES), lambda i: (0, i, 0)),
            pl.BlockSpec((heads, rows, VDIM), lambda i: (0, i, 0)),
        ],
        out_shape=[
            jax.ShapeDtypeStruct((heads, LAT, PAIR), BF16),
            jax.ShapeDtypeStruct((heads, tok, 2 * LANES), BF16),
            jax.ShapeDtypeStruct((heads, tok, VDIM), BF16),
        ],
        compiler_params=WIDE,
        cost_estimate=cost(TURN),
        name="by_head",
    )(up_weight, queries, out_grad)


def window_kernel(here_ref, prev_ref, own_ref, ids_ref, *outs, paired):
    win_ref, krope_ref, vis_ref = outs[:3]
    here = here_ref[0]
    tok = prev_ref.shape[0]
    win_ref[:tok, :] = prev_ref[:, :LAT]
    win_ref[tok:, :] = own_ref[:, :LAT]
    krope_ref[...] = jnp.zeros_like(krope_ref)
    krope_ref[:tok, :ROPE] = prev_ref[:, LAT:]
    krope_ref[tok:, :ROPE] = own_ref[:, LAT:]
    behind = jnp.maximum(here - 1, 0)
    seg_prev = jnp.where(here > 0, ids_ref[pl.ds(behind, 1), :], -1)
    seg_own = ids_ref[pl.ds(here, 1), :]
    row = lax.broadcasted_iota(jnp.int32, (tok, tok), 0)
    col = lax.broadcasted_iota(jnp.int32, (tok, tok), 1)
    seg_query = jnp.sum(jnp.where(row == col, seg_own, 0), 1, keepdims=True)
    vis_ref[:, :tok] = (seg_query == seg_prev).astype(F32)
    vis_ref[:, tok:] = ((seg_query == seg_own) & (col <= row)).astype(F32)
    if paired:
        source = lax.broadcasted_iota(jnp.int32, (LAT, LAT), 0)
        column = lax.broadcasted_iota(jnp.int32, (LAT, LAT), 1)
        place = column >> 6
        apart = ((place & 1) << 2) | (place & 2) | (place >> 2)
        wanted = ((here ^ apart) << 6) | (column & 63)
        ordered = dot(win_ref[...], (source == wanted).astype(BF16), 1, 0).astype(BF16)
        outs[3][...] = ordered[:, : LAT // 2]
        outs[4][...] = ordered[:, LAT // 2 :]


def key_window(here, prev, own, ids, paired):
    tok = prev.shape[0]
    whole = lambda i, here: (0, 0)
    shapes = [((2 * tok, LAT), BF16), ((2 * tok, LANES), BF16), ((tok, 2 * tok), F32)]
    if paired:
        shapes = shapes + [((2 * tok, LAT // 2), BF16)] * 2
    return pl.pallas_call(
        functools.partial(window_kernel, paired=paired),
        grid_spec=pltpu.PrefetchScalarGridSpec(
            num_scalar_prefetch=1,
            grid=(1,),
            in_specs=[pl.BlockSpec(array.shape, whole) for array in (prev, own, ids)],
            out_specs=[pl.BlockSpec(shape, whole) for shape, _ in shapes],
        ),
        out_shape=[jax.ShapeDtypeStruct(*shape) for shape in shapes],
        compiler_params=PARAMS,
        cost_estimate=cost(WINDOW),
        name="key_window",
    )(here, prev, own, ids)


def attention_kernel(
    win_ref, krope_ref, vis_ref, wt_ref, qt_ref, gt_ref, *refs, aliased, extra
):
    latents_ref = refs[0] if extra else None
    refs = refs[1:] if extra else refs
    refs = refs[1:] if aliased else refs
    dq_ref, dkv_ref, rope_ref, dqn_ref, dqr_ref = refs
    i = pl.program_id(0)
    tok, heads = dq_ref.shape[:2]
    scale = 1.0 / math.sqrt(PLAIN_WIDTH + ROPE)

    @pl.when(i == 0)
    def _():
        rope_ref[...] = jnp.zeros_like(rope_ref)
        if extra:
            dkv_ref[:, heads * PAIR :] = latents_ref[...]

    visible = vis_ref[...] > 0.0
    window = win_ref[...]
    krope = krope_ref[...]
    count = wt_ref.shape[0]
    keys, values = [], []
    for h in range(count):
        kv = dot(window, wt_ref[h], 1, 0).astype(BF16)
        keys.append(jnp.concatenate([kv[:, :PLAIN_WIDTH], krope], 1))
        values.append(kv[:, PLAIN_WIDTH:])
    scores = [dot(qt_ref[h], keys[h], 1, 1) for h in range(count)]
    dprobs = [dot(gt_ref[h], values[h], 1, 1) for h in range(count)]
    dscores, probs16 = [], []
    for h in range(count):
        logits = jnp.where(visible, scores[h] * scale, -1e30)
        top = jnp.max(logits, -1, keepdims=True)
        expo = jnp.exp(logits - top)
        probs = expo / jnp.sum(expo, -1, keepdims=True)
        delta = jnp.sum(probs * dprobs[h], -1, keepdims=True)
        dscores.append((probs * (dprobs[h] - delta) * scale).astype(BF16))
        probs16.append(probs.astype(BF16))
    parts, rope = [], rope_ref[...]
    for h in range(count):
        dk = dot(dscores[h], qt_ref[h], 0, 0)
        dv = dot(probs16[h], gt_ref[h], 0, 0)
        parts.append(jnp.concatenate([dk[:, :PLAIN_WIDTH], dv], 1).astype(BF16))
        rope = rope + dk[:, PLAIN_WIDTH:]
    rope_ref[...] = rope
    dkv_ref[:, pl.ds(pl.multiple_of(i * (count * PAIR), count * PAIR), count * PAIR)] = (
        jnp.concatenate(parts, 1)
    )
    for h in range(count):
        dq = dot(dscores[h], keys[h], 1, 0)
        dqn_ref[pl.ds(i * count + h, tok, stride=heads), :] = dq[:, :PLAIN_WIDTH]
        dqr_ref[pl.ds(i * count + h, tok, stride=heads), :] = dq[:, PLAIN_WIDTH:]

    @pl.when(i == pl.num_programs(0) - 1)
    def _():
        dq_ref[:, :, :PLAIN_WIDTH] = dqn_ref[...].reshape(tok, heads, LANES)
        dq_ref[:, :, PLAIN_WIDTH:] = dqr_ref[...].reshape(tok, heads, LANES)[:, :, :ROPE]


def attention(window, turned, latents, dq, chunk, heads, first, all_heads):
    weight, queries, out_grad = turned
    tok = queries.shape[1]
    width = 2 * tok
    steps = heads // STEP_HEADS
    at = first // STEP_HEADS
    extra = LAT // 2 if latents is not None else 0
    whole = lambda i: (0, 0)
    head_block = lambda i: (at + i, 0, 0)
    operands = [*window, weight, queries, out_grad]
    in_specs = [pl.BlockSpec(array.shape, whole) for array in window] + [
        pl.BlockSpec((STEP_HEADS, LAT, PAIR), head_block),
        pl.BlockSpec((STEP_HEADS, tok, 2 * LANES), head_block),
        pl.BlockSpec((STEP_HEADS, tok, VDIM), head_block),
    ]
    if latents is not None:
        in_specs.append(pl.BlockSpec(latents.shape, whole))
        operands.append(latents)
    aliases = {}
    if dq is not None:
        aliases = {len(operands): 0}
        in_specs.append(pl.BlockSpec(memory_space=pl.ANY))
        operands.append(dq)
    return pl.pallas_call(
        functools.partial(attention_kernel, aliased=dq is not None, extra=latents is not None),
        grid=(steps,),
        in_specs=in_specs,
        out_specs=[
            pl.BlockSpec((tok, heads, PLAIN_WIDTH + ROPE), lambda i: (0, chunk, 0)),
            pl.BlockSpec((width, heads * PAIR + extra), whole),
            pl.BlockSpec((width, LANES), whole),
        ],
        scratch_shapes=[
            pltpu.VMEM((tok * heads, LANES), F32),
            pltpu.VMEM((tok * heads, LANES), F32),
        ],
        out_shape=[
            jax.ShapeDtypeStruct((tok, all_heads, PLAIN_WIDTH + ROPE), F32),
            jax.ShapeDtypeStruct((width, heads * PAIR + extra), BF16),
            jax.ShapeDtypeStruct((width, LANES), F32),
        ],
        input_output_aliases=aliases,
        compiler_params=WIDE,
        cost_estimate=cost(CHUNK),
        name="attention",
    )(*operands)


def terms_kernel(
    own_ref, other_ref, mine_ref, theirs_ref, keep_ref, send_ref, latents_ref, *, along_x
):
    width = own_ref.shape[0]

    @pl.when(pl.program_id(0) == 0)
    def _():
        latents_ref[:, :width] = mine_ref[...].T
        latents_ref[:, width:] = theirs_ref[...].T

    grads = jnp.concatenate([own_ref[...], other_ref[...]], 0)
    term = dot(latents_ref[...], grads, 1, 0)
    rows = term.shape[0] // 4
    first, second = (1, 2) if along_x else (2, 1)
    keep_ref[:rows] = term[:rows]
    keep_ref[rows:] = term[first * rows : (first + 1) * rows]
    send_ref[:rows] = term[second * rows : (second + 1) * rows].astype(BF16)
    send_ref[rows:] = term[3 * rows :].astype(BF16)


def terms(own, other, mine, theirs, columns, along_x):
    width = own.shape[0]
    block = 1024
    at = theirs.shape[1] // (LAT // 2) - 1
    column_block = lambda i: (0, i)
    return pl.pallas_call(
        functools.partial(terms_kernel, along_x=along_x),
        grid=(columns // block,),
        in_specs=[
            pl.BlockSpec((width, block), column_block),
            pl.BlockSpec((width, block), column_block),
            pl.BlockSpec((width, LAT // 2), lambda i: (0, 0)),
            pl.BlockSpec((width, LAT // 2), lambda i: (0, at)),
        ],
        out_specs=[pl.BlockSpec((LAT // 4, block), column_block)] * 2,
        out_shape=[
            jax.ShapeDtypeStruct((LAT // 4, columns), F32),
            jax.ShapeDtypeStruct((LAT // 4, columns), BF16),
        ],
        scratch_shapes=[pltpu.VMEM((LAT // 2, 2 * width), BF16)],
        compiler_params=PARAMS,
        cost_estimate=cost(CHUNK),
        name="terms",
    )(own, other, mine, theirs)


def key_terms_kernel(*refs, chunks, steps, turns, shares):
    head_ref = refs[0]
    dkv_refs = refs[1 : 1 + chunks]
    wt_refs = refs[1 + chunks : 1 + chunks + turns]
    rope_refs = refs[1 + chunks + turns : 1 + 2 * chunks + turns]
    outs = refs[1 + 2 * chunks + turns : -1]
    total_ref = refs[-1]
    i = pl.program_id(0)

    @pl.when(i == 0)
    def _():
        total_ref[...] = jnp.zeros_like(total_ref)

    for k in range(chunks):

        @pl.when(i // steps == k)
        def _(k=k):
            total = total_ref[...]
            weight_ref = wt_refs[k * turns // chunks]
            for h in range(weight_ref.shape[0]):
                grads = dkv_refs[k][:, h * PAIR : (h + 1) * PAIR]
                total = total + dot(grads, weight_ref[h], 1, 1)
            total_ref[...] = total

    @pl.when(i == pl.num_programs(0) - 1)
    def _():
        rope = rope_refs[0][...]
        for k in range(1, chunks):
            rope = rope + rope_refs[k][...]
        both = jnp.concatenate([total_ref[...], rope], 1)
        if shares is None:
            outs[0][...] = both[:, : LAT + ROPE]
            return
        part = (LAT + ROPE) // shares
        for z in range(shares):
            piece = both[:, z * part : (z + 1) * part]
            for s in range(shares):

                @pl.when(lax.rem(head_ref[0] + s, shares) == z)
                def _(s=s, piece=piece):
                    outs[s][...] = piece


def key_terms(at_head, dkvs, weights, ropes, shares):
    chunks, turns = len(dkvs), len(weights)
    heads = weights[0].shape[0] * turns // chunks
    width = dkvs[0].shape[0]
    steps = heads // STEP_HEADS
    span = steps * chunks // turns
    near = lambda k, many: lambda i, at: jnp.clip(i - k * many, 0, many - 1)
    wide = (LAT + ROPE) // (shares or 1)
    return pl.pallas_call(
        functools.partial(
            key_terms_kernel, chunks=chunks, steps=steps, turns=turns, shares=shares
        ),
        grid_spec=pltpu.PrefetchScalarGridSpec(
            num_scalar_prefetch=1,
            grid=(chunks * steps,),
            in_specs=[
                pl.BlockSpec((width, STEP_HEADS * PAIR), lambda i, at, k=k: (0, near(k, steps)(i, at)))
                for k in range(chunks)
            ]
            + [
                pl.BlockSpec(
                    (STEP_HEADS, LAT, PAIR), lambda i, at, k=k: (near(k, span)(i, at), 0, 0)
                )
                for k in range(turns)
            ]
            + [pl.BlockSpec((width, LANES), lambda i, at: (0, 0))] * chunks,
            out_specs=[pl.BlockSpec((width, wide), lambda i, at: (0, 0))] * (shares or 1),
            scratch_shapes=[pltpu.VMEM((width, LAT), F32)],
        ),
        out_shape=[jax.ShapeDtypeStruct((width, wide), F32)] * (shares or 1),
        compiler_params=WIDE,
        cost_estimate=cost(CHUNK),
        name="key_terms",
    )(at_head, *dkvs, *weights, *ropes)


def weight_sum_kernel(keep_ref, first_ref, second_ref, *refs):
    out_ref, k_ref, v_ref = refs[-3:]
    rows, heads, _ = out_ref.shape
    for h in range(heads):
        columns = slice(h * PAIR, (h + 1) * PAIR)
        total = keep_ref[:, columns] + first_ref[:, columns].astype(F32)
        total = total + second_ref[:, columns].astype(F32)
        k_ref[pl.ds(h, rows, stride=heads), :] = total[:, :LANES]
        v_ref[pl.ds(h, rows, stride=heads), :] = total[:, LANES:]
    out_ref[:, :, :LANES] = k_ref[...].reshape(rows, heads, LANES)
    out_ref[:, :, LANES:] = v_ref[...].reshape(rows, heads, LANES)


def weight_sum(keep, first, second, total, chunk, all_heads):
    rows, columns = second.shape
    heads = columns // PAIR
    block = 32
    operands = [keep, first, second]
    in_specs = [pl.BlockSpec((block, columns), lambda i: (i, 0)) for _ in operands]
    aliases = {}
    if total is not None:
        aliases = {3: 0}
        in_specs.append(pl.BlockSpec(memory_space=pl.ANY))
        operands.append(total)
    return pl.pallas_call(
        weight_sum_kernel,
        grid=(rows // block,),
        in_specs=in_specs,
        out_specs=pl.BlockSpec((block, heads, PAIR), lambda i: (i, chunk, 0)),
        out_shape=jax.ShapeDtypeStruct((rows, all_heads, PAIR), F32),
        scratch_shapes=[pltpu.VMEM((block * heads, LANES), F32)] * 2,
        input_output_aliases=aliases,
        compiler_params=PARAMS,
        cost_estimate=cost(SUM),
        name="weight_sum",
    )(*operands)


def after(values, earlier):
    return lax.optimization_barrier((values, earlier))[0]


def turn_rows(block):
    rows, heads, width = block.shape
    count = min(rows, 256 // heads)
    row = lax.broadcasted_iota(jnp.int32, (count * heads, count * heads), 0)
    col = lax.broadcasted_iota(jnp.int32, (count * heads, count * heads), 1)
    order = (col == (row % count) * heads + row // count).astype(BF16)
    for start in range(0, rows, count):
        part = block[start : start + count].reshape(count * heads, width)
        turned = dot(order, part, 1, 0).astype(BF16)
        yield slice(start, start + count), turned.reshape(heads, count, width)


def in_hbm(array):
    return pltpu.with_memory_space_constraint(array, pltpu.HBM)


def turn_weight_kernel(here_ref, *refs):
    *parts, wt_ref = refs
    depth = parts[0].shape[0]
    for at, w_ref in enumerate(parts):
        for rows, turned in turn_rows(w_ref[...]):
            wt_ref[:, at * depth + rows.start : at * depth + rows.stop, :] = turned


def turn_weight(here, up_weight, heads):
    steps, parts = 4, 4
    depth = LAT // steps // parts
    part = lambda p: lambda i, here: (i * parts + p, here[0] & 1, 0)
    return pl.pallas_call(
        turn_weight_kernel,
        grid_spec=pltpu.PrefetchScalarGridSpec(
            num_scalar_prefetch=1,
            grid=(steps,),
            in_specs=[pl.BlockSpec((depth, heads, PAIR), part(p)) for p in range(parts)],
            out_specs=pl.BlockSpec((heads, depth * parts, PAIR), lambda i, here: (0, i, 0)),
        ),
        out_shape=jax.ShapeDtypeStruct((heads, LAT, PAIR), BF16),
        compiler_params=PARAMS,
        cost_estimate=cost(TURN),
        name="turn_weight",
    )(here, *[in_hbm(up_weight)] * parts)


def turn_tokens_kernel(here_ref, q1_ref, g1_ref, q0_ref, g0_ref, own_ref, give_ref, mine_ref):
    heads = mine_ref.shape[0]
    for q_ref, g_ref, out_ref in ((q1_ref, g1_ref, give_ref), (q0_ref, g0_ref, mine_ref)):
        out_ref[:, :, LANES : 2 * LANES] = jnp.zeros_like(out_ref[:, :, LANES : 2 * LANES])
        for rows, turned in turn_rows(q_ref[...]):
            out_ref[:heads, rows, : PLAIN_WIDTH + ROPE] = turned
        for rows, turned in turn_rows(g_ref[...]):
            out_ref[:heads, rows, 2 * LANES :] = turned
    rest = LAT + ROPE - 3 * LANES
    give_ref[heads] = own_ref[:, : 3 * LANES]
    give_ref[heads + 1] = jnp.zeros_like(give_ref[heads + 1])
    give_ref[heads + 1, :, :rest] = own_ref[:, 3 * LANES :]


def turn_tokens(here, queries, out_grad, latent_keys, heads):
    tok = queries.shape[0]
    q_block, g_block = (tok, heads, PLAIN_WIDTH + ROPE), (tok, heads, VDIM)
    given = lambda i, here: (0, 1 - (here[0] & 1), 0)
    kept = lambda i, here: (0, here[0] & 1, 0)
    whole = lambda i, here: (0, 0, 0)
    give, mine = (heads + 2, tok, 3 * LANES), (heads, tok, 3 * LANES)
    queries, out_grad, latent_keys = (in_hbm(x) for x in (queries, out_grad, latent_keys))
    return pl.pallas_call(
        turn_tokens_kernel,
        grid_spec=pltpu.PrefetchScalarGridSpec(
            num_scalar_prefetch=1,
            grid=(1,),
            in_specs=[
                pl.BlockSpec(q_block, given),
                pl.BlockSpec(g_block, given),
                pl.BlockSpec(q_block, kept),
                pl.BlockSpec(g_block, kept),
                pl.BlockSpec(latent_keys.shape, lambda i, here: (0, 0)),
            ],
            out_specs=[pl.BlockSpec(give, whole), pl.BlockSpec(mine, whole)],
        ),
        out_shape=[jax.ShapeDtypeStruct(give, BF16), jax.ShapeDtypeStruct(mine, BF16)],
        compiler_params=PARAMS,
        cost_estimate=cost(WINDOW),
        name="turn_tokens",
    )(here, queries, out_grad, queries, out_grad, latent_keys)


def chip_window_kernel(
    here_ref, even_ref, odd_ref, own_ref, pal_ref, ids_ref, win_ref, krope_ref, vis_ref, lat_ref
):
    here = here_ref[0]
    tok = own_ref.shape[0]
    core, chip = here & 1, here >> 1
    first = core == 0
    prev = jnp.where(first, even_ref[...].astype(F32), odd_ref[...].astype(F32)).astype(BF16)
    pal = jnp.concatenate([pal_ref[0], pal_ref[1, :, : LAT + ROPE - 3 * LANES]], 1).astype(F32)
    own = own_ref[...].astype(F32)
    low = jnp.where(first, own, pal).astype(BF16)
    high = jnp.where(first, pal, own).astype(BF16)
    krope_ref[...] = jnp.zeros_like(krope_ref)
    for at, block in enumerate((prev, low, high)):
        win_ref[at * tok : (at + 1) * tok, :] = block[:, :LAT]
        krope_ref[at * tok : (at + 1) * tok, :ROPE] = block[:, LAT:]
    behind = ids_ref[pl.ds(jnp.maximum(chip - 1, 0), 1), :]
    both = ids_ref[pl.ds(chip, 1), :]
    seg = [jnp.where(chip > 0, behind[:, tok:], -1), both[:, :tok], both[:, tok:]]
    row = lax.broadcasted_iota(jnp.int32, (tok, tok), 0)
    col = lax.broadcasted_iota(jnp.int32, (tok, tok), 1)
    for b in range(2):
        seg_query = jnp.sum(jnp.where(row == col, seg[b + 1], 0), 1, keepdims=True)
        vis_ref[b, :, :tok] = (seg_query == seg[b]).astype(F32)
        vis_ref[b, :, tok:] = ((seg_query == seg[b + 1]) & (col <= row)).astype(F32)
    column = lax.broadcasted_iota(jnp.int32, (LAT, LAT), 0)
    source = lax.broadcasted_iota(jnp.int32, (LAT, LAT), 1)
    place = column >> 6
    apart = ((place & 1) << 2) | (place & 2) | (place >> 2)
    wanted = ((here ^ apart) << 6) | (column & 63)
    order = (source == wanted).astype(BF16)
    lat_ref[...] = dot(order, win_ref[...], 1, 1).astype(BF16)


def chip_window(here, even, odd, own, got, ids):
    tok = own.shape[0]
    whole = lambda i, here: (0, 0)
    return pl.pallas_call(
        chip_window_kernel,
        grid_spec=pltpu.PrefetchScalarGridSpec(
            num_scalar_prefetch=1,
            grid=(1,),
            in_specs=[pl.BlockSpec(array.shape, whole) for array in (even, odd, own)]
            + [
                pl.BlockSpec((2,) + got.shape[1:], lambda i, here: (got.shape[0] // 2 - 1, 0, 0)),
                pl.BlockSpec(ids.shape, whole),
            ],
            out_specs=[
                pl.BlockSpec((3 * tok, LAT), whole),
                pl.BlockSpec((3 * tok, LANES), whole),
                pl.BlockSpec((2, tok, 2 * tok), lambda i, here: (0, 0, 0)),
                pl.BlockSpec((LAT, 3 * tok), whole),
            ],
        ),
        out_shape=[
            jax.ShapeDtypeStruct((3 * tok, LAT), BF16),
            jax.ShapeDtypeStruct((3 * tok, LANES), BF16),
            jax.ShapeDtypeStruct((2, tok, 2 * tok), F32),
            jax.ShapeDtypeStruct((LAT, 3 * tok), BF16),
        ],
        compiler_params=PARAMS,
        cost_estimate=cost(WINDOW),
        name="chip_window",
    )(here, even, odd, own, got, ids)


def chunk_kernel(
    here_ref,
    win_ref,
    krope_ref,
    vis_ref,
    lat_ref,
    wt_ref,
    mine_ref,
    got_ref,
    *refs,
    chained,
    along_x,
):
    before_ref = refs[0] if chained else None
    refs = refs[3:] if chained else refs
    keep_ref, send_ref, key_ref, dq_ref, back_ref = refs

    @pl.when(pl.program_id(0) == 0)
    def _():
        key_ref[...] = before_ref[...] if chained else jnp.zeros_like(key_ref)

    tok = vis_ref.shape[1]
    heads = wt_ref.shape[0]
    first = (here_ref[0] & 1) == 0
    scale = 1.0 / math.sqrt(PLAIN_WIDTH + ROPE)
    window, krope = win_ref[...], krope_ref[...]
    visible = [vis_ref[b] > 0.0 for b in range(2)]
    keys, values, queries, grads = [], [], [], []
    for h in range(heads):
        kv = dot(window, wt_ref[h], 1, 0).astype(BF16)
        keys.append(jnp.concatenate([kv[:, :PLAIN_WIDTH], krope], 1))
        values.append(kv[:, PLAIN_WIDTH:])
        mine, got = mine_ref[h], got_ref[h]
        ordered = (jnp.where(first, mine, got), jnp.where(first, got, mine))
        queries.append([block[:, : 2 * LANES] for block in ordered])
        grads.append([block[:, 2 * LANES :] for block in ordered])
    reach = [slice(b * tok, (b + 2) * tok) for b in range(2)]
    units = [(h, b) for h in range(heads) for b in range(2)]
    scores = {(h, b): dot(queries[h][b], keys[h][reach[b]], 1, 1) for h, b in units}
    dprobs = {(h, b): dot(grads[h][b], values[h][reach[b]], 1, 1) for h, b in units}
    dscores, probs16 = {}, {}
    for unit in units:
        logits = jnp.where(visible[unit[1]], scores[unit] * scale, -1e30)
        top = jnp.max(logits, -1, keepdims=True)
        expo = jnp.exp(logits - top)
        probs = expo / jnp.sum(expo, -1, keepdims=True)
        delta = jnp.sum(probs * dprobs[unit], -1, keepdims=True)
        dscores[unit] = (probs * (dprobs[unit] - delta) * scale).astype(BF16)
        probs16[unit] = probs.astype(BF16)

    def fold(low, high):
        return jnp.concatenate([low[:tok], low[tok:] + high[:tok], high[tok:]], 0)

    parts, rope = [], None
    for h in range(heads):
        dk = fold(*[dot(dscores[h, b], queries[h][b], 0, 0) for b in range(2)])
        dv = fold(*[dot(probs16[h, b], grads[h][b], 0, 0) for b in range(2)])
        parts.append(jnp.concatenate([dk[:, :PLAIN_WIDTH], dv], 1).astype(BF16))
        rope = dk[:, PLAIN_WIDTH:] if rope is None else rope + dk[:, PLAIN_WIDTH:]
    dkv = jnp.concatenate(parts, 1)
    rows = lat_ref.shape[0] // 8

    def term(low, high):
        pair = [lat_ref[g * rows : (g + 1) * rows, :] for g in (low, high)]
        return dot(jnp.concatenate(pair, 0), dkv, 1, 0)

    for at, groups in enumerate(((2, 3), (6, 7)) if along_x else ((1, 3), (5, 7))):
        send_ref[2 * at * rows : 2 * (at + 1) * rows, :] = term(*groups).astype(BF16)
    for at, groups in enumerate(((0, 1), (4, 5)) if along_x else ((0, 2), (4, 6))):
        keep_ref[2 * at * rows : 2 * (at + 1) * rows, :] = term(*groups)
    total = key_ref[:, :LAT]
    for h in range(heads):
        total = total + dot(parts[h], wt_ref[h], 1, 1)
    key_ref[:, :LAT] = total
    key_ref[:, LAT:] = key_ref[:, LAT:] + rope
    for h in range(heads):
        low, high = (dot(dscores[h, b], keys[h][reach[b]], 1, 0) for b in range(2))
        dq_ref[h] = jnp.where(first, low, high)
        back_ref[h] = jnp.where(first, high, low)


def chunk(here, window, weight, mine, got, before, index, heads, along_x):
    tok = mine.shape[1]
    whole = lambda i, here: (0, 0)
    whole3 = lambda i, here: (0, 0, 0)
    step = min(heads, STEP_HEADS)
    steps = heads // step
    at = lambda i, here: (index * steps + i, 0, 0)
    across_columns = lambda i, here: (0, i)
    columns = heads * PAIR
    operands = [*window, weight, mine, got]
    in_specs = [
        pl.BlockSpec(array.shape, whole3 if array.ndim == 3 else whole) for array in window
    ] + [
        pl.BlockSpec((step, LAT, PAIR), at),
        pl.BlockSpec((step, tok, 3 * LANES), at),
        pl.BlockSpec((step, tok, 3 * LANES), at),
    ]
    aliases = {}
    if before is not None:
        key, dq, back = before
        aliases = {len(operands) + 2: 3, len(operands) + 3: 4}
        in_specs = in_specs + [
            pl.BlockSpec(key.shape, whole),
            pl.BlockSpec(memory_space=pl.ANY),
            pl.BlockSpec(memory_space=pl.ANY),
        ]
        operands = operands + [key, dq, back]
    turned = (weight.shape[0], tok, 2 * LANES)
    return pl.pallas_call(
        functools.partial(chunk_kernel, chained=before is not None, along_x=along_x),
        grid_spec=pltpu.PrefetchScalarGridSpec(
            num_scalar_prefetch=1,
            grid=(steps,),
            in_specs=in_specs,
            out_specs=[
                pl.BlockSpec((LAT // 2, step * PAIR), across_columns),
                pl.BlockSpec((LAT // 2, step * PAIR), across_columns),
                pl.BlockSpec((3 * tok, LAT + LANES), whole),
                pl.BlockSpec((step, tok, 2 * LANES), at),
                pl.BlockSpec((step, tok, 2 * LANES), at),
            ],
        ),
        out_shape=[
            jax.ShapeDtypeStruct((LAT // 2, columns), F32),
            jax.ShapeDtypeStruct((LAT // 2, columns), BF16),
            jax.ShapeDtypeStruct((3 * tok, LAT + LANES), F32),
            jax.ShapeDtypeStruct(turned, F32),
            jax.ShapeDtypeStruct(turned, F32),
        ],
        input_output_aliases=aliases,
        compiler_params=PARAMS,
        cost_estimate=cost(CHUNK),
        name="chunk",
    )(here, *operands)


def add_rows_kernel(*refs, count, wide):
    total = refs[0][...].astype(F32)
    for ref in refs[1 : count + wide]:
        total = total + ref[...].astype(F32)
    refs[-1][...] = total.astype(refs[-1].dtype)


def add_rows(arrays, rows, index, dtype, wide=(), place=0, places=1, before=None):
    columns = arrays[0].shape[1]
    operands = [*arrays, *wide]
    in_specs = [pl.BlockSpec((rows, columns), lambda i: (index, 0)) for _ in arrays]
    in_specs = in_specs + [pl.BlockSpec((rows, columns), lambda i: (index, place)) for _ in wide]
    aliases = {}
    if before is not None:
        aliases = {len(operands): 0}
        in_specs.append(pl.BlockSpec(memory_space=pl.ANY))
        operands.append(before)
    return pl.pallas_call(
        functools.partial(add_rows_kernel, count=len(arrays), wide=len(wide)),
        grid=(1,),
        in_specs=in_specs,
        out_specs=pl.BlockSpec((rows, columns), lambda i: (0, place)),
        out_shape=jax.ShapeDtypeStruct((rows, places * columns), dtype),
        input_output_aliases=aliases,
        compiler_params=PARAMS,
        cost_estimate=cost(SHARES),
        name="add_rows",
    )(*operands)


def key_split_kernel(here_ref, key_ref, keep_ref, give_ref):
    tok = keep_ref.shape[0] // 2
    first = (here_ref[0] & 1) == 0
    behind, low, high = (key_ref[b * tok : (b + 1) * tok, :] for b in range(3))
    keep_ref[:tok] = jnp.where(first, low, high)
    keep_ref[tok:] = behind
    give_ref[:tok] = jnp.where(first, high, low)
    give_ref[tok:] = behind


def key_split(here, key):
    rows = key.shape[0] // 3 * 2
    whole = lambda i, here: (0, 0)
    return pl.pallas_call(
        key_split_kernel,
        grid_spec=pltpu.PrefetchScalarGridSpec(
            num_scalar_prefetch=1,
            grid=(1,),
            in_specs=[pl.BlockSpec(key.shape, whole)],
            out_specs=[pl.BlockSpec((rows, key.shape[1]), whole)] * 2,
        ),
        out_shape=[jax.ShapeDtypeStruct((rows, key.shape[1]), F32)] * 2,
        compiler_params=PARAMS,
        cost_estimate=cost(SHARES),
        name="key_split",
    )(here, key)


def key_shares_kernel(at_ref, keep_ref, got_ref, *outs):
    shares = len(outs)
    part = (LAT + ROPE) // shares
    total = keep_ref[...] + got_ref[...]
    for z in range(shares):
        piece = total[:, z * part : (z + 1) * part]
        for s in range(shares):

            @pl.when(lax.rem(at_ref[0] + s, shares) == z)
            def _(s=s, piece=piece):
                outs[s][...] = piece.astype(outs[s].dtype)


def key_shares(at_head, keep, got, shares):
    part = (LAT + ROPE) // shares
    rows = keep.shape[0]
    whole = lambda i, at: (0, 0)
    types = [F32] + [BF16] * (shares - 1)
    return pl.pallas_call(
        key_shares_kernel,
        grid_spec=pltpu.PrefetchScalarGridSpec(
            num_scalar_prefetch=1,
            grid=(1,),
            in_specs=[pl.BlockSpec(keep.shape, whole)] * 2,
            out_specs=[pl.BlockSpec((rows, part), whole)] * shares,
        ),
        out_shape=[jax.ShapeDtypeStruct((rows, part), kind) for kind in types],
        compiler_params=PARAMS,
        cost_estimate=cost(SHARES),
        name="key_shares",
    )(at_head, keep, got)


def query_grad_kernel(here_ref, mine_ref, got_ref, out_ref, n_ref, r_ref):
    tok, heads, _ = out_ref.shape

    def put(src_ref):
        for h in range(heads):
            n_ref[pl.ds(h, tok, stride=heads), :] = src_ref[h, :, :PLAIN_WIDTH]
            r_ref[pl.ds(h, tok, stride=heads), :] = src_ref[h, :, PLAIN_WIDTH:]

    pl.when(pl.program_id(0) == 0)(lambda: put(mine_ref))
    pl.when(pl.program_id(0) == 1)(lambda: put(got_ref))
    out_ref[:, :, :PLAIN_WIDTH] = n_ref[...].reshape(tok, heads, LANES)
    out_ref[:, :, PLAIN_WIDTH:] = r_ref[...].reshape(tok, heads, LANES)[:, :, :ROPE]


def query_grad(here, mine, got):
    heads, tok, _ = mine.shape
    whole = lambda i, here: (0, 0, 0)
    return pl.pallas_call(
        query_grad_kernel,
        grid_spec=pltpu.PrefetchScalarGridSpec(
            num_scalar_prefetch=1,
            grid=(2,),
            in_specs=[pl.BlockSpec(mine.shape, whole)] * 2,
            out_specs=pl.BlockSpec(
                (tok, heads, PLAIN_WIDTH + ROPE), lambda i, here: (0, (here[0] & 1) ^ i, 0)
            ),
            scratch_shapes=[pltpu.VMEM((tok * heads, LANES), F32)] * 2,
        ),
        out_shape=jax.ShapeDtypeStruct((tok, 2 * heads, PLAIN_WIDTH + ROPE), F32),
        compiler_params=PARAMS,
        cost_estimate=cost(QUERY),
        name="query_grad",
    )(here, mine, got)


def second_send_kernel(*refs):
    *narrow, theirs_ref, out_ref = refs
    columns = narrow[0].shape[1]
    for c in range(len(narrow) // 2):
        total = narrow[2 * c][...] + narrow[2 * c + 1][...].astype(F32)
        out_ref[:, c * columns : (c + 1) * columns] = total.astype(BF16)
    out_ref[:, len(narrow) // 2 * columns :] = theirs_ref[...]


def second_send(groups, theirs, rows):
    narrow = [array for group in groups for array in group]
    columns = narrow[0].shape[1]
    wide = theirs.shape[1]
    return pl.pallas_call(
        second_send_kernel,
        grid=(1,),
        in_specs=[pl.BlockSpec((rows, columns), lambda i: (1, 0)) for _ in narrow]
        + [pl.BlockSpec((rows, wide), lambda i: (1, 0))],
        out_specs=pl.BlockSpec((rows, 2 * wide), lambda i: (0, 0)),
        out_shape=jax.ShapeDtypeStruct((rows, 2 * wide), BF16),
        compiler_params=PARAMS,
        cost_estimate=cost(SHARES),
        name="second_send",
    )(*narrow, theirs)


def weight_grad_kernel(here_ref, *refs, count):
    narrow, theirs_ref, last_ref = refs[: 2 * count], refs[2 * count], refs[2 * count + 1]
    out_ref, k_ref, v_ref = refs[-3:]
    rows, heads, _ = out_ref.shape
    each = heads // count

    def put(c, total):
        for h in range(each):
            at = pl.ds(c * each + h, rows, stride=heads)
            k_ref[at, :] = total[:, h * PAIR : h * PAIR + LANES]
            v_ref[at, :] = total[:, h * PAIR + LANES : (h + 1) * PAIR]

    for c in range(count):
        columns = slice(c * each * PAIR, (c + 1) * each * PAIR)
        later = slice((count + c) * each * PAIR, (count + c + 1) * each * PAIR)

        @pl.when(pl.program_id(0) == 0)
        def _(c=c, columns=columns):
            keep_ref, first_ref = narrow[2 * c : 2 * c + 2]
            total = keep_ref[...] + first_ref[...].astype(F32)
            put(c, total + last_ref[:, columns].astype(F32))

        @pl.when(pl.program_id(0) == 1)
        def _(c=c, columns=columns, later=later):
            put(c, theirs_ref[:, columns].astype(F32) + last_ref[:, later].astype(F32))

    out_ref[:, :, :LANES] = k_ref[...].reshape(rows, heads, LANES)
    out_ref[:, :, LANES:] = v_ref[...].reshape(rows, heads, LANES)


def weight_grad_part(here, groups, theirs, last, total, part, parts):
    count = len(groups)
    rows, columns = last.shape[0], theirs.shape[1]
    heads = columns // PAIR
    operands = [array for group in groups for array in group] + [theirs, last]
    whole = lambda i, here: (0, 0)
    in_specs = [pl.BlockSpec((rows, columns // count), whole)] * (2 * count)
    in_specs = in_specs + [
        pl.BlockSpec((rows, columns), whole),
        pl.BlockSpec((rows, 2 * columns), whole),
    ]
    aliases = {}
    if total is not None:
        aliases = {1 + len(operands): 0}
        in_specs.append(pl.BlockSpec(memory_space=pl.ANY))
        operands.append(total)
    return pl.pallas_call(
        functools.partial(weight_grad_kernel, count=count),
        grid_spec=pltpu.PrefetchScalarGridSpec(
            num_scalar_prefetch=1,
            grid=(2,),
            in_specs=in_specs,
            out_specs=pl.BlockSpec(
                (rows, heads, PAIR), lambda i, here: (0, ((here[0] & 1) ^ i) * parts + part, 0)
            ),
            scratch_shapes=[pltpu.VMEM((rows * heads, LANES), F32)] * 2,
        ),
        out_shape=jax.ShapeDtypeStruct((rows, 2 * parts * heads, PAIR), F32),
        input_output_aliases=aliases,
        compiler_params=PARAMS,
        cost_estimate=cost(SUM),
        name="weight_grad",
    )(here, *operands)


def in_chunks(queries, latent_keys, out_grad, up_weight, here, at_head, ids):
    tok = latent_keys.shape[0]
    n_ctx, n_head = lax.axis_size("ctx"), lax.axis_size("head")
    heads, each = 16, 4
    queries = after(queries, (ids, here, at_head))
    give, mine = turn_tokens(here, queries, out_grad, latent_keys, heads)
    odd_devices = range(1, n_ctx - 1, 2)
    even = lax.ppermute(latent_keys, "ctx", [(source, source + 1) for source in odd_devices])
    odd = lax.ppermute(latent_keys, "ctx", [(source, source + 2) for source in odd_devices])
    got = across(give, 1)
    weight = turn_weight(here, up_weight, heads)
    window = chip_window(here, even, odd, latent_keys, got, ids)
    ways, blocks = ((2, 4), (4, 2)), (0, 2, 1, 3)
    before, keeps, sent = None, [], []
    for c, block in enumerate(blocks):
        keep, out, *before = chunk(
            here, window, weight, mine, got, before, block, each, c % 2 == 0
        )
        keeps.append(keep)
        sent.append(across(out, ways[c % 2][0]))
    key, dq, back = before

    def rest(c, earlier):
        return add_rows(
            (keeps[c], sent[c]), 2 * tok, 1, BF16, place=c // 2, places=2, before=earlier
        )

    key_keep, key_give = key_split(here, key)
    key_got = across(key_give, 1)
    rests = [rest(0, None)]
    keeps[1] = after(keeps[1], rests[0])
    rests.append(rest(1, None))
    key_got = after(key_got, rests)
    shares = key_shares(at_head, key_keep, key_got, n_head)
    pieces = [
        lax.ppermute(shares[s], "head", [(z, (z + s) % n_head) for z in range(n_head)])
        for s in range(1, n_head)
    ]
    back = across(after(back, key_keep), 1)
    share, behind = (add_rows((shares[0], *pieces), tok, b, F32) for b in range(2))
    keeps[2] = after(keeps[2], (share, behind))
    behind = lax.ppermute(behind, "ctx", [(source, source - 1) for source in range(2, n_ctx, 2)])
    groups = [[(keeps[c], sent[c]) for c in (p, p + 2)] for p in range(2)]
    theirs, seconds, lasts = [], [], []
    for p in range(2):
        theirs.append(across(rest(p + 2, rests[p]), 1))
        seconds.append(second_send(groups[p], theirs[p], tok))
        lasts.append(across(seconds[p], ways[p][1]))
    dq = query_grad(here, after(dq, seconds), back)
    key_grad = add_rows((after(share, dq), behind), tok, 0, F32)
    theirs = after(theirs, key_grad)
    weight_grad = None
    for p in range(2):
        weight_grad = weight_grad_part(here, groups[p], theirs[p], lasts[p], weight_grad, p, 2)
    return dq, key_grad, weight_grad


def shards(queries, latent_keys, out_grad, up_weight, segment_ids):
    tok = latent_keys.shape[0]
    heads = queries.shape[1]
    n_ctx, n_head = lax.axis_size("ctx"), lax.axis_size("head")
    here = lax.axis_index("ctx").astype(jnp.int32).reshape(1)
    at_head = lax.axis_index("head").astype(jnp.int32).reshape(1)
    if n_ctx == 8 and heads == 32 and n_head == 4:
        ids = segment_ids.reshape(n_ctx // 2, 2 * tok)
        return in_chunks(queries, latent_keys, out_grad, up_weight, here, at_head, ids)
    else:
        ids = segment_ids.reshape(n_ctx, tok)
        prev = from_behind(latent_keys, "ctx", REACH)
        turned = by_head(up_weight, queries, out_grad, 0, heads)
        window = key_window(here, prev, latent_keys, ids, False)
        dq, dkv, rope = attention(window, turned, None, None, 0, heads, 0, heads)
        (both,) = key_terms(at_head, [dkv], [turned[0]], [rope], None)
        share = lax.psum_scatter(
            both.reshape(REACH + 1, tok, LAT + ROPE), "head", scatter_dimension=2, tiled=True
        )
        term = jnp.einsum("ki,ke->ie", window[0], dkv, preferred_element_type=F32)
        rows = lax.psum_scatter(term.astype(BF16), "ctx", scatter_dimension=0, tiled=True)
        weight_grad = rows.astype(F32).reshape(rows.shape[0], heads, PAIR)
    key_grad = share[REACH] + from_behind(share[0], "ctx", 0 - REACH)
    return (dq, key_grad, weight_grad)


def solution(mesh):
    return jax.shard_map(
        shards,
        mesh=mesh,
        in_specs=(
            P("ctx", "head", None),
            P("ctx", None),
            P("ctx", "head", None),
            P(None, "head", None),
            P(),
        ),
        out_specs=(P("ctx", "head", None), P("ctx", "head"), P("ctx", "head", None)),
        check_vma=False,
    )
```

```python
import functools
import math

import jax
import jax.numpy as jnp
from jax import lax
from jax.experimental import pallas as pl
from jax.experimental.pallas import tpu as pltpu
from jax.sharding import PartitionSpec as P

LAT = 512
ROPE = 64
PLAIN_WIDTH = 128
VDIM = 128
REACH = 1
LANES = 128
PAIR = PLAIN_WIDTH + VDIM
STEP_HEADS = 4
BF16 = jnp.bfloat16
F32 = jnp.float32
WIDE = pltpu.CompilerParams(vmem_limit_bytes=56 * 1024 * 1024)
PARAMS = pltpu.CompilerParams(vmem_limit_bytes=20 * 1024 * 1024)


def from_behind(value, axis, steps):
    count = lax.axis_size(axis)
    initial, last = (max(0, -steps), min(count, count - steps))
    return lax.ppermute(value, axis, [(source, source + steps) for source in range(initial, last)])


def across(value, bit):
    count = lax.axis_size("ctx")
    return lax.ppermute(value, "ctx", [(source, source ^ bit) for source in range(count)])


def cost(share):
    return pl.CostEstimate(flops=int(share * 1e9), bytes_accessed=1024, transcendentals=0)


TURN, WINDOW, CHUNK, SHARES, QUERY, SUM = 0.1, 0.1, 0.1, 0.01, 0.01, 0.01


def dot(a, b, a_dim, b_dim):
    return lax.dot_general(a, b, (((a_dim,), (b_dim,)), ((), ())), preferred_element_type=F32)


def by_head_kernel(w_ref, q_ref, g_ref, wt_ref, qt_ref, gt_ref):
    heads = w_ref.shape[1]
    orders = {}

    def order(count):
        if count not in orders:
            size = count * heads
            row = lax.broadcasted_iota(jnp.int32, (size, size), 0)
            col = lax.broadcasted_iota(jnp.int32, (size, size), 1)
            wanted = (row % count) * heads + row // count
            orders[count] = (col == wanted).astype(BF16)
        return orders[count]

    def turn(ref, out_ref):
        rows, _, width = ref.shape
        count = min(rows, 256 // heads)
        for start in range(0, rows, count):
            block = ref[start : start + count].reshape(count * heads, width)
            turned = dot(order(count), block, 1, 0).astype(BF16)
            out_ref[:, start : start + count, :width] = turned.reshape(heads, count, width)

    turn(w_ref, wt_ref)
    qt_ref[...] = jnp.zeros_like(qt_ref)
    turn(q_ref, qt_ref)
    turn(g_ref, gt_ref)


def by_head(up_weight, queries, out_grad, chunk, heads):
    tok = queries.shape[0]
    steps = 4
    depth, rows = LAT // steps, tok // steps
    return pl.pallas_call(
        by_head_kernel,
        grid=(steps,),
        in_specs=[
            pl.BlockSpec((depth, heads, PAIR), lambda i: (i, chunk, 0)),
            pl.BlockSpec((rows, heads, PLAIN_WIDTH + ROPE), lambda i: (i, chunk, 0)),
            pl.BlockSpec((rows, heads, VDIM), lambda i: (i, chunk, 0)),
        ],
        out_specs=[
            pl.BlockSpec((heads, depth, PAIR), lambda i: (0, i, 0)),
            pl.BlockSpec((heads, rows, 2 * LANES), lambda i: (0, i, 0)),
            pl.BlockSpec((heads, rows, VDIM), lambda i: (0, i, 0)),
        ],
        out_shape=[
            jax.ShapeDtypeStruct((heads, LAT, PAIR), BF16),
            jax.ShapeDtypeStruct((heads, tok, 2 * LANES), BF16),
            jax.ShapeDtypeStruct((heads, tok, VDIM), BF16),
        ],
        compiler_params=WIDE,
        cost_estimate=cost(TURN),
        name="by_head",
    )(up_weight, queries, out_grad)


def window_kernel(here_ref, prev_ref, own_ref, ids_ref, *outs, paired):
    win_ref, krope_ref, vis_ref = outs[:3]
    here = here_ref[0]
    tok = prev_ref.shape[0]
    win_ref[:tok, :] = prev_ref[:, :LAT]
    win_ref[tok:, :] = own_ref[:, :LAT]
    krope_ref[...] = jnp.zeros_like(krope_ref)
    krope_ref[:tok, :ROPE] = prev_ref[:, LAT:]
    krope_ref[tok:, :ROPE] = own_ref[:, LAT:]
    behind = jnp.maximum(here - 1, 0)
    seg_prev = jnp.where(here > 0, ids_ref[pl.ds(behind, 1), :], -1)
    seg_own = ids_ref[pl.ds(here, 1), :]
    row = lax.broadcasted_iota(jnp.int32, (tok, tok), 0)
    col = lax.broadcasted_iota(jnp.int32, (tok, tok), 1)
    seg_query = jnp.sum(jnp.where(row == col, seg_own, 0), 1, keepdims=True)
    vis_ref[:, :tok] = (seg_query == seg_prev).astype(F32)
    vis_ref[:, tok:] = ((seg_query == seg_own) & (col <= row)).astype(F32)
    if paired:
        source = lax.broadcasted_iota(jnp.int32, (LAT, LAT), 0)
        column = lax.broadcasted_iota(jnp.int32, (LAT, LAT), 1)
        place = column >> 6
        apart = ((place & 1) << 2) | (place & 2) | (place >> 2)
        wanted = ((here ^ apart) << 6) | (column & 63)
        ordered = dot(win_ref[...], (source == wanted).astype(BF16), 1, 0).astype(BF16)
        outs[3][...] = ordered[:, : LAT // 2]
        outs[4][...] = ordered[:, LAT // 2 :]


def key_window(here, prev, own, ids, paired):
    tok = prev.shape[0]
    whole = lambda i, here: (0, 0)
    shapes = [((2 * tok, LAT), BF16), ((2 * tok, LANES), BF16), ((tok, 2 * tok), F32)]
    if paired:
        shapes = shapes + [((2 * tok, LAT // 2), BF16)] * 2
    return pl.pallas_call(
        functools.partial(window_kernel, paired=paired),
        grid_spec=pltpu.PrefetchScalarGridSpec(
            num_scalar_prefetch=1,
            grid=(1,),
            in_specs=[pl.BlockSpec(array.shape, whole) for array in (prev, own, ids)],
            out_specs=[pl.BlockSpec(shape, whole) for shape, _ in shapes],
        ),
        out_shape=[jax.ShapeDtypeStruct(*shape) for shape in shapes],
        compiler_params=PARAMS,
        cost_estimate=cost(WINDOW),
        name="key_window",
    )(here, prev, own, ids)


def attention_kernel(
    win_ref, krope_ref, vis_ref, wt_ref, qt_ref, gt_ref, *refs, aliased, extra
):
    latents_ref = refs[0] if extra else None
    refs = refs[1:] if extra else refs
    refs = refs[1:] if aliased else refs
    dq_ref, dkv_ref, rope_ref, dqn_ref, dqr_ref = refs
    i = pl.program_id(0)
    tok, heads = dq_ref.shape[:2]
    scale = 1.0 / math.sqrt(PLAIN_WIDTH + ROPE)

    @pl.when(i == 0)
    def _():
        rope_ref[...] = jnp.zeros_like(rope_ref)
        if extra:
            dkv_ref[:, heads * PAIR :] = latents_ref[...]

    visible = vis_ref[...] > 0.0
    window = win_ref[...]
    krope = krope_ref[...]
    count = wt_ref.shape[0]
    keys, values = [], []
    for h in range(count):
        kv = dot(window, wt_ref[h], 1, 0).astype(BF16)
        keys.append(jnp.concatenate([kv[:, :PLAIN_WIDTH], krope], 1))
        values.append(kv[:, PLAIN_WIDTH:])
    scores = [dot(qt_ref[h], keys[h], 1, 1) for h in range(count)]
    dprobs = [dot(gt_ref[h], values[h], 1, 1) for h in range(count)]
    dscores, probs16 = [], []
    for h in range(count):
        logits = jnp.where(visible, scores[h] * scale, -1e30)
        top = jnp.max(logits, -1, keepdims=True)
        expo = jnp.exp(logits - top)
        probs = expo / jnp.sum(expo, -1, keepdims=True)
        delta = jnp.sum(probs * dprobs[h], -1, keepdims=True)
        dscores.append((probs * (dprobs[h] - delta) * scale).astype(BF16))
        probs16.append(probs.astype(BF16))
    parts, rope = [], rope_ref[...]
    for h in range(count):
        dk = dot(dscores[h], qt_ref[h], 0, 0)
        dv = dot(probs16[h], gt_ref[h], 0, 0)
        parts.append(jnp.concatenate([dk[:, :PLAIN_WIDTH], dv], 1).astype(BF16))
        rope = rope + dk[:, PLAIN_WIDTH:]
    rope_ref[...] = rope
    dkv_ref[:, pl.ds(pl.multiple_of(i * (count * PAIR), count * PAIR), count * PAIR)] = (
        jnp.concatenate(parts, 1)
    )
    for h in range(count):
        dq = dot(dscores[h], keys[h], 1, 0)
        dqn_ref[pl.ds(i * count + h, tok, stride=heads), :] = dq[:, :PLAIN_WIDTH]
        dqr_ref[pl.ds(i * count + h, tok, stride=heads), :] = dq[:, PLAIN_WIDTH:]

    @pl.when(i == pl.num_programs(0) - 1)
    def _():
        dq_ref[:, :, :PLAIN_WIDTH] = dqn_ref[...].reshape(tok, heads, LANES)
        dq_ref[:, :, PLAIN_WIDTH:] = dqr_ref[...].reshape(tok, heads, LANES)[:, :, :ROPE]


def attention(window, turned, latents, dq, chunk, heads, first, all_heads):
    weight, queries, out_grad = turned
    tok = queries.shape[1]
    width = 2 * tok
    steps = heads // STEP_HEADS
    at = first // STEP_HEADS
    extra = LAT // 2 if latents is not None else 0
    whole = lambda i: (0, 0)
    head_block = lambda i: (at + i, 0, 0)
    operands = [*window, weight, queries, out_grad]
    in_specs = [pl.BlockSpec(array.shape, whole) for array in window] + [
        pl.BlockSpec((STEP_HEADS, LAT, PAIR), head_block),
        pl.BlockSpec((STEP_HEADS, tok, 2 * LANES), head_block),
        pl.BlockSpec((STEP_HEADS, tok, VDIM), head_block),
    ]
    if latents is not None:
        in_specs.append(pl.BlockSpec(latents.shape, whole))
        operands.append(latents)
    aliases = {}
    if dq is not None:
        aliases = {len(operands): 0}
        in_specs.append(pl.BlockSpec(memory_space=pl.ANY))
        operands.append(dq)
    return pl.pallas_call(
        functools.partial(attention_kernel, aliased=dq is not None, extra=latents is not None),
        grid=(steps,),
        in_specs=in_specs,
        out_specs=[
            pl.BlockSpec((tok, heads, PLAIN_WIDTH + ROPE), lambda i: (0, chunk, 0)),
            pl.BlockSpec((width, heads * PAIR + extra), whole),
            pl.BlockSpec((width, LANES), whole),
        ],
        scratch_shapes=[
            pltpu.VMEM((tok * heads, LANES), F32),
            pltpu.VMEM((tok * heads, LANES), F32),
        ],
        out_shape=[
            jax.ShapeDtypeStruct((tok, all_heads, PLAIN_WIDTH + ROPE), F32),
            jax.ShapeDtypeStruct((width, heads * PAIR + extra), BF16),
            jax.ShapeDtypeStruct((width, LANES), F32),
        ],
        input_output_aliases=aliases,
        compiler_params=WIDE,
        cost_estimate=cost(CHUNK),
        name="attention",
    )(*operands)


def terms_kernel(
    own_ref, other_ref, mine_ref, theirs_ref, keep_ref, send_ref, latents_ref, *, along_x
):
    width = own_ref.shape[0]

    @pl.when(pl.program_id(0) == 0)
    def _():
        latents_ref[:, :width] = mine_ref[...].T
        latents_ref[:, width:] = theirs_ref[...].T

    grads = jnp.concatenate([own_ref[...], other_ref[...]], 0)
    term = dot(latents_ref[...], grads, 1, 0)
    rows = term.shape[0] // 4
    first, second = (1, 2) if along_x else (2, 1)
    keep_ref[:rows] = term[:rows]
    keep_ref[rows:] = term[first * rows : (first + 1) * rows]
    send_ref[:rows] = term[second * rows : (second + 1) * rows].astype(BF16)
    send_ref[rows:] = term[3 * rows :].astype(BF16)


def terms(own, other, mine, theirs, columns, along_x):
    width = own.shape[0]
    block = 1024
    at = theirs.shape[1] // (LAT // 2) - 1
    column_block = lambda i: (0, i)
    return pl.pallas_call(
        functools.partial(terms_kernel, along_x=along_x),
        grid=(columns // block,),
        in_specs=[
            pl.BlockSpec((width, block), column_block),
            pl.BlockSpec((width, block), column_block),
            pl.BlockSpec((width, LAT // 2), lambda i: (0, 0)),
            pl.BlockSpec((width, LAT // 2), lambda i: (0, at)),
        ],
        out_specs=[pl.BlockSpec((LAT // 4, block), column_block)] * 2,
        out_shape=[
            jax.ShapeDtypeStruct((LAT // 4, columns), F32),
            jax.ShapeDtypeStruct((LAT // 4, columns), BF16),
        ],
        scratch_shapes=[pltpu.VMEM((LAT // 2, 2 * width), BF16)],
        compiler_params=PARAMS,
        cost_estimate=cost(CHUNK),
        name="terms",
    )(own, other, mine, theirs)


def key_terms_kernel(*refs, chunks, steps, turns, shares):
    head_ref = refs[0]
    dkv_refs = refs[1 : 1 + chunks]
    wt_refs = refs[1 + chunks : 1 + chunks + turns]
    rope_refs = refs[1 + chunks + turns : 1 + 2 * chunks + turns]
    outs = refs[1 + 2 * chunks + turns : -1]
    total_ref = refs[-1]
    i = pl.program_id(0)

    @pl.when(i == 0)
    def _():
        total_ref[...] = jnp.zeros_like(total_ref)

    for k in range(chunks):

        @pl.when(i // steps == k)
        def _(k=k):
            total = total_ref[...]
            weight_ref = wt_refs[k * turns // chunks]
            for h in range(weight_ref.shape[0]):
                grads = dkv_refs[k][:, h * PAIR : (h + 1) * PAIR]
                total = total + dot(grads, weight_ref[h], 1, 1)
            total_ref[...] = total

    @pl.when(i == pl.num_programs(0) - 1)
    def _():
        rope = rope_refs[0][...]
        for k in range(1, chunks):
            rope = rope + rope_refs[k][...]
        both = jnp.concatenate([total_ref[...], rope], 1)
        if shares is None:
            outs[0][...] = both[:, : LAT + ROPE]
            return
        part = (LAT + ROPE) // shares
        for z in range(shares):
            piece = both[:, z * part : (z + 1) * part]
            for s in range(shares):

                @pl.when(lax.rem(head_ref[0] + s, shares) == z)
                def _(s=s, piece=piece):
                    outs[s][...] = piece


def key_terms(at_head, dkvs, weights, ropes, shares):
    chunks, turns = len(dkvs), len(weights)
    heads = weights[0].shape[0] * turns // chunks
    width = dkvs[0].shape[0]
    steps = heads // STEP_HEADS
    span = steps * chunks // turns
    near = lambda k, many: lambda i, at: jnp.clip(i - k * many, 0, many - 1)
    wide = (LAT + ROPE) // (shares or 1)
    return pl.pallas_call(
        functools.partial(
            key_terms_kernel, chunks=chunks, steps=steps, turns=turns, shares=shares
        ),
        grid_spec=pltpu.PrefetchScalarGridSpec(
            num_scalar_prefetch=1,
            grid=(chunks * steps,),
            in_specs=[
                pl.BlockSpec((width, STEP_HEADS * PAIR), lambda i, at, k=k: (0, near(k, steps)(i, at)))
                for k in range(chunks)
            ]
            + [
                pl.BlockSpec(
                    (STEP_HEADS, LAT, PAIR), lambda i, at, k=k: (near(k, span)(i, at), 0, 0)
                )
                for k in range(turns)
            ]
            + [pl.BlockSpec((width, LANES), lambda i, at: (0, 0))] * chunks,
            out_specs=[pl.BlockSpec((width, wide), lambda i, at: (0, 0))] * (shares or 1),
            scratch_shapes=[pltpu.VMEM((width, LAT), F32)],
        ),
        out_shape=[jax.ShapeDtypeStruct((width, wide), F32)] * (shares or 1),
        compiler_params=WIDE,
        cost_estimate=cost(CHUNK),
        name="key_terms",
    )(at_head, *dkvs, *weights, *ropes)


def weight_sum_kernel(keep_ref, first_ref, second_ref, *refs):
    out_ref, k_ref, v_ref = refs[-3:]
    rows, heads, _ = out_ref.shape
    for h in range(heads):
        columns = slice(h * PAIR, (h + 1) * PAIR)
        total = keep_ref[:, columns] + first_ref[:, columns].astype(F32)
        total = total + second_ref[:, columns].astype(F32)
        k_ref[pl.ds(h, rows, stride=heads), :] = total[:, :LANES]
        v_ref[pl.ds(h, rows, stride=heads), :] = total[:, LANES:]
    out_ref[:, :, :LANES] = k_ref[...].reshape(rows, heads, LANES)
    out_ref[:, :, LANES:] = v_ref[...].reshape(rows, heads, LANES)


def weight_sum(keep, first, second, total, chunk, all_heads):
    rows, columns = second.shape
    heads = columns // PAIR
    block = 32
    operands = [keep, first, second]
    in_specs = [pl.BlockSpec((block, columns), lambda i: (i, 0)) for _ in operands]
    aliases = {}
    if total is not None:
        aliases = {3: 0}
        in_specs.append(pl.BlockSpec(memory_space=pl.ANY))
        operands.append(total)
    return pl.pallas_call(
        weight_sum_kernel,
        grid=(rows // block,),
        in_specs=in_specs,
        out_specs=pl.BlockSpec((block, heads, PAIR), lambda i: (i, chunk, 0)),
        out_shape=jax.ShapeDtypeStruct((rows, all_heads, PAIR), F32),
        scratch_shapes=[pltpu.VMEM((block * heads, LANES), F32)] * 2,
        input_output_aliases=aliases,
        compiler_params=PARAMS,
        cost_estimate=cost(SUM),
        name="weight_sum",
    )(*operands)


def after(values, earlier):
    return lax.optimization_barrier((values, earlier))[0]


def turn_rows(block):
    rows, heads, width = block.shape
    count = min(rows, 256 // heads)
    row = lax.broadcasted_iota(jnp.int32, (count * heads, count * heads), 0)
    col = lax.broadcasted_iota(jnp.int32, (count * heads, count * heads), 1)
    order = (col == (row % count) * heads + row // count).astype(BF16)
    for start in range(0, rows, count):
        part = block[start : start + count].reshape(count * heads, width)
        turned = dot(order, part, 1, 0).astype(BF16)
        yield slice(start, start + count), turned.reshape(heads, count, width)


def in_hbm(array):
    return pltpu.with_memory_space_constraint(array, pltpu.HBM)


def turn_weight_kernel(here_ref, *refs):
    *parts, wt_ref = refs
    depth = parts[0].shape[0]
    for at, w_ref in enumerate(parts):
        for rows, turned in turn_rows(w_ref[...]):
            wt_ref[:, at * depth + rows.start : at * depth + rows.stop, :] = turned


def turn_weight(here, up_weight, heads, half):
    steps, parts = 4, 2
    depth = LAT // steps // parts
    part = lambda p: lambda i, here: (i * parts + p, (here[0] & 1) * 2 + half, 0)
    return pl.pallas_call(
        turn_weight_kernel,
        grid_spec=pltpu.PrefetchScalarGridSpec(
            num_scalar_prefetch=1,
            grid=(steps,),
            in_specs=[pl.BlockSpec((depth, heads, PAIR), part(p)) for p in range(parts)],
            out_specs=pl.BlockSpec((heads, depth * parts, PAIR), lambda i, here: (0, i, 0)),
        ),
        out_shape=jax.ShapeDtypeStruct((heads, LAT, PAIR), BF16),
        compiler_params=PARAMS,
        cost_estimate=cost(TURN),
        name="turn_weight",
    )(here, *[in_hbm(up_weight)] * parts)


def turn_tokens_kernel(here_ref, q1_ref, g1_ref, q0_ref, g0_ref, own_ref, give_ref, mine_ref):
    heads = mine_ref.shape[0]
    for q_ref, g_ref, out_ref in ((q1_ref, g1_ref, give_ref), (q0_ref, g0_ref, mine_ref)):
        out_ref[:, :, LANES : 2 * LANES] = jnp.zeros_like(out_ref[:, :, LANES : 2 * LANES])
        for rows, turned in turn_rows(q_ref[...]):
            out_ref[:heads, rows, : PLAIN_WIDTH + ROPE] = turned
        for rows, turned in turn_rows(g_ref[...]):
            out_ref[:heads, rows, 2 * LANES :] = turned
    rest = LAT + ROPE - 3 * LANES
    give_ref[heads] = own_ref[:, : 3 * LANES]
    give_ref[heads + 1] = jnp.zeros_like(give_ref[heads + 1])
    give_ref[heads + 1, :, :rest] = own_ref[:, 3 * LANES :]


def turn_tokens(here, queries, out_grad, latent_keys, heads):
    tok = queries.shape[0]
    q_block, g_block = (tok, heads, PLAIN_WIDTH + ROPE), (tok, heads, VDIM)
    given = lambda i, here: (0, 1 - (here[0] & 1), 0)
    kept = lambda i, here: (0, here[0] & 1, 0)
    whole = lambda i, here: (0, 0, 0)
    give, mine = (heads + 2, tok, 3 * LANES), (heads, tok, 3 * LANES)
    queries, out_grad, latent_keys = (in_hbm(x) for x in (queries, out_grad, latent_keys))
    return pl.pallas_call(
        turn_tokens_kernel,
        grid_spec=pltpu.PrefetchScalarGridSpec(
            num_scalar_prefetch=1,
            grid=(1,),
            in_specs=[
                pl.BlockSpec(q_block, given),
                pl.BlockSpec(g_block, given),
                pl.BlockSpec(q_block, kept),
                pl.BlockSpec(g_block, kept),
                pl.BlockSpec(latent_keys.shape, lambda i, here: (0, 0)),
            ],
            out_specs=[pl.BlockSpec(give, whole), pl.BlockSpec(mine, whole)],
        ),
        out_shape=[jax.ShapeDtypeStruct(give, BF16), jax.ShapeDtypeStruct(mine, BF16)],
        compiler_params=PARAMS,
        cost_estimate=cost(WINDOW),
        name="turn_tokens",
    )(here, queries, out_grad, queries, out_grad, latent_keys)


def chip_window_kernel(
    here_ref, even_ref, odd_ref, own_ref, pal_ref, ids_ref, win_ref, krope_ref, vis_ref, lat_ref
):
    here = here_ref[0]
    tok = own_ref.shape[0]
    core, chip = here & 1, here >> 1
    first = core == 0
    prev = jnp.where(first, even_ref[...].astype(F32), odd_ref[...].astype(F32)).astype(BF16)
    pal = jnp.concatenate([pal_ref[0], pal_ref[1, :, : LAT + ROPE - 3 * LANES]], 1).astype(F32)
    own = own_ref[...].astype(F32)
    low = jnp.where(first, own, pal).astype(BF16)
    high = jnp.where(first, pal, own).astype(BF16)
    krope_ref[...] = jnp.zeros_like(krope_ref)
    for at, block in enumerate((prev, low, high)):
        win_ref[at * tok : (at + 1) * tok, :] = block[:, :LAT]
        krope_ref[at * tok : (at + 1) * tok, :ROPE] = block[:, LAT:]
    behind = ids_ref[pl.ds(jnp.maximum(chip - 1, 0), 1), :]
    both = ids_ref[pl.ds(chip, 1), :]
    seg = [jnp.where(chip > 0, behind[:, tok:], -1), both[:, :tok], both[:, tok:]]
    row = lax.broadcasted_iota(jnp.int32, (tok, tok), 0)
    col = lax.broadcasted_iota(jnp.int32, (tok, tok), 1)
    for b in range(2):
        seg_query = jnp.sum(jnp.where(row == col, seg[b + 1], 0), 1, keepdims=True)
        vis_ref[b, :, :tok] = (seg_query == seg[b]).astype(F32)
        vis_ref[b, :, tok:] = ((seg_query == seg[b + 1]) & (col <= row)).astype(F32)
    column = lax.broadcasted_iota(jnp.int32, (LAT, LAT), 0)
    source = lax.broadcasted_iota(jnp.int32, (LAT, LAT), 1)
    place = column >> 6
    apart = ((place & 1) << 2) | (place & 2) | (place >> 2)
    wanted = ((here ^ apart) << 6) | (column & 63)
    order = (source == wanted).astype(BF16)
    lat_ref[...] = dot(order, win_ref[...], 1, 1).astype(BF16)


def chip_window(here, even, odd, own, got, ids):
    tok = own.shape[0]
    whole = lambda i, here: (0, 0)
    return pl.pallas_call(
        chip_window_kernel,
        grid_spec=pltpu.PrefetchScalarGridSpec(
            num_scalar_prefetch=1,
            grid=(1,),
            in_specs=[pl.BlockSpec(array.shape, whole) for array in (even, odd, own)]
            + [
                pl.BlockSpec((2,) + got.shape[1:], lambda i, here: (got.shape[0] // 2 - 1, 0, 0)),
                pl.BlockSpec(ids.shape, whole),
            ],
            out_specs=[
                pl.BlockSpec((3 * tok, LAT), whole),
                pl.BlockSpec((3 * tok, LANES), whole),
                pl.BlockSpec((2, tok, 2 * tok), lambda i, here: (0, 0, 0)),
                pl.BlockSpec((LAT, 3 * tok), whole),
            ],
        ),
        out_shape=[
            jax.ShapeDtypeStruct((3 * tok, LAT), BF16),
            jax.ShapeDtypeStruct((3 * tok, LANES), BF16),
            jax.ShapeDtypeStruct((2, tok, 2 * tok), F32),
            jax.ShapeDtypeStruct((LAT, 3 * tok), BF16),
        ],
        compiler_params=PARAMS,
        cost_estimate=cost(WINDOW),
        name="chip_window",
    )(here, even, odd, own, got, ids)


def chunk_kernel(
    here_ref,
    win_ref,
    krope_ref,
    vis_ref,
    lat_ref,
    wt_ref,
    mine_ref,
    got_ref,
    *refs,
    chained,
    along_x,
):
    before_ref = refs[0] if chained else None
    refs = refs[3:] if chained else refs
    keep_ref, send_ref, key_ref, dq_ref, back_ref = refs

    @pl.when(pl.program_id(0) == 0)
    def _():
        key_ref[...] = before_ref[...] if chained else jnp.zeros_like(key_ref)

    tok = vis_ref.shape[1]
    heads = wt_ref.shape[0]
    first = (here_ref[0] & 1) == 0
    scale = 1.0 / math.sqrt(PLAIN_WIDTH + ROPE)
    window, krope = win_ref[...], krope_ref[...]
    visible = [vis_ref[b] > 0.0 for b in range(2)]
    keys, values, queries, grads = [], [], [], []
    for h in range(heads):
        kv = dot(window, wt_ref[h], 1, 0).astype(BF16)
        keys.append(jnp.concatenate([kv[:, :PLAIN_WIDTH], krope], 1))
        values.append(kv[:, PLAIN_WIDTH:])
        mine, got = mine_ref[h], got_ref[h]
        ordered = (jnp.where(first, mine, got), jnp.where(first, got, mine))
        queries.append([block[:, : 2 * LANES] for block in ordered])
        grads.append([block[:, 2 * LANES :] for block in ordered])
    reach = [slice(b * tok, (b + 2) * tok) for b in range(2)]
    units = [(h, b) for h in range(heads) for b in range(2)]
    scores = {(h, b): dot(queries[h][b], keys[h][reach[b]], 1, 1) for h, b in units}
    dprobs = {(h, b): dot(grads[h][b], values[h][reach[b]], 1, 1) for h, b in units}
    dscores, probs16 = {}, {}
    for unit in units:
        logits = jnp.where(visible[unit[1]], scores[unit] * scale, -1e30)
        top = jnp.max(logits, -1, keepdims=True)
        expo = jnp.exp(logits - top)
        probs = expo / jnp.sum(expo, -1, keepdims=True)
        delta = jnp.sum(probs * dprobs[unit], -1, keepdims=True)
        dscores[unit] = (probs * (dprobs[unit] - delta) * scale).astype(BF16)
        probs16[unit] = probs.astype(BF16)

    def fold(low, high):
        return jnp.concatenate([low[:tok], low[tok:] + high[:tok], high[tok:]], 0)

    parts, rope = [], None
    for h in range(heads):
        dk = fold(*[dot(dscores[h, b], queries[h][b], 0, 0) for b in range(2)])
        dv = fold(*[dot(probs16[h, b], grads[h][b], 0, 0) for b in range(2)])
        parts.append(jnp.concatenate([dk[:, :PLAIN_WIDTH], dv], 1).astype(BF16))
        rope = dk[:, PLAIN_WIDTH:] if rope is None else rope + dk[:, PLAIN_WIDTH:]
    dkv = jnp.concatenate(parts, 1)
    rows = lat_ref.shape[0] // 8

    def term(low, high):
        pair = [lat_ref[g * rows : (g + 1) * rows, :] for g in (low, high)]
        return dot(jnp.concatenate(pair, 0), dkv, 1, 0)

    for at, groups in enumerate(((2, 3), (6, 7)) if along_x else ((1, 3), (5, 7))):
        send_ref[2 * at * rows : 2 * (at + 1) * rows, :] = term(*groups).astype(BF16)
    for at, groups in enumerate(((0, 1), (4, 5)) if along_x else ((0, 2), (4, 6))):
        keep_ref[2 * at * rows : 2 * (at + 1) * rows, :] = term(*groups)
    total = key_ref[:, :LAT]
    for h in range(heads):
        total = total + dot(parts[h], wt_ref[h], 1, 1)
    key_ref[:, :LAT] = total
    key_ref[:, LAT:] = key_ref[:, LAT:] + rope
    for h in range(heads):
        low, high = (dot(dscores[h, b], keys[h][reach[b]], 1, 0) for b in range(2))
        dq_ref[h] = jnp.where(first, low, high)
        back_ref[h] = jnp.where(first, high, low)


def chunk(here, window, weight, mine, got, before, index, heads, along_x):
    tok = mine.shape[1]
    whole = lambda i, here: (0, 0)
    whole3 = lambda i, here: (0, 0, 0)
    step = min(heads, STEP_HEADS)
    steps = heads // step
    at = lambda i, here: (index * steps + i, 0, 0)
    in_half = lambda i, here: (index * steps + i) % (weight.shape[0] // step)
    across_columns = lambda i, here: (0, i)
    columns = heads * PAIR
    operands = [*window, weight, mine, got]
    in_specs = [
        pl.BlockSpec(array.shape, whole3 if array.ndim == 3 else whole) for array in window
    ] + [
        pl.BlockSpec((step, LAT, PAIR), lambda i, here: (in_half(i, here), 0, 0)),
        pl.BlockSpec((step, tok, 3 * LANES), at),
        pl.BlockSpec((step, tok, 3 * LANES), at),
    ]
    aliases = {}
    if before is not None:
        key, dq, back = before
        aliases = {len(operands) + 2: 3, len(operands) + 3: 4}
        in_specs = in_specs + [
            pl.BlockSpec(key.shape, whole),
            pl.BlockSpec(memory_space=pl.ANY),
            pl.BlockSpec(memory_space=pl.ANY),
        ]
        operands = operands + [key, dq, back]
    turned = (mine.shape[0], tok, 2 * LANES)
    return pl.pallas_call(
        functools.partial(chunk_kernel, chained=before is not None, along_x=along_x),
        grid_spec=pltpu.PrefetchScalarGridSpec(
            num_scalar_prefetch=1,
            grid=(steps,),
            in_specs=in_specs,
            out_specs=[
                pl.BlockSpec((LAT // 2, step * PAIR), across_columns),
                pl.BlockSpec((LAT // 2, step * PAIR), across_columns),
                pl.BlockSpec((3 * tok, LAT + LANES), whole),
                pl.BlockSpec((step, tok, 2 * LANES), at),
                pl.BlockSpec((step, tok, 2 * LANES), at),
            ],
        ),
        out_shape=[
            jax.ShapeDtypeStruct((LAT // 2, columns), F32),
            jax.ShapeDtypeStruct((LAT // 2, columns), BF16),
            jax.ShapeDtypeStruct((3 * tok, LAT + LANES), F32),
            jax.ShapeDtypeStruct(turned, F32),
            jax.ShapeDtypeStruct(turned, F32),
        ],
        input_output_aliases=aliases,
        compiler_params=PARAMS,
        cost_estimate=cost(CHUNK),
        name="chunk",
    )(here, *operands)


def add_rows_kernel(*refs, count, wide):
    total = refs[0][...].astype(F32)
    for ref in refs[1 : count + wide]:
        total = total + ref[...].astype(F32)
    refs[-1][...] = total.astype(refs[-1].dtype)


def add_rows(arrays, rows, index, dtype, wide=(), place=0, places=1, before=None):
    columns = arrays[0].shape[1]
    operands = [*arrays, *wide]
    in_specs = [pl.BlockSpec((rows, columns), lambda i: (index, 0)) for _ in arrays]
    in_specs = in_specs + [pl.BlockSpec((rows, columns), lambda i: (index, place)) for _ in wide]
    aliases = {}
    if before is not None:
        aliases = {len(operands): 0}
        in_specs.append(pl.BlockSpec(memory_space=pl.ANY))
        operands.append(before)
    return pl.pallas_call(
        functools.partial(add_rows_kernel, count=len(arrays), wide=len(wide)),
        grid=(1,),
        in_specs=in_specs,
        out_specs=pl.BlockSpec((rows, columns), lambda i: (0, place)),
        out_shape=jax.ShapeDtypeStruct((rows, places * columns), dtype),
        input_output_aliases=aliases,
        compiler_params=PARAMS,
        cost_estimate=cost(SHARES),
        name="add_rows",
    )(*operands)


def key_split_kernel(here_ref, key_ref, keep_ref, give_ref):
    tok = keep_ref.shape[0] // 2
    first = (here_ref[0] & 1) == 0
    behind, low, high = (key_ref[b * tok : (b + 1) * tok, :] for b in range(3))
    keep_ref[:tok] = jnp.where(first, low, high)
    keep_ref[tok:] = behind
    give_ref[:tok] = jnp.where(first, high, low)
    give_ref[tok:] = behind


def key_split(here, key):
    rows = key.shape[0] // 3 * 2
    whole = lambda i, here: (0, 0)
    return pl.pallas_call(
        key_split_kernel,
        grid_spec=pltpu.PrefetchScalarGridSpec(
            num_scalar_prefetch=1,
            grid=(1,),
            in_specs=[pl.BlockSpec(key.shape, whole)],
            out_specs=[pl.BlockSpec((rows, key.shape[1]), whole)] * 2,
        ),
        out_shape=[jax.ShapeDtypeStruct((rows, key.shape[1]), F32)] * 2,
        compiler_params=PARAMS,
        cost_estimate=cost(SHARES),
        name="key_split",
    )(here, key)


def key_shares_kernel(at_ref, keep_ref, got_ref, *outs):
    shares = len(outs)
    part = (LAT + ROPE) // shares
    total = keep_ref[...] + got_ref[...]
    for z in range(shares):
        piece = total[:, z * part : (z + 1) * part]
        for s in range(shares):

            @pl.when(lax.rem(at_ref[0] + s, shares) == z)
            def _(s=s, piece=piece):
                outs[s][...] = piece.astype(outs[s].dtype)


def key_shares(at_head, keep, got, shares):
    part = (LAT + ROPE) // shares
    rows = keep.shape[0]
    whole = lambda i, at: (0, 0)
    types = [F32] + [BF16] * (shares - 1)
    return pl.pallas_call(
        key_shares_kernel,
        grid_spec=pltpu.PrefetchScalarGridSpec(
            num_scalar_prefetch=1,
            grid=(1,),
            in_specs=[pl.BlockSpec(keep.shape, whole)] * 2,
            out_specs=[pl.BlockSpec((rows, part), whole)] * shares,
        ),
        out_shape=[jax.ShapeDtypeStruct((rows, part), kind) for kind in types],
        compiler_params=PARAMS,
        cost_estimate=cost(SHARES),
        name="key_shares",
    )(at_head, keep, got)


def query_grad_kernel(here_ref, mine_ref, got_ref, out_ref, n_ref, r_ref):
    tok, heads, _ = out_ref.shape

    def put(src_ref):
        for h in range(heads):
            n_ref[pl.ds(h, tok, stride=heads), :] = src_ref[h, :, :PLAIN_WIDTH]
            r_ref[pl.ds(h, tok, stride=heads), :] = src_ref[h, :, PLAIN_WIDTH:]

    pl.when(pl.program_id(0) == 0)(lambda: put(mine_ref))
    pl.when(pl.program_id(0) == 1)(lambda: put(got_ref))
    out_ref[:, :, :PLAIN_WIDTH] = n_ref[...].reshape(tok, heads, LANES)
    out_ref[:, :, PLAIN_WIDTH:] = r_ref[...].reshape(tok, heads, LANES)[:, :, :ROPE]


def query_grad(here, mine, got):
    heads, tok, _ = mine.shape
    whole = lambda i, here: (0, 0, 0)
    return pl.pallas_call(
        query_grad_kernel,
        grid_spec=pltpu.PrefetchScalarGridSpec(
            num_scalar_prefetch=1,
            grid=(2,),
            in_specs=[pl.BlockSpec(mine.shape, whole)] * 2,
            out_specs=pl.BlockSpec(
                (tok, heads, PLAIN_WIDTH + ROPE), lambda i, here: (0, (here[0] & 1) ^ i, 0)
            ),
            scratch_shapes=[pltpu.VMEM((tok * heads, LANES), F32)] * 2,
        ),
        out_shape=jax.ShapeDtypeStruct((tok, 2 * heads, PLAIN_WIDTH + ROPE), F32),
        compiler_params=PARAMS,
        cost_estimate=cost(QUERY),
        name="query_grad",
    )(here, mine, got)


def second_send_kernel(*refs):
    *narrow, theirs_ref, out_ref = refs
    columns = narrow[0].shape[1]
    for c in range(len(narrow) // 2):
        total = narrow[2 * c][...] + narrow[2 * c + 1][...].astype(F32)
        out_ref[:, c * columns : (c + 1) * columns] = total.astype(BF16)
    out_ref[:, len(narrow) // 2 * columns :] = theirs_ref[...]


def second_send(groups, theirs, rows):
    narrow = [array for group in groups for array in group]
    columns = narrow[0].shape[1]
    wide = theirs.shape[1]
    return pl.pallas_call(
        second_send_kernel,
        grid=(1,),
        in_specs=[pl.BlockSpec((rows, columns), lambda i: (1, 0)) for _ in narrow]
        + [pl.BlockSpec((rows, wide), lambda i: (1, 0))],
        out_specs=pl.BlockSpec((rows, 2 * wide), lambda i: (0, 0)),
        out_shape=jax.ShapeDtypeStruct((rows, 2 * wide), BF16),
        compiler_params=PARAMS,
        cost_estimate=cost(SHARES),
        name="second_send",
    )(*narrow, theirs)


def last_sums_kernel(here_ref, *refs, pairs):
    share_ref, behind_ref, out_ref, key_ref, k_ref, v_ref = refs[-6:]
    rows, heads, _ = out_ref.shape
    each = heads // pairs
    size = 2 * pairs + 2
    key_ref[...] = share_ref[...] + behind_ref[...]

    def put(j, total):
        for h in range(each):
            at = pl.ds(j * each + h, rows, stride=heads)
            k_ref[at, :] = total[:, h * PAIR : h * PAIR + LANES]
            v_ref[at, :] = total[:, h * PAIR + LANES : (h + 1) * PAIR]

    for q in range(2):
        for j in range(pairs):
            group = refs[j * size : (j + 1) * size]
            theirs_ref, last_ref = group[-2:]
            columns = slice(q * each * PAIR, (q + 1) * each * PAIR)
            later = slice((2 + q) * each * PAIR, (3 + q) * each * PAIR)

            @pl.when(pl.program_id(0) == 2 * q)
            def _(j=j, group=group, last_ref=last_ref, columns=columns, q=q):
                total = group[2 * q][...] + group[2 * q + 1][...].astype(F32)
                put(j, total + last_ref[:, columns].astype(F32))

            @pl.when(pl.program_id(0) == 2 * q + 1)
            def _(j=j, theirs_ref=theirs_ref, last_ref=last_ref, columns=columns, later=later):
                put(j, theirs_ref[:, columns].astype(F32) + last_ref[:, later].astype(F32))

    out_ref[:, :, :LANES] = k_ref[...].reshape(rows, heads, LANES)
    out_ref[:, :, LANES:] = v_ref[...].reshape(rows, heads, LANES)


def last_sums(here, groups, theirs, lasts, share, behind):
    pairs = len(groups)
    rows, wide = lasts[0].shape[0], theirs[0].shape[1]
    heads = pairs * wide // 2 // PAIR
    whole = lambda i, here: (0, 0)
    operands, in_specs = [], []
    for group, other, last in zip(groups, theirs, lasts):
        for array in [array for part in group for array in part] + [other, last]:
            operands.append(array)
            in_specs.append(pl.BlockSpec((rows, array.shape[1]), whole))
    in_specs = in_specs + [pl.BlockSpec(share.shape, whole)] * 2
    return pl.pallas_call(
        functools.partial(last_sums_kernel, pairs=pairs),
        grid_spec=pltpu.PrefetchScalarGridSpec(
            num_scalar_prefetch=1,
            grid=(4,),
            in_specs=in_specs,
            out_specs=[
                pl.BlockSpec(
                    (rows, heads, PAIR),
                    lambda i, here: (0, ((here[0] & 1) ^ (i & 1)) * 2 + (i >> 1), 0),
                ),
                pl.BlockSpec(share.shape, whole),
            ],
            scratch_shapes=[pltpu.VMEM((rows * heads, LANES), F32)] * 2,
        ),
        out_shape=[
            jax.ShapeDtypeStruct((rows, 4 * heads, PAIR), F32),
            jax.ShapeDtypeStruct(share.shape, F32),
        ],
        compiler_params=PARAMS,
        cost_estimate=cost(SUM),
        name="last_sums",
    )(here, *operands, share, behind)


def in_chunks(queries, latent_keys, out_grad, up_weight, here, at_head, ids):
    tok = latent_keys.shape[0]
    n_ctx, n_head = lax.axis_size("ctx"), lax.axis_size("head")
    heads, each = 16, 4
    queries = after(queries, (ids, here, at_head))
    give, mine = turn_tokens(here, queries, out_grad, latent_keys, heads)
    odd_devices = range(1, n_ctx - 1, 2)
    even = lax.ppermute(latent_keys, "ctx", [(source, source + 1) for source in odd_devices])
    odd = lax.ppermute(latent_keys, "ctx", [(source, source + 2) for source in odd_devices])
    got = across(give, 1)
    weights = [turn_weight(here, up_weight, heads // 2, 0)]
    window = chip_window(here, even, odd, latent_keys, got, ids)
    ways = ((2, 4), (4, 2))
    before, keeps, sent = None, [], []
    for c in range(4):
        if c == 2:
            weights.append(turn_weight(here, after(up_weight, out), heads // 2, 1))
        keep, out, *before = chunk(
            here, window, weights[c // 2], mine, got, before, c, each, c % 2 == 0
        )
        keeps.append(keep)
        sent.append(across(out, ways[c % 2][0]))
    key, dq, back = before

    def rest(c, earlier):
        return add_rows(
            (keeps[c], sent[c]), 2 * tok, 1, BF16, place=c // 2, places=2, before=earlier
        )

    key_keep, key_give = key_split(here, key)
    key_got = across(key_give, 1)
    rests = [rest(0, None)]
    keeps[1] = after(keeps[1], rests[0])
    rests.append(rest(1, None))
    key_got = after(key_got, rests)
    shares = key_shares(at_head, key_keep, key_got, n_head)
    pieces = [
        lax.ppermute(shares[s], "head", [(z, (z + s) % n_head) for z in range(n_head)])
        for s in range(1, n_head)
    ]
    back = across(after(back, key_keep), 1)
    share, behind = (add_rows((shares[0], *pieces), tok, b, F32) for b in range(2))
    keeps[2] = after(keeps[2], (share, behind))
    behind = lax.ppermute(behind, "ctx", [(source, source - 1) for source in range(2, n_ctx, 2)])
    groups = [[(keeps[c], sent[c]) for c in (p, p + 2)] for p in range(2)]
    theirs, seconds, lasts = [], [], []
    for p in range(2):
        theirs.append(across(rest(p + 2, rests[p]), 1))
        seconds.append(second_send(groups[p], theirs[p], tok))
        lasts.append(across(seconds[p], ways[p][1]))
    dq = query_grad(here, after(dq, seconds), back)
    theirs = after(theirs, dq)
    weight_grad, key_grad = last_sums(here, groups, theirs, lasts, share, behind)
    return dq, key_grad, weight_grad


def shards(queries, latent_keys, out_grad, up_weight, segment_ids):
    tok = latent_keys.shape[0]
    heads = queries.shape[1]
    n_ctx, n_head = lax.axis_size("ctx"), lax.axis_size("head")
    here = lax.axis_index("ctx").astype(jnp.int32).reshape(1)
    at_head = lax.axis_index("head").astype(jnp.int32).reshape(1)
    if n_ctx == 8 and heads == 32 and n_head == 4:
        ids = segment_ids.reshape(n_ctx // 2, 2 * tok)
        return in_chunks(queries, latent_keys, out_grad, up_weight, here, at_head, ids)
    else:
        ids = segment_ids.reshape(n_ctx, tok)
        prev = from_behind(latent_keys, "ctx", REACH)
        turned = by_head(up_weight, queries, out_grad, 0, heads)
        window = key_window(here, prev, latent_keys, ids, False)
        dq, dkv, rope = attention(window, turned, None, None, 0, heads, 0, heads)
        (both,) = key_terms(at_head, [dkv], [turned[0]], [rope], None)
        share = lax.psum_scatter(
            both.reshape(REACH + 1, tok, LAT + ROPE), "head", scatter_dimension=2, tiled=True
        )
        term = jnp.einsum("ki,ke->ie", window[0], dkv, preferred_element_type=F32)
        rows = lax.psum_scatter(term.astype(BF16), "ctx", scatter_dimension=0, tiled=True)
        weight_grad = rows.astype(F32).reshape(rows.shape[0], heads, PAIR)
    key_grad = share[REACH] + from_behind(share[0], "ctx", 0 - REACH)
    return (dq, key_grad, weight_grad)


def solution(mesh):
    return jax.shard_map(
        shards,
        mesh=mesh,
        in_specs=(
            P("ctx", "head", None),
            P("ctx", None),
            P("ctx", "head", None),
            P(None, "head", None),
            P(),
        ),
        out_specs=(P("ctx", "head", None), P("ctx", "head"), P("ctx", "head", None)),
        check_vma=False,
    )
```

```python
import functools
import math

import jax
import jax.numpy as jnp
from jax import lax
from jax.experimental import pallas as pl
from jax.experimental.pallas import tpu as pltpu
from jax.sharding import PartitionSpec as P

LAT = 512
ROPE = 64
PLAIN_WIDTH = 128
VDIM = 128
REACH = 1
LANES = 128
PAIR = PLAIN_WIDTH + VDIM
STEP_HEADS = 4
BF16 = jnp.bfloat16
F32 = jnp.float32
WIDE = pltpu.CompilerParams(vmem_limit_bytes=56 * 1024 * 1024)
PARAMS = pltpu.CompilerParams(vmem_limit_bytes=20 * 1024 * 1024)


def from_behind(value, axis, steps):
    count = lax.axis_size(axis)
    initial, last = (max(0, -steps), min(count, count - steps))
    return lax.ppermute(value, axis, [(source, source + steps) for source in range(initial, last)])


def across(value, bit):
    count = lax.axis_size("ctx")
    return lax.ppermute(value, "ctx", [(source, source ^ bit) for source in range(count)])


def cost(share):
    return pl.CostEstimate(flops=int(share * 1e9), bytes_accessed=1024, transcendentals=0)


TURN, WINDOW, CHUNK, SHARES, QUERY, SUM = 0.1, 0.1, 0.1, 0.01, 0.01, 0.01


def dot(a, b, a_dim, b_dim):
    return lax.dot_general(a, b, (((a_dim,), (b_dim,)), ((), ())), preferred_element_type=F32)


def by_head_kernel(w_ref, q_ref, g_ref, wt_ref, qt_ref, gt_ref):
    heads = w_ref.shape[1]
    orders = {}

    def order(count):
        if count not in orders:
            size = count * heads
            row = lax.broadcasted_iota(jnp.int32, (size, size), 0)
            col = lax.broadcasted_iota(jnp.int32, (size, size), 1)
            wanted = (row % count) * heads + row // count
            orders[count] = (col == wanted).astype(BF16)
        return orders[count]

    def turn(ref, out_ref):
        rows, _, width = ref.shape
        count = min(rows, 256 // heads)
        for start in range(0, rows, count):
            block = ref[start : start + count].reshape(count * heads, width)
            turned = dot(order(count), block, 1, 0).astype(BF16)
            out_ref[:, start : start + count, :width] = turned.reshape(heads, count, width)

    turn(w_ref, wt_ref)
    qt_ref[...] = jnp.zeros_like(qt_ref)
    turn(q_ref, qt_ref)
    turn(g_ref, gt_ref)


def by_head(up_weight, queries, out_grad, chunk, heads):
    tok = queries.shape[0]
    steps = 4
    depth, rows = LAT // steps, tok // steps
    return pl.pallas_call(
        by_head_kernel,
        grid=(steps,),
        in_specs=[
            pl.BlockSpec((depth, heads, PAIR), lambda i: (i, chunk, 0)),
            pl.BlockSpec((rows, heads, PLAIN_WIDTH + ROPE), lambda i: (i, chunk, 0)),
            pl.BlockSpec((rows, heads, VDIM), lambda i: (i, chunk, 0)),
        ],
        out_specs=[
            pl.BlockSpec((heads, depth, PAIR), lambda i: (0, i, 0)),
            pl.BlockSpec((heads, rows, 2 * LANES), lambda i: (0, i, 0)),
            pl.BlockSpec((heads, rows, VDIM), lambda i: (0, i, 0)),
        ],
        out_shape=[
            jax.ShapeDtypeStruct((heads, LAT, PAIR), BF16),
            jax.ShapeDtypeStruct((heads, tok, 2 * LANES), BF16),
            jax.ShapeDtypeStruct((heads, tok, VDIM), BF16),
        ],
        compiler_params=WIDE,
        cost_estimate=cost(TURN),
        name="by_head",
    )(up_weight, queries, out_grad)


def window_kernel(here_ref, prev_ref, own_ref, ids_ref, *outs, paired):
    win_ref, krope_ref, vis_ref = outs[:3]
    here = here_ref[0]
    tok = prev_ref.shape[0]
    win_ref[:tok, :] = prev_ref[:, :LAT]
    win_ref[tok:, :] = own_ref[:, :LAT]
    krope_ref[...] = jnp.zeros_like(krope_ref)
    krope_ref[:tok, :ROPE] = prev_ref[:, LAT:]
    krope_ref[tok:, :ROPE] = own_ref[:, LAT:]
    behind = jnp.maximum(here - 1, 0)
    seg_prev = jnp.where(here > 0, ids_ref[pl.ds(behind, 1), :], -1)
    seg_own = ids_ref[pl.ds(here, 1), :]
    row = lax.broadcasted_iota(jnp.int32, (tok, tok), 0)
    col = lax.broadcasted_iota(jnp.int32, (tok, tok), 1)
    seg_query = jnp.sum(jnp.where(row == col, seg_own, 0), 1, keepdims=True)
    vis_ref[:, :tok] = (seg_query == seg_prev).astype(F32)
    vis_ref[:, tok:] = ((seg_query == seg_own) & (col <= row)).astype(F32)
    if paired:
        source = lax.broadcasted_iota(jnp.int32, (LAT, LAT), 0)
        column = lax.broadcasted_iota(jnp.int32, (LAT, LAT), 1)
        place = column >> 6
        apart = ((place & 1) << 2) | (place & 2) | (place >> 2)
        wanted = ((here ^ apart) << 6) | (column & 63)
        ordered = dot(win_ref[...], (source == wanted).astype(BF16), 1, 0).astype(BF16)
        outs[3][...] = ordered[:, : LAT // 2]
        outs[4][...] = ordered[:, LAT // 2 :]


def key_window(here, prev, own, ids, paired):
    tok = prev.shape[0]
    whole = lambda i, here: (0, 0)
    shapes = [((2 * tok, LAT), BF16), ((2 * tok, LANES), BF16), ((tok, 2 * tok), F32)]
    if paired:
        shapes = shapes + [((2 * tok, LAT // 2), BF16)] * 2
    return pl.pallas_call(
        functools.partial(window_kernel, paired=paired),
        grid_spec=pltpu.PrefetchScalarGridSpec(
            num_scalar_prefetch=1,
            grid=(1,),
            in_specs=[pl.BlockSpec(array.shape, whole) for array in (prev, own, ids)],
            out_specs=[pl.BlockSpec(shape, whole) for shape, _ in shapes],
        ),
        out_shape=[jax.ShapeDtypeStruct(*shape) for shape in shapes],
        compiler_params=PARAMS,
        cost_estimate=cost(WINDOW),
        name="key_window",
    )(here, prev, own, ids)


def attention_kernel(
    win_ref, krope_ref, vis_ref, wt_ref, qt_ref, gt_ref, *refs, aliased, extra
):
    latents_ref = refs[0] if extra else None
    refs = refs[1:] if extra else refs
    refs = refs[1:] if aliased else refs
    dq_ref, dkv_ref, rope_ref, dqn_ref, dqr_ref = refs
    i = pl.program_id(0)
    tok, heads = dq_ref.shape[:2]
    scale = 1.0 / math.sqrt(PLAIN_WIDTH + ROPE)

    @pl.when(i == 0)
    def _():
        rope_ref[...] = jnp.zeros_like(rope_ref)
        if extra:
            dkv_ref[:, heads * PAIR :] = latents_ref[...]

    visible = vis_ref[...] > 0.0
    window = win_ref[...]
    krope = krope_ref[...]
    count = wt_ref.shape[0]
    keys, values = [], []
    for h in range(count):
        kv = dot(window, wt_ref[h], 1, 0).astype(BF16)
        keys.append(jnp.concatenate([kv[:, :PLAIN_WIDTH], krope], 1))
        values.append(kv[:, PLAIN_WIDTH:])
    scores = [dot(qt_ref[h], keys[h], 1, 1) for h in range(count)]
    dprobs = [dot(gt_ref[h], values[h], 1, 1) for h in range(count)]
    dscores, probs16 = [], []
    for h in range(count):
        logits = jnp.where(visible, scores[h] * scale, -1e30)
        top = jnp.max(logits, -1, keepdims=True)
        expo = jnp.exp(logits - top)
        probs = expo / jnp.sum(expo, -1, keepdims=True)
        delta = jnp.sum(probs * dprobs[h], -1, keepdims=True)
        dscores.append((probs * (dprobs[h] - delta) * scale).astype(BF16))
        probs16.append(probs.astype(BF16))
    parts, rope = [], rope_ref[...]
    for h in range(count):
        dk = dot(dscores[h], qt_ref[h], 0, 0)
        dv = dot(probs16[h], gt_ref[h], 0, 0)
        parts.append(jnp.concatenate([dk[:, :PLAIN_WIDTH], dv], 1).astype(BF16))
        rope = rope + dk[:, PLAIN_WIDTH:]
    rope_ref[...] = rope
    dkv_ref[:, pl.ds(pl.multiple_of(i * (count * PAIR), count * PAIR), count * PAIR)] = (
        jnp.concatenate(parts, 1)
    )
    for h in range(count):
        dq = dot(dscores[h], keys[h], 1, 0)
        dqn_ref[pl.ds(i * count + h, tok, stride=heads), :] = dq[:, :PLAIN_WIDTH]
        dqr_ref[pl.ds(i * count + h, tok, stride=heads), :] = dq[:, PLAIN_WIDTH:]

    @pl.when(i == pl.num_programs(0) - 1)
    def _():
        dq_ref[:, :, :PLAIN_WIDTH] = dqn_ref[...].reshape(tok, heads, LANES)
        dq_ref[:, :, PLAIN_WIDTH:] = dqr_ref[...].reshape(tok, heads, LANES)[:, :, :ROPE]


def attention(window, turned, latents, dq, chunk, heads, first, all_heads):
    weight, queries, out_grad = turned
    tok = queries.shape[1]
    width = 2 * tok
    steps = heads // STEP_HEADS
    at = first // STEP_HEADS
    extra = LAT // 2 if latents is not None else 0
    whole = lambda i: (0, 0)
    head_block = lambda i: (at + i, 0, 0)
    operands = [*window, weight, queries, out_grad]
    in_specs = [pl.BlockSpec(array.shape, whole) for array in window] + [
        pl.BlockSpec((STEP_HEADS, LAT, PAIR), head_block),
        pl.BlockSpec((STEP_HEADS, tok, 2 * LANES), head_block),
        pl.BlockSpec((STEP_HEADS, tok, VDIM), head_block),
    ]
    if latents is not None:
        in_specs.append(pl.BlockSpec(latents.shape, whole))
        operands.append(latents)
    aliases = {}
    if dq is not None:
        aliases = {len(operands): 0}
        in_specs.append(pl.BlockSpec(memory_space=pl.ANY))
        operands.append(dq)
    return pl.pallas_call(
        functools.partial(attention_kernel, aliased=dq is not None, extra=latents is not None),
        grid=(steps,),
        in_specs=in_specs,
        out_specs=[
            pl.BlockSpec((tok, heads, PLAIN_WIDTH + ROPE), lambda i: (0, chunk, 0)),
            pl.BlockSpec((width, heads * PAIR + extra), whole),
            pl.BlockSpec((width, LANES), whole),
        ],
        scratch_shapes=[
            pltpu.VMEM((tok * heads, LANES), F32),
            pltpu.VMEM((tok * heads, LANES), F32),
        ],
        out_shape=[
            jax.ShapeDtypeStruct((tok, all_heads, PLAIN_WIDTH + ROPE), F32),
            jax.ShapeDtypeStruct((width, heads * PAIR + extra), BF16),
            jax.ShapeDtypeStruct((width, LANES), F32),
        ],
        input_output_aliases=aliases,
        compiler_params=WIDE,
        cost_estimate=cost(CHUNK),
        name="attention",
    )(*operands)


def terms_kernel(
    own_ref, other_ref, mine_ref, theirs_ref, keep_ref, send_ref, latents_ref, *, along_x
):
    width = own_ref.shape[0]

    @pl.when(pl.program_id(0) == 0)
    def _():
        latents_ref[:, :width] = mine_ref[...].T
        latents_ref[:, width:] = theirs_ref[...].T

    grads = jnp.concatenate([own_ref[...], other_ref[...]], 0)
    term = dot(latents_ref[...], grads, 1, 0)
    rows = term.shape[0] // 4
    first, second = (1, 2) if along_x else (2, 1)
    keep_ref[:rows] = term[:rows]
    keep_ref[rows:] = term[first * rows : (first + 1) * rows]
    send_ref[:rows] = term[second * rows : (second + 1) * rows].astype(BF16)
    send_ref[rows:] = term[3 * rows :].astype(BF16)


def terms(own, other, mine, theirs, columns, along_x):
    width = own.shape[0]
    block = 1024
    at = theirs.shape[1] // (LAT // 2) - 1
    column_block = lambda i: (0, i)
    return pl.pallas_call(
        functools.partial(terms_kernel, along_x=along_x),
        grid=(columns // block,),
        in_specs=[
            pl.BlockSpec((width, block), column_block),
            pl.BlockSpec((width, block), column_block),
            pl.BlockSpec((width, LAT // 2), lambda i: (0, 0)),
            pl.BlockSpec((width, LAT // 2), lambda i: (0, at)),
        ],
        out_specs=[pl.BlockSpec((LAT // 4, block), column_block)] * 2,
        out_shape=[
            jax.ShapeDtypeStruct((LAT // 4, columns), F32),
            jax.ShapeDtypeStruct((LAT // 4, columns), BF16),
        ],
        scratch_shapes=[pltpu.VMEM((LAT // 2, 2 * width), BF16)],
        compiler_params=PARAMS,
        cost_estimate=cost(CHUNK),
        name="terms",
    )(own, other, mine, theirs)


def key_terms_kernel(*refs, chunks, steps, turns, shares):
    head_ref = refs[0]
    dkv_refs = refs[1 : 1 + chunks]
    wt_refs = refs[1 + chunks : 1 + chunks + turns]
    rope_refs = refs[1 + chunks + turns : 1 + 2 * chunks + turns]
    outs = refs[1 + 2 * chunks + turns : -1]
    total_ref = refs[-1]
    i = pl.program_id(0)

    @pl.when(i == 0)
    def _():
        total_ref[...] = jnp.zeros_like(total_ref)

    for k in range(chunks):

        @pl.when(i // steps == k)
        def _(k=k):
            total = total_ref[...]
            weight_ref = wt_refs[k * turns // chunks]
            for h in range(weight_ref.shape[0]):
                grads = dkv_refs[k][:, h * PAIR : (h + 1) * PAIR]
                total = total + dot(grads, weight_ref[h], 1, 1)
            total_ref[...] = total

    @pl.when(i == pl.num_programs(0) - 1)
    def _():
        rope = rope_refs[0][...]
        for k in range(1, chunks):
            rope = rope + rope_refs[k][...]
        both = jnp.concatenate([total_ref[...], rope], 1)
        if shares is None:
            outs[0][...] = both[:, : LAT + ROPE]
            return
        part = (LAT + ROPE) // shares
        for z in range(shares):
            piece = both[:, z * part : (z + 1) * part]
            for s in range(shares):

                @pl.when(lax.rem(head_ref[0] + s, shares) == z)
                def _(s=s, piece=piece):
                    outs[s][...] = piece


def key_terms(at_head, dkvs, weights, ropes, shares):
    chunks, turns = len(dkvs), len(weights)
    heads = weights[0].shape[0] * turns // chunks
    width = dkvs[0].shape[0]
    steps = heads // STEP_HEADS
    span = steps * chunks // turns
    near = lambda k, many: lambda i, at: jnp.clip(i - k * many, 0, many - 1)
    wide = (LAT + ROPE) // (shares or 1)
    return pl.pallas_call(
        functools.partial(
            key_terms_kernel, chunks=chunks, steps=steps, turns=turns, shares=shares
        ),
        grid_spec=pltpu.PrefetchScalarGridSpec(
            num_scalar_prefetch=1,
            grid=(chunks * steps,),
            in_specs=[
                pl.BlockSpec((width, STEP_HEADS * PAIR), lambda i, at, k=k: (0, near(k, steps)(i, at)))
                for k in range(chunks)
            ]
            + [
                pl.BlockSpec(
                    (STEP_HEADS, LAT, PAIR), lambda i, at, k=k: (near(k, span)(i, at), 0, 0)
                )
                for k in range(turns)
            ]
            + [pl.BlockSpec((width, LANES), lambda i, at: (0, 0))] * chunks,
            out_specs=[pl.BlockSpec((width, wide), lambda i, at: (0, 0))] * (shares or 1),
            scratch_shapes=[pltpu.VMEM((width, LAT), F32)],
        ),
        out_shape=[jax.ShapeDtypeStruct((width, wide), F32)] * (shares or 1),
        compiler_params=WIDE,
        cost_estimate=cost(CHUNK),
        name="key_terms",
    )(at_head, *dkvs, *weights, *ropes)


def weight_sum_kernel(keep_ref, first_ref, second_ref, *refs):
    out_ref, k_ref, v_ref = refs[-3:]
    rows, heads, _ = out_ref.shape
    for h in range(heads):
        columns = slice(h * PAIR, (h + 1) * PAIR)
        total = keep_ref[:, columns] + first_ref[:, columns].astype(F32)
        total = total + second_ref[:, columns].astype(F32)
        k_ref[pl.ds(h, rows, stride=heads), :] = total[:, :LANES]
        v_ref[pl.ds(h, rows, stride=heads), :] = total[:, LANES:]
    out_ref[:, :, :LANES] = k_ref[...].reshape(rows, heads, LANES)
    out_ref[:, :, LANES:] = v_ref[...].reshape(rows, heads, LANES)


def weight_sum(keep, first, second, total, chunk, all_heads):
    rows, columns = second.shape
    heads = columns // PAIR
    block = 32
    operands = [keep, first, second]
    in_specs = [pl.BlockSpec((block, columns), lambda i: (i, 0)) for _ in operands]
    aliases = {}
    if total is not None:
        aliases = {3: 0}
        in_specs.append(pl.BlockSpec(memory_space=pl.ANY))
        operands.append(total)
    return pl.pallas_call(
        weight_sum_kernel,
        grid=(rows // block,),
        in_specs=in_specs,
        out_specs=pl.BlockSpec((block, heads, PAIR), lambda i: (i, chunk, 0)),
        out_shape=jax.ShapeDtypeStruct((rows, all_heads, PAIR), F32),
        scratch_shapes=[pltpu.VMEM((block * heads, LANES), F32)] * 2,
        input_output_aliases=aliases,
        compiler_params=PARAMS,
        cost_estimate=cost(SUM),
        name="weight_sum",
    )(*operands)


def after(values, earlier):
    return lax.optimization_barrier((values, earlier))[0]


def turn_rows(block):
    rows, heads, width = block.shape
    count = min(rows, 256 // heads)
    row = lax.broadcasted_iota(jnp.int32, (count * heads, count * heads), 0)
    col = lax.broadcasted_iota(jnp.int32, (count * heads, count * heads), 1)
    order = (col == (row % count) * heads + row // count).astype(BF16)
    for start in range(0, rows, count):
        part = block[start : start + count].reshape(count * heads, width)
        turned = dot(order, part, 1, 0).astype(BF16)
        yield slice(start, start + count), turned.reshape(heads, count, width)


def in_hbm(array):
    return pltpu.with_memory_space_constraint(array, pltpu.HBM)


def turn_weight_kernel(here_ref, *refs):
    *parts, wt_ref = refs
    depth = parts[0].shape[0]
    for at, w_ref in enumerate(parts):
        for rows, turned in turn_rows(w_ref[...]):
            wt_ref[:, at * depth + rows.start : at * depth + rows.stop, :] = turned


def turn_weight(here, up_weight, heads):
    steps, parts = 4, 4
    depth = LAT // steps // parts
    part = lambda p: lambda i, here: (i * parts + p, here[0] & 1, 0)
    return pl.pallas_call(
        turn_weight_kernel,
        grid_spec=pltpu.PrefetchScalarGridSpec(
            num_scalar_prefetch=1,
            grid=(steps,),
            in_specs=[pl.BlockSpec((depth, heads, PAIR), part(p)) for p in range(parts)],
            out_specs=pl.BlockSpec((heads, depth * parts, PAIR), lambda i, here: (0, i, 0)),
        ),
        out_shape=jax.ShapeDtypeStruct((heads, LAT, PAIR), BF16),
        compiler_params=PARAMS,
        cost_estimate=cost(TURN),
        name="turn_weight",
    )(here, *[in_hbm(up_weight)] * parts)


def turn_tokens_kernel(here_ref, q1_ref, g1_ref, q0_ref, g0_ref, own_ref, give_ref, mine_ref):
    heads = mine_ref.shape[0]
    for q_ref, g_ref, out_ref in ((q1_ref, g1_ref, give_ref), (q0_ref, g0_ref, mine_ref)):
        out_ref[:, :, LANES : 2 * LANES] = jnp.zeros_like(out_ref[:, :, LANES : 2 * LANES])
        for rows, turned in turn_rows(q_ref[...]):
            out_ref[:heads, rows, : PLAIN_WIDTH + ROPE] = turned
        for rows, turned in turn_rows(g_ref[...]):
            out_ref[:heads, rows, 2 * LANES :] = turned
    rest = LAT + ROPE - 3 * LANES
    give_ref[heads] = own_ref[:, : 3 * LANES]
    give_ref[heads + 1] = jnp.zeros_like(give_ref[heads + 1])
    give_ref[heads + 1, :, :rest] = own_ref[:, 3 * LANES :]


def turn_tokens(here, queries, out_grad, latent_keys, heads):
    tok = queries.shape[0]
    q_block, g_block = (tok, heads, PLAIN_WIDTH + ROPE), (tok, heads, VDIM)
    given = lambda i, here: (0, 1 - (here[0] & 1), 0)
    kept = lambda i, here: (0, here[0] & 1, 0)
    whole = lambda i, here: (0, 0, 0)
    give, mine = (heads + 2, tok, 3 * LANES), (heads, tok, 3 * LANES)
    queries, out_grad, latent_keys = (in_hbm(x) for x in (queries, out_grad, latent_keys))
    return pl.pallas_call(
        turn_tokens_kernel,
        grid_spec=pltpu.PrefetchScalarGridSpec(
            num_scalar_prefetch=1,
            grid=(1,),
            in_specs=[
                pl.BlockSpec(q_block, given),
                pl.BlockSpec(g_block, given),
                pl.BlockSpec(q_block, kept),
                pl.BlockSpec(g_block, kept),
                pl.BlockSpec(latent_keys.shape, lambda i, here: (0, 0)),
            ],
            out_specs=[pl.BlockSpec(give, whole), pl.BlockSpec(mine, whole)],
        ),
        out_shape=[jax.ShapeDtypeStruct(give, BF16), jax.ShapeDtypeStruct(mine, BF16)],
        compiler_params=PARAMS,
        cost_estimate=cost(WINDOW),
        name="turn_tokens",
    )(here, queries, out_grad, queries, out_grad, latent_keys)


def chip_window_kernel(
    here_ref, even_ref, odd_ref, own_ref, pal_ref, ids_ref, win_ref, krope_ref, vis_ref, lat_ref
):
    here = here_ref[0]
    tok = own_ref.shape[0]
    core, chip = here & 1, here >> 1
    first = core == 0
    prev = jnp.where(first, even_ref[...].astype(F32), odd_ref[...].astype(F32)).astype(BF16)
    pal = jnp.concatenate([pal_ref[0], pal_ref[1, :, : LAT + ROPE - 3 * LANES]], 1).astype(F32)
    own = own_ref[...].astype(F32)
    low = jnp.where(first, own, pal).astype(BF16)
    high = jnp.where(first, pal, own).astype(BF16)
    krope_ref[...] = jnp.zeros_like(krope_ref)
    for at, block in enumerate((prev, low, high)):
        win_ref[at * tok : (at + 1) * tok, :] = block[:, :LAT]
        krope_ref[at * tok : (at + 1) * tok, :ROPE] = block[:, LAT:]
    behind = ids_ref[pl.ds(jnp.maximum(chip - 1, 0), 1), :]
    both = ids_ref[pl.ds(chip, 1), :]
    seg = [jnp.where(chip > 0, behind[:, tok:], -1), both[:, :tok], both[:, tok:]]
    row = lax.broadcasted_iota(jnp.int32, (tok, tok), 0)
    col = lax.broadcasted_iota(jnp.int32, (tok, tok), 1)
    for b in range(2):
        seg_query = jnp.sum(jnp.where(row == col, seg[b + 1], 0), 1, keepdims=True)
        vis_ref[b, :, :tok] = (seg_query == seg[b]).astype(F32)
        vis_ref[b, :, tok:] = ((seg_query == seg[b + 1]) & (col <= row)).astype(F32)
    column = lax.broadcasted_iota(jnp.int32, (LAT, LAT), 0)
    source = lax.broadcasted_iota(jnp.int32, (LAT, LAT), 1)
    place = column >> 6
    apart = ((place & 1) << 2) | (place & 2) | (place >> 2)
    wanted = ((here ^ apart) << 6) | (column & 63)
    order = (source == wanted).astype(BF16)
    lat_ref[...] = dot(order, win_ref[...], 1, 1).astype(BF16)


def chip_window(here, even, odd, own, got, ids):
    tok = own.shape[0]
    whole = lambda i, here: (0, 0)
    return pl.pallas_call(
        chip_window_kernel,
        grid_spec=pltpu.PrefetchScalarGridSpec(
            num_scalar_prefetch=1,
            grid=(1,),
            in_specs=[pl.BlockSpec(array.shape, whole) for array in (even, odd, own)]
            + [
                pl.BlockSpec((2,) + got.shape[1:], lambda i, here: (got.shape[0] // 2 - 1, 0, 0)),
                pl.BlockSpec(ids.shape, whole),
            ],
            out_specs=[
                pl.BlockSpec((3 * tok, LAT), whole),
                pl.BlockSpec((3 * tok, LANES), whole),
                pl.BlockSpec((2, tok, 2 * tok), lambda i, here: (0, 0, 0)),
                pl.BlockSpec((LAT, 3 * tok), whole),
            ],
        ),
        out_shape=[
            jax.ShapeDtypeStruct((3 * tok, LAT), BF16),
            jax.ShapeDtypeStruct((3 * tok, LANES), BF16),
            jax.ShapeDtypeStruct((2, tok, 2 * tok), F32),
            jax.ShapeDtypeStruct((LAT, 3 * tok), BF16),
        ],
        compiler_params=PARAMS,
        cost_estimate=cost(WINDOW),
        name="chip_window",
    )(here, even, odd, own, got, ids)


def chunk_kernel(
    here_ref,
    win_ref,
    krope_ref,
    vis_ref,
    lat_ref,
    wt_ref,
    mine_ref,
    got_ref,
    *refs,
    chained,
    ways,
):
    before_ref = refs[0] if chained else None
    refs = refs[3:] if chained else refs
    keep_ref, key_ref, dq_ref, back_ref, *send_refs = refs

    @pl.when(pl.program_id(0) == 0)
    def _():
        key_ref[...] = before_ref[...] if chained else jnp.zeros_like(key_ref)

    tok = vis_ref.shape[1]
    heads = wt_ref.shape[0]
    first = (here_ref[0] & 1) == 0
    scale = 1.0 / math.sqrt(PLAIN_WIDTH + ROPE)
    window, krope = win_ref[...], krope_ref[...]
    visible = [vis_ref[b] > 0.0 for b in range(2)]
    keys, values, queries, grads = [], [], [], []
    for h in range(heads):
        kv = dot(window, wt_ref[h], 1, 0).astype(BF16)
        keys.append(jnp.concatenate([kv[:, :PLAIN_WIDTH], krope], 1))
        values.append(kv[:, PLAIN_WIDTH:])
        mine, got = mine_ref[h], got_ref[h]
        ordered = (jnp.where(first, mine, got), jnp.where(first, got, mine))
        queries.append([block[:, : 2 * LANES] for block in ordered])
        grads.append([block[:, 2 * LANES :] for block in ordered])
    reach = [slice(b * tok, (b + 2) * tok) for b in range(2)]
    units = [(h, b) for h in range(heads) for b in range(2)]
    scores = {(h, b): dot(queries[h][b], keys[h][reach[b]], 1, 1) for h, b in units}
    dprobs = {(h, b): dot(grads[h][b], values[h][reach[b]], 1, 1) for h, b in units}
    dscores, probs16 = {}, {}
    for unit in units:
        logits = jnp.where(visible[unit[1]], scores[unit] * scale, -1e30)
        top = jnp.max(logits, -1, keepdims=True)
        expo = jnp.exp(logits - top)
        probs = expo / jnp.sum(expo, -1, keepdims=True)
        delta = jnp.sum(probs * dprobs[unit], -1, keepdims=True)
        dscores[unit] = (probs * (dprobs[unit] - delta) * scale).astype(BF16)
        probs16[unit] = probs.astype(BF16)

    def fold(low, high):
        return jnp.concatenate([low[:tok], low[tok:] + high[:tok], high[tok:]], 0)

    parts, rope = [], None
    for h in range(heads):
        dk = fold(*[dot(dscores[h, b], queries[h][b], 0, 0) for b in range(2)])
        dv = fold(*[dot(probs16[h, b], grads[h][b], 0, 0) for b in range(2)])
        parts.append(jnp.concatenate([dk[:, :PLAIN_WIDTH], dv], 1).astype(BF16))
        rope = dk[:, PLAIN_WIDTH:] if rope is None else rope + dk[:, PLAIN_WIDTH:]
    dkv = jnp.concatenate(parts, 1)
    rows = lat_ref.shape[0] // 8

    wide = dkv.shape[1] // len(ways)

    for k, along_x in enumerate(ways):
        columns = slice(k * wide, (k + 1) * wide)

        def term(low, high):
            pair = [lat_ref[g * rows : (g + 1) * rows, :] for g in (low, high)]
            return dot(jnp.concatenate(pair, 0), dkv[:, columns], 1, 0)

        for at, groups in enumerate(((2, 3), (6, 7)) if along_x else ((1, 3), (5, 7))):
            block = slice(2 * at * rows, 2 * (at + 1) * rows)
            send_refs[k][block, :] = term(*groups).astype(BF16)
        for at, groups in enumerate(((0, 1), (4, 5)) if along_x else ((0, 2), (4, 6))):
            block = slice(2 * at * rows, 2 * (at + 1) * rows)
            keep_ref[block, columns] = term(*groups)
    total = key_ref[:, :LAT]
    for h in range(heads):
        total = total + dot(parts[h], wt_ref[h], 1, 1)
    key_ref[:, :LAT] = total
    key_ref[:, LAT:] = key_ref[:, LAT:] + rope
    for h in range(heads):
        low, high = (dot(dscores[h, b], keys[h][reach[b]], 1, 0) for b in range(2))
        dq_ref[h] = jnp.where(first, low, high)
        back_ref[h] = jnp.where(first, high, low)


def chunk(here, window, weight, mine, got, before, index, heads, ways):
    tok = mine.shape[1]
    whole = lambda i, here: (0, 0)
    whole3 = lambda i, here: (0, 0, 0)
    step = min(heads, STEP_HEADS)
    steps = heads // step
    at = lambda i, here: (index * steps + i, 0, 0)
    in_half = lambda i, here: (index * steps + i) % (weight.shape[0] // step)
    across_columns = lambda i, here: (0, i)
    columns = heads * PAIR
    operands = [*window, weight, mine, got]
    in_specs = [
        pl.BlockSpec(array.shape, whole3 if array.ndim == 3 else whole) for array in window
    ] + [
        pl.BlockSpec((step, LAT, PAIR), lambda i, here: (in_half(i, here), 0, 0)),
        pl.BlockSpec((step, tok, 3 * LANES), at),
        pl.BlockSpec((step, tok, 3 * LANES), at),
    ]
    aliases = {}
    if before is not None:
        key, dq, back = before
        aliases = {len(operands) + 2: 2, len(operands) + 3: 3}
        in_specs = in_specs + [
            pl.BlockSpec(key.shape, whole),
            pl.BlockSpec(memory_space=pl.ANY),
            pl.BlockSpec(memory_space=pl.ANY),
        ]
        operands = operands + [key, dq, back]
    turned = (mine.shape[0], tok, 2 * LANES)
    return pl.pallas_call(
        functools.partial(chunk_kernel, chained=before is not None, ways=ways),
        grid_spec=pltpu.PrefetchScalarGridSpec(
            num_scalar_prefetch=1,
            grid=(steps,),
            in_specs=in_specs,
            out_specs=[
                pl.BlockSpec((LAT // 2, step * PAIR), across_columns),
                pl.BlockSpec((3 * tok, LAT + LANES), whole),
                pl.BlockSpec((step, tok, 2 * LANES), at),
                pl.BlockSpec((step, tok, 2 * LANES), at),
            ]
            + [pl.BlockSpec((LAT // 2, step * PAIR // len(ways)), across_columns)] * len(ways),
        ),
        out_shape=[
            jax.ShapeDtypeStruct((LAT // 2, columns), F32),
            jax.ShapeDtypeStruct((3 * tok, LAT + LANES), F32),
            jax.ShapeDtypeStruct(turned, F32),
            jax.ShapeDtypeStruct(turned, F32),
        ]
        + [jax.ShapeDtypeStruct((LAT // 2, columns // len(ways)), BF16)] * len(ways),
        input_output_aliases=aliases,
        compiler_params=PARAMS,
        cost_estimate=cost(CHUNK),
        name="chunk",
    )(here, *operands)


def add_rows_kernel(*refs, count, wide):
    total = refs[0][...].astype(F32)
    for ref in refs[1 : count + wide]:
        total = total + ref[...].astype(F32)
    refs[-1][...] = total.astype(refs[-1].dtype)


def add_rows(arrays, rows, index, dtype, wide=(), place=0, places=1, before=None):
    columns = arrays[0].shape[1]
    operands = [*arrays, *wide]
    in_specs = [pl.BlockSpec((rows, columns), lambda i: (index, 0)) for _ in arrays]
    in_specs = in_specs + [pl.BlockSpec((rows, columns), lambda i: (index, place)) for _ in wide]
    aliases = {}
    if before is not None:
        aliases = {len(operands): 0}
        in_specs.append(pl.BlockSpec(memory_space=pl.ANY))
        operands.append(before)
    return pl.pallas_call(
        functools.partial(add_rows_kernel, count=len(arrays), wide=len(wide)),
        grid=(1,),
        in_specs=in_specs,
        out_specs=pl.BlockSpec((rows, columns), lambda i: (0, place)),
        out_shape=jax.ShapeDtypeStruct((rows, places * columns), dtype),
        input_output_aliases=aliases,
        compiler_params=PARAMS,
        cost_estimate=cost(SHARES),
        name="add_rows",
    )(*operands)


def key_split_kernel(here_ref, key_ref, keep_ref, give_ref):
    tok = keep_ref.shape[0] // 2
    first = (here_ref[0] & 1) == 0
    behind, low, high = (key_ref[b * tok : (b + 1) * tok, :] for b in range(3))
    keep_ref[:tok] = jnp.where(first, low, high)
    keep_ref[tok:] = behind
    give_ref[:tok] = jnp.where(first, high, low)
    give_ref[tok:] = behind


def key_split(here, key):
    rows = key.shape[0] // 3 * 2
    whole = lambda i, here: (0, 0)
    return pl.pallas_call(
        key_split_kernel,
        grid_spec=pltpu.PrefetchScalarGridSpec(
            num_scalar_prefetch=1,
            grid=(1,),
            in_specs=[pl.BlockSpec(key.shape, whole)],
            out_specs=[pl.BlockSpec((rows, key.shape[1]), whole)] * 2,
        ),
        out_shape=[jax.ShapeDtypeStruct((rows, key.shape[1]), F32)] * 2,
        compiler_params=PARAMS,
        cost_estimate=cost(SHARES),
        name="key_split",
    )(here, key)


def key_shares_kernel(at_ref, keep_ref, got_ref, *outs):
    shares = len(outs)
    part = (LAT + ROPE) // shares
    total = keep_ref[...] + got_ref[...]
    for z in range(shares):
        piece = total[:, z * part : (z + 1) * part]
        for s in range(shares):

            @pl.when(lax.rem(at_ref[0] + s, shares) == z)
            def _(s=s, piece=piece):
                outs[s][...] = piece.astype(outs[s].dtype)


def key_shares(at_head, keep, got, shares):
    part = (LAT + ROPE) // shares
    rows = keep.shape[0]
    whole = lambda i, at: (0, 0)
    types = [F32] + [BF16] * (shares - 1)
    return pl.pallas_call(
        key_shares_kernel,
        grid_spec=pltpu.PrefetchScalarGridSpec(
            num_scalar_prefetch=1,
            grid=(1,),
            in_specs=[pl.BlockSpec(keep.shape, whole)] * 2,
            out_specs=[pl.BlockSpec((rows, part), whole)] * shares,
        ),
        out_shape=[jax.ShapeDtypeStruct((rows, part), kind) for kind in types],
        compiler_params=PARAMS,
        cost_estimate=cost(SHARES),
        name="key_shares",
    )(at_head, keep, got)


def query_grad_kernel(here_ref, mine_ref, got_ref, out_ref, n_ref, r_ref):
    tok, heads, _ = out_ref.shape

    def put(src_ref):
        for h in range(heads):
            n_ref[pl.ds(h, tok, stride=heads), :] = src_ref[h, :, :PLAIN_WIDTH]
            r_ref[pl.ds(h, tok, stride=heads), :] = src_ref[h, :, PLAIN_WIDTH:]

    pl.when(pl.program_id(0) == 0)(lambda: put(mine_ref))
    pl.when(pl.program_id(0) == 1)(lambda: put(got_ref))
    out_ref[:, :, :PLAIN_WIDTH] = n_ref[...].reshape(tok, heads, LANES)
    out_ref[:, :, PLAIN_WIDTH:] = r_ref[...].reshape(tok, heads, LANES)[:, :, :ROPE]


def query_grad(here, mine, got):
    heads, tok, _ = mine.shape
    whole = lambda i, here: (0, 0, 0)
    return pl.pallas_call(
        query_grad_kernel,
        grid_spec=pltpu.PrefetchScalarGridSpec(
            num_scalar_prefetch=1,
            grid=(2,),
            in_specs=[pl.BlockSpec(mine.shape, whole)] * 2,
            out_specs=pl.BlockSpec(
                (tok, heads, PLAIN_WIDTH + ROPE), lambda i, here: (0, (here[0] & 1) ^ i, 0)
            ),
            scratch_shapes=[pltpu.VMEM((tok * heads, LANES), F32)] * 2,
        ),
        out_shape=jax.ShapeDtypeStruct((tok, 2 * heads, PLAIN_WIDTH + ROPE), F32),
        compiler_params=PARAMS,
        cost_estimate=cost(QUERY),
        name="query_grad",
    )(here, mine, got)


def join_kernel(*refs, pieces, wide):
    out_ref = refs[-1]
    for k in range(pieces):
        total = refs[2 * k][...] + refs[2 * k + 1][...].astype(F32)
        out_ref[:, k * wide : (k + 1) * wide] = total.astype(BF16)
    if len(refs) > 2 * pieces + 1:
        out_ref[:, pieces * wide :] = refs[2 * pieces][...]


def join(pieces, rows, wide, theirs=None):
    operands, in_specs = [], []
    for piece in pieces:
        for array, column in piece:
            operands.append(array)
            in_specs.append(pl.BlockSpec((rows, wide), lambda i, column=column: (1, column)))
    columns = len(pieces) * wide
    if theirs is not None:
        operands.append(theirs)
        in_specs.append(pl.BlockSpec((rows, columns), lambda i: (1, 0)))
        columns = 2 * columns
    return pl.pallas_call(
        functools.partial(join_kernel, pieces=len(pieces), wide=wide),
        grid=(1,),
        in_specs=in_specs,
        out_specs=pl.BlockSpec((rows, columns), lambda i: (0, 0)),
        out_shape=jax.ShapeDtypeStruct((rows, columns), BF16),
        compiler_params=PARAMS,
        cost_estimate=cost(SHARES),
        name="join",
    )(*operands)


def last_sums_kernel(here_ref, *refs, order, count, wide):
    share_ref, behind_ref, out_ref, key_ref, k_ref, v_ref = refs[-6:]
    rows, heads, _ = out_ref.shape
    size = 2 * count + 2
    each = wide // PAIR
    key_ref[...] = share_ref[...] + behind_ref[...]

    def put(j, total):
        for h in range(each):
            at = pl.ds(j * each + h, rows, stride=heads)
            k_ref[at, :] = total[:, h * PAIR : h * PAIR + LANES]
            v_ref[at, :] = total[:, h * PAIR + LANES : (h + 1) * PAIR]

    for q, places in enumerate(order):
        for j, (pair, piece) in enumerate(places):
            group = refs[pair * size : (pair + 1) * size]
            kept, came = group[2 * piece : 2 * piece + 2]
            theirs_ref, last_ref = group[-2:]
            columns = slice(piece * wide, (piece + 1) * wide)
            later = slice((count + piece) * wide, (count + piece + 1) * wide)

            @pl.when(pl.program_id(0) == 2 * q)
            def _(j=j, kept=kept, came=came, last_ref=last_ref, columns=columns):
                total = kept[...] + came[...].astype(F32)
                put(j, total + last_ref[:, columns].astype(F32))

            @pl.when(pl.program_id(0) == 2 * q + 1)
            def _(j=j, theirs_ref=theirs_ref, last_ref=last_ref, columns=columns, later=later):
                put(j, theirs_ref[:, columns].astype(F32) + last_ref[:, later].astype(F32))

    out_ref[:, :, :LANES] = k_ref[...].reshape(rows, heads, LANES)
    out_ref[:, :, LANES:] = v_ref[...].reshape(rows, heads, LANES)


def last_sums(here, pieces, theirs, lasts, share, behind, order, wide):
    rows, heads = share.shape[0], len(order[0]) * wide // PAIR
    whole = lambda i, here: (0, 0)
    operands, in_specs = [], []
    for group, other, last in zip(pieces, theirs, lasts):
        for array, column in [part for piece in group for part in piece]:
            operands.append(array)
            in_specs.append(pl.BlockSpec((rows, wide), lambda i, here, column=column: (0, column)))
        for array in (other, last):
            operands.append(array)
            in_specs.append(pl.BlockSpec((rows, array.shape[1]), whole))
    in_specs = in_specs + [pl.BlockSpec(share.shape, whole)] * 2
    return pl.pallas_call(
        functools.partial(last_sums_kernel, order=order, count=len(pieces[0]), wide=wide),
        grid_spec=pltpu.PrefetchScalarGridSpec(
            num_scalar_prefetch=1,
            grid=(4,),
            in_specs=in_specs,
            out_specs=[
                pl.BlockSpec(
                    (rows, heads, PAIR),
                    lambda i, here: (0, ((here[0] & 1) ^ (i & 1)) * 2 + (i >> 1), 0),
                ),
                pl.BlockSpec(share.shape, whole),
            ],
            scratch_shapes=[pltpu.VMEM((rows * heads, LANES), F32)] * 2,
        ),
        out_shape=[
            jax.ShapeDtypeStruct((rows, 4 * heads, PAIR), F32),
            jax.ShapeDtypeStruct(share.shape, F32),
        ],
        compiler_params=PARAMS,
        cost_estimate=cost(SUM),
        name="last_sums",
    )(here, *operands, share, behind)


def in_chunks(queries, latent_keys, out_grad, up_weight, here, at_head, ids):
    tok = latent_keys.shape[0]
    n_ctx, n_head = lax.axis_size("ctx"), lax.axis_size("head")
    heads, each = 16, 4
    queries = after(queries, (ids, here, at_head))
    give, mine = turn_tokens(here, queries, out_grad, latent_keys, heads)
    odd_devices = range(1, n_ctx - 1, 2)
    even = lax.ppermute(latent_keys, "ctx", [(source, source + 1) for source in odd_devices])
    odd = lax.ppermute(latent_keys, "ctx", [(source, source + 2) for source in odd_devices])
    got = across(give, 1)
    weight = turn_weight(here, up_weight, heads)
    window = chip_window(here, even, odd, latent_keys, got, ids)
    ways, bits, wide = ((True, False), (False,), (True,), (True, False)), (2, 4), 2 * PAIR
    before, pieces = None, ([], [])
    for c in range(4):
        keep, *before = chunk(here, window, weight, mine, got, before, c, each, ways[c])
        before, outs = before[:3], before[3:]
        for k, (along_x, out) in enumerate(zip(ways[c], outs)):
            came = across(out, bits[0] if along_x else bits[1])
            for at in range(2 // len(outs)):
                pieces[0 if along_x else 1].append(((keep, k + at), (came, at)))
    order = (((0, 0), (1, 0), (1, 1), (1, 2)), ((0, 1), (0, 2), (0, 3), (1, 3)))
    key, dq, back = before
    key = after(key, [pieces[p][0][1][0] for p in range(2)])
    key_keep, key_give = key_split(here, key)
    key_got = across(key_give, 1)
    key_got = after(key_got, [pieces[1][1][1][0], pieces[0][1][1][0]])
    shares = key_shares(at_head, key_keep, key_got, n_head)
    came = [
        lax.ppermute(shares[s], "head", [(z, (z + s) % n_head) for z in range(n_head)])
        for s in range(1, n_head)
    ]
    back = across(after(back, key_keep), 1)
    share, behind = (add_rows((shares[0], *came), tok, b, F32) for b in range(2))
    behind = lax.ppermute(behind, "ctx", [(source, source - 1) for source in range(2, n_ctx, 2)])
    keep = after(keep, share)
    for p in range(2):
        pieces[p][3] = ((keep, pieces[p][3][0][1]), pieces[p][3][1])
    theirs, seconds, lasts = [], [], []
    for p in range(2):
        first = join(pieces[p], 2 * tok, wide)
        theirs.append(across(first, 1))
        seconds.append(join(pieces[p], tok, wide, theirs[p]))
        lasts.append(across(seconds[p], bits[1 - p]))
    dq = query_grad(here, after(dq, seconds), back)
    theirs = after(theirs, dq)
    weight_grad, key_grad = last_sums(
        here, pieces, theirs, lasts, share, behind, order, wide
    )
    return dq, key_grad, weight_grad


def shards(queries, latent_keys, out_grad, up_weight, segment_ids):
    tok = latent_keys.shape[0]
    heads = queries.shape[1]
    n_ctx, n_head = lax.axis_size("ctx"), lax.axis_size("head")
    here = lax.axis_index("ctx").astype(jnp.int32).reshape(1)
    at_head = lax.axis_index("head").astype(jnp.int32).reshape(1)
    if n_ctx == 8 and heads == 32 and n_head == 4:
        ids = segment_ids.reshape(n_ctx // 2, 2 * tok)
        return in_chunks(queries, latent_keys, out_grad, up_weight, here, at_head, ids)
    else:
        ids = segment_ids.reshape(n_ctx, tok)
        prev = from_behind(latent_keys, "ctx", REACH)
        turned = by_head(up_weight, queries, out_grad, 0, heads)
        window = key_window(here, prev, latent_keys, ids, False)
        dq, dkv, rope = attention(window, turned, None, None, 0, heads, 0, heads)
        (both,) = key_terms(at_head, [dkv], [turned[0]], [rope], None)
        share = lax.psum_scatter(
            both.reshape(REACH + 1, tok, LAT + ROPE), "head", scatter_dimension=2, tiled=True
        )
        term = jnp.einsum("ki,ke->ie", window[0], dkv, preferred_element_type=F32)
        rows = lax.psum_scatter(term.astype(BF16), "ctx", scatter_dimension=0, tiled=True)
        weight_grad = rows.astype(F32).reshape(rows.shape[0], heads, PAIR)
    key_grad = share[REACH] + from_behind(share[0], "ctx", 0 - REACH)
    return (dq, key_grad, weight_grad)


def solution(mesh):
    return jax.shard_map(
        shards,
        mesh=mesh,
        in_specs=(
            P("ctx", "head", None),
            P("ctx", None),
            P("ctx", "head", None),
            P(None, "head", None),
            P(),
        ),
        out_specs=(P("ctx", "head", None), P("ctx", "head"), P("ctx", "head", None)),
        check_vma=False,
    )
```

```python
import functools
import math

import jax
import jax.numpy as jnp
from jax import lax
from jax.experimental import pallas as pl
from jax.experimental.pallas import tpu as pltpu
from jax.sharding import PartitionSpec as P

LAT = 512
ROPE = 64
PLAIN_WIDTH = 128
VDIM = 128
REACH = 1
LANES = 128
PAIR = PLAIN_WIDTH + VDIM
STEP_HEADS = 4
BF16 = jnp.bfloat16
F32 = jnp.float32
WIDE = pltpu.CompilerParams(vmem_limit_bytes=56 * 1024 * 1024)
PARAMS = pltpu.CompilerParams(vmem_limit_bytes=20 * 1024 * 1024)


def from_behind(value, axis, steps):
    count = lax.axis_size(axis)
    initial, last = (max(0, -steps), min(count, count - steps))
    return lax.ppermute(value, axis, [(source, source + steps) for source in range(initial, last)])


def across(value, bit):
    count = lax.axis_size("ctx")
    return lax.ppermute(value, "ctx", [(source, source ^ bit) for source in range(count)])


def cost(share):
    return pl.CostEstimate(flops=int(share * 1e9), bytes_accessed=1024, transcendentals=0)


TURN, WINDOW, CHUNK, SHARES, QUERY, SUM = 0.1, 0.1, 0.1, 0.01, 0.01, 0.01


def dot(a, b, a_dim, b_dim):
    return lax.dot_general(a, b, (((a_dim,), (b_dim,)), ((), ())), preferred_element_type=F32)


def by_head_kernel(w_ref, q_ref, g_ref, wt_ref, qt_ref, gt_ref):
    heads = w_ref.shape[1]
    orders = {}

    def order(count):
        if count not in orders:
            size = count * heads
            row = lax.broadcasted_iota(jnp.int32, (size, size), 0)
            col = lax.broadcasted_iota(jnp.int32, (size, size), 1)
            wanted = (row % count) * heads + row // count
            orders[count] = (col == wanted).astype(BF16)
        return orders[count]

    def turn(ref, out_ref):
        rows, _, width = ref.shape
        count = min(rows, 256 // heads)
        for start in range(0, rows, count):
            block = ref[start : start + count].reshape(count * heads, width)
            turned = dot(order(count), block, 1, 0).astype(BF16)
            out_ref[:, start : start + count, :width] = turned.reshape(heads, count, width)

    turn(w_ref, wt_ref)
    qt_ref[...] = jnp.zeros_like(qt_ref)
    turn(q_ref, qt_ref)
    turn(g_ref, gt_ref)


def by_head(up_weight, queries, out_grad, chunk, heads):
    tok = queries.shape[0]
    steps = 4
    depth, rows = LAT // steps, tok // steps
    return pl.pallas_call(
        by_head_kernel,
        grid=(steps,),
        in_specs=[
            pl.BlockSpec((depth, heads, PAIR), lambda i: (i, chunk, 0)),
            pl.BlockSpec((rows, heads, PLAIN_WIDTH + ROPE), lambda i: (i, chunk, 0)),
            pl.BlockSpec((rows, heads, VDIM), lambda i: (i, chunk, 0)),
        ],
        out_specs=[
            pl.BlockSpec((heads, depth, PAIR), lambda i: (0, i, 0)),
            pl.BlockSpec((heads, rows, 2 * LANES), lambda i: (0, i, 0)),
            pl.BlockSpec((heads, rows, VDIM), lambda i: (0, i, 0)),
        ],
        out_shape=[
            jax.ShapeDtypeStruct((heads, LAT, PAIR), BF16),
            jax.ShapeDtypeStruct((heads, tok, 2 * LANES), BF16),
            jax.ShapeDtypeStruct((heads, tok, VDIM), BF16),
        ],
        compiler_params=WIDE,
        cost_estimate=cost(TURN),
        name="by_head",
    )(up_weight, queries, out_grad)


def window_kernel(here_ref, prev_ref, own_ref, ids_ref, *outs, paired):
    win_ref, krope_ref, vis_ref = outs[:3]
    here = here_ref[0]
    tok = prev_ref.shape[0]
    win_ref[:tok, :] = prev_ref[:, :LAT]
    win_ref[tok:, :] = own_ref[:, :LAT]
    krope_ref[...] = jnp.zeros_like(krope_ref)
    krope_ref[:tok, :ROPE] = prev_ref[:, LAT:]
    krope_ref[tok:, :ROPE] = own_ref[:, LAT:]
    behind = jnp.maximum(here - 1, 0)
    seg_prev = jnp.where(here > 0, ids_ref[pl.ds(behind, 1), :], -1)
    seg_own = ids_ref[pl.ds(here, 1), :]
    row = lax.broadcasted_iota(jnp.int32, (tok, tok), 0)
    col = lax.broadcasted_iota(jnp.int32, (tok, tok), 1)
    seg_query = jnp.sum(jnp.where(row == col, seg_own, 0), 1, keepdims=True)
    vis_ref[:, :tok] = (seg_query == seg_prev).astype(F32)
    vis_ref[:, tok:] = ((seg_query == seg_own) & (col <= row)).astype(F32)
    if paired:
        source = lax.broadcasted_iota(jnp.int32, (LAT, LAT), 0)
        column = lax.broadcasted_iota(jnp.int32, (LAT, LAT), 1)
        place = column >> 6
        apart = ((place & 1) << 2) | (place & 2) | (place >> 2)
        wanted = ((here ^ apart) << 6) | (column & 63)
        ordered = dot(win_ref[...], (source == wanted).astype(BF16), 1, 0).astype(BF16)
        outs[3][...] = ordered[:, : LAT // 2]
        outs[4][...] = ordered[:, LAT // 2 :]


def key_window(here, prev, own, ids, paired):
    tok = prev.shape[0]
    whole = lambda i, here: (0, 0)
    shapes = [((2 * tok, LAT), BF16), ((2 * tok, LANES), BF16), ((tok, 2 * tok), F32)]
    if paired:
        shapes = shapes + [((2 * tok, LAT // 2), BF16)] * 2
    return pl.pallas_call(
        functools.partial(window_kernel, paired=paired),
        grid_spec=pltpu.PrefetchScalarGridSpec(
            num_scalar_prefetch=1,
            grid=(1,),
            in_specs=[pl.BlockSpec(array.shape, whole) for array in (prev, own, ids)],
            out_specs=[pl.BlockSpec(shape, whole) for shape, _ in shapes],
        ),
        out_shape=[jax.ShapeDtypeStruct(*shape) for shape in shapes],
        compiler_params=PARAMS,
        cost_estimate=cost(WINDOW),
        name="key_window",
    )(here, prev, own, ids)


def attention_kernel(
    win_ref, krope_ref, vis_ref, wt_ref, qt_ref, gt_ref, *refs, aliased, extra
):
    latents_ref = refs[0] if extra else None
    refs = refs[1:] if extra else refs
    refs = refs[1:] if aliased else refs
    dq_ref, dkv_ref, rope_ref, dqn_ref, dqr_ref = refs
    i = pl.program_id(0)
    tok, heads = dq_ref.shape[:2]
    scale = 1.0 / math.sqrt(PLAIN_WIDTH + ROPE)

    @pl.when(i == 0)
    def _():
        rope_ref[...] = jnp.zeros_like(rope_ref)
        if extra:
            dkv_ref[:, heads * PAIR :] = latents_ref[...]

    visible = vis_ref[...] > 0.0
    window = win_ref[...]
    krope = krope_ref[...]
    count = wt_ref.shape[0]
    keys, values = [], []
    for h in range(count):
        kv = dot(window, wt_ref[h], 1, 0).astype(BF16)
        keys.append(jnp.concatenate([kv[:, :PLAIN_WIDTH], krope], 1))
        values.append(kv[:, PLAIN_WIDTH:])
    scores = [dot(qt_ref[h], keys[h], 1, 1) for h in range(count)]
    dprobs = [dot(gt_ref[h], values[h], 1, 1) for h in range(count)]
    dscores, probs16 = [], []
    for h in range(count):
        logits = jnp.where(visible, scores[h] * scale, -1e30)
        top = jnp.max(logits, -1, keepdims=True)
        expo = jnp.exp(logits - top)
        probs = expo / jnp.sum(expo, -1, keepdims=True)
        delta = jnp.sum(probs * dprobs[h], -1, keepdims=True)
        dscores.append((probs * (dprobs[h] - delta) * scale).astype(BF16))
        probs16.append(probs.astype(BF16))
    parts, rope = [], rope_ref[...]
    for h in range(count):
        dk = dot(dscores[h], qt_ref[h], 0, 0)
        dv = dot(probs16[h], gt_ref[h], 0, 0)
        parts.append(jnp.concatenate([dk[:, :PLAIN_WIDTH], dv], 1).astype(BF16))
        rope = rope + dk[:, PLAIN_WIDTH:]
    rope_ref[...] = rope
    dkv_ref[:, pl.ds(pl.multiple_of(i * (count * PAIR), count * PAIR), count * PAIR)] = (
        jnp.concatenate(parts, 1)
    )
    for h in range(count):
        dq = dot(dscores[h], keys[h], 1, 0)
        dqn_ref[pl.ds(i * count + h, tok, stride=heads), :] = dq[:, :PLAIN_WIDTH]
        dqr_ref[pl.ds(i * count + h, tok, stride=heads), :] = dq[:, PLAIN_WIDTH:]

    @pl.when(i == pl.num_programs(0) - 1)
    def _():
        dq_ref[:, :, :PLAIN_WIDTH] = dqn_ref[...].reshape(tok, heads, LANES)
        dq_ref[:, :, PLAIN_WIDTH:] = dqr_ref[...].reshape(tok, heads, LANES)[:, :, :ROPE]


def attention(window, turned, latents, dq, chunk, heads, first, all_heads):
    weight, queries, out_grad = turned
    tok = queries.shape[1]
    width = 2 * tok
    steps = heads // STEP_HEADS
    at = first // STEP_HEADS
    extra = LAT // 2 if latents is not None else 0
    whole = lambda i: (0, 0)
    head_block = lambda i: (at + i, 0, 0)
    operands = [*window, weight, queries, out_grad]
    in_specs = [pl.BlockSpec(array.shape, whole) for array in window] + [
        pl.BlockSpec((STEP_HEADS, LAT, PAIR), head_block),
        pl.BlockSpec((STEP_HEADS, tok, 2 * LANES), head_block),
        pl.BlockSpec((STEP_HEADS, tok, VDIM), head_block),
    ]
    if latents is not None:
        in_specs.append(pl.BlockSpec(latents.shape, whole))
        operands.append(latents)
    aliases = {}
    if dq is not None:
        aliases = {len(operands): 0}
        in_specs.append(pl.BlockSpec(memory_space=pl.ANY))
        operands.append(dq)
    return pl.pallas_call(
        functools.partial(attention_kernel, aliased=dq is not None, extra=latents is not None),
        grid=(steps,),
        in_specs=in_specs,
        out_specs=[
            pl.BlockSpec((tok, heads, PLAIN_WIDTH + ROPE), lambda i: (0, chunk, 0)),
            pl.BlockSpec((width, heads * PAIR + extra), whole),
            pl.BlockSpec((width, LANES), whole),
        ],
        scratch_shapes=[
            pltpu.VMEM((tok * heads, LANES), F32),
            pltpu.VMEM((tok * heads, LANES), F32),
        ],
        out_shape=[
            jax.ShapeDtypeStruct((tok, all_heads, PLAIN_WIDTH + ROPE), F32),
            jax.ShapeDtypeStruct((width, heads * PAIR + extra), BF16),
            jax.ShapeDtypeStruct((width, LANES), F32),
        ],
        input_output_aliases=aliases,
        compiler_params=WIDE,
        cost_estimate=cost(CHUNK),
        name="attention",
    )(*operands)


def terms_kernel(
    own_ref, other_ref, mine_ref, theirs_ref, keep_ref, send_ref, latents_ref, *, along_x
):
    width = own_ref.shape[0]

    @pl.when(pl.program_id(0) == 0)
    def _():
        latents_ref[:, :width] = mine_ref[...].T
        latents_ref[:, width:] = theirs_ref[...].T

    grads = jnp.concatenate([own_ref[...], other_ref[...]], 0)
    term = dot(latents_ref[...], grads, 1, 0)
    rows = term.shape[0] // 4
    first, second = (1, 2) if along_x else (2, 1)
    keep_ref[:rows] = term[:rows]
    keep_ref[rows:] = term[first * rows : (first + 1) * rows]
    send_ref[:rows] = term[second * rows : (second + 1) * rows].astype(BF16)
    send_ref[rows:] = term[3 * rows :].astype(BF16)


def terms(own, other, mine, theirs, columns, along_x):
    width = own.shape[0]
    block = 1024
    at = theirs.shape[1] // (LAT // 2) - 1
    column_block = lambda i: (0, i)
    return pl.pallas_call(
        functools.partial(terms_kernel, along_x=along_x),
        grid=(columns // block,),
        in_specs=[
            pl.BlockSpec((width, block), column_block),
            pl.BlockSpec((width, block), column_block),
            pl.BlockSpec((width, LAT // 2), lambda i: (0, 0)),
            pl.BlockSpec((width, LAT // 2), lambda i: (0, at)),
        ],
        out_specs=[pl.BlockSpec((LAT // 4, block), column_block)] * 2,
        out_shape=[
            jax.ShapeDtypeStruct((LAT // 4, columns), F32),
            jax.ShapeDtypeStruct((LAT // 4, columns), BF16),
        ],
        scratch_shapes=[pltpu.VMEM((LAT // 2, 2 * width), BF16)],
        compiler_params=PARAMS,
        cost_estimate=cost(CHUNK),
        name="terms",
    )(own, other, mine, theirs)


def key_terms_kernel(*refs, chunks, steps, turns, shares):
    head_ref = refs[0]
    dkv_refs = refs[1 : 1 + chunks]
    wt_refs = refs[1 + chunks : 1 + chunks + turns]
    rope_refs = refs[1 + chunks + turns : 1 + 2 * chunks + turns]
    outs = refs[1 + 2 * chunks + turns : -1]
    total_ref = refs[-1]
    i = pl.program_id(0)

    @pl.when(i == 0)
    def _():
        total_ref[...] = jnp.zeros_like(total_ref)

    for k in range(chunks):

        @pl.when(i // steps == k)
        def _(k=k):
            total = total_ref[...]
            weight_ref = wt_refs[k * turns // chunks]
            for h in range(weight_ref.shape[0]):
                grads = dkv_refs[k][:, h * PAIR : (h + 1) * PAIR]
                total = total + dot(grads, weight_ref[h], 1, 1)
            total_ref[...] = total

    @pl.when(i == pl.num_programs(0) - 1)
    def _():
        rope = rope_refs[0][...]
        for k in range(1, chunks):
            rope = rope + rope_refs[k][...]
        both = jnp.concatenate([total_ref[...], rope], 1)
        if shares is None:
            outs[0][...] = both[:, : LAT + ROPE]
            return
        part = (LAT + ROPE) // shares
        for z in range(shares):
            piece = both[:, z * part : (z + 1) * part]
            for s in range(shares):

                @pl.when(lax.rem(head_ref[0] + s, shares) == z)
                def _(s=s, piece=piece):
                    outs[s][...] = piece


def key_terms(at_head, dkvs, weights, ropes, shares):
    chunks, turns = len(dkvs), len(weights)
    heads = weights[0].shape[0] * turns // chunks
    width = dkvs[0].shape[0]
    steps = heads // STEP_HEADS
    span = steps * chunks // turns
    near = lambda k, many: lambda i, at: jnp.clip(i - k * many, 0, many - 1)
    wide = (LAT + ROPE) // (shares or 1)
    return pl.pallas_call(
        functools.partial(
            key_terms_kernel, chunks=chunks, steps=steps, turns=turns, shares=shares
        ),
        grid_spec=pltpu.PrefetchScalarGridSpec(
            num_scalar_prefetch=1,
            grid=(chunks * steps,),
            in_specs=[
                pl.BlockSpec((width, STEP_HEADS * PAIR), lambda i, at, k=k: (0, near(k, steps)(i, at)))
                for k in range(chunks)
            ]
            + [
                pl.BlockSpec(
                    (STEP_HEADS, LAT, PAIR), lambda i, at, k=k: (near(k, span)(i, at), 0, 0)
                )
                for k in range(turns)
            ]
            + [pl.BlockSpec((width, LANES), lambda i, at: (0, 0))] * chunks,
            out_specs=[pl.BlockSpec((width, wide), lambda i, at: (0, 0))] * (shares or 1),
            scratch_shapes=[pltpu.VMEM((width, LAT), F32)],
        ),
        out_shape=[jax.ShapeDtypeStruct((width, wide), F32)] * (shares or 1),
        compiler_params=WIDE,
        cost_estimate=cost(CHUNK),
        name="key_terms",
    )(at_head, *dkvs, *weights, *ropes)


def weight_sum_kernel(keep_ref, first_ref, second_ref, *refs):
    out_ref, k_ref, v_ref = refs[-3:]
    rows, heads, _ = out_ref.shape
    for h in range(heads):
        columns = slice(h * PAIR, (h + 1) * PAIR)
        total = keep_ref[:, columns] + first_ref[:, columns].astype(F32)
        total = total + second_ref[:, columns].astype(F32)
        k_ref[pl.ds(h, rows, stride=heads), :] = total[:, :LANES]
        v_ref[pl.ds(h, rows, stride=heads), :] = total[:, LANES:]
    out_ref[:, :, :LANES] = k_ref[...].reshape(rows, heads, LANES)
    out_ref[:, :, LANES:] = v_ref[...].reshape(rows, heads, LANES)


def weight_sum(keep, first, second, total, chunk, all_heads):
    rows, columns = second.shape
    heads = columns // PAIR
    block = 32
    operands = [keep, first, second]
    in_specs = [pl.BlockSpec((block, columns), lambda i: (i, 0)) for _ in operands]
    aliases = {}
    if total is not None:
        aliases = {3: 0}
        in_specs.append(pl.BlockSpec(memory_space=pl.ANY))
        operands.append(total)
    return pl.pallas_call(
        weight_sum_kernel,
        grid=(rows // block,),
        in_specs=in_specs,
        out_specs=pl.BlockSpec((block, heads, PAIR), lambda i: (i, chunk, 0)),
        out_shape=jax.ShapeDtypeStruct((rows, all_heads, PAIR), F32),
        scratch_shapes=[pltpu.VMEM((block * heads, LANES), F32)] * 2,
        input_output_aliases=aliases,
        compiler_params=PARAMS,
        cost_estimate=cost(SUM),
        name="weight_sum",
    )(*operands)


def after(values, earlier):
    return lax.optimization_barrier((values, earlier))[0]


def turn_rows(block):
    rows, heads, width = block.shape
    count = min(rows, 256 // heads)
    row = lax.broadcasted_iota(jnp.int32, (count * heads, count * heads), 0)
    col = lax.broadcasted_iota(jnp.int32, (count * heads, count * heads), 1)
    order = (col == (row % count) * heads + row // count).astype(BF16)
    for start in range(0, rows, count):
        part = block[start : start + count].reshape(count * heads, width)
        turned = dot(order, part, 1, 0).astype(BF16)
        yield slice(start, start + count), turned.reshape(heads, count, width)


def in_hbm(array):
    return pltpu.with_memory_space_constraint(array, pltpu.HBM)


def turn_weight_kernel(here_ref, *refs):
    *parts, wt_ref = refs
    depth = parts[0].shape[0]
    for at, w_ref in enumerate(parts):
        for rows, turned in turn_rows(w_ref[...]):
            wt_ref[:, at * depth + rows.start : at * depth + rows.stop, :] = turned


def turn_weight(here, up_weight, heads):
    steps, parts = 4, 4
    depth = LAT // steps // parts
    part = lambda p: lambda i, here: (i * parts + p, here[0] & 1, 0)
    return pl.pallas_call(
        turn_weight_kernel,
        grid_spec=pltpu.PrefetchScalarGridSpec(
            num_scalar_prefetch=1,
            grid=(steps,),
            in_specs=[pl.BlockSpec((depth, heads, PAIR), part(p)) for p in range(parts)],
            out_specs=pl.BlockSpec((heads, depth * parts, PAIR), lambda i, here: (0, i, 0)),
        ),
        out_shape=jax.ShapeDtypeStruct((heads, LAT, PAIR), BF16),
        compiler_params=PARAMS,
        cost_estimate=cost(TURN),
        name="turn_weight",
    )(here, *[in_hbm(up_weight)] * parts)


def turn_tokens_kernel(here_ref, q1_ref, g1_ref, q0_ref, g0_ref, own_ref, give_ref, mine_ref):
    heads = mine_ref.shape[0]
    for q_ref, g_ref, out_ref in ((q1_ref, g1_ref, give_ref), (q0_ref, g0_ref, mine_ref)):
        out_ref[:, :, LANES : 2 * LANES] = jnp.zeros_like(out_ref[:, :, LANES : 2 * LANES])
        for rows, turned in turn_rows(q_ref[...]):
            out_ref[:heads, rows, : PLAIN_WIDTH + ROPE] = turned
        for rows, turned in turn_rows(g_ref[...]):
            out_ref[:heads, rows, 2 * LANES :] = turned
    rest = LAT + ROPE - 3 * LANES
    give_ref[heads] = own_ref[:, : 3 * LANES]
    give_ref[heads + 1] = jnp.zeros_like(give_ref[heads + 1])
    give_ref[heads + 1, :, :rest] = own_ref[:, 3 * LANES :]


def turn_tokens(here, queries, out_grad, latent_keys, heads):
    tok = queries.shape[0]
    q_block, g_block = (tok, heads, PLAIN_WIDTH + ROPE), (tok, heads, VDIM)
    given = lambda i, here: (0, 1 - (here[0] & 1), 0)
    kept = lambda i, here: (0, here[0] & 1, 0)
    whole = lambda i, here: (0, 0, 0)
    give, mine = (heads + 2, tok, 3 * LANES), (heads, tok, 3 * LANES)
    queries, out_grad, latent_keys = (in_hbm(x) for x in (queries, out_grad, latent_keys))
    return pl.pallas_call(
        turn_tokens_kernel,
        grid_spec=pltpu.PrefetchScalarGridSpec(
            num_scalar_prefetch=1,
            grid=(1,),
            in_specs=[
                pl.BlockSpec(q_block, given),
                pl.BlockSpec(g_block, given),
                pl.BlockSpec(q_block, kept),
                pl.BlockSpec(g_block, kept),
                pl.BlockSpec(latent_keys.shape, lambda i, here: (0, 0)),
            ],
            out_specs=[pl.BlockSpec(give, whole), pl.BlockSpec(mine, whole)],
        ),
        out_shape=[jax.ShapeDtypeStruct(give, BF16), jax.ShapeDtypeStruct(mine, BF16)],
        compiler_params=PARAMS,
        cost_estimate=cost(WINDOW),
        name="turn_tokens",
    )(here, queries, out_grad, queries, out_grad, latent_keys)


def chip_window_kernel(
    here_ref, even_ref, odd_ref, own_ref, pal_ref, ids_ref, win_ref, krope_ref, vis_ref, lat_ref
):
    here = here_ref[0]
    tok = own_ref.shape[0]
    core, chip = here & 1, here >> 1
    first = core == 0
    prev = jnp.where(first, even_ref[...].astype(F32), odd_ref[...].astype(F32)).astype(BF16)
    pal = jnp.concatenate([pal_ref[0], pal_ref[1, :, : LAT + ROPE - 3 * LANES]], 1).astype(F32)
    own = own_ref[...].astype(F32)
    low = jnp.where(first, own, pal).astype(BF16)
    high = jnp.where(first, pal, own).astype(BF16)
    krope_ref[...] = jnp.zeros_like(krope_ref)
    for at, block in enumerate((prev, low, high)):
        win_ref[at * tok : (at + 1) * tok, :] = block[:, :LAT]
        krope_ref[at * tok : (at + 1) * tok, :ROPE] = block[:, LAT:]
    behind = ids_ref[pl.ds(jnp.maximum(chip - 1, 0), 1), :]
    both = ids_ref[pl.ds(chip, 1), :]
    seg = [jnp.where(chip > 0, behind[:, tok:], -1), both[:, :tok], both[:, tok:]]
    row = lax.broadcasted_iota(jnp.int32, (tok, tok), 0)
    col = lax.broadcasted_iota(jnp.int32, (tok, tok), 1)
    for b in range(2):
        seg_query = jnp.sum(jnp.where(row == col, seg[b + 1], 0), 1, keepdims=True)
        vis_ref[b, :, :tok] = (seg_query == seg[b]).astype(F32)
        vis_ref[b, :, tok:] = ((seg_query == seg[b + 1]) & (col <= row)).astype(F32)
    column = lax.broadcasted_iota(jnp.int32, (LAT, LAT), 0)
    source = lax.broadcasted_iota(jnp.int32, (LAT, LAT), 1)
    place = column >> 6
    apart = ((place & 1) << 2) | (place & 2) | (place >> 2)
    wanted = ((here ^ apart) << 6) | (column & 63)
    order = (source == wanted).astype(BF16)
    lat_ref[...] = dot(order, win_ref[...], 1, 1).astype(BF16)


def chip_window(here, even, odd, own, got, ids):
    tok = own.shape[0]
    whole = lambda i, here: (0, 0)
    return pl.pallas_call(
        chip_window_kernel,
        grid_spec=pltpu.PrefetchScalarGridSpec(
            num_scalar_prefetch=1,
            grid=(1,),
            in_specs=[pl.BlockSpec(array.shape, whole) for array in (even, odd, own)]
            + [
                pl.BlockSpec((2,) + got.shape[1:], lambda i, here: (got.shape[0] // 2 - 1, 0, 0)),
                pl.BlockSpec(ids.shape, whole),
            ],
            out_specs=[
                pl.BlockSpec((3 * tok, LAT), whole),
                pl.BlockSpec((3 * tok, LANES), whole),
                pl.BlockSpec((2, tok, 2 * tok), lambda i, here: (0, 0, 0)),
                pl.BlockSpec((LAT, 3 * tok), whole),
            ],
        ),
        out_shape=[
            jax.ShapeDtypeStruct((3 * tok, LAT), BF16),
            jax.ShapeDtypeStruct((3 * tok, LANES), BF16),
            jax.ShapeDtypeStruct((2, tok, 2 * tok), F32),
            jax.ShapeDtypeStruct((LAT, 3 * tok), BF16),
        ],
        compiler_params=PARAMS,
        cost_estimate=cost(WINDOW),
        name="chip_window",
    )(here, even, odd, own, got, ids)


def chunk_kernel(
    here_ref,
    win_ref,
    krope_ref,
    vis_ref,
    lat_ref,
    wt_ref,
    mine_ref,
    got_ref,
    *refs,
    chained,
    ways,
):
    before_ref = refs[0] if chained else None
    refs = refs[3:] if chained else refs
    keep_ref, key_ref, dq_ref, back_ref, *send_refs = refs

    @pl.when(pl.program_id(0) == 0)
    def _():
        key_ref[...] = before_ref[...] if chained else jnp.zeros_like(key_ref)

    tok = vis_ref.shape[1]
    heads = wt_ref.shape[0]
    first = (here_ref[0] & 1) == 0
    scale = 1.0 / math.sqrt(PLAIN_WIDTH + ROPE)
    window, krope = win_ref[...], krope_ref[...]
    visible = [vis_ref[b] > 0.0 for b in range(2)]
    keys, values, queries, grads = [], [], [], []
    for h in range(heads):
        kv = dot(window, wt_ref[h], 1, 0).astype(BF16)
        keys.append(jnp.concatenate([kv[:, :PLAIN_WIDTH], krope], 1))
        values.append(kv[:, PLAIN_WIDTH:])
        mine, got = mine_ref[h], got_ref[h]
        ordered = (jnp.where(first, mine, got), jnp.where(first, got, mine))
        queries.append([block[:, : 2 * LANES] for block in ordered])
        grads.append([block[:, 2 * LANES :] for block in ordered])
    reach = [slice(b * tok, (b + 2) * tok) for b in range(2)]
    units = [(h, b) for h in range(heads) for b in range(2)]
    scores = {(h, b): dot(queries[h][b], keys[h][reach[b]], 1, 1) for h, b in units}
    dprobs = {(h, b): dot(grads[h][b], values[h][reach[b]], 1, 1) for h, b in units}
    dscores, probs16 = {}, {}
    for unit in units:
        logits = jnp.where(visible[unit[1]], scores[unit] * scale, -1e30)
        top = jnp.max(logits, -1, keepdims=True)
        expo = jnp.exp(logits - top)
        probs = expo / jnp.sum(expo, -1, keepdims=True)
        delta = jnp.sum(probs * dprobs[unit], -1, keepdims=True)
        dscores[unit] = (probs * (dprobs[unit] - delta) * scale).astype(BF16)
        probs16[unit] = probs.astype(BF16)

    def fold(low, high):
        return jnp.concatenate([low[:tok], low[tok:] + high[:tok], high[tok:]], 0)

    parts, rope = [], None
    for h in range(heads):
        dk = fold(*[dot(dscores[h, b], queries[h][b], 0, 0) for b in range(2)])
        dv = fold(*[dot(probs16[h, b], grads[h][b], 0, 0) for b in range(2)])
        parts.append(jnp.concatenate([dk[:, :PLAIN_WIDTH], dv], 1).astype(BF16))
        rope = dk[:, PLAIN_WIDTH:] if rope is None else rope + dk[:, PLAIN_WIDTH:]
    dkv = jnp.concatenate(parts, 1)
    rows = lat_ref.shape[0] // 8

    wide = dkv.shape[1] // len(ways)

    for k, along_x in enumerate(ways):
        columns = slice(k * wide, (k + 1) * wide)

        def term(low, high):
            pair = [lat_ref[g * rows : (g + 1) * rows, :] for g in (low, high)]
            return dot(jnp.concatenate(pair, 0), dkv[:, columns], 1, 0)

        for at, groups in enumerate(((2, 3), (6, 7)) if along_x else ((1, 3), (5, 7))):
            block = slice(2 * at * rows, 2 * (at + 1) * rows)
            send_refs[k][block, :] = term(*groups).astype(BF16)
        for at, groups in enumerate(((0, 1), (4, 5)) if along_x else ((0, 2), (4, 6))):
            block = slice(2 * at * rows, 2 * (at + 1) * rows)
            keep_ref[block, columns] = term(*groups)
    total = key_ref[:, :LAT]
    for h in range(heads):
        total = total + dot(parts[h], wt_ref[h], 1, 1)
    key_ref[:, :LAT] = total
    key_ref[:, LAT:] = key_ref[:, LAT:] + rope
    for h in range(heads):
        low, high = (dot(dscores[h, b], keys[h][reach[b]], 1, 0) for b in range(2))
        dq_ref[h] = jnp.where(first, low, high)
        back_ref[h] = jnp.where(first, high, low)


def chunk(here, window, weight, mine, got, before, index, heads, ways):
    tok = mine.shape[1]
    whole = lambda i, here: (0, 0)
    whole3 = lambda i, here: (0, 0, 0)
    step = min(heads, STEP_HEADS)
    steps = heads // step
    at = lambda i, here: (index * steps + i, 0, 0)
    in_half = lambda i, here: (index * steps + i) % (weight.shape[0] // step)
    across_columns = lambda i, here: (0, i)
    columns = heads * PAIR
    operands = [*window, weight, mine, got]
    in_specs = [
        pl.BlockSpec(array.shape, whole3 if array.ndim == 3 else whole) for array in window
    ] + [
        pl.BlockSpec((step, LAT, PAIR), lambda i, here: (in_half(i, here), 0, 0)),
        pl.BlockSpec((step, tok, 3 * LANES), at),
        pl.BlockSpec((step, tok, 3 * LANES), at),
    ]
    aliases = {}
    if before is not None:
        key, dq, back = before
        aliases = {len(operands) + 2: 2, len(operands) + 3: 3}
        in_specs = in_specs + [
            pl.BlockSpec(key.shape, whole),
            pl.BlockSpec(memory_space=pl.ANY),
            pl.BlockSpec(memory_space=pl.ANY),
        ]
        operands = operands + [key, dq, back]
    turned = (mine.shape[0], tok, 2 * LANES)
    return pl.pallas_call(
        functools.partial(chunk_kernel, chained=before is not None, ways=ways),
        grid_spec=pltpu.PrefetchScalarGridSpec(
            num_scalar_prefetch=1,
            grid=(steps,),
            in_specs=in_specs,
            out_specs=[
                pl.BlockSpec((LAT // 2, step * PAIR), across_columns),
                pl.BlockSpec((3 * tok, LAT + LANES), whole),
                pl.BlockSpec((step, tok, 2 * LANES), at),
                pl.BlockSpec((step, tok, 2 * LANES), at),
            ]
            + [pl.BlockSpec((LAT // 2, step * PAIR // len(ways)), across_columns)] * len(ways),
        ),
        out_shape=[
            jax.ShapeDtypeStruct((LAT // 2, columns), F32),
            jax.ShapeDtypeStruct((3 * tok, LAT + LANES), F32),
            jax.ShapeDtypeStruct(turned, F32),
            jax.ShapeDtypeStruct(turned, F32),
        ]
        + [jax.ShapeDtypeStruct((LAT // 2, columns // len(ways)), BF16)] * len(ways),
        input_output_aliases=aliases,
        compiler_params=PARAMS,
        cost_estimate=cost(CHUNK),
        name="chunk",
    )(here, *operands)


def add_rows_kernel(*refs, count, wide):
    total = refs[0][...].astype(F32)
    for ref in refs[1 : count + wide]:
        total = total + ref[...].astype(F32)
    refs[-1][...] = total.astype(refs[-1].dtype)


def add_rows(arrays, rows, index, dtype, wide=(), place=0, places=1, before=None):
    columns = arrays[0].shape[1]
    operands = [*arrays, *wide]
    in_specs = [pl.BlockSpec((rows, columns), lambda i: (index, 0)) for _ in arrays]
    in_specs = in_specs + [pl.BlockSpec((rows, columns), lambda i: (index, place)) for _ in wide]
    aliases = {}
    if before is not None:
        aliases = {len(operands): 0}
        in_specs.append(pl.BlockSpec(memory_space=pl.ANY))
        operands.append(before)
    return pl.pallas_call(
        functools.partial(add_rows_kernel, count=len(arrays), wide=len(wide)),
        grid=(1,),
        in_specs=in_specs,
        out_specs=pl.BlockSpec((rows, columns), lambda i: (0, place)),
        out_shape=jax.ShapeDtypeStruct((rows, places * columns), dtype),
        input_output_aliases=aliases,
        compiler_params=PARAMS,
        cost_estimate=cost(SHARES),
        name="add_rows",
    )(*operands)


def key_split_kernel(here_ref, key_ref, keep_ref, give_ref):
    tok = keep_ref.shape[0] // 2
    first = (here_ref[0] & 1) == 0
    behind, low, high = (key_ref[b * tok : (b + 1) * tok, :] for b in range(3))
    keep_ref[:tok] = jnp.where(first, low, high)
    keep_ref[tok:] = behind
    give_ref[:tok] = jnp.where(first, high, low)
    give_ref[tok:] = behind


def key_split(here, key):
    rows = key.shape[0] // 3 * 2
    whole = lambda i, here: (0, 0)
    return pl.pallas_call(
        key_split_kernel,
        grid_spec=pltpu.PrefetchScalarGridSpec(
            num_scalar_prefetch=1,
            grid=(1,),
            in_specs=[pl.BlockSpec(key.shape, whole)],
            out_specs=[pl.BlockSpec((rows, key.shape[1]), whole)] * 2,
        ),
        out_shape=[jax.ShapeDtypeStruct((rows, key.shape[1]), F32)] * 2,
        compiler_params=PARAMS,
        cost_estimate=cost(SHARES),
        name="key_split",
    )(here, key)


def key_shares_kernel(at_ref, keep_ref, got_ref, *outs):
    shares = len(outs)
    part = (LAT + ROPE) // shares
    total = keep_ref[...] + got_ref[...]
    for z in range(shares):
        piece = total[:, z * part : (z + 1) * part]
        for s in range(shares):

            @pl.when(lax.rem(at_ref[0] + s, shares) == z)
            def _(s=s, piece=piece):
                outs[s][...] = piece.astype(outs[s].dtype)


def key_shares(at_head, keep, got, shares):
    part = (LAT + ROPE) // shares
    rows = keep.shape[0]
    whole = lambda i, at: (0, 0)
    types = [F32] + [BF16] * (shares - 1)
    return pl.pallas_call(
        key_shares_kernel,
        grid_spec=pltpu.PrefetchScalarGridSpec(
            num_scalar_prefetch=1,
            grid=(1,),
            in_specs=[pl.BlockSpec(keep.shape, whole)] * 2,
            out_specs=[pl.BlockSpec((rows, part), whole)] * shares,
        ),
        out_shape=[jax.ShapeDtypeStruct((rows, part), kind) for kind in types],
        compiler_params=PARAMS,
        cost_estimate=cost(SHARES),
        name="key_shares",
    )(at_head, keep, got)


def query_grad_kernel(here_ref, mine_ref, got_ref, out_ref, n_ref, r_ref):
    tok, heads, _ = out_ref.shape

    def put(src_ref):
        for h in range(heads):
            n_ref[pl.ds(h, tok, stride=heads), :] = src_ref[h, :, :PLAIN_WIDTH]
            r_ref[pl.ds(h, tok, stride=heads), :] = src_ref[h, :, PLAIN_WIDTH:]

    pl.when(pl.program_id(0) == 0)(lambda: put(mine_ref))
    pl.when(pl.program_id(0) == 1)(lambda: put(got_ref))
    out_ref[:, :, :PLAIN_WIDTH] = n_ref[...].reshape(tok, heads, LANES)
    out_ref[:, :, PLAIN_WIDTH:] = r_ref[...].reshape(tok, heads, LANES)[:, :, :ROPE]


def query_grad(here, mine, got):
    heads, tok, _ = mine.shape
    whole = lambda i, here: (0, 0, 0)
    return pl.pallas_call(
        query_grad_kernel,
        grid_spec=pltpu.PrefetchScalarGridSpec(
            num_scalar_prefetch=1,
            grid=(2,),
            in_specs=[pl.BlockSpec(mine.shape, whole)] * 2,
            out_specs=pl.BlockSpec(
                (tok, heads, PLAIN_WIDTH + ROPE), lambda i, here: (0, (here[0] & 1) ^ i, 0)
            ),
            scratch_shapes=[pltpu.VMEM((tok * heads, LANES), F32)] * 2,
        ),
        out_shape=jax.ShapeDtypeStruct((tok, 2 * heads, PLAIN_WIDTH + ROPE), F32),
        compiler_params=PARAMS,
        cost_estimate=cost(QUERY),
        name="query_grad",
    )(here, mine, got)


def join_kernel(*refs, pieces, wide):
    out_ref = refs[-1]
    for k in range(pieces):
        total = refs[2 * k][...] + refs[2 * k + 1][...].astype(F32)
        out_ref[:, k * wide : (k + 1) * wide] = total.astype(BF16)
    if len(refs) > 2 * pieces + 1:
        out_ref[:, pieces * wide :] = refs[2 * pieces][...]


def join(pieces, rows, wide, theirs=None):
    operands, in_specs = [], []
    for piece in pieces:
        for array, column in piece:
            operands.append(array)
            in_specs.append(pl.BlockSpec((rows, wide), lambda i, column=column: (1, column)))
    columns = len(pieces) * wide
    if theirs is not None:
        operands.append(theirs)
        in_specs.append(pl.BlockSpec((rows, columns), lambda i: (1, 0)))
        columns = 2 * columns
    return pl.pallas_call(
        functools.partial(join_kernel, pieces=len(pieces), wide=wide),
        grid=(1,),
        in_specs=in_specs,
        out_specs=pl.BlockSpec((rows, columns), lambda i: (0, 0)),
        out_shape=jax.ShapeDtypeStruct((rows, columns), BF16),
        compiler_params=PARAMS,
        cost_estimate=cost(SHARES),
        name="join",
    )(*operands)


def last_sums_kernel(here_ref, *refs, order, count, wide):
    share_ref, behind_ref, out_ref, key_ref, k_ref, v_ref = refs[-6:]
    rows, heads, _ = out_ref.shape
    size = 2 * count + 2
    each = wide // PAIR
    key_ref[...] = share_ref[...] + behind_ref[...]

    def put(j, total):
        for h in range(each):
            at = pl.ds(j * each + h, rows, stride=heads)
            k_ref[at, :] = total[:, h * PAIR : h * PAIR + LANES]
            v_ref[at, :] = total[:, h * PAIR + LANES : (h + 1) * PAIR]

    for q, places in enumerate(order):
        for j, (pair, piece) in enumerate(places):
            group = refs[pair * size : (pair + 1) * size]
            kept, came = group[2 * piece : 2 * piece + 2]
            theirs_ref, last_ref = group[-2:]
            columns = slice(piece * wide, (piece + 1) * wide)
            later = slice((count + piece) * wide, (count + piece + 1) * wide)

            @pl.when(pl.program_id(0) == 2 * q)
            def _(j=j, kept=kept, came=came, last_ref=last_ref, columns=columns):
                total = kept[...] + came[...].astype(F32)
                put(j, total + last_ref[:, columns].astype(F32))

            @pl.when(pl.program_id(0) == 2 * q + 1)
            def _(j=j, theirs_ref=theirs_ref, last_ref=last_ref, columns=columns, later=later):
                put(j, theirs_ref[:, columns].astype(F32) + last_ref[:, later].astype(F32))

    out_ref[:, :, :LANES] = k_ref[...].reshape(rows, heads, LANES)
    out_ref[:, :, LANES:] = v_ref[...].reshape(rows, heads, LANES)


def last_sums(here, pieces, theirs, lasts, share, behind, order, wide):
    rows, heads = share.shape[0], len(order[0]) * wide // PAIR
    whole = lambda i, here: (0, 0)
    operands, in_specs = [], []
    for group, other, last in zip(pieces, theirs, lasts):
        for array, column in [part for piece in group for part in piece]:
            operands.append(array)
            in_specs.append(pl.BlockSpec((rows, wide), lambda i, here, column=column: (0, column)))
        for array in (other, last):
            operands.append(array)
            in_specs.append(pl.BlockSpec((rows, array.shape[1]), whole))
    in_specs = in_specs + [pl.BlockSpec(share.shape, whole)] * 2
    return pl.pallas_call(
        functools.partial(last_sums_kernel, order=order, count=len(pieces[0]), wide=wide),
        grid_spec=pltpu.PrefetchScalarGridSpec(
            num_scalar_prefetch=1,
            grid=(4,),
            in_specs=in_specs,
            out_specs=[
                pl.BlockSpec(
                    (rows, heads, PAIR),
                    lambda i, here: (0, ((here[0] & 1) ^ (i & 1)) * 2 + (i >> 1), 0),
                ),
                pl.BlockSpec(share.shape, whole),
            ],
            scratch_shapes=[pltpu.VMEM((rows * heads, LANES), F32)] * 2,
        ),
        out_shape=[
            jax.ShapeDtypeStruct((rows, 4 * heads, PAIR), F32),
            jax.ShapeDtypeStruct(share.shape, F32),
        ],
        compiler_params=PARAMS,
        cost_estimate=cost(SUM),
        name="last_sums",
    )(here, *operands, share, behind)


def in_chunks(queries, latent_keys, out_grad, up_weight, here, at_head, ids):
    tok = latent_keys.shape[0]
    n_ctx, n_head = lax.axis_size("ctx"), lax.axis_size("head")
    heads, each = 16, 4
    queries = after(queries, (ids, here, at_head))
    give, mine = turn_tokens(here, queries, out_grad, latent_keys, heads)
    odd_devices = range(1, n_ctx - 1, 2)
    even = lax.ppermute(latent_keys, "ctx", [(source, source + 1) for source in odd_devices])
    odd = lax.ppermute(latent_keys, "ctx", [(source, source + 2) for source in odd_devices])
    got = across(give, 1)
    weight = turn_weight(here, up_weight, heads)
    window = chip_window(here, even, odd, latent_keys, got, ids)
    ways, bits, wide = ((True, False), (False,), (True,), (True, False)), (2, 4), 2 * PAIR
    before, pieces = None, ([], [])
    for c in range(4):
        keep, *before = chunk(here, window, weight, mine, got, before, c, each, ways[c])
        before, outs = before[:3], before[3:]
        for k, (along_x, out) in enumerate(zip(ways[c], outs)):
            came = across(out, bits[0] if along_x else bits[1])
            for at in range(2 // len(outs)):
                pieces[0 if along_x else 1].append(((keep, k + at), (came, at)))
    order = (((0, 0), (1, 0), (1, 1), (1, 2)), ((0, 1), (0, 2), (0, 3), (1, 3)))
    key, dq, back = before
    key = after(key, [pieces[p][0][1][0] for p in range(2)])
    key_keep, key_give = key_split(here, key)
    key_got = across(key_give, 1)
    shares = key_shares(at_head, key_keep, key_got, n_head)
    came = [
        lax.ppermute(shares[s], "head", [(z, (z + s) % n_head) for z in range(n_head)])
        for s in range(1, n_head)
    ]
    back = across(after(back, key_keep), 1)
    share, behind = (add_rows((shares[0], *came), tok, b, F32) for b in range(2))
    behind = lax.ppermute(behind, "ctx", [(source, source - 1) for source in range(2, n_ctx, 2)])
    keep = after(keep, share)
    for p in range(2):
        pieces[p][3] = ((keep, pieces[p][3][0][1]), pieces[p][3][1])
    theirs, seconds, lasts = [], [], []
    for p in range(2):
        first = join(pieces[p], 2 * tok, wide)
        theirs.append(across(first, 1))
        seconds.append(join(pieces[p], tok, wide, theirs[p]))
        lasts.append(across(seconds[p], bits[1 - p]))
    dq = query_grad(here, after(dq, seconds), back)
    theirs = after(theirs, dq)
    weight_grad, key_grad = last_sums(
        here, pieces, theirs, lasts, share, behind, order, wide
    )
    return dq, key_grad, weight_grad


def shards(queries, latent_keys, out_grad, up_weight, segment_ids):
    tok = latent_keys.shape[0]
    heads = queries.shape[1]
    n_ctx, n_head = lax.axis_size("ctx"), lax.axis_size("head")
    here = lax.axis_index("ctx").astype(jnp.int32).reshape(1)
    at_head = lax.axis_index("head").astype(jnp.int32).reshape(1)
    if n_ctx == 8 and heads == 32 and n_head == 4:
        ids = segment_ids.reshape(n_ctx // 2, 2 * tok)
        return in_chunks(queries, latent_keys, out_grad, up_weight, here, at_head, ids)
    else:
        ids = segment_ids.reshape(n_ctx, tok)
        prev = from_behind(latent_keys, "ctx", REACH)
        turned = by_head(up_weight, queries, out_grad, 0, heads)
        window = key_window(here, prev, latent_keys, ids, False)
        dq, dkv, rope = attention(window, turned, None, None, 0, heads, 0, heads)
        (both,) = key_terms(at_head, [dkv], [turned[0]], [rope], None)
        share = lax.psum_scatter(
            both.reshape(REACH + 1, tok, LAT + ROPE), "head", scatter_dimension=2, tiled=True
        )
        term = jnp.einsum("ki,ke->ie", window[0], dkv, preferred_element_type=F32)
        rows = lax.psum_scatter(term.astype(BF16), "ctx", scatter_dimension=0, tiled=True)
        weight_grad = rows.astype(F32).reshape(rows.shape[0], heads, PAIR)
    key_grad = share[REACH] + from_behind(share[0], "ctx", 0 - REACH)
    return (dq, key_grad, weight_grad)


def solution(mesh):
    return jax.shard_map(
        shards,
        mesh=mesh,
        in_specs=(
            P("ctx", "head", None),
            P("ctx", None),
            P("ctx", "head", None),
            P(None, "head", None),
            P(),
        ),
        out_specs=(P("ctx", "head", None), P("ctx", "head"), P("ctx", "head", None)),
        check_vma=False,
    )
```

```python
import functools
import math

import jax
import jax.numpy as jnp
from jax import lax
from jax.experimental import pallas as pl
from jax.experimental.pallas import tpu as pltpu
from jax.sharding import PartitionSpec as P

LAT = 512
ROPE = 64
PLAIN_WIDTH = 128
VDIM = 128
REACH = 1
LANES = 128
PAIR = PLAIN_WIDTH + VDIM
STEP_HEADS = 4
BF16 = jnp.bfloat16
F32 = jnp.float32
WIDE = pltpu.CompilerParams(vmem_limit_bytes=56 * 1024 * 1024)
PARAMS = pltpu.CompilerParams(vmem_limit_bytes=20 * 1024 * 1024)


def from_behind(value, axis, steps):
    count = lax.axis_size(axis)
    initial, last = (max(0, -steps), min(count, count - steps))
    return lax.ppermute(value, axis, [(source, source + steps) for source in range(initial, last)])


def across(value, bit):
    count = lax.axis_size("ctx")
    return lax.ppermute(value, "ctx", [(source, source ^ bit) for source in range(count)])


def cost(share):
    return pl.CostEstimate(flops=int(share * 1e9), bytes_accessed=1024, transcendentals=0)


TURN, WINDOW, CHUNK, SHARES, QUERY, SUM = 0.1, 0.1, 0.1, 0.01, 0.01, 0.01


def dot(a, b, a_dim, b_dim):
    return lax.dot_general(a, b, (((a_dim,), (b_dim,)), ((), ())), preferred_element_type=F32)


def by_head_kernel(w_ref, q_ref, g_ref, wt_ref, qt_ref, gt_ref):
    heads = w_ref.shape[1]
    orders = {}

    def order(count):
        if count not in orders:
            size = count * heads
            row = lax.broadcasted_iota(jnp.int32, (size, size), 0)
            col = lax.broadcasted_iota(jnp.int32, (size, size), 1)
            wanted = (row % count) * heads + row // count
            orders[count] = (col == wanted).astype(BF16)
        return orders[count]

    def turn(ref, out_ref):
        rows, _, width = ref.shape
        count = min(rows, 256 // heads)
        for start in range(0, rows, count):
            block = ref[start : start + count].reshape(count * heads, width)
            turned = dot(order(count), block, 1, 0).astype(BF16)
            out_ref[:, start : start + count, :width] = turned.reshape(heads, count, width)

    turn(w_ref, wt_ref)
    qt_ref[...] = jnp.zeros_like(qt_ref)
    turn(q_ref, qt_ref)
    turn(g_ref, gt_ref)


def by_head(up_weight, queries, out_grad, chunk, heads):
    tok = queries.shape[0]
    steps = 4
    depth, rows = LAT // steps, tok // steps
    return pl.pallas_call(
        by_head_kernel,
        grid=(steps,),
        in_specs=[
            pl.BlockSpec((depth, heads, PAIR), lambda i: (i, chunk, 0)),
            pl.BlockSpec((rows, heads, PLAIN_WIDTH + ROPE), lambda i: (i, chunk, 0)),
            pl.BlockSpec((rows, heads, VDIM), lambda i: (i, chunk, 0)),
        ],
        out_specs=[
            pl.BlockSpec((heads, depth, PAIR), lambda i: (0, i, 0)),
            pl.BlockSpec((heads, rows, 2 * LANES), lambda i: (0, i, 0)),
            pl.BlockSpec((heads, rows, VDIM), lambda i: (0, i, 0)),
        ],
        out_shape=[
            jax.ShapeDtypeStruct((heads, LAT, PAIR), BF16),
            jax.ShapeDtypeStruct((heads, tok, 2 * LANES), BF16),
            jax.ShapeDtypeStruct((heads, tok, VDIM), BF16),
        ],
        compiler_params=WIDE,
        cost_estimate=cost(TURN),
        name="by_head",
    )(up_weight, queries, out_grad)


def window_kernel(here_ref, prev_ref, own_ref, ids_ref, *outs, paired):
    win_ref, krope_ref, vis_ref = outs[:3]
    here = here_ref[0]
    tok = prev_ref.shape[0]
    win_ref[:tok, :] = prev_ref[:, :LAT]
    win_ref[tok:, :] = own_ref[:, :LAT]
    krope_ref[...] = jnp.zeros_like(krope_ref)
    krope_ref[:tok, :ROPE] = prev_ref[:, LAT:]
    krope_ref[tok:, :ROPE] = own_ref[:, LAT:]
    behind = jnp.maximum(here - 1, 0)
    seg_prev = jnp.where(here > 0, ids_ref[pl.ds(behind, 1), :], -1)
    seg_own = ids_ref[pl.ds(here, 1), :]
    row = lax.broadcasted_iota(jnp.int32, (tok, tok), 0)
    col = lax.broadcasted_iota(jnp.int32, (tok, tok), 1)
    seg_query = jnp.sum(jnp.where(row == col, seg_own, 0), 1, keepdims=True)
    vis_ref[:, :tok] = (seg_query == seg_prev).astype(F32)
    vis_ref[:, tok:] = ((seg_query == seg_own) & (col <= row)).astype(F32)
    if paired:
        source = lax.broadcasted_iota(jnp.int32, (LAT, LAT), 0)
        column = lax.broadcasted_iota(jnp.int32, (LAT, LAT), 1)
        place = column >> 6
        apart = ((place & 1) << 2) | (place & 2) | (place >> 2)
        wanted = ((here ^ apart) << 6) | (column & 63)
        ordered = dot(win_ref[...], (source == wanted).astype(BF16), 1, 0).astype(BF16)
        outs[3][...] = ordered[:, : LAT // 2]
        outs[4][...] = ordered[:, LAT // 2 :]


def key_window(here, prev, own, ids, paired):
    tok = prev.shape[0]
    whole = lambda i, here: (0, 0)
    shapes = [((2 * tok, LAT), BF16), ((2 * tok, LANES), BF16), ((tok, 2 * tok), F32)]
    if paired:
        shapes = shapes + [((2 * tok, LAT // 2), BF16)] * 2
    return pl.pallas_call(
        functools.partial(window_kernel, paired=paired),
        grid_spec=pltpu.PrefetchScalarGridSpec(
            num_scalar_prefetch=1,
            grid=(1,),
            in_specs=[pl.BlockSpec(array.shape, whole) for array in (prev, own, ids)],
            out_specs=[pl.BlockSpec(shape, whole) for shape, _ in shapes],
        ),
        out_shape=[jax.ShapeDtypeStruct(*shape) for shape in shapes],
        compiler_params=PARAMS,
        cost_estimate=cost(WINDOW),
        name="key_window",
    )(here, prev, own, ids)


def attention_kernel(
    win_ref, krope_ref, vis_ref, wt_ref, qt_ref, gt_ref, *refs, aliased, extra
):
    latents_ref = refs[0] if extra else None
    refs = refs[1:] if extra else refs
    refs = refs[1:] if aliased else refs
    dq_ref, dkv_ref, rope_ref, dqn_ref, dqr_ref = refs
    i = pl.program_id(0)
    tok, heads = dq_ref.shape[:2]
    scale = 1.0 / math.sqrt(PLAIN_WIDTH + ROPE)

    @pl.when(i == 0)
    def _():
        rope_ref[...] = jnp.zeros_like(rope_ref)
        if extra:
            dkv_ref[:, heads * PAIR :] = latents_ref[...]

    visible = vis_ref[...] > 0.0
    window = win_ref[...]
    krope = krope_ref[...]
    count = wt_ref.shape[0]
    keys, values = [], []
    for h in range(count):
        kv = dot(window, wt_ref[h], 1, 0).astype(BF16)
        keys.append(jnp.concatenate([kv[:, :PLAIN_WIDTH], krope], 1))
        values.append(kv[:, PLAIN_WIDTH:])
    scores = [dot(qt_ref[h], keys[h], 1, 1) for h in range(count)]
    dprobs = [dot(gt_ref[h], values[h], 1, 1) for h in range(count)]
    dscores, probs16 = [], []
    for h in range(count):
        logits = jnp.where(visible, scores[h] * scale, -1e30)
        top = jnp.max(logits, -1, keepdims=True)
        expo = jnp.exp(logits - top)
        probs = expo / jnp.sum(expo, -1, keepdims=True)
        delta = jnp.sum(probs * dprobs[h], -1, keepdims=True)
        dscores.append((probs * (dprobs[h] - delta) * scale).astype(BF16))
        probs16.append(probs.astype(BF16))
    parts, rope = [], rope_ref[...]
    for h in range(count):
        dk = dot(dscores[h], qt_ref[h], 0, 0)
        dv = dot(probs16[h], gt_ref[h], 0, 0)
        parts.append(jnp.concatenate([dk[:, :PLAIN_WIDTH], dv], 1).astype(BF16))
        rope = rope + dk[:, PLAIN_WIDTH:]
    rope_ref[...] = rope
    dkv_ref[:, pl.ds(pl.multiple_of(i * (count * PAIR), count * PAIR), count * PAIR)] = (
        jnp.concatenate(parts, 1)
    )
    for h in range(count):
        dq = dot(dscores[h], keys[h], 1, 0)
        dqn_ref[pl.ds(i * count + h, tok, stride=heads), :] = dq[:, :PLAIN_WIDTH]
        dqr_ref[pl.ds(i * count + h, tok, stride=heads), :] = dq[:, PLAIN_WIDTH:]

    @pl.when(i == pl.num_programs(0) - 1)
    def _():
        dq_ref[:, :, :PLAIN_WIDTH] = dqn_ref[...].reshape(tok, heads, LANES)
        dq_ref[:, :, PLAIN_WIDTH:] = dqr_ref[...].reshape(tok, heads, LANES)[:, :, :ROPE]


def attention(window, turned, latents, dq, chunk, heads, first, all_heads):
    weight, queries, out_grad = turned
    tok = queries.shape[1]
    width = 2 * tok
    steps = heads // STEP_HEADS
    at = first // STEP_HEADS
    extra = LAT // 2 if latents is not None else 0
    whole = lambda i: (0, 0)
    head_block = lambda i: (at + i, 0, 0)
    operands = [*window, weight, queries, out_grad]
    in_specs = [pl.BlockSpec(array.shape, whole) for array in window] + [
        pl.BlockSpec((STEP_HEADS, LAT, PAIR), head_block),
        pl.BlockSpec((STEP_HEADS, tok, 2 * LANES), head_block),
        pl.BlockSpec((STEP_HEADS, tok, VDIM), head_block),
    ]
    if latents is not None:
        in_specs.append(pl.BlockSpec(latents.shape, whole))
        operands.append(latents)
    aliases = {}
    if dq is not None:
        aliases = {len(operands): 0}
        in_specs.append(pl.BlockSpec(memory_space=pl.ANY))
        operands.append(dq)
    return pl.pallas_call(
        functools.partial(attention_kernel, aliased=dq is not None, extra=latents is not None),
        grid=(steps,),
        in_specs=in_specs,
        out_specs=[
            pl.BlockSpec((tok, heads, PLAIN_WIDTH + ROPE), lambda i: (0, chunk, 0)),
            pl.BlockSpec((width, heads * PAIR + extra), whole),
            pl.BlockSpec((width, LANES), whole),
        ],
        scratch_shapes=[
            pltpu.VMEM((tok * heads, LANES), F32),
            pltpu.VMEM((tok * heads, LANES), F32),
        ],
        out_shape=[
            jax.ShapeDtypeStruct((tok, all_heads, PLAIN_WIDTH + ROPE), F32),
            jax.ShapeDtypeStruct((width, heads * PAIR + extra), BF16),
            jax.ShapeDtypeStruct((width, LANES), F32),
        ],
        input_output_aliases=aliases,
        compiler_params=WIDE,
        cost_estimate=cost(CHUNK),
        name="attention",
    )(*operands)


def terms_kernel(
    own_ref, other_ref, mine_ref, theirs_ref, keep_ref, send_ref, latents_ref, *, along_x
):
    width = own_ref.shape[0]

    @pl.when(pl.program_id(0) == 0)
    def _():
        latents_ref[:, :width] = mine_ref[...].T
        latents_ref[:, width:] = theirs_ref[...].T

    grads = jnp.concatenate([own_ref[...], other_ref[...]], 0)
    term = dot(latents_ref[...], grads, 1, 0)
    rows = term.shape[0] // 4
    first, second = (1, 2) if along_x else (2, 1)
    keep_ref[:rows] = term[:rows]
    keep_ref[rows:] = term[first * rows : (first + 1) * rows]
    send_ref[:rows] = term[second * rows : (second + 1) * rows].astype(BF16)
    send_ref[rows:] = term[3 * rows :].astype(BF16)


def terms(own, other, mine, theirs, columns, along_x):
    width = own.shape[0]
    block = 1024
    at = theirs.shape[1] // (LAT // 2) - 1
    column_block = lambda i: (0, i)
    return pl.pallas_call(
        functools.partial(terms_kernel, along_x=along_x),
        grid=(columns // block,),
        in_specs=[
            pl.BlockSpec((width, block), column_block),
            pl.BlockSpec((width, block), column_block),
            pl.BlockSpec((width, LAT // 2), lambda i: (0, 0)),
            pl.BlockSpec((width, LAT // 2), lambda i: (0, at)),
        ],
        out_specs=[pl.BlockSpec((LAT // 4, block), column_block)] * 2,
        out_shape=[
            jax.ShapeDtypeStruct((LAT // 4, columns), F32),
            jax.ShapeDtypeStruct((LAT // 4, columns), BF16),
        ],
        scratch_shapes=[pltpu.VMEM((LAT // 2, 2 * width), BF16)],
        compiler_params=PARAMS,
        cost_estimate=cost(CHUNK),
        name="terms",
    )(own, other, mine, theirs)


def key_terms_kernel(*refs, chunks, steps, turns, shares):
    head_ref = refs[0]
    dkv_refs = refs[1 : 1 + chunks]
    wt_refs = refs[1 + chunks : 1 + chunks + turns]
    rope_refs = refs[1 + chunks + turns : 1 + 2 * chunks + turns]
    outs = refs[1 + 2 * chunks + turns : -1]
    total_ref = refs[-1]
    i = pl.program_id(0)

    @pl.when(i == 0)
    def _():
        total_ref[...] = jnp.zeros_like(total_ref)

    for k in range(chunks):

        @pl.when(i // steps == k)
        def _(k=k):
            total = total_ref[...]
            weight_ref = wt_refs[k * turns // chunks]
            for h in range(weight_ref.shape[0]):
                grads = dkv_refs[k][:, h * PAIR : (h + 1) * PAIR]
                total = total + dot(grads, weight_ref[h], 1, 1)
            total_ref[...] = total

    @pl.when(i == pl.num_programs(0) - 1)
    def _():
        rope = rope_refs[0][...]
        for k in range(1, chunks):
            rope = rope + rope_refs[k][...]
        both = jnp.concatenate([total_ref[...], rope], 1)
        if shares is None:
            outs[0][...] = both[:, : LAT + ROPE]
            return
        part = (LAT + ROPE) // shares
        for z in range(shares):
            piece = both[:, z * part : (z + 1) * part]
            for s in range(shares):

                @pl.when(lax.rem(head_ref[0] + s, shares) == z)
                def _(s=s, piece=piece):
                    outs[s][...] = piece


def key_terms(at_head, dkvs, weights, ropes, shares):
    chunks, turns = len(dkvs), len(weights)
    heads = weights[0].shape[0] * turns // chunks
    width = dkvs[0].shape[0]
    steps = heads // STEP_HEADS
    span = steps * chunks // turns
    near = lambda k, many: lambda i, at: jnp.clip(i - k * many, 0, many - 1)
    wide = (LAT + ROPE) // (shares or 1)
    return pl.pallas_call(
        functools.partial(
            key_terms_kernel, chunks=chunks, steps=steps, turns=turns, shares=shares
        ),
        grid_spec=pltpu.PrefetchScalarGridSpec(
            num_scalar_prefetch=1,
            grid=(chunks * steps,),
            in_specs=[
                pl.BlockSpec((width, STEP_HEADS * PAIR), lambda i, at, k=k: (0, near(k, steps)(i, at)))
                for k in range(chunks)
            ]
            + [
                pl.BlockSpec(
                    (STEP_HEADS, LAT, PAIR), lambda i, at, k=k: (near(k, span)(i, at), 0, 0)
                )
                for k in range(turns)
            ]
            + [pl.BlockSpec((width, LANES), lambda i, at: (0, 0))] * chunks,
            out_specs=[pl.BlockSpec((width, wide), lambda i, at: (0, 0))] * (shares or 1),
            scratch_shapes=[pltpu.VMEM((width, LAT), F32)],
        ),
        out_shape=[jax.ShapeDtypeStruct((width, wide), F32)] * (shares or 1),
        compiler_params=WIDE,
        cost_estimate=cost(CHUNK),
        name="key_terms",
    )(at_head, *dkvs, *weights, *ropes)


def weight_sum_kernel(keep_ref, first_ref, second_ref, *refs):
    out_ref, k_ref, v_ref = refs[-3:]
    rows, heads, _ = out_ref.shape
    for h in range(heads):
        columns = slice(h * PAIR, (h + 1) * PAIR)
        total = keep_ref[:, columns] + first_ref[:, columns].astype(F32)
        total = total + second_ref[:, columns].astype(F32)
        k_ref[pl.ds(h, rows, stride=heads), :] = total[:, :LANES]
        v_ref[pl.ds(h, rows, stride=heads), :] = total[:, LANES:]
    out_ref[:, :, :LANES] = k_ref[...].reshape(rows, heads, LANES)
    out_ref[:, :, LANES:] = v_ref[...].reshape(rows, heads, LANES)


def weight_sum(keep, first, second, total, chunk, all_heads):
    rows, columns = second.shape
    heads = columns // PAIR
    block = 32
    operands = [keep, first, second]
    in_specs = [pl.BlockSpec((block, columns), lambda i: (i, 0)) for _ in operands]
    aliases = {}
    if total is not None:
        aliases = {3: 0}
        in_specs.append(pl.BlockSpec(memory_space=pl.ANY))
        operands.append(total)
    return pl.pallas_call(
        weight_sum_kernel,
        grid=(rows // block,),
        in_specs=in_specs,
        out_specs=pl.BlockSpec((block, heads, PAIR), lambda i: (i, chunk, 0)),
        out_shape=jax.ShapeDtypeStruct((rows, all_heads, PAIR), F32),
        scratch_shapes=[pltpu.VMEM((block * heads, LANES), F32)] * 2,
        input_output_aliases=aliases,
        compiler_params=PARAMS,
        cost_estimate=cost(SUM),
        name="weight_sum",
    )(*operands)


def after(values, earlier):
    return lax.optimization_barrier((values, earlier))[0]


def turn_rows(block):
    rows, heads, width = block.shape
    count = min(rows, 256 // heads)
    row = lax.broadcasted_iota(jnp.int32, (count * heads, count * heads), 0)
    col = lax.broadcasted_iota(jnp.int32, (count * heads, count * heads), 1)
    order = (col == (row % count) * heads + row // count).astype(BF16)
    for start in range(0, rows, count):
        part = block[start : start + count].reshape(count * heads, width)
        turned = dot(order, part, 1, 0).astype(BF16)
        yield slice(start, start + count), turned.reshape(heads, count, width)


def in_hbm(array):
    return pltpu.with_memory_space_constraint(array, pltpu.HBM)


def turn_weight_kernel(here_ref, *refs):
    *parts, wt_ref = refs
    depth = parts[0].shape[0]
    for at, w_ref in enumerate(parts):
        for rows, turned in turn_rows(w_ref[...]):
            wt_ref[:, at * depth + rows.start : at * depth + rows.stop, :] = turned


def turn_weight(here, up_weight, heads):
    steps, parts = 4, 4
    depth = LAT // steps // parts
    part = lambda p: lambda i, here: (i * parts + p, here[0] & 1, 0)
    return pl.pallas_call(
        turn_weight_kernel,
        grid_spec=pltpu.PrefetchScalarGridSpec(
            num_scalar_prefetch=1,
            grid=(steps,),
            in_specs=[pl.BlockSpec((depth, heads, PAIR), part(p)) for p in range(parts)],
            out_specs=pl.BlockSpec((heads, depth * parts, PAIR), lambda i, here: (0, i, 0)),
        ),
        out_shape=jax.ShapeDtypeStruct((heads, LAT, PAIR), BF16),
        compiler_params=PARAMS,
        cost_estimate=cost(TURN),
        name="turn_weight",
    )(here, *[in_hbm(up_weight)] * parts)


def turn_tokens_kernel(here_ref, q1_ref, g1_ref, q0_ref, g0_ref, own_ref, give_ref, mine_ref):
    heads = mine_ref.shape[0]
    for q_ref, g_ref, out_ref in ((q1_ref, g1_ref, give_ref), (q0_ref, g0_ref, mine_ref)):
        out_ref[:, :, LANES : 2 * LANES] = jnp.zeros_like(out_ref[:, :, LANES : 2 * LANES])
        for rows, turned in turn_rows(q_ref[...]):
            out_ref[:heads, rows, : PLAIN_WIDTH + ROPE] = turned
        for rows, turned in turn_rows(g_ref[...]):
            out_ref[:heads, rows, 2 * LANES :] = turned
    rest = LAT + ROPE - 3 * LANES
    give_ref[heads] = own_ref[:, : 3 * LANES]
    give_ref[heads + 1] = jnp.zeros_like(give_ref[heads + 1])
    give_ref[heads + 1, :, :rest] = own_ref[:, 3 * LANES :]


def turn_tokens(here, queries, out_grad, latent_keys, heads):
    tok = queries.shape[0]
    q_block, g_block = (tok, heads, PLAIN_WIDTH + ROPE), (tok, heads, VDIM)
    given = lambda i, here: (0, 1 - (here[0] & 1), 0)
    kept = lambda i, here: (0, here[0] & 1, 0)
    whole = lambda i, here: (0, 0, 0)
    give, mine = (heads + 2, tok, 3 * LANES), (heads, tok, 3 * LANES)
    queries, out_grad, latent_keys = (in_hbm(x) for x in (queries, out_grad, latent_keys))
    return pl.pallas_call(
        turn_tokens_kernel,
        grid_spec=pltpu.PrefetchScalarGridSpec(
            num_scalar_prefetch=1,
            grid=(1,),
            in_specs=[
                pl.BlockSpec(q_block, given),
                pl.BlockSpec(g_block, given),
                pl.BlockSpec(q_block, kept),
                pl.BlockSpec(g_block, kept),
                pl.BlockSpec(latent_keys.shape, lambda i, here: (0, 0)),
            ],
            out_specs=[pl.BlockSpec(give, whole), pl.BlockSpec(mine, whole)],
        ),
        out_shape=[jax.ShapeDtypeStruct(give, BF16), jax.ShapeDtypeStruct(mine, BF16)],
        compiler_params=PARAMS,
        cost_estimate=cost(WINDOW),
        name="turn_tokens",
    )(here, queries, out_grad, queries, out_grad, latent_keys)


def chip_window_kernel(
    here_ref, even_ref, odd_ref, own_ref, pal_ref, ids_ref, win_ref, krope_ref, vis_ref, lat_ref
):
    here = here_ref[0]
    tok = own_ref.shape[0]
    core, chip = here & 1, here >> 1
    first = core == 0
    prev = jnp.where(first, even_ref[...].astype(F32), odd_ref[...].astype(F32)).astype(BF16)
    pal = jnp.concatenate([pal_ref[0], pal_ref[1, :, : LAT + ROPE - 3 * LANES]], 1).astype(F32)
    own = own_ref[...].astype(F32)
    low = jnp.where(first, own, pal).astype(BF16)
    high = jnp.where(first, pal, own).astype(BF16)
    krope_ref[...] = jnp.zeros_like(krope_ref)
    for at, block in enumerate((prev, low, high)):
        win_ref[at * tok : (at + 1) * tok, :] = block[:, :LAT]
        krope_ref[at * tok : (at + 1) * tok, :ROPE] = block[:, LAT:]
    behind = ids_ref[pl.ds(jnp.maximum(chip - 1, 0), 1), :]
    both = ids_ref[pl.ds(chip, 1), :]
    seg = [jnp.where(chip > 0, behind[:, tok:], -1), both[:, :tok], both[:, tok:]]
    row = lax.broadcasted_iota(jnp.int32, (tok, tok), 0)
    col = lax.broadcasted_iota(jnp.int32, (tok, tok), 1)
    for b in range(2):
        seg_query = jnp.sum(jnp.where(row == col, seg[b + 1], 0), 1, keepdims=True)
        vis_ref[b, :, :tok] = (seg_query == seg[b]).astype(F32)
        vis_ref[b, :, tok:] = ((seg_query == seg[b + 1]) & (col <= row)).astype(F32)
    column = lax.broadcasted_iota(jnp.int32, (LAT, LAT), 0)
    source = lax.broadcasted_iota(jnp.int32, (LAT, LAT), 1)
    place = column >> 6
    apart = ((place & 1) << 2) | (place & 2) | (place >> 2)
    wanted = ((here ^ apart) << 6) | (column & 63)
    order = (source == wanted).astype(BF16)
    lat_ref[...] = dot(order, win_ref[...], 1, 1).astype(BF16)


def chip_window(here, even, odd, own, got, ids):
    tok = own.shape[0]
    whole = lambda i, here: (0, 0)
    return pl.pallas_call(
        chip_window_kernel,
        grid_spec=pltpu.PrefetchScalarGridSpec(
            num_scalar_prefetch=1,
            grid=(1,),
            in_specs=[pl.BlockSpec(array.shape, whole) for array in (even, odd, own)]
            + [
                pl.BlockSpec((2,) + got.shape[1:], lambda i, here: (got.shape[0] // 2 - 1, 0, 0)),
                pl.BlockSpec(ids.shape, whole),
            ],
            out_specs=[
                pl.BlockSpec((3 * tok, LAT), whole),
                pl.BlockSpec((3 * tok, LANES), whole),
                pl.BlockSpec((2, tok, 2 * tok), lambda i, here: (0, 0, 0)),
                pl.BlockSpec((LAT, 3 * tok), whole),
            ],
        ),
        out_shape=[
            jax.ShapeDtypeStruct((3 * tok, LAT), BF16),
            jax.ShapeDtypeStruct((3 * tok, LANES), BF16),
            jax.ShapeDtypeStruct((2, tok, 2 * tok), F32),
            jax.ShapeDtypeStruct((LAT, 3 * tok), BF16),
        ],
        compiler_params=PARAMS,
        cost_estimate=cost(WINDOW),
        name="chip_window",
    )(here, even, odd, own, got, ids)


def chunk_kernel(
    here_ref,
    win_ref,
    krope_ref,
    vis_ref,
    lat_ref,
    wt_ref,
    mine_ref,
    got_ref,
    *refs,
    chained,
    ways,
):
    before_ref = refs[0] if chained else None
    refs = refs[3:] if chained else refs
    keep_ref, key_ref, dq_ref, back_ref, *send_refs = refs

    @pl.when(pl.program_id(0) == 0)
    def _():
        key_ref[...] = before_ref[...] if chained else jnp.zeros_like(key_ref)

    tok = vis_ref.shape[1]
    heads = wt_ref.shape[0]
    first = (here_ref[0] & 1) == 0
    scale = 1.0 / math.sqrt(PLAIN_WIDTH + ROPE)
    window, krope = win_ref[...], krope_ref[...]
    visible = [vis_ref[b] > 0.0 for b in range(2)]
    keys, values, queries, grads = [], [], [], []
    for h in range(heads):
        kv = dot(window, wt_ref[h], 1, 0).astype(BF16)
        keys.append(jnp.concatenate([kv[:, :PLAIN_WIDTH], krope], 1))
        values.append(kv[:, PLAIN_WIDTH:])
        mine, got = mine_ref[h], got_ref[h]
        ordered = (jnp.where(first, mine, got), jnp.where(first, got, mine))
        queries.append([block[:, : 2 * LANES] for block in ordered])
        grads.append([block[:, 2 * LANES :] for block in ordered])
    reach = [slice(b * tok, (b + 2) * tok) for b in range(2)]
    units = [(h, b) for h in range(heads) for b in range(2)]
    scores = {(h, b): dot(queries[h][b], keys[h][reach[b]], 1, 1) for h, b in units}
    dprobs = {(h, b): dot(grads[h][b], values[h][reach[b]], 1, 1) for h, b in units}
    dscores, probs16 = {}, {}
    for unit in units:
        logits = jnp.where(visible[unit[1]], scores[unit] * scale, -1e30)
        top = jnp.max(logits, -1, keepdims=True)
        expo = jnp.exp(logits - top)
        probs = expo / jnp.sum(expo, -1, keepdims=True)
        delta = jnp.sum(probs * dprobs[unit], -1, keepdims=True)
        dscores[unit] = (probs * (dprobs[unit] - delta) * scale).astype(BF16)
        probs16[unit] = probs.astype(BF16)

    def fold(low, high):
        return jnp.concatenate([low[:tok], low[tok:] + high[:tok], high[tok:]], 0)

    parts, rope = [], None
    for h in range(heads):
        dk = fold(*[dot(dscores[h, b], queries[h][b], 0, 0) for b in range(2)])
        dv = fold(*[dot(probs16[h, b], grads[h][b], 0, 0) for b in range(2)])
        parts.append(jnp.concatenate([dk[:, :PLAIN_WIDTH], dv], 1).astype(BF16))
        rope = dk[:, PLAIN_WIDTH:] if rope is None else rope + dk[:, PLAIN_WIDTH:]
    dkv = jnp.concatenate(parts, 1)
    rows = lat_ref.shape[0] // 8

    wide = dkv.shape[1] // len(ways)

    for k, along_x in enumerate(ways):
        columns = slice(k * wide, (k + 1) * wide)

        def term(low, high):
            pair = [lat_ref[g * rows : (g + 1) * rows, :] for g in (low, high)]
            return dot(jnp.concatenate(pair, 0), dkv[:, columns], 1, 0)

        for at, groups in enumerate(((2, 3), (6, 7)) if along_x else ((1, 3), (5, 7))):
            block = slice(2 * at * rows, 2 * (at + 1) * rows)
            send_refs[k][block, :] = term(*groups).astype(BF16)
        for at, groups in enumerate(((0, 1), (4, 5)) if along_x else ((0, 2), (4, 6))):
            block = slice(2 * at * rows, 2 * (at + 1) * rows)
            keep_ref[block, columns] = term(*groups)
    total = key_ref[:, :LAT]
    for h in range(heads):
        total = total + dot(parts[h], wt_ref[h], 1, 1)
    key_ref[:, :LAT] = total
    key_ref[:, LAT:] = key_ref[:, LAT:] + rope
    for h in range(heads):
        low, high = (dot(dscores[h, b], keys[h][reach[b]], 1, 0) for b in range(2))
        dq_ref[h] = jnp.where(first, low, high)
        back_ref[h] = jnp.where(first, high, low)


def chunk(here, window, weight, mine, got, before, index, heads, ways):
    tok = mine.shape[1]
    whole = lambda i, here: (0, 0)
    whole3 = lambda i, here: (0, 0, 0)
    step = min(heads, STEP_HEADS)
    steps = heads // step
    at = lambda i, here: (index * steps + i, 0, 0)
    in_half = lambda i, here: (index * steps + i) % (weight.shape[0] // step)
    across_columns = lambda i, here: (0, i)
    columns = heads * PAIR
    operands = [*window, weight, mine, got]
    in_specs = [
        pl.BlockSpec(array.shape, whole3 if array.ndim == 3 else whole) for array in window
    ] + [
        pl.BlockSpec((step, LAT, PAIR), lambda i, here: (in_half(i, here), 0, 0)),
        pl.BlockSpec((step, tok, 3 * LANES), at),
        pl.BlockSpec((step, tok, 3 * LANES), at),
    ]
    aliases = {}
    if before is not None:
        key, dq, back = before
        aliases = {len(operands) + 2: 2, len(operands) + 3: 3}
        in_specs = in_specs + [
            pl.BlockSpec(key.shape, whole),
            pl.BlockSpec(memory_space=pl.ANY),
            pl.BlockSpec(memory_space=pl.ANY),
        ]
        operands = operands + [key, dq, back]
    turned = (mine.shape[0], tok, 2 * LANES)
    return pl.pallas_call(
        functools.partial(chunk_kernel, chained=before is not None, ways=ways),
        grid_spec=pltpu.PrefetchScalarGridSpec(
            num_scalar_prefetch=1,
            grid=(steps,),
            in_specs=in_specs,
            out_specs=[
                pl.BlockSpec((LAT // 2, step * PAIR), across_columns),
                pl.BlockSpec((3 * tok, LAT + LANES), whole),
                pl.BlockSpec((step, tok, 2 * LANES), at),
                pl.BlockSpec((step, tok, 2 * LANES), at),
            ]
            + [pl.BlockSpec((LAT // 2, step * PAIR // len(ways)), across_columns)] * len(ways),
        ),
        out_shape=[
            jax.ShapeDtypeStruct((LAT // 2, columns), F32),
            jax.ShapeDtypeStruct((3 * tok, LAT + LANES), F32),
            jax.ShapeDtypeStruct(turned, F32),
            jax.ShapeDtypeStruct(turned, F32),
        ]
        + [jax.ShapeDtypeStruct((LAT // 2, columns // len(ways)), BF16)] * len(ways),
        input_output_aliases=aliases,
        compiler_params=PARAMS,
        cost_estimate=cost(CHUNK),
        name="chunk",
    )(here, *operands)


def add_rows_kernel(*refs, count, wide):
    total = refs[0][...].astype(F32)
    for ref in refs[1 : count + wide]:
        total = total + ref[...].astype(F32)
    refs[-1][...] = total.astype(refs[-1].dtype)


def add_rows(arrays, rows, index, dtype, wide=(), place=0, places=1, before=None):
    columns = arrays[0].shape[1]
    operands = [*arrays, *wide]
    in_specs = [pl.BlockSpec((rows, columns), lambda i: (index, 0)) for _ in arrays]
    in_specs = in_specs + [pl.BlockSpec((rows, columns), lambda i: (index, place)) for _ in wide]
    aliases = {}
    if before is not None:
        aliases = {len(operands): 0}
        in_specs.append(pl.BlockSpec(memory_space=pl.ANY))
        operands.append(before)
    return pl.pallas_call(
        functools.partial(add_rows_kernel, count=len(arrays), wide=len(wide)),
        grid=(1,),
        in_specs=in_specs,
        out_specs=pl.BlockSpec((rows, columns), lambda i: (0, place)),
        out_shape=jax.ShapeDtypeStruct((rows, places * columns), dtype),
        input_output_aliases=aliases,
        compiler_params=PARAMS,
        cost_estimate=cost(SHARES),
        name="add_rows",
    )(*operands)


def key_split_kernel(here_ref, key_ref, keep_ref, give_ref):
    tok = keep_ref.shape[0] // 2
    first = (here_ref[0] & 1) == 0
    behind, low, high = (key_ref[b * tok : (b + 1) * tok, :] for b in range(3))
    keep_ref[:tok] = jnp.where(first, low, high)
    keep_ref[tok:] = behind
    give_ref[:tok] = jnp.where(first, high, low)
    give_ref[tok:] = behind


def key_split(here, key):
    rows = key.shape[0] // 3 * 2
    whole = lambda i, here: (0, 0)
    return pl.pallas_call(
        key_split_kernel,
        grid_spec=pltpu.PrefetchScalarGridSpec(
            num_scalar_prefetch=1,
            grid=(1,),
            in_specs=[pl.BlockSpec(key.shape, whole)],
            out_specs=[pl.BlockSpec((rows, key.shape[1]), whole)] * 2,
        ),
        out_shape=[jax.ShapeDtypeStruct((rows, key.shape[1]), F32)] * 2,
        compiler_params=PARAMS,
        cost_estimate=cost(SHARES),
        name="key_split",
    )(here, key)


def key_shares_kernel(at_ref, keep_ref, got_ref, *outs):
    shares = len(outs)
    part = (LAT + ROPE) // shares
    total = keep_ref[...] + got_ref[...]
    for z in range(shares):
        piece = total[:, z * part : (z + 1) * part]
        for s in range(shares):

            @pl.when(lax.rem(at_ref[0] + s, shares) == z)
            def _(s=s, piece=piece):
                outs[s][...] = piece.astype(outs[s].dtype)


def key_shares(at_head, keep, got, shares):
    part = (LAT + ROPE) // shares
    rows = keep.shape[0]
    whole = lambda i, at: (0, 0)
    types = [F32] + [BF16] * (shares - 1)
    return pl.pallas_call(
        key_shares_kernel,
        grid_spec=pltpu.PrefetchScalarGridSpec(
            num_scalar_prefetch=1,
            grid=(1,),
            in_specs=[pl.BlockSpec(keep.shape, whole)] * 2,
            out_specs=[pl.BlockSpec((rows, part), whole)] * shares,
        ),
        out_shape=[jax.ShapeDtypeStruct((rows, part), kind) for kind in types],
        compiler_params=PARAMS,
        cost_estimate=cost(SHARES),
        name="key_shares",
    )(at_head, keep, got)


def query_grad_kernel(here_ref, mine_ref, got_ref, out_ref, n_ref, r_ref):
    tok, heads, _ = out_ref.shape

    def put(src_ref):
        for h in range(heads):
            n_ref[pl.ds(h, tok, stride=heads), :] = src_ref[h, :, :PLAIN_WIDTH]
            r_ref[pl.ds(h, tok, stride=heads), :] = src_ref[h, :, PLAIN_WIDTH:]

    pl.when(pl.program_id(0) == 0)(lambda: put(mine_ref))
    pl.when(pl.program_id(0) == 1)(lambda: put(got_ref))
    out_ref[:, :, :PLAIN_WIDTH] = n_ref[...].reshape(tok, heads, LANES)
    out_ref[:, :, PLAIN_WIDTH:] = r_ref[...].reshape(tok, heads, LANES)[:, :, :ROPE]


def query_grad(here, mine, got):
    heads, tok, _ = mine.shape
    whole = lambda i, here: (0, 0, 0)
    return pl.pallas_call(
        query_grad_kernel,
        grid_spec=pltpu.PrefetchScalarGridSpec(
            num_scalar_prefetch=1,
            grid=(2,),
            in_specs=[pl.BlockSpec(mine.shape, whole)] * 2,
            out_specs=pl.BlockSpec(
                (tok, heads, PLAIN_WIDTH + ROPE), lambda i, here: (0, (here[0] & 1) ^ i, 0)
            ),
            scratch_shapes=[pltpu.VMEM((tok * heads, LANES), F32)] * 2,
        ),
        out_shape=jax.ShapeDtypeStruct((tok, 2 * heads, PLAIN_WIDTH + ROPE), F32),
        compiler_params=PARAMS,
        cost_estimate=cost(QUERY),
        name="query_grad",
    )(here, mine, got)


def join_kernel(*refs, pieces, wide):
    out_ref = refs[-1]
    for k in range(pieces):
        total = refs[2 * k][...] + refs[2 * k + 1][...].astype(F32)
        out_ref[:, k * wide : (k + 1) * wide] = total.astype(BF16)
    if len(refs) > 2 * pieces + 1:
        out_ref[:, pieces * wide :] = refs[2 * pieces][...]


def join(pieces, rows, wide, theirs=None):
    operands, in_specs = [], []
    for piece in pieces:
        for array, column in piece:
            operands.append(array)
            in_specs.append(pl.BlockSpec((rows, wide), lambda i, column=column: (1, column)))
    columns = len(pieces) * wide
    if theirs is not None:
        operands.append(theirs)
        in_specs.append(pl.BlockSpec((rows, columns), lambda i: (1, 0)))
        columns = 2 * columns
    return pl.pallas_call(
        functools.partial(join_kernel, pieces=len(pieces), wide=wide),
        grid=(1,),
        in_specs=in_specs,
        out_specs=pl.BlockSpec((rows, columns), lambda i: (0, 0)),
        out_shape=jax.ShapeDtypeStruct((rows, columns), BF16),
        compiler_params=PARAMS,
        cost_estimate=cost(SHARES),
        name="join",
    )(*operands)


def last_sums_kernel(here_ref, *refs, order, count, wide):
    share_ref, behind_ref, out_ref, key_ref, k_ref, v_ref = refs[-6:]
    rows, heads, _ = out_ref.shape
    size = 2 * count + 2
    each = wide // PAIR
    key_ref[...] = share_ref[...] + behind_ref[...]

    def put(j, total):
        for h in range(each):
            at = pl.ds(j * each + h, rows, stride=heads)
            k_ref[at, :] = total[:, h * PAIR : h * PAIR + LANES]
            v_ref[at, :] = total[:, h * PAIR + LANES : (h + 1) * PAIR]

    for q, places in enumerate(order):
        for j, (pair, piece) in enumerate(places):
            group = refs[pair * size : (pair + 1) * size]
            kept, came = group[2 * piece : 2 * piece + 2]
            theirs_ref, last_ref = group[-2:]
            columns = slice(piece * wide, (piece + 1) * wide)
            later = slice((count + piece) * wide, (count + piece + 1) * wide)

            @pl.when(pl.program_id(0) == 2 * q)
            def _(j=j, kept=kept, came=came, last_ref=last_ref, columns=columns):
                total = kept[...] + came[...].astype(F32)
                put(j, total + last_ref[:, columns].astype(F32))

            @pl.when(pl.program_id(0) == 2 * q + 1)
            def _(j=j, theirs_ref=theirs_ref, last_ref=last_ref, columns=columns, later=later):
                put(j, theirs_ref[:, columns].astype(F32) + last_ref[:, later].astype(F32))

    out_ref[:, :, :LANES] = k_ref[...].reshape(rows, heads, LANES)
    out_ref[:, :, LANES:] = v_ref[...].reshape(rows, heads, LANES)


def last_sums(here, pieces, theirs, lasts, share, behind, order, wide):
    rows, heads = share.shape[0], len(order[0]) * wide // PAIR
    whole = lambda i, here: (0, 0)
    operands, in_specs = [], []
    for group, other, last in zip(pieces, theirs, lasts):
        for array, column in [part for piece in group for part in piece]:
            operands.append(array)
            in_specs.append(pl.BlockSpec((rows, wide), lambda i, here, column=column: (0, column)))
        for array in (other, last):
            operands.append(array)
            in_specs.append(pl.BlockSpec((rows, array.shape[1]), whole))
    in_specs = in_specs + [pl.BlockSpec(share.shape, whole)] * 2
    return pl.pallas_call(
        functools.partial(last_sums_kernel, order=order, count=len(pieces[0]), wide=wide),
        grid_spec=pltpu.PrefetchScalarGridSpec(
            num_scalar_prefetch=1,
            grid=(4,),
            in_specs=in_specs,
            out_specs=[
                pl.BlockSpec(
                    (rows, heads, PAIR),
                    lambda i, here: (0, ((here[0] & 1) ^ (i & 1)) * 2 + (i >> 1), 0),
                ),
                pl.BlockSpec(share.shape, whole),
            ],
            scratch_shapes=[pltpu.VMEM((rows * heads, LANES), F32)] * 2,
        ),
        out_shape=[
            jax.ShapeDtypeStruct((rows, 4 * heads, PAIR), F32),
            jax.ShapeDtypeStruct(share.shape, F32),
        ],
        compiler_params=PARAMS,
        cost_estimate=cost(SUM),
        name="last_sums",
    )(here, *operands, share, behind)


def in_chunks(queries, latent_keys, out_grad, up_weight, here, at_head, ids):
    tok = latent_keys.shape[0]
    n_ctx, n_head = lax.axis_size("ctx"), lax.axis_size("head")
    heads, each = 16, 4
    queries = after(queries, (ids, here, at_head))
    give, mine = turn_tokens(here, queries, out_grad, latent_keys, heads)
    odd_devices = range(1, n_ctx - 1, 2)
    even = lax.ppermute(latent_keys, "ctx", [(source, source + 1) for source in odd_devices])
    odd = lax.ppermute(latent_keys, "ctx", [(source, source + 2) for source in odd_devices])
    got = across(give, 1)
    weight = turn_weight(here, up_weight, heads)
    window = chip_window(here, even, odd, latent_keys, got, ids)
    ways, bits, wide = ((True, False), (False,), (True,), (True, False)), (2, 4), 2 * PAIR
    before, pieces = None, ([], [])
    for c in range(4):
        keep, *before = chunk(here, window, weight, mine, got, before, c, each, ways[c])
        before, outs = before[:3], before[3:]
        for k, (along_x, out) in enumerate(zip(ways[c], outs)):
            came = across(out, bits[0] if along_x else bits[1])
            for at in range(2 // len(outs)):
                pieces[0 if along_x else 1].append(((keep, k + at), (came, at)))
    order = (((0, 0), (1, 0), (1, 1), (1, 2)), ((0, 1), (0, 2), (0, 3), (1, 3)))
    key, dq, back = before
    key = after(key, [pieces[p][0][1][0] for p in range(2)])
    key_keep, key_give = key_split(here, key)
    key_got = across(key_give, 1)
    shares = key_shares(at_head, key_keep, key_got, n_head)
    came = [
        lax.ppermute(shares[s], "head", [(z, (z + s) % n_head) for z in range(n_head)])
        for s in range(1, n_head)
    ]
    back = across(after(back, key_keep), 1)
    keep = after(keep, shares)
    for p in range(2):
        pieces[p][3] = ((keep, pieces[p][3][0][1]), pieces[p][3][1])
    theirs, seconds, lasts = [], [], []
    for p in range(2):
        first = join(pieces[p], 2 * tok, wide)
        theirs.append(across(first, 1))
        seconds.append(join(pieces[p], tok, wide, theirs[p]))
        lasts.append(across(seconds[p], bits[1 - p]))
    came = after(came, seconds)
    share, behind = (add_rows((shares[0], *came), tok, b, F32) for b in range(2))
    behind = lax.ppermute(behind, "ctx", [(source, source - 1) for source in range(2, n_ctx, 2)])
    dq = query_grad(here, after(dq, share), back)
    theirs = after(theirs, dq)
    weight_grad, key_grad = last_sums(
        here, pieces, theirs, lasts, share, behind, order, wide
    )
    return dq, key_grad, weight_grad


def shards(queries, latent_keys, out_grad, up_weight, segment_ids):
    tok = latent_keys.shape[0]
    heads = queries.shape[1]
    n_ctx, n_head = lax.axis_size("ctx"), lax.axis_size("head")
    here = lax.axis_index("ctx").astype(jnp.int32).reshape(1)
    at_head = lax.axis_index("head").astype(jnp.int32).reshape(1)
    if n_ctx == 8 and heads == 32 and n_head == 4:
        ids = segment_ids.reshape(n_ctx // 2, 2 * tok)
        return in_chunks(queries, latent_keys, out_grad, up_weight, here, at_head, ids)
    else:
        ids = segment_ids.reshape(n_ctx, tok)
        prev = from_behind(latent_keys, "ctx", REACH)
        turned = by_head(up_weight, queries, out_grad, 0, heads)
        window = key_window(here, prev, latent_keys, ids, False)
        dq, dkv, rope = attention(window, turned, None, None, 0, heads, 0, heads)
        (both,) = key_terms(at_head, [dkv], [turned[0]], [rope], None)
        share = lax.psum_scatter(
            both.reshape(REACH + 1, tok, LAT + ROPE), "head", scatter_dimension=2, tiled=True
        )
        term = jnp.einsum("ki,ke->ie", window[0], dkv, preferred_element_type=F32)
        rows = lax.psum_scatter(term.astype(BF16), "ctx", scatter_dimension=0, tiled=True)
        weight_grad = rows.astype(F32).reshape(rows.shape[0], heads, PAIR)
    key_grad = share[REACH] + from_behind(share[0], "ctx", 0 - REACH)
    return (dq, key_grad, weight_grad)


def solution(mesh):
    return jax.shard_map(
        shards,
        mesh=mesh,
        in_specs=(
            P("ctx", "head", None),
            P("ctx", None),
            P("ctx", "head", None),
            P(None, "head", None),
            P(),
        ),
        out_specs=(P("ctx", "head", None), P("ctx", "head"), P("ctx", "head", None)),
        check_vma=False,
    )
```

```python
import functools
import math

import jax
import jax.numpy as jnp
from jax import lax
from jax.experimental import pallas as pl
from jax.experimental.pallas import tpu as pltpu
from jax.sharding import PartitionSpec as P

LAT = 512
ROPE = 64
PLAIN_WIDTH = 128
VDIM = 128
REACH = 1
LANES = 128
PAIR = PLAIN_WIDTH + VDIM
STEP_HEADS = 4
BF16 = jnp.bfloat16
F32 = jnp.float32
WIDE = pltpu.CompilerParams(vmem_limit_bytes=56 * 1024 * 1024)
PARAMS = pltpu.CompilerParams(vmem_limit_bytes=20 * 1024 * 1024)


def from_behind(value, axis, steps):
    count = lax.axis_size(axis)
    initial, last = (max(0, -steps), min(count, count - steps))
    return lax.ppermute(value, axis, [(source, source + steps) for source in range(initial, last)])


def across(value, bit):
    count = lax.axis_size("ctx")
    return lax.ppermute(value, "ctx", [(source, source ^ bit) for source in range(count)])


def cost(share):
    return pl.CostEstimate(flops=int(share * 1e9), bytes_accessed=1024, transcendentals=0)


TURN, WINDOW, CHUNK, SHARES, QUERY, SUM = 3.0, 0.5, 1.5, 0.1, 0.1, 0.1


def dot(a, b, a_dim, b_dim):
    return lax.dot_general(a, b, (((a_dim,), (b_dim,)), ((), ())), preferred_element_type=F32)


def by_head_kernel(w_ref, q_ref, g_ref, wt_ref, qt_ref, gt_ref):
    heads = w_ref.shape[1]
    orders = {}

    def order(count):
        if count not in orders:
            size = count * heads
            row = lax.broadcasted_iota(jnp.int32, (size, size), 0)
            col = lax.broadcasted_iota(jnp.int32, (size, size), 1)
            wanted = (row % count) * heads + row // count
            orders[count] = (col == wanted).astype(BF16)
        return orders[count]

    def turn(ref, out_ref):
        rows, _, width = ref.shape
        count = min(rows, 256 // heads)
        for start in range(0, rows, count):
            block = ref[start : start + count].reshape(count * heads, width)
            turned = dot(order(count), block, 1, 0).astype(BF16)
            out_ref[:, start : start + count, :width] = turned.reshape(heads, count, width)

    turn(w_ref, wt_ref)
    qt_ref[...] = jnp.zeros_like(qt_ref)
    turn(q_ref, qt_ref)
    turn(g_ref, gt_ref)


def by_head(up_weight, queries, out_grad, chunk, heads):
    tok = queries.shape[0]
    steps = 4
    depth, rows = LAT // steps, tok // steps
    return pl.pallas_call(
        by_head_kernel,
        grid=(steps,),
        in_specs=[
            pl.BlockSpec((depth, heads, PAIR), lambda i: (i, chunk, 0)),
            pl.BlockSpec((rows, heads, PLAIN_WIDTH + ROPE), lambda i: (i, chunk, 0)),
            pl.BlockSpec((rows, heads, VDIM), lambda i: (i, chunk, 0)),
        ],
        out_specs=[
            pl.BlockSpec((heads, depth, PAIR), lambda i: (0, i, 0)),
            pl.BlockSpec((heads, rows, 2 * LANES), lambda i: (0, i, 0)),
            pl.BlockSpec((heads, rows, VDIM), lambda i: (0, i, 0)),
        ],
        out_shape=[
            jax.ShapeDtypeStruct((heads, LAT, PAIR), BF16),
            jax.ShapeDtypeStruct((heads, tok, 2 * LANES), BF16),
            jax.ShapeDtypeStruct((heads, tok, VDIM), BF16),
        ],
        compiler_params=WIDE,
        cost_estimate=cost(TURN),
        name="by_head",
    )(up_weight, queries, out_grad)


def window_kernel(here_ref, prev_ref, own_ref, ids_ref, *outs, paired):
    win_ref, krope_ref, vis_ref = outs[:3]
    here = here_ref[0]
    tok = prev_ref.shape[0]
    win_ref[:tok, :] = prev_ref[:, :LAT]
    win_ref[tok:, :] = own_ref[:, :LAT]
    krope_ref[...] = jnp.zeros_like(krope_ref)
    krope_ref[:tok, :ROPE] = prev_ref[:, LAT:]
    krope_ref[tok:, :ROPE] = own_ref[:, LAT:]
    behind = jnp.maximum(here - 1, 0)
    seg_prev = jnp.where(here > 0, ids_ref[pl.ds(behind, 1), :], -1)
    seg_own = ids_ref[pl.ds(here, 1), :]
    row = lax.broadcasted_iota(jnp.int32, (tok, tok), 0)
    col = lax.broadcasted_iota(jnp.int32, (tok, tok), 1)
    seg_query = jnp.sum(jnp.where(row == col, seg_own, 0), 1, keepdims=True)
    vis_ref[:, :tok] = (seg_query == seg_prev).astype(F32)
    vis_ref[:, tok:] = ((seg_query == seg_own) & (col <= row)).astype(F32)
    if paired:
        source = lax.broadcasted_iota(jnp.int32, (LAT, LAT), 0)
        column = lax.broadcasted_iota(jnp.int32, (LAT, LAT), 1)
        place = column >> 6
        apart = ((place & 1) << 2) | (place & 2) | (place >> 2)
        wanted = ((here ^ apart) << 6) | (column & 63)
        ordered = dot(win_ref[...], (source == wanted).astype(BF16), 1, 0).astype(BF16)
        outs[3][...] = ordered[:, : LAT // 2]
        outs[4][...] = ordered[:, LAT // 2 :]


def key_window(here, prev, own, ids, paired):
    tok = prev.shape[0]
    whole = lambda i, here: (0, 0)
    shapes = [((2 * tok, LAT), BF16), ((2 * tok, LANES), BF16), ((tok, 2 * tok), F32)]
    if paired:
        shapes = shapes + [((2 * tok, LAT // 2), BF16)] * 2
    return pl.pallas_call(
        functools.partial(window_kernel, paired=paired),
        grid_spec=pltpu.PrefetchScalarGridSpec(
            num_scalar_prefetch=1,
            grid=(1,),
            in_specs=[pl.BlockSpec(array.shape, whole) for array in (prev, own, ids)],
            out_specs=[pl.BlockSpec(shape, whole) for shape, _ in shapes],
        ),
        out_shape=[jax.ShapeDtypeStruct(*shape) for shape in shapes],
        compiler_params=PARAMS,
        cost_estimate=cost(WINDOW),
        name="key_window",
    )(here, prev, own, ids)


def attention_kernel(
    win_ref, krope_ref, vis_ref, wt_ref, qt_ref, gt_ref, *refs, aliased, extra
):
    latents_ref = refs[0] if extra else None
    refs = refs[1:] if extra else refs
    refs = refs[1:] if aliased else refs
    dq_ref, dkv_ref, rope_ref, dqn_ref, dqr_ref = refs
    i = pl.program_id(0)
    tok, heads = dq_ref.shape[:2]
    scale = 1.0 / math.sqrt(PLAIN_WIDTH + ROPE)

    @pl.when(i == 0)
    def _():
        rope_ref[...] = jnp.zeros_like(rope_ref)
        if extra:
            dkv_ref[:, heads * PAIR :] = latents_ref[...]

    visible = vis_ref[...] > 0.0
    window = win_ref[...]
    krope = krope_ref[...]
    count = wt_ref.shape[0]
    keys, values = [], []
    for h in range(count):
        kv = dot(window, wt_ref[h], 1, 0).astype(BF16)
        keys.append(jnp.concatenate([kv[:, :PLAIN_WIDTH], krope], 1))
        values.append(kv[:, PLAIN_WIDTH:])
    scores = [dot(qt_ref[h], keys[h], 1, 1) for h in range(count)]
    dprobs = [dot(gt_ref[h], values[h], 1, 1) for h in range(count)]
    dscores, probs16 = [], []
    for h in range(count):
        logits = jnp.where(visible, scores[h] * scale, -1e30)
        top = jnp.max(logits, -1, keepdims=True)
        expo = jnp.exp(logits - top)
        probs = expo / jnp.sum(expo, -1, keepdims=True)
        delta = jnp.sum(probs * dprobs[h], -1, keepdims=True)
        dscores.append((probs * (dprobs[h] - delta) * scale).astype(BF16))
        probs16.append(probs.astype(BF16))
    parts, rope = [], rope_ref[...]
    for h in range(count):
        dk = dot(dscores[h], qt_ref[h], 0, 0)
        dv = dot(probs16[h], gt_ref[h], 0, 0)
        parts.append(jnp.concatenate([dk[:, :PLAIN_WIDTH], dv], 1).astype(BF16))
        rope = rope + dk[:, PLAIN_WIDTH:]
    rope_ref[...] = rope
    dkv_ref[:, pl.ds(pl.multiple_of(i * (count * PAIR), count * PAIR), count * PAIR)] = (
        jnp.concatenate(parts, 1)
    )
    for h in range(count):
        dq = dot(dscores[h], keys[h], 1, 0)
        dqn_ref[pl.ds(i * count + h, tok, stride=heads), :] = dq[:, :PLAIN_WIDTH]
        dqr_ref[pl.ds(i * count + h, tok, stride=heads), :] = dq[:, PLAIN_WIDTH:]

    @pl.when(i == pl.num_programs(0) - 1)
    def _():
        dq_ref[:, :, :PLAIN_WIDTH] = dqn_ref[...].reshape(tok, heads, LANES)
        dq_ref[:, :, PLAIN_WIDTH:] = dqr_ref[...].reshape(tok, heads, LANES)[:, :, :ROPE]


def attention(window, turned, latents, dq, chunk, heads, first, all_heads):
    weight, queries, out_grad = turned
    tok = queries.shape[1]
    width = 2 * tok
    steps = heads // STEP_HEADS
    at = first // STEP_HEADS
    extra = LAT // 2 if latents is not None else 0
    whole = lambda i: (0, 0)
    head_block = lambda i: (at + i, 0, 0)
    operands = [*window, weight, queries, out_grad]
    in_specs = [pl.BlockSpec(array.shape, whole) for array in window] + [
        pl.BlockSpec((STEP_HEADS, LAT, PAIR), head_block),
        pl.BlockSpec((STEP_HEADS, tok, 2 * LANES), head_block),
        pl.BlockSpec((STEP_HEADS, tok, VDIM), head_block),
    ]
    if latents is not None:
        in_specs.append(pl.BlockSpec(latents.shape, whole))
        operands.append(latents)
    aliases = {}
    if dq is not None:
        aliases = {len(operands): 0}
        in_specs.append(pl.BlockSpec(memory_space=pl.ANY))
        operands.append(dq)
    return pl.pallas_call(
        functools.partial(attention_kernel, aliased=dq is not None, extra=latents is not None),
        grid=(steps,),
        in_specs=in_specs,
        out_specs=[
            pl.BlockSpec((tok, heads, PLAIN_WIDTH + ROPE), lambda i: (0, chunk, 0)),
            pl.BlockSpec((width, heads * PAIR + extra), whole),
            pl.BlockSpec((width, LANES), whole),
        ],
        scratch_shapes=[
            pltpu.VMEM((tok * heads, LANES), F32),
            pltpu.VMEM((tok * heads, LANES), F32),
        ],
        out_shape=[
            jax.ShapeDtypeStruct((tok, all_heads, PLAIN_WIDTH + ROPE), F32),
            jax.ShapeDtypeStruct((width, heads * PAIR + extra), BF16),
            jax.ShapeDtypeStruct((width, LANES), F32),
        ],
        input_output_aliases=aliases,
        compiler_params=WIDE,
        cost_estimate=cost(CHUNK),
        name="attention",
    )(*operands)


def terms_kernel(
    own_ref, other_ref, mine_ref, theirs_ref, keep_ref, send_ref, latents_ref, *, along_x
):
    width = own_ref.shape[0]

    @pl.when(pl.program_id(0) == 0)
    def _():
        latents_ref[:, :width] = mine_ref[...].T
        latents_ref[:, width:] = theirs_ref[...].T

    grads = jnp.concatenate([own_ref[...], other_ref[...]], 0)
    term = dot(latents_ref[...], grads, 1, 0)
    rows = term.shape[0] // 4
    first, second = (1, 2) if along_x else (2, 1)
    keep_ref[:rows] = term[:rows]
    keep_ref[rows:] = term[first * rows : (first + 1) * rows]
    send_ref[:rows] = term[second * rows : (second + 1) * rows].astype(BF16)
    send_ref[rows:] = term[3 * rows :].astype(BF16)


def terms(own, other, mine, theirs, columns, along_x):
    width = own.shape[0]
    block = 1024
    at = theirs.shape[1] // (LAT // 2) - 1
    column_block = lambda i: (0, i)
    return pl.pallas_call(
        functools.partial(terms_kernel, along_x=along_x),
        grid=(columns // block,),
        in_specs=[
            pl.BlockSpec((width, block), column_block),
            pl.BlockSpec((width, block), column_block),
            pl.BlockSpec((width, LAT // 2), lambda i: (0, 0)),
            pl.BlockSpec((width, LAT // 2), lambda i: (0, at)),
        ],
        out_specs=[pl.BlockSpec((LAT // 4, block), column_block)] * 2,
        out_shape=[
            jax.ShapeDtypeStruct((LAT // 4, columns), F32),
            jax.ShapeDtypeStruct((LAT // 4, columns), BF16),
        ],
        scratch_shapes=[pltpu.VMEM((LAT // 2, 2 * width), BF16)],
        compiler_params=PARAMS,
        cost_estimate=cost(CHUNK),
        name="terms",
    )(own, other, mine, theirs)


def key_terms_kernel(*refs, chunks, steps, turns, shares):
    head_ref = refs[0]
    dkv_refs = refs[1 : 1 + chunks]
    wt_refs = refs[1 + chunks : 1 + chunks + turns]
    rope_refs = refs[1 + chunks + turns : 1 + 2 * chunks + turns]
    outs = refs[1 + 2 * chunks + turns : -1]
    total_ref = refs[-1]
    i = pl.program_id(0)

    @pl.when(i == 0)
    def _():
        total_ref[...] = jnp.zeros_like(total_ref)

    for k in range(chunks):

        @pl.when(i // steps == k)
        def _(k=k):
            total = total_ref[...]
            weight_ref = wt_refs[k * turns // chunks]
            for h in range(weight_ref.shape[0]):
                grads = dkv_refs[k][:, h * PAIR : (h + 1) * PAIR]
                total = total + dot(grads, weight_ref[h], 1, 1)
            total_ref[...] = total

    @pl.when(i == pl.num_programs(0) - 1)
    def _():
        rope = rope_refs[0][...]
        for k in range(1, chunks):
            rope = rope + rope_refs[k][...]
        both = jnp.concatenate([total_ref[...], rope], 1)
        if shares is None:
            outs[0][...] = both[:, : LAT + ROPE]
            return
        part = (LAT + ROPE) // shares
        for z in range(shares):
            piece = both[:, z * part : (z + 1) * part]
            for s in range(shares):

                @pl.when(lax.rem(head_ref[0] + s, shares) == z)
                def _(s=s, piece=piece):
                    outs[s][...] = piece


def key_terms(at_head, dkvs, weights, ropes, shares):
    chunks, turns = len(dkvs), len(weights)
    heads = weights[0].shape[0] * turns // chunks
    width = dkvs[0].shape[0]
    steps = heads // STEP_HEADS
    span = steps * chunks // turns
    near = lambda k, many: lambda i, at: jnp.clip(i - k * many, 0, many - 1)
    wide = (LAT + ROPE) // (shares or 1)
    return pl.pallas_call(
        functools.partial(
            key_terms_kernel, chunks=chunks, steps=steps, turns=turns, shares=shares
        ),
        grid_spec=pltpu.PrefetchScalarGridSpec(
            num_scalar_prefetch=1,
            grid=(chunks * steps,),
            in_specs=[
                pl.BlockSpec((width, STEP_HEADS * PAIR), lambda i, at, k=k: (0, near(k, steps)(i, at)))
                for k in range(chunks)
            ]
            + [
                pl.BlockSpec(
                    (STEP_HEADS, LAT, PAIR), lambda i, at, k=k: (near(k, span)(i, at), 0, 0)
                )
                for k in range(turns)
            ]
            + [pl.BlockSpec((width, LANES), lambda i, at: (0, 0))] * chunks,
            out_specs=[pl.BlockSpec((width, wide), lambda i, at: (0, 0))] * (shares or 1),
            scratch_shapes=[pltpu.VMEM((width, LAT), F32)],
        ),
        out_shape=[jax.ShapeDtypeStruct((width, wide), F32)] * (shares or 1),
        compiler_params=WIDE,
        cost_estimate=cost(CHUNK),
        name="key_terms",
    )(at_head, *dkvs, *weights, *ropes)


def weight_sum_kernel(keep_ref, first_ref, second_ref, *refs):
    out_ref, k_ref, v_ref = refs[-3:]
    rows, heads, _ = out_ref.shape
    for h in range(heads):
        columns = slice(h * PAIR, (h + 1) * PAIR)
        total = keep_ref[:, columns] + first_ref[:, columns].astype(F32)
        total = total + second_ref[:, columns].astype(F32)
        k_ref[pl.ds(h, rows, stride=heads), :] = total[:, :LANES]
        v_ref[pl.ds(h, rows, stride=heads), :] = total[:, LANES:]
    out_ref[:, :, :LANES] = k_ref[...].reshape(rows, heads, LANES)
    out_ref[:, :, LANES:] = v_ref[...].reshape(rows, heads, LANES)


def weight_sum(keep, first, second, total, chunk, all_heads):
    rows, columns = second.shape
    heads = columns // PAIR
    block = 32
    operands = [keep, first, second]
    in_specs = [pl.BlockSpec((block, columns), lambda i: (i, 0)) for _ in operands]
    aliases = {}
    if total is not None:
        aliases = {3: 0}
        in_specs.append(pl.BlockSpec(memory_space=pl.ANY))
        operands.append(total)
    return pl.pallas_call(
        weight_sum_kernel,
        grid=(rows // block,),
        in_specs=in_specs,
        out_specs=pl.BlockSpec((block, heads, PAIR), lambda i: (i, chunk, 0)),
        out_shape=jax.ShapeDtypeStruct((rows, all_heads, PAIR), F32),
        scratch_shapes=[pltpu.VMEM((block * heads, LANES), F32)] * 2,
        input_output_aliases=aliases,
        compiler_params=PARAMS,
        cost_estimate=cost(SUM),
        name="weight_sum",
    )(*operands)


def after(values, earlier):
    return lax.optimization_barrier((values, earlier))[0]


def turn_rows(block):
    rows, heads, width = block.shape
    count = min(rows, 256 // heads)
    row = lax.broadcasted_iota(jnp.int32, (count * heads, count * heads), 0)
    col = lax.broadcasted_iota(jnp.int32, (count * heads, count * heads), 1)
    order = (col == (row % count) * heads + row // count).astype(BF16)
    for start in range(0, rows, count):
        part = block[start : start + count].reshape(count * heads, width)
        turned = dot(order, part, 1, 0).astype(BF16)
        yield slice(start, start + count), turned.reshape(heads, count, width)


def in_hbm(array):
    return pltpu.with_memory_space_constraint(array, pltpu.HBM)


def turn_weight_kernel(here_ref, *refs):
    *parts, wt_ref = refs
    depth = parts[0].shape[0]
    for at, w_ref in enumerate(parts):
        for rows, turned in turn_rows(w_ref[...]):
            wt_ref[:, at * depth + rows.start : at * depth + rows.stop, :] = turned


def turn_weight(here, up_weight, heads):
    steps, parts = 4, 4
    depth = LAT // steps // parts
    part = lambda p: lambda i, here: (i * parts + p, here[0] & 1, 0)
    return pl.pallas_call(
        turn_weight_kernel,
        grid_spec=pltpu.PrefetchScalarGridSpec(
            num_scalar_prefetch=1,
            grid=(steps,),
            in_specs=[pl.BlockSpec((depth, heads, PAIR), part(p)) for p in range(parts)],
            out_specs=pl.BlockSpec((heads, depth * parts, PAIR), lambda i, here: (0, i, 0)),
        ),
        out_shape=jax.ShapeDtypeStruct((heads, LAT, PAIR), BF16),
        compiler_params=PARAMS,
        cost_estimate=cost(TURN),
        name="turn_weight",
    )(here, *[in_hbm(up_weight)] * parts)


def turn_tokens_kernel(here_ref, q1_ref, g1_ref, q0_ref, g0_ref, own_ref, give_ref, mine_ref):
    heads = mine_ref.shape[0]
    for q_ref, g_ref, out_ref in ((q1_ref, g1_ref, give_ref), (q0_ref, g0_ref, mine_ref)):
        out_ref[:, :, LANES : 2 * LANES] = jnp.zeros_like(out_ref[:, :, LANES : 2 * LANES])
        for rows, turned in turn_rows(q_ref[...]):
            out_ref[:heads, rows, : PLAIN_WIDTH + ROPE] = turned
        for rows, turned in turn_rows(g_ref[...]):
            out_ref[:heads, rows, 2 * LANES :] = turned
    rest = LAT + ROPE - 3 * LANES
    give_ref[heads] = own_ref[:, : 3 * LANES]
    give_ref[heads + 1] = jnp.zeros_like(give_ref[heads + 1])
    give_ref[heads + 1, :, :rest] = own_ref[:, 3 * LANES :]


def turn_tokens(here, queries, out_grad, latent_keys, heads):
    tok = queries.shape[0]
    q_block, g_block = (tok, heads, PLAIN_WIDTH + ROPE), (tok, heads, VDIM)
    given = lambda i, here: (0, 1 - (here[0] & 1), 0)
    kept = lambda i, here: (0, here[0] & 1, 0)
    whole = lambda i, here: (0, 0, 0)
    give, mine = (heads + 2, tok, 3 * LANES), (heads, tok, 3 * LANES)
    queries, out_grad, latent_keys = (in_hbm(x) for x in (queries, out_grad, latent_keys))
    return pl.pallas_call(
        turn_tokens_kernel,
        grid_spec=pltpu.PrefetchScalarGridSpec(
            num_scalar_prefetch=1,
            grid=(1,),
            in_specs=[
                pl.BlockSpec(q_block, given),
                pl.BlockSpec(g_block, given),
                pl.BlockSpec(q_block, kept),
                pl.BlockSpec(g_block, kept),
                pl.BlockSpec(latent_keys.shape, lambda i, here: (0, 0)),
            ],
            out_specs=[pl.BlockSpec(give, whole), pl.BlockSpec(mine, whole)],
        ),
        out_shape=[jax.ShapeDtypeStruct(give, BF16), jax.ShapeDtypeStruct(mine, BF16)],
        compiler_params=PARAMS,
        cost_estimate=cost(WINDOW),
        name="turn_tokens",
    )(here, queries, out_grad, queries, out_grad, latent_keys)


def chip_window_kernel(
    here_ref, even_ref, odd_ref, own_ref, pal_ref, ids_ref, win_ref, krope_ref, vis_ref, lat_ref
):
    here = here_ref[0]
    tok = own_ref.shape[0]
    core, chip = here & 1, here >> 1
    first = core == 0
    prev = jnp.where(first, even_ref[...].astype(F32), odd_ref[...].astype(F32)).astype(BF16)
    pal = jnp.concatenate([pal_ref[0], pal_ref[1, :, : LAT + ROPE - 3 * LANES]], 1).astype(F32)
    own = own_ref[...].astype(F32)
    low = jnp.where(first, own, pal).astype(BF16)
    high = jnp.where(first, pal, own).astype(BF16)
    krope_ref[...] = jnp.zeros_like(krope_ref)
    for at, block in enumerate((prev, low, high)):
        win_ref[at * tok : (at + 1) * tok, :] = block[:, :LAT]
        krope_ref[at * tok : (at + 1) * tok, :ROPE] = block[:, LAT:]
    behind = ids_ref[pl.ds(jnp.maximum(chip - 1, 0), 1), :]
    both = ids_ref[pl.ds(chip, 1), :]
    seg = [jnp.where(chip > 0, behind[:, tok:], -1), both[:, :tok], both[:, tok:]]
    row = lax.broadcasted_iota(jnp.int32, (tok, tok), 0)
    col = lax.broadcasted_iota(jnp.int32, (tok, tok), 1)
    for b in range(2):
        seg_query = jnp.sum(jnp.where(row == col, seg[b + 1], 0), 1, keepdims=True)
        vis_ref[b, :, :tok] = (seg_query == seg[b]).astype(F32)
        vis_ref[b, :, tok:] = ((seg_query == seg[b + 1]) & (col <= row)).astype(F32)
    column = lax.broadcasted_iota(jnp.int32, (LAT, LAT), 0)
    source = lax.broadcasted_iota(jnp.int32, (LAT, LAT), 1)
    place = column >> 6
    apart = ((place & 1) << 2) | (place & 2) | (place >> 2)
    wanted = ((here ^ apart) << 6) | (column & 63)
    order = (source == wanted).astype(BF16)
    lat_ref[...] = dot(order, win_ref[...], 1, 1).astype(BF16)


def chip_window(here, even, odd, own, got, ids):
    tok = own.shape[0]
    whole = lambda i, here: (0, 0)
    return pl.pallas_call(
        chip_window_kernel,
        grid_spec=pltpu.PrefetchScalarGridSpec(
            num_scalar_prefetch=1,
            grid=(1,),
            in_specs=[pl.BlockSpec(array.shape, whole) for array in (even, odd, own)]
            + [
                pl.BlockSpec((2,) + got.shape[1:], lambda i, here: (got.shape[0] // 2 - 1, 0, 0)),
                pl.BlockSpec(ids.shape, whole),
            ],
            out_specs=[
                pl.BlockSpec((3 * tok, LAT), whole),
                pl.BlockSpec((3 * tok, LANES), whole),
                pl.BlockSpec((2, tok, 2 * tok), lambda i, here: (0, 0, 0)),
                pl.BlockSpec((LAT, 3 * tok), whole),
            ],
        ),
        out_shape=[
            jax.ShapeDtypeStruct((3 * tok, LAT), BF16),
            jax.ShapeDtypeStruct((3 * tok, LANES), BF16),
            jax.ShapeDtypeStruct((2, tok, 2 * tok), F32),
            jax.ShapeDtypeStruct((LAT, 3 * tok), BF16),
        ],
        compiler_params=PARAMS,
        cost_estimate=cost(WINDOW),
        name="chip_window",
    )(here, even, odd, own, got, ids)


def chunk_kernel(
    here_ref,
    win_ref,
    krope_ref,
    vis_ref,
    lat_ref,
    wt_ref,
    mine_ref,
    got_ref,
    *refs,
    chained,
    along_x,
):
    before_ref = refs[0] if chained else None
    refs = refs[3:] if chained else refs
    keep_ref, send_ref, key_ref, dq_ref, back_ref = refs

    @pl.when(pl.program_id(0) == 0)
    def _():
        key_ref[...] = before_ref[...] if chained else jnp.zeros_like(key_ref)

    tok = vis_ref.shape[1]
    heads = wt_ref.shape[0]
    first = (here_ref[0] & 1) == 0
    scale = 1.0 / math.sqrt(PLAIN_WIDTH + ROPE)
    window, krope = win_ref[...], krope_ref[...]
    visible = [vis_ref[b] > 0.0 for b in range(2)]
    keys, values, queries, grads = [], [], [], []
    for h in range(heads):
        kv = dot(window, wt_ref[h], 1, 0).astype(BF16)
        keys.append(jnp.concatenate([kv[:, :PLAIN_WIDTH], krope], 1))
        values.append(kv[:, PLAIN_WIDTH:])
        mine, got = mine_ref[h], got_ref[h]
        ordered = (jnp.where(first, mine, got), jnp.where(first, got, mine))
        queries.append([block[:, : 2 * LANES] for block in ordered])
        grads.append([block[:, 2 * LANES :] for block in ordered])
    reach = [slice(b * tok, (b + 2) * tok) for b in range(2)]
    units = [(h, b) for h in range(heads) for b in range(2)]
    scores = {(h, b): dot(queries[h][b], keys[h][reach[b]], 1, 1) for h, b in units}
    dprobs = {(h, b): dot(grads[h][b], values[h][reach[b]], 1, 1) for h, b in units}
    dscores, probs16 = {}, {}
    for unit in units:
        logits = jnp.where(visible[unit[1]], scores[unit] * scale, -1e30)
        top = jnp.max(logits, -1, keepdims=True)
        expo = jnp.exp(logits - top)
        probs = expo / jnp.sum(expo, -1, keepdims=True)
        delta = jnp.sum(probs * dprobs[unit], -1, keepdims=True)
        dscores[unit] = (probs * (dprobs[unit] - delta) * scale).astype(BF16)
        probs16[unit] = probs.astype(BF16)

    def fold(low, high):
        return jnp.concatenate([low[:tok], low[tok:] + high[:tok], high[tok:]], 0)

    parts, rope = [], None
    for h in range(heads):
        dk = fold(*[dot(dscores[h, b], queries[h][b], 0, 0) for b in range(2)])
        dv = fold(*[dot(probs16[h, b], grads[h][b], 0, 0) for b in range(2)])
        parts.append(jnp.concatenate([dk[:, :PLAIN_WIDTH], dv], 1).astype(BF16))
        rope = dk[:, PLAIN_WIDTH:] if rope is None else rope + dk[:, PLAIN_WIDTH:]
    dkv = jnp.concatenate(parts, 1)
    rows = lat_ref.shape[0] // 8

    def term(low, high):
        pair = [lat_ref[g * rows : (g + 1) * rows, :] for g in (low, high)]
        return dot(jnp.concatenate(pair, 0), dkv, 1, 0)

    for at, groups in enumerate(((2, 3), (6, 7)) if along_x else ((1, 3), (5, 7))):
        send_ref[2 * at * rows : 2 * (at + 1) * rows, :] = term(*groups).astype(BF16)
    for at, groups in enumerate(((0, 1), (4, 5)) if along_x else ((0, 2), (4, 6))):
        keep_ref[2 * at * rows : 2 * (at + 1) * rows, :] = term(*groups)
    total = key_ref[:, :LAT]
    for h in range(heads):
        total = total + dot(parts[h], wt_ref[h], 1, 1)
    key_ref[:, :LAT] = total
    key_ref[:, LAT:] = key_ref[:, LAT:] + rope
    for h in range(heads):
        low, high = (dot(dscores[h, b], keys[h][reach[b]], 1, 0) for b in range(2))
        dq_ref[h] = jnp.where(first, low, high)
        back_ref[h] = jnp.where(first, high, low)


def chunk(here, window, weight, mine, got, before, index, heads, along_x):
    tok = mine.shape[1]
    whole = lambda i, here: (0, 0)
    whole3 = lambda i, here: (0, 0, 0)
    step = min(heads, STEP_HEADS)
    steps = heads // step
    at = lambda i, here: (index * steps + i, 0, 0)
    across_columns = lambda i, here: (0, i)
    columns = heads * PAIR
    operands = [*window, weight, mine, got]
    in_specs = [
        pl.BlockSpec(array.shape, whole3 if array.ndim == 3 else whole) for array in window
    ] + [
        pl.BlockSpec((step, LAT, PAIR), at),
        pl.BlockSpec((step, tok, 3 * LANES), at),
        pl.BlockSpec((step, tok, 3 * LANES), at),
    ]
    aliases = {}
    if before is not None:
        key, dq, back = before
        aliases = {len(operands) + 2: 3, len(operands) + 3: 4}
        in_specs = in_specs + [
            pl.BlockSpec(key.shape, whole),
            pl.BlockSpec(memory_space=pl.ANY),
            pl.BlockSpec(memory_space=pl.ANY),
        ]
        operands = operands + [key, dq, back]
    turned = (weight.shape[0], tok, 2 * LANES)
    return pl.pallas_call(
        functools.partial(chunk_kernel, chained=before is not None, along_x=along_x),
        grid_spec=pltpu.PrefetchScalarGridSpec(
            num_scalar_prefetch=1,
            grid=(steps,),
            in_specs=in_specs,
            out_specs=[
                pl.BlockSpec((LAT // 2, step * PAIR), across_columns),
                pl.BlockSpec((LAT // 2, step * PAIR), across_columns),
                pl.BlockSpec((3 * tok, LAT + LANES), whole),
                pl.BlockSpec((step, tok, 2 * LANES), at),
                pl.BlockSpec((step, tok, 2 * LANES), at),
            ],
        ),
        out_shape=[
            jax.ShapeDtypeStruct((LAT // 2, columns), F32),
            jax.ShapeDtypeStruct((LAT // 2, columns), BF16),
            jax.ShapeDtypeStruct((3 * tok, LAT + LANES), F32),
            jax.ShapeDtypeStruct(turned, F32),
            jax.ShapeDtypeStruct(turned, F32),
        ],
        input_output_aliases=aliases,
        compiler_params=PARAMS,
        cost_estimate=cost(CHUNK),
        name="chunk",
    )(here, *operands)


def add_rows_kernel(*refs, count, wide):
    total = refs[0][...].astype(F32)
    for ref in refs[1 : count + wide]:
        total = total + ref[...].astype(F32)
    refs[-1][...] = total.astype(refs[-1].dtype)


def add_rows(arrays, rows, index, dtype, wide=(), place=0, places=1, before=None):
    columns = arrays[0].shape[1]
    operands = [*arrays, *wide]
    in_specs = [pl.BlockSpec((rows, columns), lambda i: (index, 0)) for _ in arrays]
    in_specs = in_specs + [pl.BlockSpec((rows, columns), lambda i: (index, place)) for _ in wide]
    aliases = {}
    if before is not None:
        aliases = {len(operands): 0}
        in_specs.append(pl.BlockSpec(memory_space=pl.ANY))
        operands.append(before)
    return pl.pallas_call(
        functools.partial(add_rows_kernel, count=len(arrays), wide=len(wide)),
        grid=(1,),
        in_specs=in_specs,
        out_specs=pl.BlockSpec((rows, columns), lambda i: (0, place)),
        out_shape=jax.ShapeDtypeStruct((rows, places * columns), dtype),
        input_output_aliases=aliases,
        compiler_params=PARAMS,
        cost_estimate=cost(SHARES),
        name="add_rows",
    )(*operands)


def key_split_kernel(here_ref, key_ref, keep_ref, give_ref):
    tok = keep_ref.shape[0] // 2
    first = (here_ref[0] & 1) == 0
    behind, low, high = (key_ref[b * tok : (b + 1) * tok, :] for b in range(3))
    keep_ref[:tok] = jnp.where(first, low, high)
    keep_ref[tok:] = behind
    give_ref[:tok] = jnp.where(first, high, low)
    give_ref[tok:] = behind


def key_split(here, key):
    rows = key.shape[0] // 3 * 2
    whole = lambda i, here: (0, 0)
    return pl.pallas_call(
        key_split_kernel,
        grid_spec=pltpu.PrefetchScalarGridSpec(
            num_scalar_prefetch=1,
            grid=(1,),
            in_specs=[pl.BlockSpec(key.shape, whole)],
            out_specs=[pl.BlockSpec((rows, key.shape[1]), whole)] * 2,
        ),
        out_shape=[jax.ShapeDtypeStruct((rows, key.shape[1]), F32)] * 2,
        compiler_params=PARAMS,
        cost_estimate=cost(SHARES),
        name="key_split",
    )(here, key)


def key_shares_kernel(at_ref, keep_ref, got_ref, *outs):
    shares = len(outs)
    part = (LAT + ROPE) // shares
    total = keep_ref[...] + got_ref[...]
    for z in range(shares):
        piece = total[:, z * part : (z + 1) * part]
        for s in range(shares):

            @pl.when(lax.rem(at_ref[0] + s, shares) == z)
            def _(s=s, piece=piece):
                outs[s][...] = piece.astype(outs[s].dtype)


def key_shares(at_head, keep, got, shares):
    part = (LAT + ROPE) // shares
    rows = keep.shape[0]
    whole = lambda i, at: (0, 0)
    types = [F32] + [BF16] * (shares - 1)
    return pl.pallas_call(
        key_shares_kernel,
        grid_spec=pltpu.PrefetchScalarGridSpec(
            num_scalar_prefetch=1,
            grid=(1,),
            in_specs=[pl.BlockSpec(keep.shape, whole)] * 2,
            out_specs=[pl.BlockSpec((rows, part), whole)] * shares,
        ),
        out_shape=[jax.ShapeDtypeStruct((rows, part), kind) for kind in types],
        compiler_params=PARAMS,
        cost_estimate=cost(SHARES),
        name="key_shares",
    )(at_head, keep, got)


def query_grad_kernel(here_ref, mine_ref, got_ref, out_ref, n_ref, r_ref):
    tok, heads, _ = out_ref.shape

    def put(src_ref):
        for h in range(heads):
            n_ref[pl.ds(h, tok, stride=heads), :] = src_ref[h, :, :PLAIN_WIDTH]
            r_ref[pl.ds(h, tok, stride=heads), :] = src_ref[h, :, PLAIN_WIDTH:]

    pl.when(pl.program_id(0) == 0)(lambda: put(mine_ref))
    pl.when(pl.program_id(0) == 1)(lambda: put(got_ref))
    out_ref[:, :, :PLAIN_WIDTH] = n_ref[...].reshape(tok, heads, LANES)
    out_ref[:, :, PLAIN_WIDTH:] = r_ref[...].reshape(tok, heads, LANES)[:, :, :ROPE]


def query_grad(here, mine, got):
    heads, tok, _ = mine.shape
    whole = lambda i, here: (0, 0, 0)
    return pl.pallas_call(
        query_grad_kernel,
        grid_spec=pltpu.PrefetchScalarGridSpec(
            num_scalar_prefetch=1,
            grid=(2,),
            in_specs=[pl.BlockSpec(mine.shape, whole)] * 2,
            out_specs=pl.BlockSpec(
                (tok, heads, PLAIN_WIDTH + ROPE), lambda i, here: (0, (here[0] & 1) ^ i, 0)
            ),
            scratch_shapes=[pltpu.VMEM((tok * heads, LANES), F32)] * 2,
        ),
        out_shape=jax.ShapeDtypeStruct((tok, 2 * heads, PLAIN_WIDTH + ROPE), F32),
        compiler_params=PARAMS,
        cost_estimate=cost(QUERY),
        name="query_grad",
    )(here, mine, got)


def second_send_kernel(*refs):
    *narrow, theirs_ref, out_ref = refs
    columns = narrow[0].shape[1]
    for c in range(len(narrow) // 2):
        total = narrow[2 * c][...] + narrow[2 * c + 1][...].astype(F32)
        out_ref[:, c * columns : (c + 1) * columns] = total.astype(BF16)
    out_ref[:, len(narrow) // 2 * columns :] = theirs_ref[...]


def second_send(groups, theirs, rows):
    narrow = [array for group in groups for array in group]
    columns = narrow[0].shape[1]
    wide = theirs.shape[1]
    return pl.pallas_call(
        second_send_kernel,
        grid=(1,),
        in_specs=[pl.BlockSpec((rows, columns), lambda i: (1, 0)) for _ in narrow]
        + [pl.BlockSpec((rows, wide), lambda i: (1, 0))],
        out_specs=pl.BlockSpec((rows, 2 * wide), lambda i: (0, 0)),
        out_shape=jax.ShapeDtypeStruct((rows, 2 * wide), BF16),
        compiler_params=PARAMS,
        cost_estimate=cost(SHARES),
        name="second_send",
    )(*narrow, theirs)


def last_sums_kernel(here_ref, *refs, order, count, wide):
    share_ref, behind_ref, out_ref, key_ref, k_ref, v_ref = refs[-6:]
    rows, heads, _ = out_ref.shape
    size = 2 * count + 2
    each = wide // PAIR
    key_ref[...] = share_ref[...] + behind_ref[...]

    def put(j, total):
        for h in range(each):
            at = pl.ds(j * each + h, rows, stride=heads)
            k_ref[at, :] = total[:, h * PAIR : h * PAIR + LANES]
            v_ref[at, :] = total[:, h * PAIR + LANES : (h + 1) * PAIR]

    for q, places in enumerate(order):
        for j, (pair, piece) in enumerate(places):
            group = refs[pair * size : (pair + 1) * size]
            kept, came = group[2 * piece : 2 * piece + 2]
            theirs_ref, last_ref = group[-2:]
            columns = slice(piece * wide, (piece + 1) * wide)
            later = slice((count + piece) * wide, (count + piece + 1) * wide)

            @pl.when(pl.program_id(0) == 2 * q)
            def _(j=j, kept=kept, came=came, last_ref=last_ref, columns=columns):
                total = kept[...] + came[...].astype(F32)
                put(j, total + last_ref[:, columns].astype(F32))

            @pl.when(pl.program_id(0) == 2 * q + 1)
            def _(j=j, theirs_ref=theirs_ref, last_ref=last_ref, columns=columns, later=later):
                put(j, theirs_ref[:, columns].astype(F32) + last_ref[:, later].astype(F32))

    out_ref[:, :, :LANES] = k_ref[...].reshape(rows, heads, LANES)
    out_ref[:, :, LANES:] = v_ref[...].reshape(rows, heads, LANES)


def last_sums(here, pieces, theirs, lasts, share, behind, order, wide):
    rows, heads = share.shape[0], len(order[0]) * wide // PAIR
    whole = lambda i, here: (0, 0)
    operands, in_specs = [], []
    for group, other, last in zip(pieces, theirs, lasts):
        for array, column in [part for piece in group for part in piece]:
            operands.append(array)
            in_specs.append(pl.BlockSpec((rows, wide), lambda i, here, column=column: (0, column)))
        for array in (other, last):
            operands.append(array)
            in_specs.append(pl.BlockSpec((rows, array.shape[1]), whole))
    in_specs = in_specs + [pl.BlockSpec(share.shape, whole)] * 2
    return pl.pallas_call(
        functools.partial(last_sums_kernel, order=order, count=len(pieces[0]), wide=wide),
        grid_spec=pltpu.PrefetchScalarGridSpec(
            num_scalar_prefetch=1,
            grid=(4,),
            in_specs=in_specs,
            out_specs=[
                pl.BlockSpec(
                    (rows, heads, PAIR),
                    lambda i, here: (0, ((here[0] & 1) ^ (i & 1)) * 2 + (i >> 1), 0),
                ),
                pl.BlockSpec(share.shape, whole),
            ],
            scratch_shapes=[pltpu.VMEM((rows * heads, LANES), F32)] * 2,
        ),
        out_shape=[
            jax.ShapeDtypeStruct((rows, 4 * heads, PAIR), F32),
            jax.ShapeDtypeStruct(share.shape, F32),
        ],
        compiler_params=PARAMS,
        cost_estimate=cost(SUM),
        name="last_sums",
    )(here, *operands, share, behind)


def in_chunks(queries, latent_keys, out_grad, up_weight, here, at_head, ids):
    tok = latent_keys.shape[0]
    n_ctx, n_head = lax.axis_size("ctx"), lax.axis_size("head")
    heads, each = 16, 4
    queries = after(queries, (ids, here, at_head))
    give, mine = turn_tokens(here, queries, out_grad, latent_keys, heads)
    odd_devices = range(1, n_ctx - 1, 2)
    even = lax.ppermute(latent_keys, "ctx", [(source, source + 1) for source in odd_devices])
    odd = lax.ppermute(latent_keys, "ctx", [(source, source + 2) for source in odd_devices])
    got = across(give, 1)
    weight = turn_weight(here, up_weight, heads)
    window = chip_window(here, even, odd, latent_keys, got, ids)
    ways, blocks = ((2, 4), (4, 2)), (0, 2, 1, 3)
    before, keeps, sent = None, [], []
    for c, block in enumerate(blocks):
        keep, out, *before = chunk(
            here, window, weight, mine, got, before, block, each, c % 2 == 0
        )
        keeps.append(keep)
        sent.append(across(out, ways[c % 2][0]))
    key, dq, back = before

    def rest(c, earlier):
        return add_rows(
            (keeps[c], sent[c]), 2 * tok, 1, BF16, place=c // 2, places=2, before=earlier
        )

    key_keep, key_give = key_split(here, key)
    key_got = across(key_give, 1)
    rests = [rest(0, None)]
    keeps[1] = after(keeps[1], rests[0])
    rests.append(rest(1, None))
    key_got = after(key_got, rests)
    shares = key_shares(at_head, key_keep, key_got, n_head)
    pieces = [
        lax.ppermute(shares[s], "head", [(z, (z + s) % n_head) for z in range(n_head)])
        for s in range(1, n_head)
    ]
    back = across(after(back, key_keep), 1)
    share, behind = (add_rows((shares[0], *pieces), tok, b, F32) for b in range(2))
    keeps[2] = after(keeps[2], (share, behind))
    behind = lax.ppermute(behind, "ctx", [(source, source - 1) for source in range(2, n_ctx, 2)])
    groups = [[(keeps[c], sent[c]) for c in (p, p + 2)] for p in range(2)]
    theirs, seconds, lasts = [], [], []
    for p in range(2):
        theirs.append(across(rest(p + 2, rests[p]), 1))
        seconds.append(second_send(groups[p], theirs[p], tok))
        lasts.append(across(seconds[p], ways[p][1]))
    dq = query_grad(here, after(dq, seconds), back)
    theirs = after(theirs, dq)
    theirs[1] = after(theirs[1], lasts[0])
    pieces = [[tuple((array, 0) for array in part) for part in group] for group in groups]
    order = (((0, 0), (0, 1)), ((1, 0), (1, 1)))
    weight_grad, key_grad = last_sums(
        here, pieces, theirs, lasts, share, behind, order, each * PAIR
    )
    return dq, key_grad, weight_grad


def shards(queries, latent_keys, out_grad, up_weight, segment_ids):
    tok = latent_keys.shape[0]
    heads = queries.shape[1]
    n_ctx, n_head = lax.axis_size("ctx"), lax.axis_size("head")
    here = lax.axis_index("ctx").astype(jnp.int32).reshape(1)
    at_head = lax.axis_index("head").astype(jnp.int32).reshape(1)
    if n_ctx == 8 and heads == 32 and n_head == 4:
        ids = segment_ids.reshape(n_ctx // 2, 2 * tok)
        return in_chunks(queries, latent_keys, out_grad, up_weight, here, at_head, ids)
    else:
        ids = segment_ids.reshape(n_ctx, tok)
        prev = from_behind(latent_keys, "ctx", REACH)
        turned = by_head(up_weight, queries, out_grad, 0, heads)
        window = key_window(here, prev, latent_keys, ids, False)
        dq, dkv, rope = attention(window, turned, None, None, 0, heads, 0, heads)
        (both,) = key_terms(at_head, [dkv], [turned[0]], [rope], None)
        share = lax.psum_scatter(
            both.reshape(REACH + 1, tok, LAT + ROPE), "head", scatter_dimension=2, tiled=True
        )
        term = jnp.einsum("ki,ke->ie", window[0], dkv, preferred_element_type=F32)
        rows = lax.psum_scatter(term.astype(BF16), "ctx", scatter_dimension=0, tiled=True)
        weight_grad = rows.astype(F32).reshape(rows.shape[0], heads, PAIR)
    key_grad = share[REACH] + from_behind(share[0], "ctx", 0 - REACH)
    return (dq, key_grad, weight_grad)


def solution(mesh):
    return jax.shard_map(
        shards,
        mesh=mesh,
        in_specs=(
            P("ctx", "head", None),
            P("ctx", None),
            P("ctx", "head", None),
            P(None, "head", None),
            P(),
        ),
        out_specs=(P("ctx", "head", None), P("ctx", "head"), P("ctx", "head", None)),
        check_vma=False,
    )
```

```python
import functools
import math

import jax
import jax.numpy as jnp
from jax import lax
from jax.experimental import pallas as pl
from jax.experimental.pallas import tpu as pltpu
from jax.sharding import PartitionSpec as P

LAT = 512
ROPE = 64
PLAIN_WIDTH = 128
VDIM = 128
REACH = 1
LANES = 128
PAIR = PLAIN_WIDTH + VDIM
STEP_HEADS = 4
BF16 = jnp.bfloat16
F32 = jnp.float32
WIDE = pltpu.CompilerParams(vmem_limit_bytes=56 * 1024 * 1024)
PARAMS = pltpu.CompilerParams(vmem_limit_bytes=20 * 1024 * 1024)


def from_behind(value, axis, steps):
    count = lax.axis_size(axis)
    initial, last = (max(0, -steps), min(count, count - steps))
    return lax.ppermute(value, axis, [(source, source + steps) for source in range(initial, last)])


def across(value, bit):
    count = lax.axis_size("ctx")
    return lax.ppermute(value, "ctx", [(source, source ^ bit) for source in range(count)])


def cost(share):
    return pl.CostEstimate(flops=int(share * 1e9), bytes_accessed=1024, transcendentals=0)


TURN, WINDOW, CHUNK, SHARES, QUERY, SUM = 3.0, 0.5, 1.5, 0.1, 0.1, 0.1


def dot(a, b, a_dim, b_dim):
    return lax.dot_general(a, b, (((a_dim,), (b_dim,)), ((), ())), preferred_element_type=F32)


def by_head_kernel(w_ref, q_ref, g_ref, wt_ref, qt_ref, gt_ref):
    heads = w_ref.shape[1]
    orders = {}

    def order(count):
        if count not in orders:
            size = count * heads
            row = lax.broadcasted_iota(jnp.int32, (size, size), 0)
            col = lax.broadcasted_iota(jnp.int32, (size, size), 1)
            wanted = (row % count) * heads + row // count
            orders[count] = (col == wanted).astype(BF16)
        return orders[count]

    def turn(ref, out_ref):
        rows, _, width = ref.shape
        count = min(rows, 256 // heads)
        for start in range(0, rows, count):
            block = ref[start : start + count].reshape(count * heads, width)
            turned = dot(order(count), block, 1, 0).astype(BF16)
            out_ref[:, start : start + count, :width] = turned.reshape(heads, count, width)

    turn(w_ref, wt_ref)
    qt_ref[...] = jnp.zeros_like(qt_ref)
    turn(q_ref, qt_ref)
    turn(g_ref, gt_ref)


def by_head(up_weight, queries, out_grad, chunk, heads):
    tok = queries.shape[0]
    steps = 4
    depth, rows = LAT // steps, tok // steps
    return pl.pallas_call(
        by_head_kernel,
        grid=(steps,),
        in_specs=[
            pl.BlockSpec((depth, heads, PAIR), lambda i: (i, chunk, 0)),
            pl.BlockSpec((rows, heads, PLAIN_WIDTH + ROPE), lambda i: (i, chunk, 0)),
            pl.BlockSpec((rows, heads, VDIM), lambda i: (i, chunk, 0)),
        ],
        out_specs=[
            pl.BlockSpec((heads, depth, PAIR), lambda i: (0, i, 0)),
            pl.BlockSpec((heads, rows, 2 * LANES), lambda i: (0, i, 0)),
            pl.BlockSpec((heads, rows, VDIM), lambda i: (0, i, 0)),
        ],
        out_shape=[
            jax.ShapeDtypeStruct((heads, LAT, PAIR), BF16),
            jax.ShapeDtypeStruct((heads, tok, 2 * LANES), BF16),
            jax.ShapeDtypeStruct((heads, tok, VDIM), BF16),
        ],
        compiler_params=WIDE,
        cost_estimate=cost(TURN),
        name="by_head",
    )(up_weight, queries, out_grad)


def window_kernel(here_ref, prev_ref, own_ref, ids_ref, *outs, paired):
    win_ref, krope_ref, vis_ref = outs[:3]
    here = here_ref[0]
    tok = prev_ref.shape[0]
    win_ref[:tok, :] = prev_ref[:, :LAT]
    win_ref[tok:, :] = own_ref[:, :LAT]
    krope_ref[...] = jnp.zeros_like(krope_ref)
    krope_ref[:tok, :ROPE] = prev_ref[:, LAT:]
    krope_ref[tok:, :ROPE] = own_ref[:, LAT:]
    behind = jnp.maximum(here - 1, 0)
    seg_prev = jnp.where(here > 0, ids_ref[pl.ds(behind, 1), :], -1)
    seg_own = ids_ref[pl.ds(here, 1), :]
    row = lax.broadcasted_iota(jnp.int32, (tok, tok), 0)
    col = lax.broadcasted_iota(jnp.int32, (tok, tok), 1)
    seg_query = jnp.sum(jnp.where(row == col, seg_own, 0), 1, keepdims=True)
    vis_ref[:, :tok] = (seg_query == seg_prev).astype(F32)
    vis_ref[:, tok:] = ((seg_query == seg_own) & (col <= row)).astype(F32)
    if paired:
        source = lax.broadcasted_iota(jnp.int32, (LAT, LAT), 0)
        column = lax.broadcasted_iota(jnp.int32, (LAT, LAT), 1)
        place = column >> 6
        apart = ((place & 1) << 2) | (place & 2) | (place >> 2)
        wanted = ((here ^ apart) << 6) | (column & 63)
        ordered = dot(win_ref[...], (source == wanted).astype(BF16), 1, 0).astype(BF16)
        outs[3][...] = ordered[:, : LAT // 2]
        outs[4][...] = ordered[:, LAT // 2 :]


def key_window(here, prev, own, ids, paired):
    tok = prev.shape[0]
    whole = lambda i, here: (0, 0)
    shapes = [((2 * tok, LAT), BF16), ((2 * tok, LANES), BF16), ((tok, 2 * tok), F32)]
    if paired:
        shapes = shapes + [((2 * tok, LAT // 2), BF16)] * 2
    return pl.pallas_call(
        functools.partial(window_kernel, paired=paired),
        grid_spec=pltpu.PrefetchScalarGridSpec(
            num_scalar_prefetch=1,
            grid=(1,),
            in_specs=[pl.BlockSpec(array.shape, whole) for array in (prev, own, ids)],
            out_specs=[pl.BlockSpec(shape, whole) for shape, _ in shapes],
        ),
        out_shape=[jax.ShapeDtypeStruct(*shape) for shape in shapes],
        compiler_params=PARAMS,
        cost_estimate=cost(WINDOW),
        name="key_window",
    )(here, prev, own, ids)


def attention_kernel(
    win_ref, krope_ref, vis_ref, wt_ref, qt_ref, gt_ref, *refs, aliased, extra
):
    latents_ref = refs[0] if extra else None
    refs = refs[1:] if extra else refs
    refs = refs[1:] if aliased else refs
    dq_ref, dkv_ref, rope_ref, dqn_ref, dqr_ref = refs
    i = pl.program_id(0)
    tok, heads = dq_ref.shape[:2]
    scale = 1.0 / math.sqrt(PLAIN_WIDTH + ROPE)

    @pl.when(i == 0)
    def _():
        rope_ref[...] = jnp.zeros_like(rope_ref)
        if extra:
            dkv_ref[:, heads * PAIR :] = latents_ref[...]

    visible = vis_ref[...] > 0.0
    window = win_ref[...]
    krope = krope_ref[...]
    count = wt_ref.shape[0]
    keys, values = [], []
    for h in range(count):
        kv = dot(window, wt_ref[h], 1, 0).astype(BF16)
        keys.append(jnp.concatenate([kv[:, :PLAIN_WIDTH], krope], 1))
        values.append(kv[:, PLAIN_WIDTH:])
    scores = [dot(qt_ref[h], keys[h], 1, 1) for h in range(count)]
    dprobs = [dot(gt_ref[h], values[h], 1, 1) for h in range(count)]
    dscores, probs16 = [], []
    for h in range(count):
        logits = jnp.where(visible, scores[h] * scale, -1e30)
        top = jnp.max(logits, -1, keepdims=True)
        expo = jnp.exp(logits - top)
        probs = expo / jnp.sum(expo, -1, keepdims=True)
        delta = jnp.sum(probs * dprobs[h], -1, keepdims=True)
        dscores.append((probs * (dprobs[h] - delta) * scale).astype(BF16))
        probs16.append(probs.astype(BF16))
    parts, rope = [], rope_ref[...]
    for h in range(count):
        dk = dot(dscores[h], qt_ref[h], 0, 0)
        dv = dot(probs16[h], gt_ref[h], 0, 0)
        parts.append(jnp.concatenate([dk[:, :PLAIN_WIDTH], dv], 1).astype(BF16))
        rope = rope + dk[:, PLAIN_WIDTH:]
    rope_ref[...] = rope
    dkv_ref[:, pl.ds(pl.multiple_of(i * (count * PAIR), count * PAIR), count * PAIR)] = (
        jnp.concatenate(parts, 1)
    )
    for h in range(count):
        dq = dot(dscores[h], keys[h], 1, 0)
        dqn_ref[pl.ds(i * count + h, tok, stride=heads), :] = dq[:, :PLAIN_WIDTH]
        dqr_ref[pl.ds(i * count + h, tok, stride=heads), :] = dq[:, PLAIN_WIDTH:]

    @pl.when(i == pl.num_programs(0) - 1)
    def _():
        dq_ref[:, :, :PLAIN_WIDTH] = dqn_ref[...].reshape(tok, heads, LANES)
        dq_ref[:, :, PLAIN_WIDTH:] = dqr_ref[...].reshape(tok, heads, LANES)[:, :, :ROPE]


def attention(window, turned, latents, dq, chunk, heads, first, all_heads):
    weight, queries, out_grad = turned
    tok = queries.shape[1]
    width = 2 * tok
    steps = heads // STEP_HEADS
    at = first // STEP_HEADS
    extra = LAT // 2 if latents is not None else 0
    whole = lambda i: (0, 0)
    head_block = lambda i: (at + i, 0, 0)
    operands = [*window, weight, queries, out_grad]
    in_specs = [pl.BlockSpec(array.shape, whole) for array in window] + [
        pl.BlockSpec((STEP_HEADS, LAT, PAIR), head_block),
        pl.BlockSpec((STEP_HEADS, tok, 2 * LANES), head_block),
        pl.BlockSpec((STEP_HEADS, tok, VDIM), head_block),
    ]
    if latents is not None:
        in_specs.append(pl.BlockSpec(latents.shape, whole))
        operands.append(latents)
    aliases = {}
    if dq is not None:
        aliases = {len(operands): 0}
        in_specs.append(pl.BlockSpec(memory_space=pl.ANY))
        operands.append(dq)
    return pl.pallas_call(
        functools.partial(attention_kernel, aliased=dq is not None, extra=latents is not None),
        grid=(steps,),
        in_specs=in_specs,
        out_specs=[
            pl.BlockSpec((tok, heads, PLAIN_WIDTH + ROPE), lambda i: (0, chunk, 0)),
            pl.BlockSpec((width, heads * PAIR + extra), whole),
            pl.BlockSpec((width, LANES), whole),
        ],
        scratch_shapes=[
            pltpu.VMEM((tok * heads, LANES), F32),
            pltpu.VMEM((tok * heads, LANES), F32),
        ],
        out_shape=[
            jax.ShapeDtypeStruct((tok, all_heads, PLAIN_WIDTH + ROPE), F32),
            jax.ShapeDtypeStruct((width, heads * PAIR + extra), BF16),
            jax.ShapeDtypeStruct((width, LANES), F32),
        ],
        input_output_aliases=aliases,
        compiler_params=WIDE,
        cost_estimate=cost(CHUNK),
        name="attention",
    )(*operands)


def terms_kernel(
    own_ref, other_ref, mine_ref, theirs_ref, keep_ref, send_ref, latents_ref, *, along_x
):
    width = own_ref.shape[0]

    @pl.when(pl.program_id(0) == 0)
    def _():
        latents_ref[:, :width] = mine_ref[...].T
        latents_ref[:, width:] = theirs_ref[...].T

    grads = jnp.concatenate([own_ref[...], other_ref[...]], 0)
    term = dot(latents_ref[...], grads, 1, 0)
    rows = term.shape[0] // 4
    first, second = (1, 2) if along_x else (2, 1)
    keep_ref[:rows] = term[:rows]
    keep_ref[rows:] = term[first * rows : (first + 1) * rows]
    send_ref[:rows] = term[second * rows : (second + 1) * rows].astype(BF16)
    send_ref[rows:] = term[3 * rows :].astype(BF16)


def terms(own, other, mine, theirs, columns, along_x):
    width = own.shape[0]
    block = 1024
    at = theirs.shape[1] // (LAT // 2) - 1
    column_block = lambda i: (0, i)
    return pl.pallas_call(
        functools.partial(terms_kernel, along_x=along_x),
        grid=(columns // block,),
        in_specs=[
            pl.BlockSpec((width, block), column_block),
            pl.BlockSpec((width, block), column_block),
            pl.BlockSpec((width, LAT // 2), lambda i: (0, 0)),
            pl.BlockSpec((width, LAT // 2), lambda i: (0, at)),
        ],
        out_specs=[pl.BlockSpec((LAT // 4, block), column_block)] * 2,
        out_shape=[
            jax.ShapeDtypeStruct((LAT // 4, columns), F32),
            jax.ShapeDtypeStruct((LAT // 4, columns), BF16),
        ],
        scratch_shapes=[pltpu.VMEM((LAT // 2, 2 * width), BF16)],
        compiler_params=PARAMS,
        cost_estimate=cost(CHUNK),
        name="terms",
    )(own, other, mine, theirs)


def key_terms_kernel(*refs, chunks, steps, turns, shares):
    head_ref = refs[0]
    dkv_refs = refs[1 : 1 + chunks]
    wt_refs = refs[1 + chunks : 1 + chunks + turns]
    rope_refs = refs[1 + chunks + turns : 1 + 2 * chunks + turns]
    outs = refs[1 + 2 * chunks + turns : -1]
    total_ref = refs[-1]
    i = pl.program_id(0)

    @pl.when(i == 0)
    def _():
        total_ref[...] = jnp.zeros_like(total_ref)

    for k in range(chunks):

        @pl.when(i // steps == k)
        def _(k=k):
            total = total_ref[...]
            weight_ref = wt_refs[k * turns // chunks]
            for h in range(weight_ref.shape[0]):
                grads = dkv_refs[k][:, h * PAIR : (h + 1) * PAIR]
                total = total + dot(grads, weight_ref[h], 1, 1)
            total_ref[...] = total

    @pl.when(i == pl.num_programs(0) - 1)
    def _():
        rope = rope_refs[0][...]
        for k in range(1, chunks):
            rope = rope + rope_refs[k][...]
        both = jnp.concatenate([total_ref[...], rope], 1)
        if shares is None:
            outs[0][...] = both[:, : LAT + ROPE]
            return
        part = (LAT + ROPE) // shares
        for z in range(shares):
            piece = both[:, z * part : (z + 1) * part]
            for s in range(shares):

                @pl.when(lax.rem(head_ref[0] + s, shares) == z)
                def _(s=s, piece=piece):
                    outs[s][...] = piece


def key_terms(at_head, dkvs, weights, ropes, shares):
    chunks, turns = len(dkvs), len(weights)
    heads = weights[0].shape[0] * turns // chunks
    width = dkvs[0].shape[0]
    steps = heads // STEP_HEADS
    span = steps * chunks // turns
    near = lambda k, many: lambda i, at: jnp.clip(i - k * many, 0, many - 1)
    wide = (LAT + ROPE) // (shares or 1)
    return pl.pallas_call(
        functools.partial(
            key_terms_kernel, chunks=chunks, steps=steps, turns=turns, shares=shares
        ),
        grid_spec=pltpu.PrefetchScalarGridSpec(
            num_scalar_prefetch=1,
            grid=(chunks * steps,),
            in_specs=[
                pl.BlockSpec((width, STEP_HEADS * PAIR), lambda i, at, k=k: (0, near(k, steps)(i, at)))
                for k in range(chunks)
            ]
            + [
                pl.BlockSpec(
                    (STEP_HEADS, LAT, PAIR), lambda i, at, k=k: (near(k, span)(i, at), 0, 0)
                )
                for k in range(turns)
            ]
            + [pl.BlockSpec((width, LANES), lambda i, at: (0, 0))] * chunks,
            out_specs=[pl.BlockSpec((width, wide), lambda i, at: (0, 0))] * (shares or 1),
            scratch_shapes=[pltpu.VMEM((width, LAT), F32)],
        ),
        out_shape=[jax.ShapeDtypeStruct((width, wide), F32)] * (shares or 1),
        compiler_params=WIDE,
        cost_estimate=cost(CHUNK),
        name="key_terms",
    )(at_head, *dkvs, *weights, *ropes)


def weight_sum_kernel(keep_ref, first_ref, second_ref, *refs):
    out_ref, k_ref, v_ref = refs[-3:]
    rows, heads, _ = out_ref.shape
    for h in range(heads):
        columns = slice(h * PAIR, (h + 1) * PAIR)
        total = keep_ref[:, columns] + first_ref[:, columns].astype(F32)
        total = total + second_ref[:, columns].astype(F32)
        k_ref[pl.ds(h, rows, stride=heads), :] = total[:, :LANES]
        v_ref[pl.ds(h, rows, stride=heads), :] = total[:, LANES:]
    out_ref[:, :, :LANES] = k_ref[...].reshape(rows, heads, LANES)
    out_ref[:, :, LANES:] = v_ref[...].reshape(rows, heads, LANES)


def weight_sum(keep, first, second, total, chunk, all_heads):
    rows, columns = second.shape
    heads = columns // PAIR
    block = 32
    operands = [keep, first, second]
    in_specs = [pl.BlockSpec((block, columns), lambda i: (i, 0)) for _ in operands]
    aliases = {}
    if total is not None:
        aliases = {3: 0}
        in_specs.append(pl.BlockSpec(memory_space=pl.ANY))
        operands.append(total)
    return pl.pallas_call(
        weight_sum_kernel,
        grid=(rows // block,),
        in_specs=in_specs,
        out_specs=pl.BlockSpec((block, heads, PAIR), lambda i: (i, chunk, 0)),
        out_shape=jax.ShapeDtypeStruct((rows, all_heads, PAIR), F32),
        scratch_shapes=[pltpu.VMEM((block * heads, LANES), F32)] * 2,
        input_output_aliases=aliases,
        compiler_params=PARAMS,
        cost_estimate=cost(SUM),
        name="weight_sum",
    )(*operands)


def after(values, earlier):
    return lax.optimization_barrier((values, earlier))[0]


def turn_rows(block):
    rows, heads, width = block.shape
    count = min(rows, 256 // heads)
    row = lax.broadcasted_iota(jnp.int32, (count * heads, count * heads), 0)
    col = lax.broadcasted_iota(jnp.int32, (count * heads, count * heads), 1)
    order = (col == (row % count) * heads + row // count).astype(BF16)
    for start in range(0, rows, count):
        part = block[start : start + count].reshape(count * heads, width)
        turned = dot(order, part, 1, 0).astype(BF16)
        yield slice(start, start + count), turned.reshape(heads, count, width)


def in_hbm(array):
    return pltpu.with_memory_space_constraint(array, pltpu.HBM)


def turn_weight_kernel(here_ref, w_ref, wt_ref, held_ref, sem_ref):
    heads, depth = wt_ref.shape[0], wt_ref.shape[1]
    i = pl.program_id(0)
    first = pl.multiple_of((here_ref[0] & 1) * heads, heads)

    def load(k):
        rows = pl.ds(pl.multiple_of(k * depth, depth), depth)
        return pltpu.make_async_copy(
            w_ref.at[rows, pl.ds(first, heads), :], held_ref.at[rows], sem_ref.at[k]
        )

    @pl.when(i == 0)
    def _():
        for k in range(LAT // depth):
            load(k).start()

    load(i).wait()
    block = held_ref[pl.ds(pl.multiple_of(i * depth, depth), depth)]
    for rows, turned in turn_rows(block):
        wt_ref[:, rows, :] = turned


def turn_weight(here, up_weight, heads):
    steps = 8
    depth = LAT // steps
    return pl.pallas_call(
        turn_weight_kernel,
        grid_spec=pltpu.PrefetchScalarGridSpec(
            num_scalar_prefetch=1,
            grid=(steps,),
            in_specs=[pl.BlockSpec(memory_space=pl.ANY)],
            out_specs=pl.BlockSpec((heads, depth, PAIR), lambda i, here: (0, i, 0)),
            scratch_shapes=[
                pltpu.VMEM((LAT, heads, PAIR), BF16),
                pltpu.SemaphoreType.DMA((steps,)),
            ],
        ),
        out_shape=jax.ShapeDtypeStruct((heads, LAT, PAIR), BF16),
        compiler_params=PARAMS,
        cost_estimate=cost(TURN),
        name="turn_weight",
    )(here, in_hbm(up_weight))


def turn_tokens_kernel(here_ref, q1_ref, g1_ref, q0_ref, g0_ref, own_ref, give_ref, mine_ref):
    heads = mine_ref.shape[0]
    for q_ref, g_ref, out_ref in ((q1_ref, g1_ref, give_ref), (q0_ref, g0_ref, mine_ref)):
        out_ref[:, :, LANES : 2 * LANES] = jnp.zeros_like(out_ref[:, :, LANES : 2 * LANES])
        for rows, turned in turn_rows(q_ref[...]):
            out_ref[:heads, rows, : PLAIN_WIDTH + ROPE] = turned
        for rows, turned in turn_rows(g_ref[...]):
            out_ref[:heads, rows, 2 * LANES :] = turned
    rest = LAT + ROPE - 3 * LANES
    give_ref[heads] = own_ref[:, : 3 * LANES]
    give_ref[heads + 1] = jnp.zeros_like(give_ref[heads + 1])
    give_ref[heads + 1, :, :rest] = own_ref[:, 3 * LANES :]


def turn_tokens(here, queries, out_grad, latent_keys, heads):
    tok = queries.shape[0]
    q_block, g_block = (tok, heads, PLAIN_WIDTH + ROPE), (tok, heads, VDIM)
    given = lambda i, here: (0, 1 - (here[0] & 1), 0)
    kept = lambda i, here: (0, here[0] & 1, 0)
    whole = lambda i, here: (0, 0, 0)
    give, mine = (heads + 2, tok, 3 * LANES), (heads, tok, 3 * LANES)
    queries, out_grad, latent_keys = (in_hbm(x) for x in (queries, out_grad, latent_keys))
    return pl.pallas_call(
        turn_tokens_kernel,
        grid_spec=pltpu.PrefetchScalarGridSpec(
            num_scalar_prefetch=1,
            grid=(1,),
            in_specs=[
                pl.BlockSpec(q_block, given),
                pl.BlockSpec(g_block, given),
                pl.BlockSpec(q_block, kept),
                pl.BlockSpec(g_block, kept),
                pl.BlockSpec(latent_keys.shape, lambda i, here: (0, 0)),
            ],
            out_specs=[pl.BlockSpec(give, whole), pl.BlockSpec(mine, whole)],
        ),
        out_shape=[jax.ShapeDtypeStruct(give, BF16), jax.ShapeDtypeStruct(mine, BF16)],
        compiler_params=PARAMS,
        cost_estimate=cost(WINDOW),
        name="turn_tokens",
    )(here, queries, out_grad, queries, out_grad, latent_keys)


def chip_window_kernel(
    here_ref, even_ref, odd_ref, own_ref, pal_ref, ids_ref, win_ref, krope_ref, vis_ref, lat_ref
):
    here = here_ref[0]
    tok = own_ref.shape[0]
    core, chip = here & 1, here >> 1
    first = core == 0
    prev = jnp.where(first, even_ref[...].astype(F32), odd_ref[...].astype(F32)).astype(BF16)
    pal = jnp.concatenate([pal_ref[0], pal_ref[1, :, : LAT + ROPE - 3 * LANES]], 1).astype(F32)
    own = own_ref[...].astype(F32)
    low = jnp.where(first, own, pal).astype(BF16)
    high = jnp.where(first, pal, own).astype(BF16)
    krope_ref[...] = jnp.zeros_like(krope_ref)
    for at, block in enumerate((prev, low, high)):
        win_ref[at * tok : (at + 1) * tok, :] = block[:, :LAT]
        krope_ref[at * tok : (at + 1) * tok, :ROPE] = block[:, LAT:]
    behind = ids_ref[pl.ds(jnp.maximum(chip - 1, 0), 1), :]
    both = ids_ref[pl.ds(chip, 1), :]
    seg = [jnp.where(chip > 0, behind[:, tok:], -1), both[:, :tok], both[:, tok:]]
    row = lax.broadcasted_iota(jnp.int32, (tok, tok), 0)
    col = lax.broadcasted_iota(jnp.int32, (tok, tok), 1)
    for b in range(2):
        seg_query = jnp.sum(jnp.where(row == col, seg[b + 1], 0), 1, keepdims=True)
        vis_ref[b, :, :tok] = (seg_query == seg[b]).astype(F32)
        vis_ref[b, :, tok:] = ((seg_query == seg[b + 1]) & (col <= row)).astype(F32)
    column = lax.broadcasted_iota(jnp.int32, (LAT, LAT), 0)
    source = lax.broadcasted_iota(jnp.int32, (LAT, LAT), 1)
    place = column >> 6
    apart = ((place & 1) << 2) | (place & 2) | (place >> 2)
    wanted = ((here ^ apart) << 6) | (column & 63)
    order = (source == wanted).astype(BF16)
    lat_ref[...] = dot(order, win_ref[...], 1, 1).astype(BF16)


def chip_window(here, even, odd, own, got, ids):
    tok = own.shape[0]
    whole = lambda i, here: (0, 0)
    return pl.pallas_call(
        chip_window_kernel,
        grid_spec=pltpu.PrefetchScalarGridSpec(
            num_scalar_prefetch=1,
            grid=(1,),
            in_specs=[pl.BlockSpec(array.shape, whole) for array in (even, odd, own)]
            + [
                pl.BlockSpec((2,) + got.shape[1:], lambda i, here: (got.shape[0] // 2 - 1, 0, 0)),
                pl.BlockSpec(ids.shape, whole),
            ],
            out_specs=[
                pl.BlockSpec((3 * tok, LAT), whole),
                pl.BlockSpec((3 * tok, LANES), whole),
                pl.BlockSpec((2, tok, 2 * tok), lambda i, here: (0, 0, 0)),
                pl.BlockSpec((LAT, 3 * tok), whole),
            ],
        ),
        out_shape=[
            jax.ShapeDtypeStruct((3 * tok, LAT), BF16),
            jax.ShapeDtypeStruct((3 * tok, LANES), BF16),
            jax.ShapeDtypeStruct((2, tok, 2 * tok), F32),
            jax.ShapeDtypeStruct((LAT, 3 * tok), BF16),
        ],
        compiler_params=PARAMS,
        cost_estimate=cost(WINDOW),
        name="chip_window",
    )(here, even, odd, own, got, ids)


def chunk_kernel(
    here_ref,
    win_ref,
    krope_ref,
    vis_ref,
    lat_ref,
    wt_ref,
    mine_ref,
    got_ref,
    *refs,
    chained,
    along_x,
):
    before_ref = refs[0] if chained else None
    refs = refs[3:] if chained else refs
    keep_ref, send_ref, key_ref, dq_ref, back_ref = refs

    @pl.when(pl.program_id(0) == 0)
    def _():
        key_ref[...] = before_ref[...] if chained else jnp.zeros_like(key_ref)

    tok = vis_ref.shape[1]
    heads = wt_ref.shape[0]
    first = (here_ref[0] & 1) == 0
    scale = 1.0 / math.sqrt(PLAIN_WIDTH + ROPE)
    window, krope = win_ref[...], krope_ref[...]
    visible = [vis_ref[b] > 0.0 for b in range(2)]
    keys, values, queries, grads = [], [], [], []
    for h in range(heads):
        kv = dot(window, wt_ref[h], 1, 0).astype(BF16)
        keys.append(jnp.concatenate([kv[:, :PLAIN_WIDTH], krope], 1))
        values.append(kv[:, PLAIN_WIDTH:])
        mine, got = mine_ref[h], got_ref[h]
        ordered = (jnp.where(first, mine, got), jnp.where(first, got, mine))
        queries.append([block[:, : 2 * LANES] for block in ordered])
        grads.append([block[:, 2 * LANES :] for block in ordered])
    reach = [slice(b * tok, (b + 2) * tok) for b in range(2)]
    units = [(h, b) for h in range(heads) for b in range(2)]
    scores = {(h, b): dot(queries[h][b], keys[h][reach[b]], 1, 1) for h, b in units}
    dprobs = {(h, b): dot(grads[h][b], values[h][reach[b]], 1, 1) for h, b in units}
    dscores, probs16 = {}, {}
    for unit in units:
        logits = jnp.where(visible[unit[1]], scores[unit] * scale, -1e30)
        top = jnp.max(logits, -1, keepdims=True)
        expo = jnp.exp(logits - top)
        probs = expo / jnp.sum(expo, -1, keepdims=True)
        delta = jnp.sum(probs * dprobs[unit], -1, keepdims=True)
        dscores[unit] = (probs * (dprobs[unit] - delta) * scale).astype(BF16)
        probs16[unit] = probs.astype(BF16)

    def fold(low, high):
        return jnp.concatenate([low[:tok], low[tok:] + high[:tok], high[tok:]], 0)

    parts, rope = [], None
    for h in range(heads):
        dk = fold(*[dot(dscores[h, b], queries[h][b], 0, 0) for b in range(2)])
        dv = fold(*[dot(probs16[h, b], grads[h][b], 0, 0) for b in range(2)])
        parts.append(jnp.concatenate([dk[:, :PLAIN_WIDTH], dv], 1).astype(BF16))
        rope = dk[:, PLAIN_WIDTH:] if rope is None else rope + dk[:, PLAIN_WIDTH:]
    dkv = jnp.concatenate(parts, 1)
    rows = lat_ref.shape[0] // 8

    def term(low, high):
        pair = [lat_ref[g * rows : (g + 1) * rows, :] for g in (low, high)]
        return dot(jnp.concatenate(pair, 0), dkv, 1, 0)

    for at, groups in enumerate(((2, 3), (6, 7)) if along_x else ((1, 3), (5, 7))):
        send_ref[2 * at * rows : 2 * (at + 1) * rows, :] = term(*groups).astype(BF16)
    for at, groups in enumerate(((0, 1), (4, 5)) if along_x else ((0, 2), (4, 6))):
        keep_ref[2 * at * rows : 2 * (at + 1) * rows, :] = term(*groups)
    total = key_ref[:, :LAT]
    for h in range(heads):
        total = total + dot(parts[h], wt_ref[h], 1, 1)
    key_ref[:, :LAT] = total
    key_ref[:, LAT:] = key_ref[:, LAT:] + rope
    for h in range(heads):
        low, high = (dot(dscores[h, b], keys[h][reach[b]], 1, 0) for b in range(2))
        dq_ref[h] = jnp.where(first, low, high)
        back_ref[h] = jnp.where(first, high, low)


def chunk(here, window, weight, mine, got, before, index, heads, along_x):
    tok = mine.shape[1]
    whole = lambda i, here: (0, 0)
    whole3 = lambda i, here: (0, 0, 0)
    step = min(heads, STEP_HEADS)
    steps = heads // step
    at = lambda i, here: (index * steps + i, 0, 0)
    across_columns = lambda i, here: (0, i)
    columns = heads * PAIR
    operands = [*window, weight, mine, got]
    in_specs = [
        pl.BlockSpec(array.shape, whole3 if array.ndim == 3 else whole) for array in window
    ] + [
        pl.BlockSpec((step, LAT, PAIR), at),
        pl.BlockSpec((step, tok, 3 * LANES), at),
        pl.BlockSpec((step, tok, 3 * LANES), at),
    ]
    aliases = {}
    if before is not None:
        key, dq, back = before
        aliases = {len(operands) + 2: 3, len(operands) + 3: 4}
        in_specs = in_specs + [
            pl.BlockSpec(key.shape, whole),
            pl.BlockSpec(memory_space=pl.ANY),
            pl.BlockSpec(memory_space=pl.ANY),
        ]
        operands = operands + [key, dq, back]
    turned = (weight.shape[0], tok, 2 * LANES)
    return pl.pallas_call(
        functools.partial(chunk_kernel, chained=before is not None, along_x=along_x),
        grid_spec=pltpu.PrefetchScalarGridSpec(
            num_scalar_prefetch=1,
            grid=(steps,),
            in_specs=in_specs,
            out_specs=[
                pl.BlockSpec((LAT // 2, step * PAIR), across_columns),
                pl.BlockSpec((LAT // 2, step * PAIR), across_columns),
                pl.BlockSpec((3 * tok, LAT + LANES), whole),
                pl.BlockSpec((step, tok, 2 * LANES), at),
                pl.BlockSpec((step, tok, 2 * LANES), at),
            ],
        ),
        out_shape=[
            jax.ShapeDtypeStruct((LAT // 2, columns), F32),
            jax.ShapeDtypeStruct((LAT // 2, columns), BF16),
            jax.ShapeDtypeStruct((3 * tok, LAT + LANES), F32),
            jax.ShapeDtypeStruct(turned, F32),
            jax.ShapeDtypeStruct(turned, F32),
        ],
        input_output_aliases=aliases,
        compiler_params=PARAMS,
        cost_estimate=cost(CHUNK),
        name="chunk",
    )(here, *operands)


def add_rows_kernel(*refs, count, wide):
    total = refs[0][...].astype(F32)
    for ref in refs[1 : count + wide]:
        total = total + ref[...].astype(F32)
    refs[-1][...] = total.astype(refs[-1].dtype)


def add_rows(arrays, rows, index, dtype, wide=(), place=0, places=1, before=None):
    columns = arrays[0].shape[1]
    operands = [*arrays, *wide]
    in_specs = [pl.BlockSpec((rows, columns), lambda i: (index, 0)) for _ in arrays]
    in_specs = in_specs + [pl.BlockSpec((rows, columns), lambda i: (index, place)) for _ in wide]
    aliases = {}
    if before is not None:
        aliases = {len(operands): 0}
        in_specs.append(pl.BlockSpec(memory_space=pl.ANY))
        operands.append(before)
    return pl.pallas_call(
        functools.partial(add_rows_kernel, count=len(arrays), wide=len(wide)),
        grid=(1,),
        in_specs=in_specs,
        out_specs=pl.BlockSpec((rows, columns), lambda i: (0, place)),
        out_shape=jax.ShapeDtypeStruct((rows, places * columns), dtype),
        input_output_aliases=aliases,
        compiler_params=PARAMS,
        cost_estimate=cost(SHARES),
        name="add_rows",
    )(*operands)


def key_split_kernel(here_ref, key_ref, keep_ref, give_ref):
    tok = keep_ref.shape[0] // 2
    first = (here_ref[0] & 1) == 0
    behind, low, high = (key_ref[b * tok : (b + 1) * tok, :] for b in range(3))
    keep_ref[:tok] = jnp.where(first, low, high)
    keep_ref[tok:] = behind
    give_ref[:tok] = jnp.where(first, high, low)
    give_ref[tok:] = behind


def key_split(here, key):
    rows = key.shape[0] // 3 * 2
    whole = lambda i, here: (0, 0)
    return pl.pallas_call(
        key_split_kernel,
        grid_spec=pltpu.PrefetchScalarGridSpec(
            num_scalar_prefetch=1,
            grid=(1,),
            in_specs=[pl.BlockSpec(key.shape, whole)],
            out_specs=[pl.BlockSpec((rows, key.shape[1]), whole)] * 2,
        ),
        out_shape=[jax.ShapeDtypeStruct((rows, key.shape[1]), F32)] * 2,
        compiler_params=PARAMS,
        cost_estimate=cost(SHARES),
        name="key_split",
    )(here, key)


def key_shares_kernel(at_ref, keep_ref, got_ref, *outs):
    shares = len(outs)
    part = (LAT + ROPE) // shares
    total = keep_ref[...] + got_ref[...]
    for z in range(shares):
        piece = total[:, z * part : (z + 1) * part]
        for s in range(shares):

            @pl.when(lax.rem(at_ref[0] + s, shares) == z)
            def _(s=s, piece=piece):
                outs[s][...] = piece.astype(outs[s].dtype)


def key_shares(at_head, keep, got, shares):
    part = (LAT + ROPE) // shares
    rows = keep.shape[0]
    whole = lambda i, at: (0, 0)
    types = [F32] + [BF16] * (shares - 1)
    return pl.pallas_call(
        key_shares_kernel,
        grid_spec=pltpu.PrefetchScalarGridSpec(
            num_scalar_prefetch=1,
            grid=(1,),
            in_specs=[pl.BlockSpec(keep.shape, whole)] * 2,
            out_specs=[pl.BlockSpec((rows, part), whole)] * shares,
        ),
        out_shape=[jax.ShapeDtypeStruct((rows, part), kind) for kind in types],
        compiler_params=PARAMS,
        cost_estimate=cost(SHARES),
        name="key_shares",
    )(at_head, keep, got)


def query_grad_kernel(here_ref, mine_ref, got_ref, out_ref, n_ref, r_ref):
    tok, heads, _ = out_ref.shape

    def put(src_ref):
        for h in range(heads):
            n_ref[pl.ds(h, tok, stride=heads), :] = src_ref[h, :, :PLAIN_WIDTH]
            r_ref[pl.ds(h, tok, stride=heads), :] = src_ref[h, :, PLAIN_WIDTH:]

    pl.when(pl.program_id(0) == 0)(lambda: put(mine_ref))
    pl.when(pl.program_id(0) == 1)(lambda: put(got_ref))
    out_ref[:, :, :PLAIN_WIDTH] = n_ref[...].reshape(tok, heads, LANES)
    out_ref[:, :, PLAIN_WIDTH:] = r_ref[...].reshape(tok, heads, LANES)[:, :, :ROPE]


def query_grad(here, mine, got):
    heads, tok, _ = mine.shape
    whole = lambda i, here: (0, 0, 0)
    return pl.pallas_call(
        query_grad_kernel,
        grid_spec=pltpu.PrefetchScalarGridSpec(
            num_scalar_prefetch=1,
            grid=(2,),
            in_specs=[pl.BlockSpec(mine.shape, whole)] * 2,
            out_specs=pl.BlockSpec(
                (tok, heads, PLAIN_WIDTH + ROPE), lambda i, here: (0, (here[0] & 1) ^ i, 0)
            ),
            scratch_shapes=[pltpu.VMEM((tok * heads, LANES), F32)] * 2,
        ),
        out_shape=jax.ShapeDtypeStruct((tok, 2 * heads, PLAIN_WIDTH + ROPE), F32),
        compiler_params=PARAMS,
        cost_estimate=cost(QUERY),
        name="query_grad",
    )(here, mine, got)


def second_send_kernel(*refs):
    *narrow, theirs_ref, out_ref = refs
    columns = narrow[0].shape[1]
    for c in range(len(narrow) // 2):
        total = narrow[2 * c][...] + narrow[2 * c + 1][...].astype(F32)
        out_ref[:, c * columns : (c + 1) * columns] = total.astype(BF16)
    out_ref[:, len(narrow) // 2 * columns :] = theirs_ref[...]


def second_send(groups, theirs, rows):
    narrow = [array for group in groups for array in group]
    columns = narrow[0].shape[1]
    wide = theirs.shape[1]
    return pl.pallas_call(
        second_send_kernel,
        grid=(1,),
        in_specs=[pl.BlockSpec((rows, columns), lambda i: (1, 0)) for _ in narrow]
        + [pl.BlockSpec((rows, wide), lambda i: (1, 0))],
        out_specs=pl.BlockSpec((rows, 2 * wide), lambda i: (0, 0)),
        out_shape=jax.ShapeDtypeStruct((rows, 2 * wide), BF16),
        compiler_params=PARAMS,
        cost_estimate=cost(SHARES),
        name="second_send",
    )(*narrow, theirs)


def last_sums_kernel(here_ref, *refs, order, count, wide):
    share_ref, behind_ref, out_ref, key_ref, k_ref, v_ref = refs[-6:]
    rows, heads, _ = out_ref.shape
    size = 2 * count + 2
    each = wide // PAIR
    key_ref[...] = share_ref[...] + behind_ref[...]

    def put(j, total):
        for h in range(each):
            at = pl.ds(j * each + h, rows, stride=heads)
            k_ref[at, :] = total[:, h * PAIR : h * PAIR + LANES]
            v_ref[at, :] = total[:, h * PAIR + LANES : (h + 1) * PAIR]

    for q, places in enumerate(order):
        for j, (pair, piece) in enumerate(places):
            group = refs[pair * size : (pair + 1) * size]
            kept, came = group[2 * piece : 2 * piece + 2]
            theirs_ref, last_ref = group[-2:]
            columns = slice(piece * wide, (piece + 1) * wide)
            later = slice((count + piece) * wide, (count + piece + 1) * wide)

            @pl.when(pl.program_id(0) == 2 * q)
            def _(j=j, kept=kept, came=came, last_ref=last_ref, columns=columns):
                total = kept[...] + came[...].astype(F32)
                put(j, total + last_ref[:, columns].astype(F32))

            @pl.when(pl.program_id(0) == 2 * q + 1)
            def _(j=j, theirs_ref=theirs_ref, last_ref=last_ref, columns=columns, later=later):
                put(j, theirs_ref[:, columns].astype(F32) + last_ref[:, later].astype(F32))

    out_ref[:, :, :LANES] = k_ref[...].reshape(rows, heads, LANES)
    out_ref[:, :, LANES:] = v_ref[...].reshape(rows, heads, LANES)


def last_sums(here, pieces, theirs, lasts, share, behind, order, wide):
    rows, heads = share.shape[0], len(order[0]) * wide // PAIR
    whole = lambda i, here: (0, 0)
    operands, in_specs = [], []
    for group, other, last in zip(pieces, theirs, lasts):
        for array, column in [part for piece in group for part in piece]:
            operands.append(array)
            in_specs.append(pl.BlockSpec((rows, wide), lambda i, here, column=column: (0, column)))
        for array in (other, last):
            operands.append(array)
            in_specs.append(pl.BlockSpec((rows, array.shape[1]), whole))
    in_specs = in_specs + [pl.BlockSpec(share.shape, whole)] * 2
    return pl.pallas_call(
        functools.partial(last_sums_kernel, order=order, count=len(pieces[0]), wide=wide),
        grid_spec=pltpu.PrefetchScalarGridSpec(
            num_scalar_prefetch=1,
            grid=(4,),
            in_specs=in_specs,
            out_specs=[
                pl.BlockSpec(
                    (rows, heads, PAIR),
                    lambda i, here: (0, ((here[0] & 1) ^ (i & 1)) * 2 + (i >> 1), 0),
                ),
                pl.BlockSpec(share.shape, whole),
            ],
            scratch_shapes=[pltpu.VMEM((rows * heads, LANES), F32)] * 2,
        ),
        out_shape=[
            jax.ShapeDtypeStruct((rows, 4 * heads, PAIR), F32),
            jax.ShapeDtypeStruct(share.shape, F32),
        ],
        compiler_params=PARAMS,
        cost_estimate=cost(SUM),
        name="last_sums",
    )(here, *operands, share, behind)


def in_chunks(queries, latent_keys, out_grad, up_weight, here, at_head, ids):
    tok = latent_keys.shape[0]
    n_ctx, n_head = lax.axis_size("ctx"), lax.axis_size("head")
    heads, each = 16, 4
    queries = after(queries, (ids, here, at_head))
    give, mine = turn_tokens(here, queries, out_grad, latent_keys, heads)
    odd_devices = range(1, n_ctx - 1, 2)
    even = lax.ppermute(latent_keys, "ctx", [(source, source + 1) for source in odd_devices])
    odd = lax.ppermute(latent_keys, "ctx", [(source, source + 2) for source in odd_devices])
    got = across(give, 1)
    weight = turn_weight(here, up_weight, heads)
    window = chip_window(here, even, odd, latent_keys, got, ids)
    ways, blocks = ((2, 4), (4, 2)), (0, 2, 1, 3)
    before, keeps, sent = None, [], []
    for c, block in enumerate(blocks):
        keep, out, *before = chunk(
            here, window, weight, mine, got, before, block, each, c % 2 == 0
        )
        keeps.append(keep)
        sent.append(across(out, ways[c % 2][0]))
    key, dq, back = before

    def rest(c, earlier):
        return add_rows(
            (keeps[c], sent[c]), 2 * tok, 1, BF16, place=c // 2, places=2, before=earlier
        )

    key_keep, key_give = key_split(here, key)
    key_got = across(key_give, 1)
    rests = [rest(0, None)]
    keeps[1] = after(keeps[1], rests[0])
    rests.append(rest(1, None))
    key_got = after(key_got, rests)
    shares = key_shares(at_head, key_keep, key_got, n_head)
    pieces = [
        lax.ppermute(shares[s], "head", [(z, (z + s) % n_head) for z in range(n_head)])
        for s in range(1, n_head)
    ]
    back = across(after(back, key_keep), 1)
    share, behind = (add_rows((shares[0], *pieces), tok, b, F32) for b in range(2))
    keeps[2] = after(keeps[2], (share, behind))
    behind = lax.ppermute(behind, "ctx", [(source, source - 1) for source in range(2, n_ctx, 2)])
    groups = [[(keeps[c], sent[c]) for c in (p, p + 2)] for p in range(2)]
    theirs, seconds, lasts = [], [], []
    for p in range(2):
        theirs.append(across(rest(p + 2, rests[p]), 1))
        seconds.append(second_send(groups[p], theirs[p], tok))
        lasts.append(across(seconds[p], ways[p][1]))
    dq = query_grad(here, after(dq, seconds), back)
    theirs = after(theirs, dq)
    theirs[1] = after(theirs[1], lasts[0])
    pieces = [[tuple((array, 0) for array in part) for part in group] for group in groups]
    order = (((0, 0), (0, 1)), ((1, 0), (1, 1)))
    weight_grad, key_grad = last_sums(
        here, pieces, theirs, lasts, share, behind, order, each * PAIR
    )
    return dq, key_grad, weight_grad


def shards(queries, latent_keys, out_grad, up_weight, segment_ids):
    tok = latent_keys.shape[0]
    heads = queries.shape[1]
    n_ctx, n_head = lax.axis_size("ctx"), lax.axis_size("head")
    here = lax.axis_index("ctx").astype(jnp.int32).reshape(1)
    at_head = lax.axis_index("head").astype(jnp.int32).reshape(1)
    if n_ctx == 8 and heads == 32 and n_head == 4:
        ids = segment_ids.reshape(n_ctx // 2, 2 * tok)
        return in_chunks(queries, latent_keys, out_grad, up_weight, here, at_head, ids)
    else:
        ids = segment_ids.reshape(n_ctx, tok)
        prev = from_behind(latent_keys, "ctx", REACH)
        turned = by_head(up_weight, queries, out_grad, 0, heads)
        window = key_window(here, prev, latent_keys, ids, False)
        dq, dkv, rope = attention(window, turned, None, None, 0, heads, 0, heads)
        (both,) = key_terms(at_head, [dkv], [turned[0]], [rope], None)
        share = lax.psum_scatter(
            both.reshape(REACH + 1, tok, LAT + ROPE), "head", scatter_dimension=2, tiled=True
        )
        term = jnp.einsum("ki,ke->ie", window[0], dkv, preferred_element_type=F32)
        rows = lax.psum_scatter(term.astype(BF16), "ctx", scatter_dimension=0, tiled=True)
        weight_grad = rows.astype(F32).reshape(rows.shape[0], heads, PAIR)
    key_grad = share[REACH] + from_behind(share[0], "ctx", 0 - REACH)
    return (dq, key_grad, weight_grad)


def solution(mesh):
    return jax.shard_map(
        shards,
        mesh=mesh,
        in_specs=(
            P("ctx", "head", None),
            P("ctx", None),
            P("ctx", "head", None),
            P(None, "head", None),
            P(),
        ),
        out_specs=(P("ctx", "head", None), P("ctx", "head"), P("ctx", "head", None)),
        check_vma=False,
    )
```

```python
import functools
import math

import jax
import jax.numpy as jnp
from jax import lax
from jax.experimental import pallas as pl
from jax.experimental.pallas import tpu as pltpu
from jax.sharding import PartitionSpec as P

LAT = 512
ROPE = 64
PLAIN_WIDTH = 128
VDIM = 128
REACH = 1
LANES = 128
PAIR = PLAIN_WIDTH + VDIM
STEP_HEADS = 4
BF16 = jnp.bfloat16
F32 = jnp.float32
WIDE = pltpu.CompilerParams(vmem_limit_bytes=56 * 1024 * 1024)
PARAMS = pltpu.CompilerParams(vmem_limit_bytes=20 * 1024 * 1024)


def from_behind(value, axis, steps):
    count = lax.axis_size(axis)
    initial, last = (max(0, -steps), min(count, count - steps))
    return lax.ppermute(value, axis, [(source, source + steps) for source in range(initial, last)])


def across(value, bit):
    count = lax.axis_size("ctx")
    return lax.ppermute(value, "ctx", [(source, source ^ bit) for source in range(count)])


def cost(share):
    return pl.CostEstimate(flops=int(share * 1e9), bytes_accessed=1024, transcendentals=0)


TURN, WINDOW, CHUNK, SHARES, QUERY, SUM = 3.0, 0.5, 1.5, 0.1, 0.1, 0.1


def dot(a, b, a_dim, b_dim):
    return lax.dot_general(a, b, (((a_dim,), (b_dim,)), ((), ())), preferred_element_type=F32)


def by_head_kernel(w_ref, q_ref, g_ref, wt_ref, qt_ref, gt_ref):
    heads = w_ref.shape[1]
    orders = {}

    def order(count):
        if count not in orders:
            size = count * heads
            row = lax.broadcasted_iota(jnp.int32, (size, size), 0)
            col = lax.broadcasted_iota(jnp.int32, (size, size), 1)
            wanted = (row % count) * heads + row // count
            orders[count] = (col == wanted).astype(BF16)
        return orders[count]

    def turn(ref, out_ref):
        rows, _, width = ref.shape
        count = min(rows, 256 // heads)
        for start in range(0, rows, count):
            block = ref[start : start + count].reshape(count * heads, width)
            turned = dot(order(count), block, 1, 0).astype(BF16)
            out_ref[:, start : start + count, :width] = turned.reshape(heads, count, width)

    turn(w_ref, wt_ref)
    qt_ref[...] = jnp.zeros_like(qt_ref)
    turn(q_ref, qt_ref)
    turn(g_ref, gt_ref)


def by_head(up_weight, queries, out_grad, chunk, heads):
    tok = queries.shape[0]
    steps = 4
    depth, rows = LAT // steps, tok // steps
    return pl.pallas_call(
        by_head_kernel,
        grid=(steps,),
        in_specs=[
            pl.BlockSpec((depth, heads, PAIR), lambda i: (i, chunk, 0)),
            pl.BlockSpec((rows, heads, PLAIN_WIDTH + ROPE), lambda i: (i, chunk, 0)),
            pl.BlockSpec((rows, heads, VDIM), lambda i: (i, chunk, 0)),
        ],
        out_specs=[
            pl.BlockSpec((heads, depth, PAIR), lambda i: (0, i, 0)),
            pl.BlockSpec((heads, rows, 2 * LANES), lambda i: (0, i, 0)),
            pl.BlockSpec((heads, rows, VDIM), lambda i: (0, i, 0)),
        ],
        out_shape=[
            jax.ShapeDtypeStruct((heads, LAT, PAIR), BF16),
            jax.ShapeDtypeStruct((heads, tok, 2 * LANES), BF16),
            jax.ShapeDtypeStruct((heads, tok, VDIM), BF16),
        ],
        compiler_params=WIDE,
        cost_estimate=cost(TURN),
        name="by_head",
    )(up_weight, queries, out_grad)


def window_kernel(here_ref, prev_ref, own_ref, ids_ref, *outs, paired):
    win_ref, krope_ref, vis_ref = outs[:3]
    here = here_ref[0]
    tok = prev_ref.shape[0]
    win_ref[:tok, :] = prev_ref[:, :LAT]
    win_ref[tok:, :] = own_ref[:, :LAT]
    krope_ref[...] = jnp.zeros_like(krope_ref)
    krope_ref[:tok, :ROPE] = prev_ref[:, LAT:]
    krope_ref[tok:, :ROPE] = own_ref[:, LAT:]
    behind = jnp.maximum(here - 1, 0)
    seg_prev = jnp.where(here > 0, ids_ref[pl.ds(behind, 1), :], -1)
    seg_own = ids_ref[pl.ds(here, 1), :]
    row = lax.broadcasted_iota(jnp.int32, (tok, tok), 0)
    col = lax.broadcasted_iota(jnp.int32, (tok, tok), 1)
    seg_query = jnp.sum(jnp.where(row == col, seg_own, 0), 1, keepdims=True)
    vis_ref[:, :tok] = (seg_query == seg_prev).astype(F32)
    vis_ref[:, tok:] = ((seg_query == seg_own) & (col <= row)).astype(F32)
    if paired:
        source = lax.broadcasted_iota(jnp.int32, (LAT, LAT), 0)
        column = lax.broadcasted_iota(jnp.int32, (LAT, LAT), 1)
        place = column >> 6
        apart = ((place & 1) << 2) | (place & 2) | (place >> 2)
        wanted = ((here ^ apart) << 6) | (column & 63)
        ordered = dot(win_ref[...], (source == wanted).astype(BF16), 1, 0).astype(BF16)
        outs[3][...] = ordered[:, : LAT // 2]
        outs[4][...] = ordered[:, LAT // 2 :]


def key_window(here, prev, own, ids, paired):
    tok = prev.shape[0]
    whole = lambda i, here: (0, 0)
    shapes = [((2 * tok, LAT), BF16), ((2 * tok, LANES), BF16), ((tok, 2 * tok), F32)]
    if paired:
        shapes = shapes + [((2 * tok, LAT // 2), BF16)] * 2
    return pl.pallas_call(
        functools.partial(window_kernel, paired=paired),
        grid_spec=pltpu.PrefetchScalarGridSpec(
            num_scalar_prefetch=1,
            grid=(1,),
            in_specs=[pl.BlockSpec(array.shape, whole) for array in (prev, own, ids)],
            out_specs=[pl.BlockSpec(shape, whole) for shape, _ in shapes],
        ),
        out_shape=[jax.ShapeDtypeStruct(*shape) for shape in shapes],
        compiler_params=PARAMS,
        cost_estimate=cost(WINDOW),
        name="key_window",
    )(here, prev, own, ids)


def attention_kernel(
    win_ref, krope_ref, vis_ref, wt_ref, qt_ref, gt_ref, *refs, aliased, extra
):
    latents_ref = refs[0] if extra else None
    refs = refs[1:] if extra else refs
    refs = refs[1:] if aliased else refs
    dq_ref, dkv_ref, rope_ref, dqn_ref, dqr_ref = refs
    i = pl.program_id(0)
    tok, heads = dq_ref.shape[:2]
    scale = 1.0 / math.sqrt(PLAIN_WIDTH + ROPE)

    @pl.when(i == 0)
    def _():
        rope_ref[...] = jnp.zeros_like(rope_ref)
        if extra:
            dkv_ref[:, heads * PAIR :] = latents_ref[...]

    visible = vis_ref[...] > 0.0
    window = win_ref[...]
    krope = krope_ref[...]
    count = wt_ref.shape[0]
    keys, values = [], []
    for h in range(count):
        kv = dot(window, wt_ref[h], 1, 0).astype(BF16)
        keys.append(jnp.concatenate([kv[:, :PLAIN_WIDTH], krope], 1))
        values.append(kv[:, PLAIN_WIDTH:])
    scores = [dot(qt_ref[h], keys[h], 1, 1) for h in range(count)]
    dprobs = [dot(gt_ref[h], values[h], 1, 1) for h in range(count)]
    dscores, probs16 = [], []
    for h in range(count):
        logits = jnp.where(visible, scores[h] * scale, -1e30)
        top = jnp.max(logits, -1, keepdims=True)
        expo = jnp.exp(logits - top)
        probs = expo / jnp.sum(expo, -1, keepdims=True)
        delta = jnp.sum(probs * dprobs[h], -1, keepdims=True)
        dscores.append((probs * (dprobs[h] - delta) * scale).astype(BF16))
        probs16.append(probs.astype(BF16))
    parts, rope = [], rope_ref[...]
    for h in range(count):
        dk = dot(dscores[h], qt_ref[h], 0, 0)
        dv = dot(probs16[h], gt_ref[h], 0, 0)
        parts.append(jnp.concatenate([dk[:, :PLAIN_WIDTH], dv], 1).astype(BF16))
        rope = rope + dk[:, PLAIN_WIDTH:]
    rope_ref[...] = rope
    dkv_ref[:, pl.ds(pl.multiple_of(i * (count * PAIR), count * PAIR), count * PAIR)] = (
        jnp.concatenate(parts, 1)
    )
    for h in range(count):
        dq = dot(dscores[h], keys[h], 1, 0)
        dqn_ref[pl.ds(i * count + h, tok, stride=heads), :] = dq[:, :PLAIN_WIDTH]
        dqr_ref[pl.ds(i * count + h, tok, stride=heads), :] = dq[:, PLAIN_WIDTH:]

    @pl.when(i == pl.num_programs(0) - 1)
    def _():
        dq_ref[:, :, :PLAIN_WIDTH] = dqn_ref[...].reshape(tok, heads, LANES)
        dq_ref[:, :, PLAIN_WIDTH:] = dqr_ref[...].reshape(tok, heads, LANES)[:, :, :ROPE]


def attention(window, turned, latents, dq, chunk, heads, first, all_heads):
    weight, queries, out_grad = turned
    tok = queries.shape[1]
    width = 2 * tok
    steps = heads // STEP_HEADS
    at = first // STEP_HEADS
    extra = LAT // 2 if latents is not None else 0
    whole = lambda i: (0, 0)
    head_block = lambda i: (at + i, 0, 0)
    operands = [*window, weight, queries, out_grad]
    in_specs = [pl.BlockSpec(array.shape, whole) for array in window] + [
        pl.BlockSpec((STEP_HEADS, LAT, PAIR), head_block),
        pl.BlockSpec((STEP_HEADS, tok, 2 * LANES), head_block),
        pl.BlockSpec((STEP_HEADS, tok, VDIM), head_block),
    ]
    if latents is not None:
        in_specs.append(pl.BlockSpec(latents.shape, whole))
        operands.append(latents)
    aliases = {}
    if dq is not None:
        aliases = {len(operands): 0}
        in_specs.append(pl.BlockSpec(memory_space=pl.ANY))
        operands.append(dq)
    return pl.pallas_call(
        functools.partial(attention_kernel, aliased=dq is not None, extra=latents is not None),
        grid=(steps,),
        in_specs=in_specs,
        out_specs=[
            pl.BlockSpec((tok, heads, PLAIN_WIDTH + ROPE), lambda i: (0, chunk, 0)),
            pl.BlockSpec((width, heads * PAIR + extra), whole),
            pl.BlockSpec((width, LANES), whole),
        ],
        scratch_shapes=[
            pltpu.VMEM((tok * heads, LANES), F32),
            pltpu.VMEM((tok * heads, LANES), F32),
        ],
        out_shape=[
            jax.ShapeDtypeStruct((tok, all_heads, PLAIN_WIDTH + ROPE), F32),
            jax.ShapeDtypeStruct((width, heads * PAIR + extra), BF16),
            jax.ShapeDtypeStruct((width, LANES), F32),
        ],
        input_output_aliases=aliases,
        compiler_params=WIDE,
        cost_estimate=cost(CHUNK),
        name="attention",
    )(*operands)


def terms_kernel(
    own_ref, other_ref, mine_ref, theirs_ref, keep_ref, send_ref, latents_ref, *, along_x
):
    width = own_ref.shape[0]

    @pl.when(pl.program_id(0) == 0)
    def _():
        latents_ref[:, :width] = mine_ref[...].T
        latents_ref[:, width:] = theirs_ref[...].T

    grads = jnp.concatenate([own_ref[...], other_ref[...]], 0)
    term = dot(latents_ref[...], grads, 1, 0)
    rows = term.shape[0] // 4
    first, second = (1, 2) if along_x else (2, 1)
    keep_ref[:rows] = term[:rows]
    keep_ref[rows:] = term[first * rows : (first + 1) * rows]
    send_ref[:rows] = term[second * rows : (second + 1) * rows].astype(BF16)
    send_ref[rows:] = term[3 * rows :].astype(BF16)


def terms(own, other, mine, theirs, columns, along_x):
    width = own.shape[0]
    block = 1024
    at = theirs.shape[1] // (LAT // 2) - 1
    column_block = lambda i: (0, i)
    return pl.pallas_call(
        functools.partial(terms_kernel, along_x=along_x),
        grid=(columns // block,),
        in_specs=[
            pl.BlockSpec((width, block), column_block),
            pl.BlockSpec((width, block), column_block),
            pl.BlockSpec((width, LAT // 2), lambda i: (0, 0)),
            pl.BlockSpec((width, LAT // 2), lambda i: (0, at)),
        ],
        out_specs=[pl.BlockSpec((LAT // 4, block), column_block)] * 2,
        out_shape=[
            jax.ShapeDtypeStruct((LAT // 4, columns), F32),
            jax.ShapeDtypeStruct((LAT // 4, columns), BF16),
        ],
        scratch_shapes=[pltpu.VMEM((LAT // 2, 2 * width), BF16)],
        compiler_params=PARAMS,
        cost_estimate=cost(CHUNK),
        name="terms",
    )(own, other, mine, theirs)


def key_terms_kernel(*refs, chunks, steps, turns, shares):
    head_ref = refs[0]
    dkv_refs = refs[1 : 1 + chunks]
    wt_refs = refs[1 + chunks : 1 + chunks + turns]
    rope_refs = refs[1 + chunks + turns : 1 + 2 * chunks + turns]
    outs = refs[1 + 2 * chunks + turns : -1]
    total_ref = refs[-1]
    i = pl.program_id(0)

    @pl.when(i == 0)
    def _():
        total_ref[...] = jnp.zeros_like(total_ref)

    for k in range(chunks):

        @pl.when(i // steps == k)
        def _(k=k):
            total = total_ref[...]
            weight_ref = wt_refs[k * turns // chunks]
            for h in range(weight_ref.shape[0]):
                grads = dkv_refs[k][:, h * PAIR : (h + 1) * PAIR]
                total = total + dot(grads, weight_ref[h], 1, 1)
            total_ref[...] = total

    @pl.when(i == pl.num_programs(0) - 1)
    def _():
        rope = rope_refs[0][...]
        for k in range(1, chunks):
            rope = rope + rope_refs[k][...]
        both = jnp.concatenate([total_ref[...], rope], 1)
        if shares is None:
            outs[0][...] = both[:, : LAT + ROPE]
            return
        part = (LAT + ROPE) // shares
        for z in range(shares):
            piece = both[:, z * part : (z + 1) * part]
            for s in range(shares):

                @pl.when(lax.rem(head_ref[0] + s, shares) == z)
                def _(s=s, piece=piece):
                    outs[s][...] = piece


def key_terms(at_head, dkvs, weights, ropes, shares):
    chunks, turns = len(dkvs), len(weights)
    heads = weights[0].shape[0] * turns // chunks
    width = dkvs[0].shape[0]
    steps = heads // STEP_HEADS
    span = steps * chunks // turns
    near = lambda k, many: lambda i, at: jnp.clip(i - k * many, 0, many - 1)
    wide = (LAT + ROPE) // (shares or 1)
    return pl.pallas_call(
        functools.partial(
            key_terms_kernel, chunks=chunks, steps=steps, turns=turns, shares=shares
        ),
        grid_spec=pltpu.PrefetchScalarGridSpec(
            num_scalar_prefetch=1,
            grid=(chunks * steps,),
            in_specs=[
                pl.BlockSpec((width, STEP_HEADS * PAIR), lambda i, at, k=k: (0, near(k, steps)(i, at)))
                for k in range(chunks)
            ]
            + [
                pl.BlockSpec(
                    (STEP_HEADS, LAT, PAIR), lambda i, at, k=k: (near(k, span)(i, at), 0, 0)
                )
                for k in range(turns)
            ]
            + [pl.BlockSpec((width, LANES), lambda i, at: (0, 0))] * chunks,
            out_specs=[pl.BlockSpec((width, wide), lambda i, at: (0, 0))] * (shares or 1),
            scratch_shapes=[pltpu.VMEM((width, LAT), F32)],
        ),
        out_shape=[jax.ShapeDtypeStruct((width, wide), F32)] * (shares or 1),
        compiler_params=WIDE,
        cost_estimate=cost(CHUNK),
        name="key_terms",
    )(at_head, *dkvs, *weights, *ropes)


def weight_sum_kernel(keep_ref, first_ref, second_ref, *refs):
    out_ref, k_ref, v_ref = refs[-3:]
    rows, heads, _ = out_ref.shape
    for h in range(heads):
        columns = slice(h * PAIR, (h + 1) * PAIR)
        total = keep_ref[:, columns] + first_ref[:, columns].astype(F32)
        total = total + second_ref[:, columns].astype(F32)
        k_ref[pl.ds(h, rows, stride=heads), :] = total[:, :LANES]
        v_ref[pl.ds(h, rows, stride=heads), :] = total[:, LANES:]
    out_ref[:, :, :LANES] = k_ref[...].reshape(rows, heads, LANES)
    out_ref[:, :, LANES:] = v_ref[...].reshape(rows, heads, LANES)


def weight_sum(keep, first, second, total, chunk, all_heads):
    rows, columns = second.shape
    heads = columns // PAIR
    block = 32
    operands = [keep, first, second]
    in_specs = [pl.BlockSpec((block, columns), lambda i: (i, 0)) for _ in operands]
    aliases = {}
    if total is not None:
        aliases = {3: 0}
        in_specs.append(pl.BlockSpec(memory_space=pl.ANY))
        operands.append(total)
    return pl.pallas_call(
        weight_sum_kernel,
        grid=(rows // block,),
        in_specs=in_specs,
        out_specs=pl.BlockSpec((block, heads, PAIR), lambda i: (i, chunk, 0)),
        out_shape=jax.ShapeDtypeStruct((rows, all_heads, PAIR), F32),
        scratch_shapes=[pltpu.VMEM((block * heads, LANES), F32)] * 2,
        input_output_aliases=aliases,
        compiler_params=PARAMS,
        cost_estimate=cost(SUM),
        name="weight_sum",
    )(*operands)


def after(values, earlier):
    return lax.optimization_barrier((values, earlier))[0]


def turn_rows(block):
    rows, heads, width = block.shape
    count = min(rows, 256 // heads)
    row = lax.broadcasted_iota(jnp.int32, (count * heads, count * heads), 0)
    col = lax.broadcasted_iota(jnp.int32, (count * heads, count * heads), 1)
    order = (col == (row % count) * heads + row // count).astype(BF16)
    for start in range(0, rows, count):
        part = block[start : start + count].reshape(count * heads, width)
        turned = dot(order, part, 1, 0).astype(BF16)
        yield slice(start, start + count), turned.reshape(heads, count, width)


def in_hbm(array):
    return pltpu.with_memory_space_constraint(array, pltpu.HBM)


def turn_weight_kernel(here_ref, w_ref, wt_ref, held_ref, sem_ref):
    heads, depth = wt_ref.shape[0], wt_ref.shape[1]
    i = pl.program_id(0)
    first = pl.multiple_of((here_ref[0] & 1) * heads, heads)

    part = depth // 2

    def load(k):
        rows = pl.ds(pl.multiple_of(k * part, part), part)
        return pltpu.make_async_copy(
            w_ref.at[rows, pl.ds(first, heads), :], held_ref.at[rows], sem_ref.at[k]
        )

    @pl.when(i == 0)
    def _():
        for k in range(LAT // part):
            load(k).start()

    for k in range(2):
        load(2 * i + k).wait()
        block = held_ref[pl.ds(pl.multiple_of((2 * i + k) * part, part), part)]
        for rows, turned in turn_rows(block):
            wt_ref[:, k * part + rows.start : k * part + rows.stop, :] = turned


def turn_weight(here, up_weight, heads):
    steps = 4
    depth = LAT // steps
    return pl.pallas_call(
        turn_weight_kernel,
        grid_spec=pltpu.PrefetchScalarGridSpec(
            num_scalar_prefetch=1,
            grid=(steps,),
            in_specs=[pl.BlockSpec(memory_space=pl.ANY)],
            out_specs=pl.BlockSpec((heads, depth, PAIR), lambda i, here: (0, i, 0)),
            scratch_shapes=[
                pltpu.VMEM((LAT, heads, PAIR), BF16),
                pltpu.SemaphoreType.DMA((2 * steps,)),
            ],
        ),
        out_shape=jax.ShapeDtypeStruct((heads, LAT, PAIR), BF16),
        compiler_params=PARAMS,
        cost_estimate=cost(TURN),
        name="turn_weight",
    )(here, in_hbm(up_weight))


def turn_tokens_kernel(here_ref, q1_ref, g1_ref, q0_ref, g0_ref, own_ref, give_ref, mine_ref):
    heads = mine_ref.shape[0]
    for q_ref, g_ref, out_ref in ((q1_ref, g1_ref, give_ref), (q0_ref, g0_ref, mine_ref)):
        out_ref[:, :, LANES : 2 * LANES] = jnp.zeros_like(out_ref[:, :, LANES : 2 * LANES])
        for rows, turned in turn_rows(q_ref[...]):
            out_ref[:heads, rows, : PLAIN_WIDTH + ROPE] = turned
        for rows, turned in turn_rows(g_ref[...]):
            out_ref[:heads, rows, 2 * LANES :] = turned
    rest = LAT + ROPE - 3 * LANES
    give_ref[heads] = own_ref[:, : 3 * LANES]
    give_ref[heads + 1] = jnp.zeros_like(give_ref[heads + 1])
    give_ref[heads + 1, :, :rest] = own_ref[:, 3 * LANES :]


def turn_tokens(here, queries, out_grad, latent_keys, heads):
    tok = queries.shape[0]
    q_block, g_block = (tok, heads, PLAIN_WIDTH + ROPE), (tok, heads, VDIM)
    given = lambda i, here: (0, 1 - (here[0] & 1), 0)
    kept = lambda i, here: (0, here[0] & 1, 0)
    whole = lambda i, here: (0, 0, 0)
    give, mine = (heads + 2, tok, 3 * LANES), (heads, tok, 3 * LANES)
    queries, out_grad, latent_keys = (in_hbm(x) for x in (queries, out_grad, latent_keys))
    return pl.pallas_call(
        turn_tokens_kernel,
        grid_spec=pltpu.PrefetchScalarGridSpec(
            num_scalar_prefetch=1,
            grid=(1,),
            in_specs=[
                pl.BlockSpec(q_block, given),
                pl.BlockSpec(g_block, given),
                pl.BlockSpec(q_block, kept),
                pl.BlockSpec(g_block, kept),
                pl.BlockSpec(latent_keys.shape, lambda i, here: (0, 0)),
            ],
            out_specs=[pl.BlockSpec(give, whole), pl.BlockSpec(mine, whole)],
        ),
        out_shape=[jax.ShapeDtypeStruct(give, BF16), jax.ShapeDtypeStruct(mine, BF16)],
        compiler_params=PARAMS,
        cost_estimate=cost(WINDOW),
        name="turn_tokens",
    )(here, queries, out_grad, queries, out_grad, latent_keys)


def chip_window_kernel(
    here_ref, even_ref, odd_ref, own_ref, pal_ref, ids_ref, win_ref, krope_ref, vis_ref, lat_ref
):
    here = here_ref[0]
    tok = own_ref.shape[0]
    core, chip = here & 1, here >> 1
    first = core == 0
    prev = jnp.where(first, even_ref[...].astype(F32), odd_ref[...].astype(F32)).astype(BF16)
    pal = jnp.concatenate([pal_ref[0], pal_ref[1, :, : LAT + ROPE - 3 * LANES]], 1).astype(F32)
    own = own_ref[...].astype(F32)
    low = jnp.where(first, own, pal).astype(BF16)
    high = jnp.where(first, pal, own).astype(BF16)
    krope_ref[...] = jnp.zeros_like(krope_ref)
    for at, block in enumerate((prev, low, high)):
        win_ref[at * tok : (at + 1) * tok, :] = block[:, :LAT]
        krope_ref[at * tok : (at + 1) * tok, :ROPE] = block[:, LAT:]
    behind = ids_ref[pl.ds(jnp.maximum(chip - 1, 0), 1), :]
    both = ids_ref[pl.ds(chip, 1), :]
    seg = [jnp.where(chip > 0, behind[:, tok:], -1), both[:, :tok], both[:, tok:]]
    row = lax.broadcasted_iota(jnp.int32, (tok, tok), 0)
    col = lax.broadcasted_iota(jnp.int32, (tok, tok), 1)
    for b in range(2):
        seg_query = jnp.sum(jnp.where(row == col, seg[b + 1], 0), 1, keepdims=True)
        vis_ref[b, :, :tok] = (seg_query == seg[b]).astype(F32)
        vis_ref[b, :, tok:] = ((seg_query == seg[b + 1]) & (col <= row)).astype(F32)
    column = lax.broadcasted_iota(jnp.int32, (LAT, LAT), 0)
    source = lax.broadcasted_iota(jnp.int32, (LAT, LAT), 1)
    place = column >> 6
    apart = ((place & 1) << 2) | (place & 2) | (place >> 2)
    wanted = ((here ^ apart) << 6) | (column & 63)
    order = (source == wanted).astype(BF16)
    lat_ref[...] = dot(order, win_ref[...], 1, 1).astype(BF16)


def chip_window(here, even, odd, own, got, ids):
    tok = own.shape[0]
    whole = lambda i, here: (0, 0)
    return pl.pallas_call(
        chip_window_kernel,
        grid_spec=pltpu.PrefetchScalarGridSpec(
            num_scalar_prefetch=1,
            grid=(1,),
            in_specs=[pl.BlockSpec(array.shape, whole) for array in (even, odd, own)]
            + [
                pl.BlockSpec((2,) + got.shape[1:], lambda i, here: (got.shape[0] // 2 - 1, 0, 0)),
                pl.BlockSpec(ids.shape, whole),
            ],
            out_specs=[
                pl.BlockSpec((3 * tok, LAT), whole),
                pl.BlockSpec((3 * tok, LANES), whole),
                pl.BlockSpec((2, tok, 2 * tok), lambda i, here: (0, 0, 0)),
                pl.BlockSpec((LAT, 3 * tok), whole),
            ],
        ),
        out_shape=[
            jax.ShapeDtypeStruct((3 * tok, LAT), BF16),
            jax.ShapeDtypeStruct((3 * tok, LANES), BF16),
            jax.ShapeDtypeStruct((2, tok, 2 * tok), F32),
            jax.ShapeDtypeStruct((LAT, 3 * tok), BF16),
        ],
        compiler_params=PARAMS,
        cost_estimate=cost(WINDOW),
        name="chip_window",
    )(here, even, odd, own, got, ids)


def chunk_kernel(
    here_ref,
    win_ref,
    krope_ref,
    vis_ref,
    lat_ref,
    wt_ref,
    mine_ref,
    got_ref,
    *refs,
    chained,
    along_x,
):
    before_ref = refs[0] if chained else None
    refs = refs[3:] if chained else refs
    keep_ref, send_ref, key_ref, dq_ref, back_ref = refs

    @pl.when(pl.program_id(0) == 0)
    def _():
        key_ref[...] = before_ref[...] if chained else jnp.zeros_like(key_ref)

    tok = vis_ref.shape[1]
    heads = wt_ref.shape[0]
    first = (here_ref[0] & 1) == 0
    scale = 1.0 / math.sqrt(PLAIN_WIDTH + ROPE)
    window, krope = win_ref[...], krope_ref[...]
    visible = [vis_ref[b] > 0.0 for b in range(2)]
    keys, values, queries, grads = [], [], [], []
    for h in range(heads):
        kv = dot(window, wt_ref[h], 1, 0).astype(BF16)
        keys.append(jnp.concatenate([kv[:, :PLAIN_WIDTH], krope], 1))
        values.append(kv[:, PLAIN_WIDTH:])
        mine, got = mine_ref[h], got_ref[h]
        ordered = (jnp.where(first, mine, got), jnp.where(first, got, mine))
        queries.append([block[:, : 2 * LANES] for block in ordered])
        grads.append([block[:, 2 * LANES :] for block in ordered])
    reach = [slice(b * tok, (b + 2) * tok) for b in range(2)]
    units = [(h, b) for h in range(heads) for b in range(2)]
    scores = {(h, b): dot(queries[h][b], keys[h][reach[b]], 1, 1) for h, b in units}
    dprobs = {(h, b): dot(grads[h][b], values[h][reach[b]], 1, 1) for h, b in units}
    dscores, probs16 = {}, {}
    for unit in units:
        logits = jnp.where(visible[unit[1]], scores[unit] * scale, -1e30)
        top = jnp.max(logits, -1, keepdims=True)
        expo = jnp.exp(logits - top)
        probs = expo / jnp.sum(expo, -1, keepdims=True)
        delta = jnp.sum(probs * dprobs[unit], -1, keepdims=True)
        dscores[unit] = (probs * (dprobs[unit] - delta) * scale).astype(BF16)
        probs16[unit] = probs.astype(BF16)

    def fold(low, high):
        return jnp.concatenate([low[:tok], low[tok:] + high[:tok], high[tok:]], 0)

    parts, rope = [], None
    for h in range(heads):
        dk = fold(*[dot(dscores[h, b], queries[h][b], 0, 0) for b in range(2)])
        dv = fold(*[dot(probs16[h, b], grads[h][b], 0, 0) for b in range(2)])
        parts.append(jnp.concatenate([dk[:, :PLAIN_WIDTH], dv], 1).astype(BF16))
        rope = dk[:, PLAIN_WIDTH:] if rope is None else rope + dk[:, PLAIN_WIDTH:]
    dkv = jnp.concatenate(parts, 1)
    rows = lat_ref.shape[0] // 8

    def term(low, high):
        pair = [lat_ref[g * rows : (g + 1) * rows, :] for g in (low, high)]
        return dot(jnp.concatenate(pair, 0), dkv, 1, 0)

    for at, groups in enumerate(((2, 3), (6, 7)) if along_x else ((1, 3), (5, 7))):
        send_ref[2 * at * rows : 2 * (at + 1) * rows, :] = term(*groups).astype(BF16)
    for at, groups in enumerate(((0, 1), (4, 5)) if along_x else ((0, 2), (4, 6))):
        keep_ref[2 * at * rows : 2 * (at + 1) * rows, :] = term(*groups)
    total = key_ref[:, :LAT]
    for h in range(heads):
        total = total + dot(parts[h], wt_ref[h], 1, 1)
    key_ref[:, :LAT] = total
    key_ref[:, LAT:] = key_ref[:, LAT:] + rope
    for h in range(heads):
        low, high = (dot(dscores[h, b], keys[h][reach[b]], 1, 0) for b in range(2))
        dq_ref[h] = jnp.where(first, low, high)
        back_ref[h] = jnp.where(first, high, low)


def chunk(here, window, weight, mine, got, before, index, heads, along_x):
    tok = mine.shape[1]
    whole = lambda i, here: (0, 0)
    whole3 = lambda i, here: (0, 0, 0)
    step = min(heads, STEP_HEADS)
    steps = heads // step
    at = lambda i, here: (index * steps + i, 0, 0)
    across_columns = lambda i, here: (0, i)
    columns = heads * PAIR
    operands = [*window, weight, mine, got]
    in_specs = [
        pl.BlockSpec(array.shape, whole3 if array.ndim == 3 else whole) for array in window
    ] + [
        pl.BlockSpec((step, LAT, PAIR), at),
        pl.BlockSpec((step, tok, 3 * LANES), at),
        pl.BlockSpec((step, tok, 3 * LANES), at),
    ]
    aliases = {}
    if before is not None:
        key, dq, back = before
        aliases = {len(operands) + 2: 3, len(operands) + 3: 4}
        in_specs = in_specs + [
            pl.BlockSpec(key.shape, whole),
            pl.BlockSpec(memory_space=pl.ANY),
            pl.BlockSpec(memory_space=pl.ANY),
        ]
        operands = operands + [key, dq, back]
    turned = (weight.shape[0], tok, 2 * LANES)
    return pl.pallas_call(
        functools.partial(chunk_kernel, chained=before is not None, along_x=along_x),
        grid_spec=pltpu.PrefetchScalarGridSpec(
            num_scalar_prefetch=1,
            grid=(steps,),
            in_specs=in_specs,
            out_specs=[
                pl.BlockSpec((LAT // 2, step * PAIR), across_columns),
                pl.BlockSpec((LAT // 2, step * PAIR), across_columns),
                pl.BlockSpec((3 * tok, LAT + LANES), whole),
                pl.BlockSpec((step, tok, 2 * LANES), at),
                pl.BlockSpec((step, tok, 2 * LANES), at),
            ],
        ),
        out_shape=[
            jax.ShapeDtypeStruct((LAT // 2, columns), F32),
            jax.ShapeDtypeStruct((LAT // 2, columns), BF16),
            jax.ShapeDtypeStruct((3 * tok, LAT + LANES), F32),
            jax.ShapeDtypeStruct(turned, F32),
            jax.ShapeDtypeStruct(turned, F32),
        ],
        input_output_aliases=aliases,
        compiler_params=PARAMS,
        cost_estimate=cost(CHUNK),
        name="chunk",
    )(here, *operands)


def add_rows_kernel(*refs, count, wide):
    total = refs[0][...].astype(F32)
    for ref in refs[1 : count + wide]:
        total = total + ref[...].astype(F32)
    refs[-1][...] = total.astype(refs[-1].dtype)


def add_rows(arrays, rows, index, dtype, wide=(), place=0, places=1, before=None):
    columns = arrays[0].shape[1]
    operands = [*arrays, *wide]
    in_specs = [pl.BlockSpec((rows, columns), lambda i: (index, 0)) for _ in arrays]
    in_specs = in_specs + [pl.BlockSpec((rows, columns), lambda i: (index, place)) for _ in wide]
    aliases = {}
    if before is not None:
        aliases = {len(operands): 0}
        in_specs.append(pl.BlockSpec(memory_space=pl.ANY))
        operands.append(before)
    return pl.pallas_call(
        functools.partial(add_rows_kernel, count=len(arrays), wide=len(wide)),
        grid=(1,),
        in_specs=in_specs,
        out_specs=pl.BlockSpec((rows, columns), lambda i: (0, place)),
        out_shape=jax.ShapeDtypeStruct((rows, places * columns), dtype),
        input_output_aliases=aliases,
        compiler_params=PARAMS,
        cost_estimate=cost(SHARES),
        name="add_rows",
    )(*operands)


def key_split_kernel(here_ref, key_ref, keep_ref, give_ref):
    tok = keep_ref.shape[0] // 2
    first = (here_ref[0] & 1) == 0
    behind, low, high = (key_ref[b * tok : (b + 1) * tok, :] for b in range(3))
    keep_ref[:tok] = jnp.where(first, low, high)
    keep_ref[tok:] = behind
    give_ref[:tok] = jnp.where(first, high, low)
    give_ref[tok:] = behind


def key_split(here, key):
    rows = key.shape[0] // 3 * 2
    whole = lambda i, here: (0, 0)
    return pl.pallas_call(
        key_split_kernel,
        grid_spec=pltpu.PrefetchScalarGridSpec(
            num_scalar_prefetch=1,
            grid=(1,),
            in_specs=[pl.BlockSpec(key.shape, whole)],
            out_specs=[pl.BlockSpec((rows, key.shape[1]), whole)] * 2,
        ),
        out_shape=[jax.ShapeDtypeStruct((rows, key.shape[1]), F32)] * 2,
        compiler_params=PARAMS,
        cost_estimate=cost(SHARES),
        name="key_split",
    )(here, key)


def key_shares_kernel(at_ref, keep_ref, got_ref, *outs):
    shares = len(outs)
    part = (LAT + ROPE) // shares
    total = keep_ref[...] + got_ref[...]
    for z in range(shares):
        piece = total[:, z * part : (z + 1) * part]
        for s in range(shares):

            @pl.when(lax.rem(at_ref[0] + s, shares) == z)
            def _(s=s, piece=piece):
                outs[s][...] = piece.astype(outs[s].dtype)


def key_shares(at_head, keep, got, shares):
    part = (LAT + ROPE) // shares
    rows = keep.shape[0]
    whole = lambda i, at: (0, 0)
    types = [F32] + [BF16] * (shares - 1)
    return pl.pallas_call(
        key_shares_kernel,
        grid_spec=pltpu.PrefetchScalarGridSpec(
            num_scalar_prefetch=1,
            grid=(1,),
            in_specs=[pl.BlockSpec(keep.shape, whole)] * 2,
            out_specs=[pl.BlockSpec((rows, part), whole)] * shares,
        ),
        out_shape=[jax.ShapeDtypeStruct((rows, part), kind) for kind in types],
        compiler_params=PARAMS,
        cost_estimate=cost(SHARES),
        name="key_shares",
    )(at_head, keep, got)


def query_grad_kernel(here_ref, mine_ref, got_ref, out_ref, n_ref, r_ref):
    tok, heads, _ = out_ref.shape

    def put(src_ref):
        for h in range(heads):
            n_ref[pl.ds(h, tok, stride=heads), :] = src_ref[h, :, :PLAIN_WIDTH]
            r_ref[pl.ds(h, tok, stride=heads), :] = src_ref[h, :, PLAIN_WIDTH:]

    pl.when(pl.program_id(0) == 0)(lambda: put(mine_ref))
    pl.when(pl.program_id(0) == 1)(lambda: put(got_ref))
    out_ref[:, :, :PLAIN_WIDTH] = n_ref[...].reshape(tok, heads, LANES)
    out_ref[:, :, PLAIN_WIDTH:] = r_ref[...].reshape(tok, heads, LANES)[:, :, :ROPE]


def query_grad(here, mine, got):
    heads, tok, _ = mine.shape
    whole = lambda i, here: (0, 0, 0)
    return pl.pallas_call(
        query_grad_kernel,
        grid_spec=pltpu.PrefetchScalarGridSpec(
            num_scalar_prefetch=1,
            grid=(2,),
            in_specs=[pl.BlockSpec(mine.shape, whole)] * 2,
            out_specs=pl.BlockSpec(
                (tok, heads, PLAIN_WIDTH + ROPE), lambda i, here: (0, (here[0] & 1) ^ i, 0)
            ),
            scratch_shapes=[pltpu.VMEM((tok * heads, LANES), F32)] * 2,
        ),
        out_shape=jax.ShapeDtypeStruct((tok, 2 * heads, PLAIN_WIDTH + ROPE), F32),
        compiler_params=PARAMS,
        cost_estimate=cost(QUERY),
        name="query_grad",
    )(here, mine, got)


def second_send_kernel(*refs):
    *narrow, theirs_ref, out_ref = refs
    columns = narrow[0].shape[1]
    for c in range(len(narrow) // 2):
        total = narrow[2 * c][...] + narrow[2 * c + 1][...].astype(F32)
        out_ref[:, c * columns : (c + 1) * columns] = total.astype(BF16)
    out_ref[:, len(narrow) // 2 * columns :] = theirs_ref[...]


def second_send(groups, theirs, rows):
    narrow = [array for group in groups for array in group]
    columns = narrow[0].shape[1]
    wide = theirs.shape[1]
    return pl.pallas_call(
        second_send_kernel,
        grid=(1,),
        in_specs=[pl.BlockSpec((rows, columns), lambda i: (1, 0)) for _ in narrow]
        + [pl.BlockSpec((rows, wide), lambda i: (1, 0))],
        out_specs=pl.BlockSpec((rows, 2 * wide), lambda i: (0, 0)),
        out_shape=jax.ShapeDtypeStruct((rows, 2 * wide), BF16),
        compiler_params=PARAMS,
        cost_estimate=cost(SHARES),
        name="second_send",
    )(*narrow, theirs)


def last_sums_kernel(here_ref, *refs, order, count, wide):
    share_ref, behind_ref, out_ref, key_ref, k_ref, v_ref = refs[-6:]
    rows, heads, _ = out_ref.shape
    size = 2 * count + 2
    each = wide // PAIR
    key_ref[...] = share_ref[...] + behind_ref[...]

    def put(j, total):
        for h in range(each):
            at = pl.ds(j * each + h, rows, stride=heads)
            k_ref[at, :] = total[:, h * PAIR : h * PAIR + LANES]
            v_ref[at, :] = total[:, h * PAIR + LANES : (h + 1) * PAIR]

    for q, places in enumerate(order):
        for j, (pair, piece) in enumerate(places):
            group = refs[pair * size : (pair + 1) * size]
            kept, came = group[2 * piece : 2 * piece + 2]
            theirs_ref, last_ref = group[-2:]
            columns = slice(piece * wide, (piece + 1) * wide)
            later = slice((count + piece) * wide, (count + piece + 1) * wide)

            @pl.when(pl.program_id(0) == 2 * q)
            def _(j=j, kept=kept, came=came, last_ref=last_ref, columns=columns):
                total = kept[...] + came[...].astype(F32)
                put(j, total + last_ref[:, columns].astype(F32))

            @pl.when(pl.program_id(0) == 2 * q + 1)
            def _(j=j, theirs_ref=theirs_ref, last_ref=last_ref, columns=columns, later=later):
                put(j, theirs_ref[:, columns].astype(F32) + last_ref[:, later].astype(F32))

    out_ref[:, :, :LANES] = k_ref[...].reshape(rows, heads, LANES)
    out_ref[:, :, LANES:] = v_ref[...].reshape(rows, heads, LANES)


def last_sums(here, pieces, theirs, lasts, share, behind, order, wide):
    rows, heads = share.shape[0], len(order[0]) * wide // PAIR
    whole = lambda i, here: (0, 0)
    operands, in_specs = [], []
    for group, other, last in zip(pieces, theirs, lasts):
        for array, column in [part for piece in group for part in piece]:
            operands.append(array)
            in_specs.append(pl.BlockSpec((rows, wide), lambda i, here, column=column: (0, column)))
        for array in (other, last):
            operands.append(array)
            in_specs.append(pl.BlockSpec((rows, array.shape[1]), whole))
    in_specs = in_specs + [pl.BlockSpec(share.shape, whole)] * 2
    return pl.pallas_call(
        functools.partial(last_sums_kernel, order=order, count=len(pieces[0]), wide=wide),
        grid_spec=pltpu.PrefetchScalarGridSpec(
            num_scalar_prefetch=1,
            grid=(4,),
            in_specs=in_specs,
            out_specs=[
                pl.BlockSpec(
                    (rows, heads, PAIR),
                    lambda i, here: (0, ((here[0] & 1) ^ (i & 1)) * 2 + (i >> 1), 0),
                ),
                pl.BlockSpec(share.shape, whole),
            ],
            scratch_shapes=[pltpu.VMEM((rows * heads, LANES), F32)] * 2,
        ),
        out_shape=[
            jax.ShapeDtypeStruct((rows, 4 * heads, PAIR), F32),
            jax.ShapeDtypeStruct(share.shape, F32),
        ],
        compiler_params=PARAMS,
        cost_estimate=cost(SUM),
        name="last_sums",
    )(here, *operands, share, behind)


def in_chunks(queries, latent_keys, out_grad, up_weight, here, at_head, ids):
    tok = latent_keys.shape[0]
    n_ctx, n_head = lax.axis_size("ctx"), lax.axis_size("head")
    heads, each = 16, 4
    queries = after(queries, (ids, here, at_head))
    give, mine = turn_tokens(here, queries, out_grad, latent_keys, heads)
    odd_devices = range(1, n_ctx - 1, 2)
    even = lax.ppermute(latent_keys, "ctx", [(source, source + 1) for source in odd_devices])
    odd = lax.ppermute(latent_keys, "ctx", [(source, source + 2) for source in odd_devices])
    got = across(give, 1)
    weight = turn_weight(here, up_weight, heads)
    window = chip_window(here, even, odd, latent_keys, got, ids)
    ways, blocks = ((2, 4), (4, 2)), (0, 2, 1, 3)
    before, keeps, sent = None, [], []
    for c, block in enumerate(blocks):
        keep, out, *before = chunk(
            here, window, weight, mine, got, before, block, each, c % 2 == 0
        )
        keeps.append(keep)
        sent.append(across(out, ways[c % 2][0]))
    key, dq, back = before

    def rest(c, earlier):
        return add_rows(
            (keeps[c], sent[c]), 2 * tok, 1, BF16, place=c // 2, places=2, before=earlier
        )

    key_keep, key_give = key_split(here, key)
    key_got = across(key_give, 1)
    rests = [rest(0, None)]
    keeps[1] = after(keeps[1], rests[0])
    rests.append(rest(1, None))
    key_got = after(key_got, rests)
    shares = key_shares(at_head, key_keep, key_got, n_head)
    pieces = [
        lax.ppermute(shares[s], "head", [(z, (z + s) % n_head) for z in range(n_head)])
        for s in range(1, n_head)
    ]
    back = across(after(back, key_keep), 1)
    share, behind = (add_rows((shares[0], *pieces), tok, b, F32) for b in range(2))
    keeps[2] = after(keeps[2], (share, behind))
    behind = lax.ppermute(behind, "ctx", [(source, source - 1) for source in range(2, n_ctx, 2)])
    groups = [[(keeps[c], sent[c]) for c in (p, p + 2)] for p in range(2)]
    theirs, seconds, lasts = [], [], []
    for p in range(2):
        theirs.append(across(rest(p + 2, rests[p]), 1))
        seconds.append(second_send(groups[p], theirs[p], tok))
        lasts.append(across(seconds[p], ways[p][1]))
    dq = query_grad(here, after(dq, seconds), back)
    theirs = after(theirs, dq)
    theirs[1] = after(theirs[1], lasts[0])
    pieces = [[tuple((array, 0) for array in part) for part in group] for group in groups]
    order = (((0, 0), (0, 1)), ((1, 0), (1, 1)))
    weight_grad, key_grad = last_sums(
        here, pieces, theirs, lasts, share, behind, order, each * PAIR
    )
    return dq, key_grad, weight_grad


def shards(queries, latent_keys, out_grad, up_weight, segment_ids):
    tok = latent_keys.shape[0]
    heads = queries.shape[1]
    n_ctx, n_head = lax.axis_size("ctx"), lax.axis_size("head")
    here = lax.axis_index("ctx").astype(jnp.int32).reshape(1)
    at_head = lax.axis_index("head").astype(jnp.int32).reshape(1)
    if n_ctx == 8 and heads == 32 and n_head == 4:
        ids = segment_ids.reshape(n_ctx // 2, 2 * tok)
        return in_chunks(queries, latent_keys, out_grad, up_weight, here, at_head, ids)
    else:
        ids = segment_ids.reshape(n_ctx, tok)
        prev = from_behind(latent_keys, "ctx", REACH)
        turned = by_head(up_weight, queries, out_grad, 0, heads)
        window = key_window(here, prev, latent_keys, ids, False)
        dq, dkv, rope = attention(window, turned, None, None, 0, heads, 0, heads)
        (both,) = key_terms(at_head, [dkv], [turned[0]], [rope], None)
        share = lax.psum_scatter(
            both.reshape(REACH + 1, tok, LAT + ROPE), "head", scatter_dimension=2, tiled=True
        )
        term = jnp.einsum("ki,ke->ie", window[0], dkv, preferred_element_type=F32)
        rows = lax.psum_scatter(term.astype(BF16), "ctx", scatter_dimension=0, tiled=True)
        weight_grad = rows.astype(F32).reshape(rows.shape[0], heads, PAIR)
    key_grad = share[REACH] + from_behind(share[0], "ctx", 0 - REACH)
    return (dq, key_grad, weight_grad)


def solution(mesh):
    return jax.shard_map(
        shards,
        mesh=mesh,
        in_specs=(
            P("ctx", "head", None),
            P("ctx", None),
            P("ctx", "head", None),
            P(None, "head", None),
            P(),
        ),
        out_specs=(P("ctx", "head", None), P("ctx", "head"), P("ctx", "head", None)),
        check_vma=False,
    )
```
